32 devices in a mesh: samp: 4 (over x, core), blk: 8 (over z, y).
Axes of the slice: x: 2, y: 2, z: 4, core: 2. Of those that a mesh axis runs over, the one named last changes fastest.
Arguments:
- inputs: bfloat16 [4, 1024, 1024], P('samp', 'blk'), may hold values from -6 to 6
- cot_first: bfloat16 [4, 1024, 1024], P('samp', 'blk'), may hold values from -6 to 6
- cot_second: bfloat16 [4, 1024, 1024], P('samp', 'blk'), may hold values from -6 to 6
- valid_flags: int32 [4, 1024], P('samp', 'blk'), may hold values from 0 to 1, as said below
- lead_steps: int32 [2, 4], P(None, 'samp'), may hold values from 0 to 7
- masters: float32 [192, 256, 256], P('blk'), may hold values from -4 to 4
- assignment: int32 [192], replicated, may hold values from 0 to 191, as said below
- left_start: float32 [192, 256], P('blk'), may hold values from 256 to 1024
- right_start: float32 [192, 256], P('blk'), may hold values from 256 to 1024
- vectors: float32 [20, 1024], replicated, may hold values from -1.6 to 1.6
- vec_moment: float32 [20, 1024], replicated, may hold values from 0.5 to 8
Outputs:
- pred_first: bfloat16 [4, 1024, 1024], P('samp', 'blk')
- pred_second: bfloat16 [4, 1024, 1024], P('samp', 'blk')
- input_grad: float32 [4, 1024, 1024], P('samp', 'blk')
- matrix_grads: float32 [192, 256, 256], P('blk')
- left_stats: float32 [192, 256, 256], P('blk')
- right_stats: float32 [192, 256, 256], P('blk')
- new_masters: float32 [192, 256, 256], P('blk')
- new_copies: bfloat16 [192, 256, 256], P('blk')
- vec_grads: float32 [20, 1024], replicated
- vec_moments: float32 [20, 1024], replicated
- new_vectors: float32 [20, 1024], replicated
The draws below stay inside these ranges and needn't reach their ends.
Inputs may be any that keep to these rules, and one draw needn't show every extreme that they name: `valid_flags`: 1 where a patch has data; the first and the last patch of every sample are 1. `assignment`: a permutation of 0 to 191; slots are dealt to the devices of blk in order, 24 each.
All inputs are finite; a program needn't handle non-finite values.
Results may differ from the reference program's by a relative error of at most 0.02.
Values may be sent and summed in bfloat16 or wider, within the bound.
A program may use at most 320 MiB of HBM per device.

```python
import math
import jax
import jax.numpy as jnp
from jax import lax

D = 1024
HEADS = 16
FF = 4096
HD = 64
LEADS = 8
BS = 256
ITERS = 6
SAMPLES = 4
SEQ = 1024
NB = 192
NVEC = 20


def dealt(key):
    return jax.random.permutation(key, NB).astype(jnp.int32)


def draw_assignment(key, part):
    return dealt(key)


def draw_masters(key, part):
    ordering = dealt(key)
    key = jax.random.fold_in(key, 2)
    first_end = 3 * D * D // (BS * BS)
    second_end = first_end + D * D // (BS * BS)
    third_end = second_end + D * FF // (BS * BS)
    indices = jnp.arange(NB, dtype=jnp.int32)
    spreads = jnp.where(indices < first_end, (2.0 / D) ** 0.5, jnp.where(indices < second_end, (SEQ / (184.0 * D)) ** 0.5, jnp.where(indices < third_end, (1.0 / D) ** 0.5, (2.0 / FF) ** 0.5)))
    slot_spread = jnp.zeros((NB,), jnp.float32).at[ordering].set(spreads.astype(jnp.float32))
    key_rows, key_cols, key_noise = jax.random.split(key, 3)
    lower = math.log(0.216)
    upper = math.log(2.16)
    row_factor = jnp.exp(jax.random.uniform(key_rows, (NB, BS, 1), jnp.float32, lower, upper))
    col_factor = jnp.exp(jax.random.uniform(key_cols, (NB, 1, BS), jnp.float32, lower, upper))
    noise = jnp.clip(jax.random.normal(key_noise, (NB, BS, BS), jnp.float32), -4.0, 4.0)
    return slot_spread[:, None, None] * row_factor * col_factor * noise


def draw_valid_flags(key, part):
    key = jax.random.fold_in(key, 3)
    positions = jnp.arange(SEQ, dtype=jnp.int32)
    chance = 250 + 700 * positions // SEQ
    rolled = jax.random.randint(key, (SAMPLES, SEQ), 0, 1000, dtype=jnp.int32)
    edges = (positions == 0) | (positions == SEQ - 1)
    flags = (rolled < chance[None, :]) | edges[None, :]
    return flags.astype(jnp.int32)


def draw_vectors(key, part):
    key = jax.random.fold_in(key, 4)
    noise = jnp.clip(jax.random.normal(key, (NVEC, D), jnp.float32), -3.0, 3.0)
    row_ids = jnp.arange(NVEC, dtype=jnp.int32)[:, None]
    gains = 1.0 + 0.2 * noise
    biases = 0.3 * noise
    leads = 0.5 * noise
    is_gain = (row_ids == 0) | (row_ids == 5)
    is_lead = row_ids >= 8 + FF // D
    return jnp.where(is_gain, gains, jnp.where(is_lead, leads, biases))


def set_ends(result, stream_key, smallest, largest):
    longest = result.shape.index(max(result.shape))
    spots = []
    for shift in (0, 1):
        where = [jax.random.randint(jax.random.fold_in(stream_key, axis), (), 0, length) for axis, length in enumerate(result.shape)]
        where[longest] = (where[longest] + shift) % result.shape[longest]
        spots.append(tuple(where))
    return result.at[spots[0]].set(smallest).at[spots[1]].set(largest)


def steps_of(rng, dims, shards, low, top_value):
    level = 1.0
    for axis_at, parts in shards:
        steps = jax.random.uniform(jax.random.fold_in(jax.random.fold_in(rng, 6), axis_at), (parts,), jnp.float32, low / len(shards), top_value / len(shards))
        level = level * jnp.repeat(jnp.exp(steps), dims[axis_at] // parts).reshape((-1,) + (1,) * (len(dims) - 1 - axis_at))
    return level


def scatter_about(key, dims, scale, limit, cuts=(), held_as=jnp.bfloat16):
    level = steps_of(key, dims, cuts, -0.22, 0.18) if cuts else 1.0
    result = jax.random.normal(key, dims, jnp.float32) * scale * level
    return jnp.minimum(jnp.maximum(result, -limit), limit).astype(held_as)


def setup_inputs(seed: int = 0) -> dict:
    streams_of = jax.random.split(jax.random.key(seed), 12)
    inputs = scatter_about(streams_of[0], (SAMPLES, SEQ, D), 1.0, 6.0, ((0, 4), (1, 8)))
    cot_first = scatter_about(streams_of[1], (SAMPLES, SEQ, D), 1.0, 6.0, ((0, 4), (1, 8)))
    cot_second = scatter_about(streams_of[2], (SAMPLES, SEQ, D), 1.0, 6.0, ((0, 4), (1, 8)))
    valid_flags = draw_valid_flags(jax.random.fold_in(streams_of[11], 71), 0)
    lead_steps = set_ends(jax.random.randint(streams_of[4], (2, SAMPLES), 0, LEADS), jax.random.fold_in(streams_of[4], 1), 0, LEADS - 1).astype(jnp.int32)
    masters = draw_masters(jax.random.fold_in(streams_of[11], 71), 0)
    assignment = draw_assignment(jax.random.fold_in(streams_of[11], 71), 0)
    left_start = jnp.clip(jnp.exp(math.log(1024.0) - 1.3862944 * jax.random.uniform(streams_of[7], (NB, BS), jnp.float32) ** steps_of(streams_of[7], (NB, BS), ((0, 8),), -0.2, 0.2)), 256.0, 1024.0)
    right_start = jnp.clip(jnp.exp(math.log(1024.0) - 1.3862944 * jax.random.uniform(streams_of[8], (NB, BS), jnp.float32) ** steps_of(streams_of[8], (NB, BS), ((0, 8),), -0.2, 0.2)), 256.0, 1024.0)
    vectors = draw_vectors(jax.random.fold_in(streams_of[11], 71), 0)
    vec_moment = jnp.clip(jnp.exp(jax.random.uniform(streams_of[10], (NVEC, D), jnp.float32, math.log(0.5), math.log(8.0))), 0.5, 8.0)
    return dict(inputs=inputs, cot_first=cot_first, cot_second=cot_second, valid_flags=valid_flags, lead_steps=lead_steps, masters=masters, assignment=assignment, left_start=left_start, right_start=right_start, vectors=vectors, vec_moment=vec_moment)


HIGH = lax.Precision.HIGHEST
step_rate = 0.5
vector_rate = 0.3

@jax.custom_vjp
def low(v):
    return lax.optimization_barrier(v.astype(jnp.bfloat16)).astype(jnp.float32)

@jax.custom_vjp
def low_back(v):
    return v

def low_keep(v):
    return (low(v), None)

def low_pass(kept, grad):
    return (grad,)

def back_keep(v):
    return (v, None)

def back_low(kept, grad):
    return (low(grad),)
low.defvjp(low_keep, low_pass)
low_back.defvjp(back_keep, back_low)

def matmul(left_side, right_side):
    return jnp.dot(left_side, right_side, precision=HIGH, preferred_element_type=jnp.float32)

def assemble(blocks, height, breadth):
    return blocks.reshape(height // BS, breadth // BS, BS, BS).transpose(0, 2, 1, 3).reshape(height, breadth)

def unpack(blocks):
    first_end = 3 * D * D // (BS * BS)
    second_end = first_end + D * D // (BS * BS)
    third_end = second_end + D * FF // (BS * BS)
    qkv_weight = assemble(blocks[:first_end], D, 3 * D)
    out_weight = assemble(blocks[first_end:second_end], D, D)
    up_weight = assemble(blocks[second_end:third_end], D, FF)
    down_weight = assemble(blocks[third_end:], FF, D)
    return (qkv_weight, out_weight, up_weight, down_weight)

def norm_layer(value, gain, shift):
    centred = value - lax.optimization_barrier(jnp.mean(value, axis=-1, keepdims=True))
    spread = lax.optimization_barrier(jnp.mean(centred * centred, axis=-1, keepdims=True))
    return centred * lax.rsqrt(spread + 1e-06) * gain + shift

def attend(queries, keys_low, values_low, key_bias):
    scaling = HD ** (-0.5)

    def split_heads(tensor):
        return tensor.reshape(SEQ, HEADS, HD).transpose(1, 0, 2)

    def one_head(pieces):
        query_head, key_head, value_head = pieces
        scores = low_back(matmul(query_head, key_head.T) * scaling + key_bias[None, :])
        weights = jax.nn.softmax(scores, axis=-1)
        return matmul(low(weights), value_head)
    outcome = lax.map(jax.checkpoint(one_head), (split_heads(queries), split_heads(keys_low), split_heads(values_low)))
    return outcome.transpose(1, 0, 2).reshape(SEQ, D)

def layer_step(hidden_in, vecs, mats, lead_row, key_bias):
    qkv_weight, out_weight, up_weight, down_weight = mats
    hidden = hidden_in + lead_row[None, :]
    normed = low(norm_layer(hidden, vecs[0], vecs[1]))
    packed = matmul(normed, qkv_weight)
    queries = low(low_back(packed[:, :D] + vecs[2]))
    keys_low = low(low_back(packed[:, D:2 * D]))
    values_low = low(low_back(packed[:, 2 * D:] + vecs[3]))
    attended = low(low_back(attend(queries, keys_low, values_low, key_bias)))
    branch_one = low_back(matmul(attended, out_weight) + vecs[4])
    middle = hidden + branch_one
    normed_two = low(norm_layer(middle, vecs[5], vecs[6]))
    upward = low_back(matmul(normed_two, up_weight) + vecs[8:8 + FF // D].reshape(FF))
    activated = low(jax.nn.gelu(upward, approximate=False))
    branch_two = low_back(matmul(activated, down_weight) + vecs[7])
    return middle + branch_two

def chain(sample_in, vecs, blocks, sample_leads, sample_valid):
    mats = unpack(low(blocks))
    key_bias = (sample_valid.astype(jnp.float32) - 1.0) * 1000000000.0
    lead_base = 8 + FF // D
    earlier = layer_step(sample_in, vecs, mats, vecs[lead_base + sample_leads[0]], key_bias)
    later = layer_step(earlier, vecs, mats, vecs[lead_base + sample_leads[1]], key_bias)
    return (earlier, later)

def invert_root(stat):
    identity = jnp.eye(stat.shape[0], dtype=jnp.float32)
    frobenius = jnp.sqrt(jnp.sum(stat * stat))
    approx = identity * lax.rsqrt(jnp.sqrt(frobenius))
    moving = stat / frobenius
    for iteration in range(ITERS):
        factor = (5.0 * identity - moving) * 0.25
        approx = matmul(approx, factor)
        square = matmul(factor, factor)
        moving = matmul(matmul(square, square), moving)
    return approx

def precondition(gradient, left_diag, right_diag, weight):
    scaled = gradient * lax.rsqrt(jnp.mean(gradient * gradient) + 1e-06)
    identity = jnp.eye(BS, dtype=jnp.float32)
    left_new = 0.5 * identity * left_diag[None, :] + 0.5 * matmul(scaled, scaled.T)
    right_new = 0.5 * identity * right_diag[None, :] + 0.5 * matmul(scaled.T, scaled)
    direction = matmul(matmul(invert_root(left_new), scaled), invert_root(right_new))
    ratio = jnp.sqrt(jnp.mean(weight * weight)) * lax.rsqrt(jnp.mean(direction * direction) + 1e-06)
    return (left_new, right_new, weight - step_rate * ratio * direction)

def reference(inputs, cot_first, cot_second, valid_flags, lead_steps, masters, assignment, left_start, right_start, vectors, vec_moment):
    blocks = jnp.take(masters, assignment.astype(jnp.int32), axis=0)

    def per_sample(totals, pieces):
        sample_in, cot_one, cot_two, sample_valid, sample_leads = pieces

        def run_chain(start_rows, vec_rows, block_rows):
            return chain(start_rows, vec_rows, block_rows, sample_leads, sample_valid)
        outputs, pull_back = jax.vjp(run_chain, sample_in.astype(jnp.float32), vectors, blocks)
        grad_start, grad_vecs, grad_blocks = pull_back((cot_one.astype(jnp.float32), cot_two.astype(jnp.float32)))
        return ((totals[0] + grad_vecs, totals[1] + grad_blocks), (outputs[0].astype(jnp.bfloat16), outputs[1].astype(jnp.bfloat16), grad_start))
    start_totals = (jnp.zeros_like(vectors), jnp.zeros_like(blocks))
    sums, stacked = lax.scan(per_sample, start_totals, (inputs, cot_first, cot_second, valid_flags, lead_steps.T))
    vec_grads, block_grads = sums
    pred_first, pred_second, input_grad = stacked
    matrix_grads = jnp.zeros_like(block_grads).at[assignment.astype(jnp.int32)].set(block_grads)
    left_stats, right_stats, new_masters = jax.vmap(precondition)(matrix_grads, left_start, right_start, masters)
    scaled_vec = vec_grads * lax.rsqrt(lax.optimization_barrier(jnp.mean(vec_grads * vec_grads, axis=1, keepdims=True)) + 1e-06)
    vec_moments = 0.5 * vec_moment + 0.5 * scaled_vec * scaled_vec
    new_vectors = vectors - vector_rate * scaled_vec * lax.rsqrt(vec_moments)
    return (pred_first, pred_second, input_grad, matrix_grads, left_stats, right_stats, new_masters, new_masters.astype(jnp.bfloat16), vec_grads, vec_moments, new_vectors)
```

```python
import functools
import math

import jax
import ml_dtypes
import jax.numpy as jnp
from jax import lax
from jax.experimental import pallas as pl
from jax.experimental.pallas import tpu as pltpu
from jax.sharding import PartitionSpec as P

D = 1024
HEADS = 16
FF = 4096
HD = 64
LEADS = 8
BS = 256
ITERS = 6
NB = 192


HIGH = lax.Precision.HIGHEST
step_rate = 0.5
vector_rate = 0.3
masked = 1000000000.0


def assemble(blocks, height, breadth):
    return (
        blocks.reshape(height // BS, breadth // BS, BS, BS)
        .transpose(0, 2, 1, 3)
        .reshape(height, breadth)
    )


def carve(matrix):
    height, breadth = matrix.shape
    return (
        matrix.reshape(height // BS, BS, breadth // BS, BS)
        .transpose(0, 2, 1, 3)
        .reshape(-1, BS, BS)
    )


def unpack(blocks):
    first_end = 3 * D * D // (BS * BS)
    second_end = first_end + D * D // (BS * BS)
    third_end = second_end + D * FF // (BS * BS)
    qkv_weight = assemble(blocks[:first_end], D, 3 * D)
    out_weight = assemble(blocks[first_end:second_end], D, D)
    up_weight = assemble(blocks[second_end:third_end], D, FF)
    down_weight = assemble(blocks[third_end:], FF, D)
    return (qkv_weight, out_weight, up_weight, down_weight)


def norm_layer(value, gain, shift):
    centred = value - jnp.mean(value, axis=-1, keepdims=True)
    spread = jnp.mean(centred * centred, axis=-1, keepdims=True)
    return centred * lax.rsqrt(spread + 1e-06) * gain + shift


def gelu_exact(value):
    return jax.nn.gelu(value, approximate=False)


def heads_of(tensor):
    return tensor.reshape(tensor.shape[0], tensor.shape[1], HEADS, HD)


def split_rows(member, count, width):
    shaped = member.reshape((member.shape[0], count, width) + member.shape[2:])
    return jnp.moveaxis(shaped, 1, 0)


def in_blocks(update, carry, members, length):
    width = math.gcd(length, 1024)
    count = length // width
    if count == 1:
        return update(carry, members, 0)
    stacked = tuple([split_rows(member, count, width) for member in members])
    offsets = jnp.arange(count, dtype=jnp.int32) * width

    def advance(state, item):
        return (update(state, item[0], item[1]), None)

    result, unused = lax.scan(advance, carry, (stacked, offsets))
    return result


def forward_update(query_heads, scaling):

    def update(carry, members, offset):
        running_max, running_sum, weighted = carry
        key_part, value_part, flag_part = members
        bias = (flag_part.astype(jnp.float32) - 1.0) * masked
        scores = (
            jnp.einsum(
                "sqhd,skhd->shqk",
                query_heads,
                heads_of(key_part),
                preferred_element_type=jnp.float32,
            )
            * scaling
            + bias[:, None, None, :]
        )
        new_max = jnp.maximum(running_max, jnp.max(scores, axis=-1))
        shrink = jnp.exp(running_max - new_max)
        expos = jnp.exp(scores - new_max[..., None])
        running_sum = running_sum * shrink + jnp.sum(expos, axis=-1)
        weighted = weighted * shrink[..., None] + jnp.einsum(
            "shqk,skhd->shqd",
            expos.astype(jnp.bfloat16),
            heads_of(value_part),
            preferred_element_type=jnp.float32,
        )
        return (new_max, running_sum, weighted)

    return update


def query_grad_update(query_heads, dout_heads, log_total, inner, scaling):

    def update(carry, members, offset):
        key_part, value_part, flag_part = members
        bias = (flag_part.astype(jnp.float32) - 1.0) * masked
        scores = (
            jnp.einsum(
                "sqhd,skhd->shqk",
                query_heads,
                heads_of(key_part),
                preferred_element_type=jnp.float32,
            )
            * scaling
            + bias[:, None, None, :]
        )
        probs = jnp.exp(scores - log_total[..., None])
        dprobs = jnp.einsum(
            "sqhd,skhd->shqk", dout_heads, heads_of(value_part), preferred_element_type=jnp.float32
        )
        dscores = (probs * (dprobs - inner[..., None])).astype(jnp.bfloat16)
        return (
            carry
            + jnp.einsum(
                "shqk,skhd->sqhd", dscores, heads_of(key_part), preferred_element_type=jnp.float32
            )
            * scaling
        )

    return update


def key_grad_update(key_heads, value_heads, key_bias, total_rows, inner_rows, scaling, anchor):

    def update(carry, members, offset):
        grad_keys, grad_values = carry
        query_part, dout_part = members
        length = query_part.shape[1]
        total_part = jnp.transpose(
            lax.dynamic_slice_in_dim(total_rows, anchor + offset, length, 1), (0, 2, 1)
        )
        inner_part = jnp.transpose(
            lax.dynamic_slice_in_dim(inner_rows, anchor + offset, length, 1), (0, 2, 1)
        )
        query_heads = heads_of(query_part)
        dout_heads = heads_of(dout_part)
        scores = (
            jnp.einsum(
                "sqhd,skhd->shqk", query_heads, key_heads, preferred_element_type=jnp.float32
            )
            * scaling
            + key_bias[:, None, None, :]
        )
        probs = jnp.exp(scores - total_part[..., None])
        dprobs = jnp.einsum(
            "sqhd,skhd->shqk", dout_heads, value_heads, preferred_element_type=jnp.float32
        )
        dscores = (probs * (dprobs - inner_part[..., None])).astype(jnp.bfloat16)
        grad_values = grad_values + jnp.einsum(
            "shqk,sqhd->skhd",
            probs.astype(jnp.bfloat16),
            dout_heads,
            preferred_element_type=jnp.float32,
        )
        grad_keys = (
            grad_keys
            + jnp.einsum(
                "shqk,sqhd->skhd", dscores, query_heads, preferred_element_type=jnp.float32
            )
            * scaling
        )
        return (grad_keys, grad_values)

    return update


def invert_root(stat):
    identity = jnp.eye(stat.shape[0], dtype=jnp.float32)
    frobenius = jnp.sqrt(jnp.sum(stat * stat))
    approx = identity * lax.rsqrt(jnp.sqrt(frobenius))
    moving = stat / frobenius
    for iteration in range(ITERS):
        factor = (5.0 * identity - moving) * 0.25
        approx = jnp.dot(approx, factor, precision=HIGH)
        square = jnp.dot(factor, factor, precision=HIGH)
        moving = jnp.dot(jnp.dot(square, square, precision=HIGH), moving, precision=HIGH)
    return approx


def precondition(gradient, left_diag, right_diag, weight):
    scaled = gradient * lax.rsqrt(jnp.mean(gradient * gradient) + 1e-06)
    identity = jnp.eye(BS, dtype=jnp.float32)
    left_new = 0.5 * identity * left_diag[None, :] + 0.5 * jnp.dot(scaled, scaled.T, precision=HIGH)
    right_new = 0.5 * identity * right_diag[None, :] + 0.5 * jnp.dot(
        scaled.T, scaled, precision=HIGH
    )
    direction = jnp.dot(
        jnp.dot(invert_root(left_new), scaled, precision=HIGH),
        invert_root(right_new),
        precision=HIGH,
    )
    ratio = jnp.sqrt(jnp.mean(weight * weight)) * lax.rsqrt(jnp.mean(direction * direction) + 1e-06)
    return (left_new, right_new, weight - step_rate * ratio * direction)


MESH = pl.DeviceIdType.MESH
LOW = jnp.bfloat16
FULL = jnp.float32
VMEM_ASK = 60 * 1024 * 1024
GROUP = 24
HALF = 12
QUART = 4


def place():
    samp = lax.axis_index("samp")
    blk = lax.axis_index("blk")
    return (lax.div(samp, 2), lax.rem(samp, 2), lax.div(blk, 2), lax.rem(blk, 2))


def meet(devices):
    barrier = pltpu.get_barrier_semaphore()
    for device in devices:
        pl.semaphore_signal(barrier, inc=1, device_id=device, device_id_type=MESH)
    pl.semaphore_wait(barrier, len(devices))


def meet_all():
    barrier = pltpu.get_barrier_semaphore()
    samp = lax.axis_index("samp")
    blk = lax.axis_index("blk")

    def tell(at, carry):
        to = lax.rem(samp * 8 + blk + at, 32)
        pl.semaphore_signal(
            barrier, inc=1, device_id=(lax.div(to, 8), lax.rem(to, 8)), device_id_type=MESH
        )
        return carry

    lax.fori_loop(1, 32, tell, 0)
    pl.semaphore_wait(barrier, 31)


def turned_pair(n):
    return 2 * lax.rem(n, 2) + lax.div(n, 2)


class Swap:
    def __init__(self, local_sems, send_sems, recv_sems):
        x, c, z, y = place()
        self.stays = z == turned_pair(2 * x + c)
        self.to = (turned_pair(z), 2 * turned_pair(2 * x + c) + y)
        self.sems = (local_sems, send_sems, recv_sems)
        self.pairs = []

    def start(self, src, dst):
        at = len(self.pairs)
        local_sems, send_sems, recv_sems = self.sems
        local = pltpu.make_async_copy(src, dst, local_sems.at[at])
        away = pltpu.make_async_remote_copy(
            src_ref=src, dst_ref=dst, send_sem=send_sems.at[at], recv_sem=recv_sems.at[at],
            device_id=self.to, device_id_type=MESH,
        )
        self.pairs.append((local, away))

        @pl.when(self.stays)
        def keep():
            local.start()

        @pl.when(jnp.logical_not(self.stays))
        def send():
            away.start()

    def finish(self):
        @pl.when(self.stays)
        def kept():
            for local, away in self.pairs:
                local.wait()

        @pl.when(jnp.logical_not(self.stays))
        def sent():
            for local, away in self.pairs:
                away.wait()


def push(src, dst, send, recv, device):
    copy = pltpu.make_async_remote_copy(
        src_ref=src, dst_ref=dst, send_sem=send, recv_sem=recv, device_id=device, device_id_type=MESH
    )
    copy.start()
    return copy


FIRST, SECOND, BOTH, CROSS = range(4)
SIZES = (2, 2, 3, 1)


def weights_kernel(
    masters, notes, rows_in, out, notes_out, rows_out,
    wide, low, load_sems, local_sems, z_sems, y_sems, x_sems, core_sems, far_sems,
    swap_local, swap_send, swap_recv, note_send, note_recv,
):
    x, c, z, y = place()
    samp = 2 * x + c
    blk = 2 * z + y
    to_y = (samp, 2 * z + 1 - y)
    to_x = (2 * (1 - x) + c, blk)
    to_c = (2 * x + 1 - c, blk)
    base = c * HALF
    starts = (base + x * 8, base + x * 8 + 2, base + QUART, base + QUART + 3)
    far_starts = (base + (1 - x) * 8, base + (1 - x) * 8 + 2)
    parts = [
        (base + x * 8, QUART), (base + QUART, QUART), (base + (1 - x) * 8, QUART), ((1 - c) * HALF, HALF),
    ]
    loads = []
    for at, (start, size) in enumerate(parts):
        loads.append(
            pltpu.make_async_copy(masters.at[pl.ds(start, size)], wide.at[pl.ds(start, size)], load_sems.at[at])
        )
        loads[-1].start()
    meet_all()
    swap = Swap(swap_local, swap_send, swap_recv)
    swap.start(rows_in, rows_out)
    keeps = []

    def ready(at):
        start, size = parts[at]
        loads[at].wait()
        low[pl.ds(start, size)] = wide[pl.ds(start, size)].astype(LOW)
        keeps.append(
            pltpu.make_async_copy(
                low.at[pl.ds(start, size)], out.at[pl.ds(blk * GROUP + start, size)], local_sems.at[at]
            )
        )
        keeps[-1].start()

    def copy(src, group, start, size, sems, at, device):
        place_out = out.at[pl.ds(group * GROUP + start, size)]
        return pltpu.make_async_remote_copy(
            src_ref=place_out if src is None else src, dst_ref=place_out,
            send_sem=sems.at[(0,) + at], recv_sem=sems.at[(1,) + at], device_id=device, device_id_type=MESH,
        )

    def mine(kind):
        return low.at[pl.ds(starts[kind], SIZES[kind])]

    def z_copy(kind, way, origin, own=False):
        group = 2 * origin + y
        to = (samp, blk + (2 if way == 0 else -2))
        return copy(mine(kind) if own else None, group, starts[kind], SIZES[kind], z_sems, (kind, way, origin), to)

    def z_cross(way, origin, side, own=False):
        group = 2 * origin + side
        to = (samp, blk + (2 if way == 0 else -2))
        return copy(
            mine(CROSS) if own else None, group, starts[CROSS], 1, z_sems, (CROSS + side, way, origin), to
        )

    def y_copy(kind, origin, own=False):
        group = 2 * origin + y
        return copy(mine(kind) if own else None, group, starts[kind], SIZES[kind], y_sems, (kind, origin), to_y)

    def y_landed(kind, origin):
        group = 2 * origin + 1 - y
        return copy(None, group, starts[kind], SIZES[kind], y_sems, (kind, origin), to_y)

    def x_copy(kind, group):
        return copy(None, group, starts[kind], SIZES[kind], x_sems, (kind, group), to_x)

    def x_landed(kind, group):
        return copy(None, group, far_starts[kind], SIZES[kind], x_sems, (kind, group), to_x)

    def core_copy(kind, group):
        return copy(None, group, starts[kind], SIZES[kind], core_sems, (kind, group), to_c)

    def far_copy(kind, group):
        return copy(None, group, far_starts[kind], SIZES[kind], far_sems, (kind, group), to_c)

    def on_from_here(kind, group):
        if kind in (FIRST, SECOND):
            x_copy(kind, group).start()
        core_copy(kind, group).start()

    def begin(kind):
        @pl.when(z < 3)
        def up():
            z_copy(kind, 0, z, True).start()

        @pl.when(z > 0)
        def down():
            z_copy(kind, 1, z, True).start()

        y_copy(kind, z, True).start()

    def z_step(kind, distance):
        for way in (0, 1):
            origin = z - distance if way == 0 else z + distance

            @pl.when(origin >= 0 if way == 0 else origin <= 3)
            def arrived():
                z_copy(kind, way, origin).wait_recv()

                @pl.when(z < 3 if way == 0 else z > 0)
                def onward():
                    z_copy(kind, way, origin).start()

                y_copy(kind, origin).start()
                on_from_here(kind, 2 * origin + y)

    def y_step(kind, distance):
        for way in (0, 1):
            origin = z - distance if way == 0 else z + distance

            @pl.when(origin >= 0 if way == 0 else origin <= 3)
            def arrived():
                y_landed(kind, origin).wait_recv()
                on_from_here(kind, 2 * origin + 1 - y)

    def y_own(kind):
        y_landed(kind, z).wait_recv()
        on_from_here(kind, 2 * z + 1 - y)

    def cross_step(distance):
        for side in (0, 1):
            for way in (0, 1):
                origin = z - distance if way == 0 else z + distance

                @pl.when(origin >= 0 if way == 0 else origin <= 3)
                def arrived():
                    z_cross(way, origin, side).wait_recv()

                    @pl.when(z < 3 if way == 0 else z > 0)
                    def onward():
                        z_cross(way, origin, side).start()

                    core_copy(CROSS, 2 * origin + side).start()

    def x_step(kind, distance, same):
        for way in (0, 1):
            origin = z - distance if way == 0 else z + distance

            @pl.when(origin >= 0 if way == 0 else origin <= 3)
            def arrived():
                group = 2 * origin + (y if same else 1 - y)
                x_landed(kind, group).wait_recv()
                far_copy(kind, group).start()

    def x_own(kind):
        x_landed(kind, 2 * z + 1 - y).wait_recv()
        far_copy(kind, 2 * z + 1 - y).start()

    note_local = pltpu.make_async_copy(notes, notes_out.at[blk], local_sems.at[4])

    def note_copy(j, origin):
        return pltpu.make_async_remote_copy(
            src_ref=notes, dst_ref=notes_out.at[origin], send_sem=note_send.at[j], recv_sem=note_recv.at[origin],
            device_id=(j // 2, 2 * turned_pair(samp) + j % 2), device_id_type=MESH,
        )

    stays = z == turned_pair(samp)

    def is_me(j):
        return jnp.logical_and(stays, 2 * samp + y == j)

    def here_from(j):
        return jnp.logical_and(stays, blk == j)

    ready(0)
    begin(FIRST)
    begin(SECOND)
    ready(1)
    y_copy(CROSS, z, True).start()
    for j in range(8):

        @pl.when(jnp.logical_not(is_me(j)))
        def send_note():
            note_copy(j, blk).start()

    @pl.when(stays)
    def keep_note():
        note_local.start()

    ready(2)
    ready(3)
    z_step(FIRST, 1)
    y_own(FIRST)
    z_step(SECOND, 1)
    y_own(SECOND)
    begin(BOTH)
    y_landed(CROSS, z).wait_recv()
    core_copy(CROSS, 2 * z + 1 - y).start()
    for way, there in ((0, z < 3), (1, z > 0)):
        for side in (0, 1):
            @pl.when(jnp.logical_and(there, y == side))
            def own_side():
                z_cross(way, z, side, True).start()

            @pl.when(jnp.logical_and(there, y != side))
            def other_side():
                z_cross(way, z, side).start()

    z_step(FIRST, 2)
    y_step(FIRST, 1)
    z_step(SECOND, 2)
    y_step(SECOND, 1)
    x_own(FIRST)
    z_step(FIRST, 3)
    x_own(SECOND)
    y_step(FIRST, 2)
    z_step(SECOND, 3)
    x_step(FIRST, 1, True)
    y_step(SECOND, 2)
    x_step(SECOND, 1, True)
    y_step(FIRST, 3)
    y_step(SECOND, 3)
    z_step(BOTH, 1)
    x_step(FIRST, 1, False)
    x_step(FIRST, 2, True)
    y_own(BOTH)
    cross_step(1)
    x_step(SECOND, 1, False)
    x_step(SECOND, 2, True)
    z_step(BOTH, 2)
    x_step(FIRST, 3, True)
    y_step(BOTH, 1)
    cross_step(2)
    x_step(FIRST, 2, False)
    z_step(BOTH, 3)
    x_step(SECOND, 3, True)
    y_step(BOTH, 2)
    x_step(SECOND, 2, False)
    cross_step(3)
    x_step(FIRST, 3, False)
    y_step(BOTH, 3)
    x_step(SECOND, 3, False)

    other = (1 - c) * HALF
    other_starts = (other + x * 8, other + x * 8 + 2, other + QUART, other + QUART + 3)
    other_far = (other + (1 - x) * 8, other + (1 - x) * 8 + 2)

    def settle(group, carry):
        @pl.when(group != blk)
        def other_group():
            for kind in range(4):
                copy(None, group, other_starts[kind], SIZES[kind], core_sems, (kind, group), to_c).wait_recv()
                core_copy(kind, group).wait_send()
            for kind in (FIRST, SECOND):
                copy(None, group, other_far[kind], SIZES[kind], far_sems, (kind, group), to_c).wait_recv()
                far_copy(kind, group).wait_send()
                x_copy(kind, group).wait_send()

        return carry

    lax.fori_loop(0, 8, settle, 0)

    def sent_along(origin, carry):
        for kind in (FIRST, SECOND, BOTH):
            y_copy(kind, origin).wait_send()

            @pl.when(jnp.logical_and(origin <= z, z < 3))
            def up():
                z_copy(kind, 0, origin).wait_send()

            @pl.when(jnp.logical_and(origin >= z, z > 0))
            def down():
                z_copy(kind, 1, origin).wait_send()

        for side in (0, 1):
            @pl.when(jnp.logical_and(origin <= z, z < 3))
            def cross_up():
                z_cross(0, origin, side).wait_send()

            @pl.when(jnp.logical_and(origin >= z, z > 0))
            def cross_down():
                z_cross(1, origin, side).wait_send()

        return carry

    lax.fori_loop(0, 4, sent_along, 0)
    y_copy(CROSS, z).wait_send()
    for keep in keeps:
        keep.wait()
    swap.finish()
    for j in range(8):

        @pl.when(jnp.logical_not(is_me(j)))
        def sent_note():
            note_copy(j, blk).wait_send()

        @pl.when(jnp.logical_not(here_from(j)))
        def got_note():
            note_copy(j, j).wait_recv()

    @pl.when(stays)
    def kept_note():
        note_local.wait()


def gather_weights(masters, notes, rows):
    any_at = pl.BlockSpec(memory_space=pl.ANY)
    return pl.pallas_call(
        weights_kernel,
        out_shape=(
            jax.ShapeDtypeStruct((NB, BS, BS), LOW),
            jax.ShapeDtypeStruct((8,) + notes.shape, notes.dtype),
            jax.ShapeDtypeStruct(rows.shape, rows.dtype),
        ),
        in_specs=[any_at] * 3,
        out_specs=[any_at] * 3,
        scratch_shapes=[
            pltpu.VMEM((GROUP, BS, BS), FULL),
            pltpu.VMEM((GROUP, BS, BS), LOW),
            pltpu.SemaphoreType.DMA((4,)),
            pltpu.SemaphoreType.DMA((5,)),
            pltpu.SemaphoreType.DMA((2, 5, 2, 4)),
            pltpu.SemaphoreType.DMA((2, 4, 4)),
            pltpu.SemaphoreType.DMA((2, 2, 8)),
            pltpu.SemaphoreType.DMA((2, 4, 8)),
            pltpu.SemaphoreType.DMA((2, 2, 8)),
            pltpu.SemaphoreType.DMA((1,)),
            pltpu.SemaphoreType.DMA((1,)),
            pltpu.SemaphoreType.DMA((1,)),
            pltpu.SemaphoreType.DMA((8,)),
            pltpu.SemaphoreType.DMA((8,)),
        ],
        compiler_params=pltpu.CompilerParams(
            collective_id=0, has_side_effects=True, vmem_limit_bytes=VMEM_ASK
        ),
        name="gather_weights",
    )(masters, notes, rows)


def local_any(
    inputs,
    cot_first,
    cot_second,
    valid_flags,
    lead_steps,
    masters,
    assignment,
    left_start,
    right_start,
    vectors,
    vec_moment,
):
    copies = lax.all_gather(masters.astype(jnp.bfloat16), "blk", axis=0, tiled=True)
    blocks = jnp.take(copies, assignment, axis=0)
    qkv_weight, out_weight, up_weight, down_weight = unpack(blocks)
    scaling = HD ** (-0.5)
    flags_low = valid_flags.astype(jnp.bfloat16)
    key_bias = (valid_flags.astype(jnp.float32) - 1.0) * masked
    lead_base = 8 + FF // D
    lead_table = vectors[lead_base:]
    samples = inputs.shape[0]
    patches = inputs.shape[1]

    def forward(hidden_in, lead_ids):
        chosen = (lead_ids[:, None] == jnp.arange(LEADS, dtype=jnp.int32)[None, :]).astype(
            jnp.float32
        )
        lead_rows = jnp.dot(chosen, lead_table, precision=HIGH)
        hidden = hidden_in + lead_rows[:, None, :]
        normed_low = norm_layer(hidden, vectors[0], vectors[1]).astype(jnp.bfloat16)
        packed = jnp.einsum(
            "spd,de->spe", normed_low, qkv_weight, preferred_element_type=jnp.float32
        )
        queries = (packed[..., :D] + vectors[2]).astype(jnp.bfloat16)
        keys_low = packed[..., D : 2 * D].astype(jnp.bfloat16)
        values_low = (packed[..., 2 * D :] + vectors[3]).astype(jnp.bfloat16)
        start_state = (
            jnp.full((samples, HEADS, patches), -1e30, jnp.float32),
            jnp.zeros((samples, HEADS, patches), jnp.float32),
            jnp.zeros((samples, HEADS, patches, HD), jnp.float32),
        )
        update = forward_update(heads_of(queries), scaling)
        gathered = None
        piece = (
            lax.all_gather(keys_low, "blk", axis=1, tiled=True),
            lax.all_gather(values_low, "blk", axis=1, tiled=True),
            lax.all_gather(flags_low, "blk", axis=1, tiled=True),
        )
        running_max, running_sum, weighted = in_blocks(
            update, start_state, piece, piece[0].shape[1]
        )
        attended = jnp.transpose(weighted / running_sum[..., None], (0, 2, 1, 3)).reshape(
            samples, patches, D
        )
        log_total = running_max + jnp.log(running_sum)
        attended_low = attended.astype(jnp.bfloat16)
        middle = (
            hidden
            + jnp.einsum(
                "spd,de->spe", attended_low, out_weight, preferred_element_type=jnp.float32
            )
            + vectors[4]
        )
        normed_two = norm_layer(middle, vectors[5], vectors[6]).astype(jnp.bfloat16)
        upward = jnp.einsum(
            "spd,df->spf", normed_two, up_weight, preferred_element_type=jnp.float32
        ) + vectors[8:lead_base].reshape(FF)
        activated = gelu_exact(upward).astype(jnp.bfloat16)
        result = (
            middle
            + jnp.einsum("spf,fd->spd", activated, down_weight, preferred_element_type=jnp.float32)
            + vectors[7]
        )
        saved = (
            hidden,
            normed_low,
            queries,
            keys_low,
            values_low,
            attended,
            attended_low,
            log_total,
            middle,
            normed_two,
            upward,
            activated,
            chosen,
            gathered,
        )
        return (result, saved)

    def backward(grad_out, saved):
        (
            hidden,
            normed_low,
            queries,
            keys_low,
            values_low,
            attended,
            attended_low,
            log_total,
            middle,
            normed_two,
            upward,
            activated,
            chosen,
            gathered,
        ) = saved
        grad_two = grad_out.astype(jnp.bfloat16)
        down_grad = jnp.einsum(
            "spf,spd->fd", activated, grad_two, preferred_element_type=jnp.float32
        )
        down_bias = jnp.sum(grad_two.astype(jnp.float32), axis=(0, 1))
        grad_act = jnp.einsum(
            "spd,fd->spf", grad_two, down_weight, preferred_element_type=jnp.float32
        )
        gelu_value, gelu_pull = jax.vjp(gelu_exact, upward)
        grad_up = gelu_pull(grad_act)[0].astype(jnp.bfloat16)
        up_grad = jnp.einsum("spd,spf->df", normed_two, grad_up, preferred_element_type=jnp.float32)
        up_bias = jnp.sum(grad_up.astype(jnp.float32), axis=(0, 1))
        grad_normed_two = jnp.einsum(
            "spf,df->spd", grad_up, up_weight, preferred_element_type=jnp.float32
        )
        norm_value, norm_pull = jax.vjp(norm_layer, middle, vectors[5], vectors[6])
        grad_middle_norm, gain_two, shift_two = norm_pull(grad_normed_two)
        grad_middle = grad_out + grad_middle_norm
        grad_one = grad_middle.astype(jnp.bfloat16)
        out_grad = jnp.einsum(
            "spd,spe->de", attended_low, grad_one, preferred_element_type=jnp.float32
        )
        out_bias = jnp.sum(grad_one.astype(jnp.float32), axis=(0, 1))
        grad_attended = jnp.einsum(
            "spe,de->spd", grad_one, out_weight, preferred_element_type=jnp.float32
        ).astype(jnp.bfloat16)
        inner = jnp.sum(
            (grad_attended.astype(jnp.float32) * attended).reshape(samples, patches, HEADS, HD),
            axis=-1,
        )
        inner_heads = jnp.transpose(inner, (0, 2, 1))
        zero_query = jnp.zeros((samples, patches, HEADS, HD), jnp.float32)
        update_query = query_grad_update(
            heads_of(queries), heads_of(grad_attended), log_total, inner_heads, scaling
        )
        piece = (
            lax.all_gather(keys_low, "blk", axis=1, tiled=True),
            lax.all_gather(values_low, "blk", axis=1, tiled=True),
            lax.all_gather(flags_low, "blk", axis=1, tiled=True),
        )
        grad_query = in_blocks(update_query, zero_query, piece, piece[0].shape[1])
        total_rows, inner_rows = (
            lax.all_gather(jnp.transpose(log_total, (0, 2, 1)), "blk", axis=1, tiled=True),
            lax.all_gather(inner, "blk", axis=1, tiled=True),
        )
        key_heads = heads_of(keys_low)
        value_heads = heads_of(values_low)
        zero_pair = (zero_query, zero_query)
        piece = (
            lax.all_gather(queries, "blk", axis=1, tiled=True),
            lax.all_gather(grad_attended, "blk", axis=1, tiled=True),
        )
        update_keys = key_grad_update(
            key_heads, value_heads, key_bias, total_rows, inner_rows, scaling, jnp.int32(0)
        )
        grad_keys, grad_values = in_blocks(update_keys, zero_pair, piece, piece[0].shape[1])
        grad_packed = jnp.concatenate(
            [
                grad_query.reshape(samples, patches, D),
                grad_keys.reshape(samples, patches, D),
                grad_values.reshape(samples, patches, D),
            ],
            axis=-1,
        ).astype(jnp.bfloat16)
        qkv_grad = jnp.einsum(
            "spd,spe->de", normed_low, grad_packed, preferred_element_type=jnp.float32
        )
        query_bias = jnp.sum(grad_packed[..., :D].astype(jnp.float32), axis=(0, 1))
        value_bias = jnp.sum(grad_packed[..., 2 * D :].astype(jnp.float32), axis=(0, 1))
        grad_normed = jnp.einsum(
            "spe,de->spd", grad_packed, qkv_weight, preferred_element_type=jnp.float32
        )
        first_value, first_pull = jax.vjp(norm_layer, hidden, vectors[0], vectors[1])
        grad_hidden_norm, gain_one, shift_one = first_pull(grad_normed)
        grad_hidden = grad_middle + grad_hidden_norm
        lead_grad = jnp.dot(chosen.T, jnp.sum(grad_hidden, axis=1), precision=HIGH)
        vec_rows = jnp.concatenate(
            [
                gain_one[None],
                shift_one[None],
                query_bias[None],
                value_bias[None],
                out_bias[None],
                gain_two[None],
                shift_two[None],
                down_bias[None],
                up_bias.reshape(FF // D, D),
                lead_grad,
            ],
            axis=0,
        )
        return (grad_hidden, (qkv_grad, out_grad, up_grad, down_grad), vec_rows)

    earlier, saved_one = forward(inputs.astype(jnp.float32), lead_steps[0])
    later, saved_two = forward(earlier, lead_steps[1])
    grad_between, mats_two, vec_two = backward(cot_second.astype(jnp.float32), saved_two)
    input_grad, mats_one, vec_one = backward(
        cot_first.astype(jnp.float32) + grad_between, saved_one
    )
    grad_blocks = jnp.concatenate(
        [
            carve(mats_one[0] + mats_two[0]),
            carve(mats_one[1] + mats_two[1]),
            carve(mats_one[2] + mats_two[2]),
            carve(mats_one[3] + mats_two[3]),
        ],
        axis=0,
    )
    position = jnp.arange(NB, dtype=jnp.int32)
    inverse = jnp.sum(
        jnp.where(assignment[None, :] == position[:, None], position[None, :], 0), axis=1
    )
    slotted = jnp.take(grad_blocks, inverse, axis=0)
    shared = lax.psum_scatter(slotted, "blk", scatter_dimension=0, tiled=True)
    matrix_grads = lax.psum(shared.astype(jnp.bfloat16), "samp").astype(jnp.float32)
    vec_grads = lax.psum(vec_one + vec_two, ("samp", "blk"))
    left_stats, right_stats, new_masters = jax.vmap(precondition)(
        matrix_grads, left_start, right_start, masters
    )
    scaled_vec = vec_grads * lax.rsqrt(
        jnp.mean(vec_grads * vec_grads, axis=1, keepdims=True) + 1e-06
    )
    vec_moments = 0.5 * vec_moment + 0.5 * scaled_vec * scaled_vec
    new_vectors = vectors - vector_rate * scaled_vec * lax.rsqrt(vec_moments)
    return (
        earlier.astype(jnp.bfloat16),
        later.astype(jnp.bfloat16),
        input_grad,
        matrix_grads,
        left_stats,
        right_stats,
        new_masters,
        new_masters.astype(jnp.bfloat16),
        vec_grads,
        vec_moments,
        new_vectors,
    )


TOKENS = 128
PAIR = 2 * HD
SEQ_ALL = 8 * TOKENS
QKV_AT, OUT_AT, UP_AT, DOWN_AT = 0, 48, 64, 128
WIDE = D // BS
DEEP = FF // BS
LEAD_AT = 8 + FF // D


def dot(left, right):
    return jnp.dot(left, right, preferred_element_type=FULL)


def dot_t(left, right):
    return lax.dot_general(left, right, (((1,), (1,)), ((), ())), preferred_element_type=FULL)


def fetch(copies, slots, base, rows, cols, target, sem):
    def start(at, carry):
        row = lax.div(at, cols)
        pltpu.make_async_copy(
            copies.at[slots[base + at]], target(row, at - row * cols), sem
        ).start()
        return carry

    lax.fori_loop(0, rows * cols, start, 0)


def fetch_qkv(copies, slots, held, sem):
    fetch(copies, slots, QKV_AT, WIDE, 3 * WIDE, lambda k, n: held.at[n, pl.ds(k * BS, BS)], sem)


def fetch_out(copies, slots, held, sem):
    fetch(
        copies, slots, OUT_AT, WIDE, WIDE, lambda k, n: held.at[pl.ds(k * BS, BS), pl.ds(n * BS, BS)], sem
    )


def fetch_up(copies, slots, held, sem):
    fetch(copies, slots, UP_AT, WIDE, DEEP, lambda k, n: held.at[n, pl.ds(k * BS, BS)], sem)


def fetch_down(copies, slots, held, sem):
    fetch(copies, slots, DOWN_AT, DEEP, WIDE, lambda k, n: held.at[k, :, pl.ds(n * BS, BS)], sem)


def landed(held, sem):
    pltpu.make_async_copy(held, held, sem).wait()


def normal(value):
    centred = value - jnp.mean(value, axis=-1, keepdims=True)
    rate = lax.rsqrt(jnp.mean(centred * centred, axis=-1, keepdims=True) + 1e-06)
    return (centred * rate, rate)


def normal_back(grad, unit, rate, gain):
    scaled = grad * gain
    return rate * (
        scaled
        - jnp.mean(scaled, axis=-1, keepdims=True)
        - unit * jnp.mean(scaled * unit, axis=-1, keepdims=True)
    )


def total(value):
    return jnp.sum(value, axis=0, keepdims=True)


def gelu_parts(value):
    phi = 0.5 + 0.5 * lax.erf(value * (0.5**0.5))
    return phi, value * phi


def gelu_slope(value):
    phi, unused = gelu_parts(value)
    return phi + value * jnp.exp(-0.5 * value * value) * ((2.0 * math.pi) ** -0.5)


def project(hidden, vecs, qkv, a_out, packed_out):
    unit, unused = normal(hidden)
    normed = unit * vecs[0:1] + vecs[1:2]
    for k in range(WIDE):
        a_out[k] = normed[:, k * BS : (k + 1) * BS].T.astype(LOW)
    normed = normed.astype(LOW)
    for n in range(3 * WIDE):
        part = dot(normed, qkv[n])
        kind, within = divmod(n, WIDE)
        if kind != 1:
            row = 2 if kind == 0 else 3
            part = part + vecs[row : row + 1, within * BS : (within + 1) * BS]
        part = part.astype(LOW)
        for half in range(2):
            packed_out[2 * within + half, :, kind * PAIR : (kind + 1) * PAIR] = part[
                :, half * PAIR : (half + 1) * PAIR
            ]


def feed(hidden, o_in, vecs, out_w, up, down, sems, o_out, n2_out, act_out, u_out, act_held):
    landed(out_w, sems.at[0])
    attended = jnp.concatenate([o_in[j] for j in range(8)], axis=1)
    for k in range(WIDE):
        o_out[k] = attended[:, k * BS : (k + 1) * BS].astype(FULL).T.astype(LOW)
    middle = hidden + dot(attended, out_w[...]) + vecs[4:5]
    unit, unused = normal(middle)
    normed = unit * vecs[5:6] + vecs[6:7]
    for k in range(WIDE):
        n2_out[k] = normed[:, k * BS : (k + 1) * BS].T.astype(LOW)
    normed = normed.astype(LOW)
    landed(up, sems.at[1])
    per = D // BS
    for f in range(DEEP):
        bias = vecs[8 + f // per : 9 + f // per, (f % per) * BS : (f % per + 1) * BS]
        upward = dot(normed, up[f]) + bias
        u_out[f] = upward
        activated = gelu_parts(upward)[1]
        act_held[f] = activated.astype(LOW)
        act_out[f] = activated.T.astype(LOW)
    landed(down, sems.at[2])
    result = middle + vecs[7:8]
    for f in range(DEEP):
        result = result + dot(act_held[f], down[f])
    return middle, result


def feed_back(grad_out, middle, u_in, vecs, out_w, up, down, du_out, dz1_out, dz2_out, do_out, rows):
    grad_two = grad_out.astype(LOW)
    for k in range(WIDE):
        dz2_out[k] = grad_two[:, k * BS : (k + 1) * BS]
    rows[7:8] += total(grad_two.astype(FULL))
    per = D // BS
    grad_normed = None
    for f in range(DEEP):
        grad_act = dot_t(grad_two, down[f])
        grad_up = (grad_act * gelu_slope(u_in[f])).astype(LOW)
        du_out[f] = grad_up
        rows[8 + f // per : 9 + f // per, (f % per) * BS : (f % per + 1) * BS] += total(
            grad_up.astype(FULL)
        )
        term = dot_t(grad_up, up[f])
        grad_normed = term if grad_normed is None else grad_normed + term
    unit, rate = normal(middle)
    rows[5:6] += total(grad_normed * unit)
    rows[6:7] += total(grad_normed)
    grad_middle = grad_out + normal_back(grad_normed, unit, rate, vecs[5:6])
    grad_one = grad_middle.astype(LOW)
    for k in range(WIDE):
        dz1_out[k] = grad_one[:, k * BS : (k + 1) * BS]
    rows[4:5] += total(grad_one.astype(FULL))
    grad_attended = dot_t(grad_one, out_w[...]).astype(LOW)
    for j in range(8):
        do_out[j] = grad_attended[:, j * PAIR : (j + 1) * PAIR]
    return grad_middle


def project_back(grad_middle, hidden, dq_in, dkv_in, vecs, qkv, dqkv_out, rows, lead):
    grad_normed = None
    for n in range(3 * WIDE):
        kind, within = divmod(n, WIDE)
        source, cols = (dq_in, slice(0, PAIR)) if kind == 0 else (dkv_in, slice((kind - 1) * PAIR, kind * PAIR))
        part = jnp.concatenate([source[2 * within, :, cols], source[2 * within + 1, :, cols]], axis=1)
        dqkv_out[n] = part
        if kind != 1:
            row = 2 if kind == 0 else 3
            rows[row : row + 1, within * BS : (within + 1) * BS] += total(part.astype(FULL))
        term = dot_t(part, qkv[n])
        grad_normed = term if grad_normed is None else grad_normed + term
    unit, rate = normal(hidden)
    rows[0:1] += total(grad_normed * unit)
    rows[1:2] += total(grad_normed)
    grad_hidden = grad_middle + normal_back(grad_normed, unit, rate, vecs[0:1])
    rows[pl.ds(LEAD_AT + lead, 1)] += total(grad_hidden)
    return grad_hidden


def first_kernel(slots, leads, x, vecs, copies, h_out, a_out, packed_out, qkv, sems):
    fetch_qkv(copies, slots, qkv, sems.at[0])
    hidden = x[0].astype(FULL) + vecs[pl.ds(LEAD_AT + leads[0, 0], 1)]
    h_out[...] = hidden
    landed(qkv, sems.at[0])
    project(hidden, vecs, qkv, a_out, packed_out)


def between_kernel(
    slots, leads, h_in, o_in, vecs, copies,
    m_out, u_out, o_out, n2_out, act_out, y_out, h_out, a_out, packed_out,
    out_w, up, down, qkv, act_held, sems,
):
    fetch_out(copies, slots, out_w, sems.at[0])
    fetch_up(copies, slots, up, sems.at[1])
    fetch_down(copies, slots, down, sems.at[2])
    fetch_qkv(copies, slots, qkv, sems.at[3])
    middle, result = feed(
        h_in[...], o_in, vecs, out_w, up, down, sems, o_out, n2_out, act_out, u_out, act_held
    )
    m_out[...] = middle
    y_out[0] = result.astype(LOW)
    hidden = result + vecs[pl.ds(LEAD_AT + leads[1, 0], 1)]
    h_out[...] = hidden
    landed(qkv, sems.at[3])
    project(hidden, vecs, qkv, a_out, packed_out)


def turn_kernel(
    slots, h_in, o_in, cot, vecs, copies,
    o_out, n2_out, act_out, y_out, du_out, dz1_out, dz2_out, do_out, dm_out, rows,
    out_w, up, down, u_held, act_held, sems,
):
    fetch_out(copies, slots, out_w, sems.at[0])
    fetch_up(copies, slots, up, sems.at[1])
    fetch_down(copies, slots, down, sems.at[2])
    middle, result = feed(
        h_in[...], o_in, vecs, out_w, up, down, sems, o_out, n2_out, act_out, u_held, act_held
    )
    y_out[0] = result.astype(LOW)
    rows[...] = jnp.zeros_like(rows)
    dm_out[...] = feed_back(
        cot[0].astype(FULL), middle, u_held, vecs, out_w, up, down, du_out, dz1_out, dz2_out, do_out, rows
    )


def back_between_kernel(
    slots, leads, dm_in, h_in, dq_in, dkv_in, rows_in, cot, m_in, u_in, vecs, copies,
    dqkv_out, du_out, dz1_out, dz2_out, do_out, dm_out, rows,
    out_w, up, down, qkv, sems,
):
    fetch_qkv(copies, slots, qkv, sems.at[3])
    fetch_down(copies, slots, down, sems.at[2])
    fetch_up(copies, slots, up, sems.at[1])
    fetch_out(copies, slots, out_w, sems.at[0])
    rows[...] = rows_in[...]
    landed(qkv, sems.at[3])
    grad = project_back(dm_in[...], h_in[...], dq_in, dkv_in, vecs, qkv, dqkv_out, rows, leads[1, 0])
    grad = grad + cot[0].astype(FULL)
    landed(down, sems.at[2])
    landed(up, sems.at[1])
    landed(out_w, sems.at[0])
    dm_out[...] = feed_back(
        grad, m_in[...], u_in, vecs, out_w, up, down, du_out, dz1_out, dz2_out, do_out, rows
    )


def last_kernel(
    slots, leads, dm_in, h_in, dq_in, dkv_in, rows_in, vecs, copies, dqkv_out, grad_out, rows, qkv, sems
):
    fetch_qkv(copies, slots, qkv, sems.at[0])
    rows[...] = rows_in[...]
    landed(qkv, sems.at[0])
    grad_out[0] = project_back(
        dm_in[...], h_in[...], dq_in, dkv_in, vecs, qkv, dqkv_out, rows, leads[0, 0]
    ).astype(LOW)


SMEM_IN = pl.BlockSpec(memory_space=pltpu.SMEM)
VMEM_AT = pl.BlockSpec(memory_space=pltpu.VMEM)
ANY_AT = pl.BlockSpec(memory_space=pl.ANY)


def shape(dims, kind=LOW):
    return jax.ShapeDtypeStruct(dims, kind)


HELD = {
    "qkv": pltpu.VMEM((3 * WIDE, D, BS), LOW),
    "out": pltpu.VMEM((D, D), LOW),
    "up": pltpu.VMEM((DEEP, D, BS), LOW),
    "down": pltpu.VMEM((DEEP, BS, D), LOW),
}
SHAPES = {
    "wide": shape((TOKENS, D), FULL),
    "four": shape((WIDE, TOKENS, BS)),
    "four_t": shape((WIDE, BS, TOKENS)),
    "sixteen_t": shape((DEEP, BS, TOKENS)),
    "double": shape((8, TOKENS, 2 * PAIR)),
    "stats": shape((8, SEQ_ALL), FULL),
    "turned": shape((SEQ_ALL // BS, PAIR, BS), FULL),
    "twelve": shape((3 * WIDE, TOKENS, BS)),
    "sixteen": shape((DEEP, TOKENS, BS)),
    "up": shape((DEEP, TOKENS, BS), FULL),
    "packed": shape((8, TOKENS, 3 * PAIR)),
    "pair": shape((8, TOKENS, PAIR)),
    "pred": shape((1, TOKENS, D)),
    "rows": shape((20, D), FULL),
}


def plain(kernel, specs, outs, held, flops, name, extra=()):
    return pl.pallas_call(
        kernel,
        out_shape=tuple(SHAPES[out] for out in outs),
        in_specs=specs,
        out_specs=tuple(VMEM_AT for out in outs),
        scratch_shapes=[HELD[part] for part in held] + list(extra) + [pltpu.SemaphoreType.DMA((4,))],
        compiler_params=pltpu.CompilerParams(vmem_limit_bytes=VMEM_ASK),
        cost_estimate=pl.CostEstimate(flops=flops, bytes_accessed=24 << 20, transcendentals=0),
        name=name,
    )


def bias_pieces():
    left = masked
    pieces = []
    for unused in range(3):
        piece = float(ml_dtypes.bfloat16(left))
        pieces.append(piece)
        left -= piece
    assert left == 0.0
    return pieces


MASK_PIECES = bias_pieces()


def head_sides(queries, keys, neg, head):
    lane = lax.broadcasted_iota(jnp.int32, queries.shape, 1)
    own = (lane < HD) if head == 0 else (lane >= HD)
    spot = lane - (HD if head == 0 else 0)
    key_side = jnp.zeros_like(keys)
    for at, piece in enumerate(MASK_PIECES):
        key_side = jnp.where(spot == at, neg * piece, key_side)
    key_side = jnp.where(own, keys, key_side)
    ones = jnp.where((spot >= 0) & (spot < 3), 1.0, 0.0)
    query_side = jnp.where(own, queries * HD**-0.5, ones)
    return query_side, key_side, own


class Plane:
    def __init__(self):
        x, c, z, y = place()
        self.z = z
        self.me = 4 * c + 2 * x + y

    def device(self, j):
        return (turned_pair(lax.div(j, 2)), 2 * self.z + lax.rem(j, 2))

    def other(self, step):
        return lax.rem(self.me + step, 8)

    def others(self):
        return [self.device(self.other(step)) for step in range(1, 8)]

    def copy(self, src, dst, sems, send_at, recv_at, to):
        return pltpu.make_async_remote_copy(
            src_ref=src, dst_ref=dst, send_sem=sems.at[0, send_at], recv_sem=sems.at[1, recv_at],
            device_id=self.device(to), device_id_type=MESH,
        )

    def send(self, source, target, sems, to):
        self.copy(source.at[to], target.at[self.me], sems, to, self.me, to).start()

    def send_or_keep(self, source, target, sems, to):
        @pl.when(to != self.me)
        def away():
            self.send(source, target, sems, to)

        @pl.when(to == self.me)
        def keep():
            target[to] = source[to]

    def send_all(self, source, target, sems):
        for step in range(1, 8):
            self.send(source, target, sems, self.other(step))
        target[self.me] = source[self.me]

    def received(self, target, sems):
        for step in range(1, 8):
            j = self.other(step)
            self.copy(target.at[j], target.at[j], sems, j, j, j).wait_recv()

    def sent(self, source, sems):
        for step in range(1, 8):
            j = self.other(step)
            self.copy(source.at[j], source.at[j], sems, j, j, j).wait_send()


def mask_columns(notes, neg):
    for j in range(8):
        neg[j * TOKENS : (j + 1) * TOKENS] = jnp.broadcast_to(notes[j, 0:1], (TOKENS, TOKENS)).T


def attend_kernel(give, packed, notes, *refs):
    if give:
        pred, o_out, held, stats, turned, pred_out = refs[:6]
        refs = refs[6:]
    else:
        o_out, held, stats, turned = refs[:4]
        refs = refs[4:]
    neg, query_side, key_side, message, in_sems, out_sems, swap_local, swap_send, swap_recv = refs
    plane = Plane()
    swap = Swap(swap_local, swap_send, swap_recv)
    if give:
        greet_all(plane, swap)
        swap.start(pred, pred_out)
    else:
        meet(plane.others())
    plane.send_all(packed, held, in_sems)
    mask_columns(notes, neg)
    stats[...] = jnp.zeros_like(stats)
    plane.received(held, in_sems)
    both = held[...].reshape(SEQ_ALL, 3 * PAIR)
    queries = both[:, :PAIR].astype(FULL)
    keys = both[:, PAIR : 2 * PAIR].astype(FULL)
    values_t = both[:, 2 * PAIR :].astype(FULL).T.astype(LOW)
    for head in range(2):
        q_side, k_side, unused = head_sides(queries, keys, neg[...], head)
        query_side[head] = q_side.astype(LOW)
        key_side[head] = k_side.astype(LOW)

    def chunk(step, carry):
        at = lax.rem(step + lax.div(plane.me, 2), 4)
        first = pl.multiple_of(at * BS, BS)
        for head in range(2):
            scores = dot_t(key_side[head], query_side[head, pl.ds(first, BS)])
            most = jnp.max(scores, axis=0, keepdims=True)
            expos = jnp.exp(scores - most)
            sums = jnp.sum(expos, axis=0, keepdims=True)
            part = dot(values_t[head * HD : (head + 1) * HD], expos.astype(LOW)) / sums
            turned[at, head * HD : (head + 1) * HD] = part
            stats[head : head + 1, pl.ds(first, BS)] = most + jnp.log(sums)
        for half in range(2):
            to = 2 * at + half
            message[to] = turned[at, :, half * TOKENS : (half + 1) * TOKENS].T.astype(LOW)
            plane.send_or_keep(message, o_out, out_sems, to)
        return carry

    lax.fori_loop(0, SEQ_ALL // BS, chunk, 0)
    plane.received(o_out, out_sems)
    plane.sent(packed, in_sems)
    plane.sent(message, out_sems)
    if give:
        swap.finish()


def greet_all(plane, swap):
    barrier = pltpu.get_barrier_semaphore()
    for device in plane.others():
        pl.semaphore_signal(barrier, inc=1, device_id=device, device_id_type=MESH)

    @pl.when(jnp.logical_not(swap.stays))
    def partner():
        pl.semaphore_signal(barrier, inc=1, device_id=swap.to, device_id_type=MESH)

    pl.semaphore_wait(barrier, 7 + jnp.where(swap.stays, 0, 1))


def swap_sems(count):
    return [pltpu.SemaphoreType.DMA((count,))] * 3


def attend(packed, notes, pred, collective, name):
    give = pred is not None
    return pl.pallas_call(
        functools.partial(attend_kernel, give),
        out_shape=(SHAPES["pair"], SHAPES["packed"], SHAPES["stats"], SHAPES["turned"])
        + ((SHAPES["pred"],) if give else ()),
        in_specs=[VMEM_AT] * 2 + ([ANY_AT] if give else []),
        out_specs=(VMEM_AT,) * 4 + ((ANY_AT,) if give else ()),
        scratch_shapes=[
            pltpu.VMEM((SEQ_ALL, PAIR), FULL),
            pltpu.VMEM((2, SEQ_ALL, PAIR), LOW),
            pltpu.VMEM((2, SEQ_ALL, PAIR), LOW),
            pltpu.VMEM((8, TOKENS, PAIR), LOW),
            pltpu.SemaphoreType.DMA((2, 8)),
            pltpu.SemaphoreType.DMA((2, 8)),
        ]
        + swap_sems(1),
        compiler_params=pltpu.CompilerParams(
            collective_id=collective, has_side_effects=True, vmem_limit_bytes=VMEM_ASK
        ),
        cost_estimate=pl.CostEstimate(flops=1 << 30, bytes_accessed=2 << 20, transcendentals=1 << 21),
        name=name,
    )(packed, notes, *((pred,) if give else ()))


def attend_back_kernel(n_pool, give, do_in, held, notes, stats, turned, *refs):
    pools, refs = refs[:n_pool], refs[n_pool:]
    if give:
        pred, refs = refs[0], refs[1:]
    dq_out, dkv_out, refs = refs[0], refs[1], refs[2:]
    pools_out, refs = refs[:n_pool], refs[n_pool:]
    if give:
        pred_out, refs = refs[0], refs[1:]
    (
        neg, do_held, query_side, query_plain, key_side, do_side, grad_q, dq_message, dkv_message,
        in_sems, dq_sems, dkv_sems, swap_local, swap_send, swap_recv, pool_sems,
    ) = refs
    x, c, z, y = place()
    plane = Plane()
    swap = Swap(swap_local, swap_send, swap_recv)
    sibling = (2 * x + 1 - c, 2 * z + y)
    if give:
        greet_all(plane, swap)
        swap.start(pred, pred_out)
    else:
        meet(plane.others())
    plane.send_all(do_in, do_held, in_sems)
    pool_copies = [
        push(pools[at], pools_out[at], pool_sems.at[0, at], pool_sems.at[1, at], sibling) for at in range(n_pool)
    ]
    mask_columns(notes, neg)
    both = held[...].reshape(SEQ_ALL, 3 * PAIR)
    queries = both[:, :PAIR].astype(FULL)
    keys = both[:, PAIR : 2 * PAIR].astype(FULL)
    keys_t = keys.T.astype(LOW)
    grad_q[...] = jnp.zeros_like(grad_q)
    for head in range(2):
        q_side, k_side, own = head_sides(queries, keys, neg[...], head)
        query_side[head] = q_side.astype(LOW)
        query_plain[head] = jnp.where(own, q_side, 0.0).astype(LOW)
        key_side[head] = k_side.astype(LOW)
    plane.received(do_held, in_sems)
    grads = do_held[...].reshape(SEQ_ALL, PAIR).astype(FULL)
    inner = []
    for head in range(2):
        lane = lax.broadcasted_iota(jnp.int32, grads.shape, 1)
        own = (lane < HD) if head == 0 else (lane >= HD)
        do_side[head] = jnp.where(own, grads, 0.0).astype(LOW)
    grads_t = grads.T
    for head in range(2):
        side = slice(head * HD, (head + 1) * HD)
        inner.append(
            jnp.concatenate(
                [
                    jnp.sum(turned[at, side] * grads_t[side, at * BS : (at + 1) * BS], axis=0, keepdims=True)
                    for at in range(SEQ_ALL // BS)
                ],
                axis=1,
            )
        )
    left = lax.broadcasted_iota(jnp.int32, (BS, PAIR), 1) < HD
    keys_held = [keys_t[head * HD : (head + 1) * HD] for head in range(2)]

    def chunk(at, keys_slice):
        first = at * BS
        grad_k = []
        grad_v = None
        values = held[2 * at : 2 * at + 2, :, 2 * PAIR :].reshape(BS, PAIR)
        for head in range(2):
            scores = dot_t(key_side[head, first : first + BS], query_side[head])
            probs = jnp.exp(scores - stats[head : head + 1])
            dprobs = dot_t(values, do_side[head])
            dscores = (probs * (dprobs - inner[head])).astype(LOW)
            term = dot(probs.astype(LOW), do_side[head])
            grad_v = term if grad_v is None else grad_v + term
            grad_k.append(dot(dscores, query_plain[head]))
            grad_q[head * HD : (head + 1) * HD] += dot(keys_slice[head], dscores)
        grad_k = jnp.where(left, grad_k[0], grad_k[1]).astype(LOW)
        grad_v = grad_v.astype(LOW)
        for half in range(2):
            to = 2 * at + half
            rows = slice(half * TOKENS, (half + 1) * TOKENS)
            dkv_message[to, :, :PAIR] = grad_k[rows]
            dkv_message[to, :, PAIR:] = grad_v[rows]
            plane.send_or_keep(dkv_message, dkv_out, dkv_sems, to)

    for at in range(SEQ_ALL // BS):
        chunk(at, [part[:, at * BS : (at + 1) * BS] for part in keys_held])
    for j in range(8):
        dq_message[j] = (grad_q[:, j * TOKENS : (j + 1) * TOKENS].T * HD**-0.5).astype(LOW)
        plane.send_or_keep(dq_message, dq_out, dq_sems, j)
    plane.received(dkv_out, dkv_sems)
    plane.received(dq_out, dq_sems)
    plane.sent(do_in, in_sems)
    plane.sent(dkv_message, dkv_sems)
    plane.sent(dq_message, dq_sems)
    for copy in pool_copies:
        copy.wait()
    if give:
        swap.finish()


def attend_back(do, held, notes, stats, turned, pools, pred, collective, name):
    give = pred is not None
    pools = list(pools)
    return pl.pallas_call(
        functools.partial(attend_back_kernel, len(pools), give),
        out_shape=(SHAPES["pair"], SHAPES["double"])
        + tuple(shape(pool.shape) for pool in pools)
        + ((SHAPES["pred"],) if give else ()),
        in_specs=[VMEM_AT] * 5 + [ANY_AT] * (len(pools) + (1 if give else 0)),
        out_specs=(VMEM_AT,) * 2 + (ANY_AT,) * (len(pools) + (1 if give else 0)),
        scratch_shapes=[
            pltpu.VMEM((SEQ_ALL, PAIR), FULL),
            pltpu.VMEM((8, TOKENS, PAIR), LOW),
            pltpu.VMEM((2, SEQ_ALL, PAIR), LOW),
            pltpu.VMEM((2, SEQ_ALL, PAIR), LOW),
            pltpu.VMEM((2, SEQ_ALL, PAIR), LOW),
            pltpu.VMEM((2, SEQ_ALL, PAIR), LOW),
            pltpu.VMEM((PAIR, SEQ_ALL), FULL),
            pltpu.VMEM((8, TOKENS, PAIR), LOW),
            pltpu.VMEM((8, TOKENS, 2 * PAIR), LOW),
            pltpu.SemaphoreType.DMA((2, 8)),
            pltpu.SemaphoreType.DMA((2, 8)),
            pltpu.SemaphoreType.DMA((2, 8)),
        ]
        + swap_sems(1)
        + [pltpu.SemaphoreType.DMA((2, max(1, len(pools))))],
        compiler_params=pltpu.CompilerParams(
            collective_id=collective, has_side_effects=True, vmem_limit_bytes=VMEM_ASK
        ),
        cost_estimate=pl.CostEstimate(flops=1 << 31, bytes_accessed=2 << 20, transcendentals=1 << 21),
        name=name,
    )(do, held, notes, stats, turned, *pools, *((pred,) if give else ()))


LEFTS = (WIDE, WIDE, WIDE, DEEP)
RIGHTS = (3 * WIDE, WIDE, DEEP, WIDE)
LEFT_AT = (0, WIDE, 2 * WIDE, 3 * WIDE)
RIGHT_AT = (0, 3 * WIDE, 4 * WIDE, 4 * WIDE + DEEP)
N_LEFT = 3 * WIDE + DEEP
N_RIGHT = 5 * WIDE + DEEP


def pools_of(block):
    left = jnp.zeros_like(block)
    right = jnp.zeros_like(block)
    for at, base in enumerate((QKV_AT, OUT_AT, UP_AT, DOWN_AT)):
        inside = block >= base
        cols = RIGHTS[at]
        left = jnp.where(inside, LEFT_AT[at] + (block - base) // cols, left)
        right = jnp.where(inside, RIGHT_AT[at] + (block - base) % cols, right)
    return left, right


def reduce_kernel(left_ids, right_ids, rows_in, *refs):
    lefts, rights, other_lefts, other_rights = refs[:8], refs[8:16], refs[16:24], refs[24:31]
    own_out, rows_out = refs[31:33]
    left_t, right_pool = refs[33:35]
    x_stage, x_land, yb_stage, yb_land, ym_stage, ym_land = refs[35:41]
    zb_stage, zb_land, zm_stage, zm_land, both_stage, both_land = refs[41:47]
    pair_rows, chip_rows, plane_rows, row_land, row_z = refs[47:52]
    pool_sems, pool_send, pool_recv, send_sems, recv_sems, row_send, row_recv = refs[52:59]
    x, c, z, y = place()
    samp = 2 * x + c
    blk = 2 * z + y
    to_c = (2 * x + 1 - c, blk)
    to_x = (2 * (1 - x) + c, blk)
    to_y = (samp, 2 * z + 1 - y)
    to_z = [(samp, 2 * lax.rem(z + step, 4) + y) for step in (1, 2, 3)]
    meet_all()
    first = pl.ds(RIGHT_AT[0], RIGHTS[0])
    dqkv_copy = push(
        rights[0], right_pool.at[first, pl.ds(2 * TOKENS, TOKENS)], pool_send.at[0], pool_recv.at[0], to_c
    )
    row_copy = push(rows_in, row_land.at[0], row_send.at[0], row_recv.at[0], to_c)
    here = []

    def load(part, layer, kind, left):
        counts, bases = (LEFTS, LEFT_AT) if left else (RIGHTS, RIGHT_AT)
        ids = pl.ds(bases[kind], counts[kind])
        tokens = pl.ds(layer * TOKENS, TOKENS)
        target = left_t.at[ids, :, tokens] if left else right_pool.at[ids, tokens]
        here.append(pltpu.make_async_copy(part, target, pool_sems.at[len(here)]))
        here[-1].start()

    for at in range(8):
        layer, kind = divmod(at, 4)
        load(lefts[at], layer, kind, True)
        load(other_lefts[at], 2 + layer, kind, True)
        load(rights[at], layer, kind, False)
        if at > 0:
            load(other_rights[at - 1], 2 + layer, kind, False)
    row_copy.wait_recv()
    pair_rows[...] = rows_in[...] + row_land[0]
    row_copies = [row_copy, push(pair_rows, row_land.at[1], row_send.at[1], row_recv.at[1], to_x)]
    for copy in here:
        copy.wait()
    dqkv_copy.wait_recv()

    def group(half, k):
        return 2 * lax.rem(z + 1 + k, 4) + (1 - y if half == 0 else y)

    def part(half, k, offset):
        slot = group(half, k) * GROUP + c * HALF + offset
        return [dot(left_t[left_ids[slot + i]], right_pool[right_ids[slot + i]]) for i in range(QUART)]

    mine, other, both = x * 8, (1 - x) * 8, QUART

    def link(kind, k, stage, land, to):
        return pltpu.make_async_remote_copy(
            src_ref=stage, dst_ref=land, send_sem=send_sems.at[kind, k], recv_sem=recv_sems.at[kind, k],
            device_id=to, device_id_type=MESH,
        )

    def along_x(half, k):
        return link(half, k, x_stage.at[half, k], x_land.at[half, k], to_x)

    def along_y_both(k):
        return link(2, k, yb_stage.at[k], yb_land.at[k], to_y)

    def along_y_mine(k):
        return link(3, k, ym_stage.at[k], ym_land.at[k], to_y)

    def along_z_both(k):
        return link(4, k, zb_stage.at[k], zb_land.at[k], (samp, group(1, k)))

    def along_z_mine(k):
        return link(5, k, zm_stage.at[k], zm_land.at[k], (samp, group(1, k)))

    def begin(k, carry):
        for i, value in enumerate(part(0, k, both)):
            yb_stage[k, i] = value.astype(LOW)
        along_y_both(k).start()
        for i, value in enumerate(part(0, k, other)):
            x_stage[0, k, i] = value.astype(LOW)
        along_x(0, k).start()
        return carry

    lax.fori_loop(0, 4, begin, 0)

    def more(k, carry):
        for i, value in enumerate(part(1, k, other)):
            x_stage[1, k, i] = value.astype(LOW)
        along_x(1, k).start()
        return carry

    lax.fori_loop(0, 4, more, 0)

    def middle(k, carry):
        values = part(0, k, mine)
        along_x(0, k).wait_recv()
        for i, value in enumerate(values):
            ym_stage[k, i] = (value + x_land[0, k, i].astype(FULL)).astype(LOW)
        along_y_mine(k).start()
        values = part(1, k, both)
        along_y_both(k).wait_recv()
        for i, value in enumerate(values):
            zb_stage[k, i] = (value + yb_land[k, i].astype(FULL)).astype(LOW)

        @pl.when(k < 3)
        def send_on():
            along_z_both(k).start()

        return carry

    lax.fori_loop(0, 4, middle, 0)
    row_copies[1].wait_recv()
    chip_rows[...] = pair_rows[...] + row_land[1]
    row_copies.append(push(chip_rows, row_land.at[2], row_send.at[2], row_recv.at[2], to_y))

    def late(k, carry):
        values = part(1, k, mine)
        along_x(1, k).wait_recv()
        values = [value + x_land[1, k, i].astype(FULL) for i, value in enumerate(values)]
        along_y_mine(k).wait_recv()
        for i, value in enumerate(values):
            zm_stage[k, i] = (value + ym_land[k, i].astype(FULL)).astype(LOW)

        @pl.when(k < 3)
        def send_on():
            along_z_mine(k).start()

        return carry

    lax.fori_loop(0, 4, late, 0)
    row_copies[2].wait_recv()
    plane_rows[...] = chip_rows[...] + row_land[2]
    for step in range(3):
        row_copies.append(
            push(plane_rows, row_z.at[z], row_send.at[3 + step], row_recv.at[3 + step], to_z[step])
        )
    row_z[z] = plane_rows[...]
    for k in range(3):
        along_z_both(k).wait_recv()
    for i in range(QUART):
        value = zb_stage[3, i].astype(FULL)
        for k in range(3):
            value = value + zb_land[k, i].astype(FULL)
        both_stage[i // 2, i % 2] = value.astype(LOW)
    last = link(6, 0, both_stage.at[1 - x], both_land, to_x)
    last.start()
    for k in range(3):
        along_z_mine(k).wait_recv()
    for i in range(QUART):
        value = zm_stage[3, i].astype(FULL)
        for k in range(3):
            value = value + zm_land[k, i].astype(FULL)
        own_out[i] = value.astype(LOW)
    last.wait_recv()
    for i in range(2):
        own_out[QUART + i] = (both_stage[x, i].astype(FULL) + both_land[i].astype(FULL)).astype(LOW)
    for step in range(3):
        row_copies[3 + step].wait_recv()
    rows_out[...] = (row_z[0] + row_z[1]) + (row_z[2] + row_z[3])
    for copy in [dqkv_copy] + row_copies + [last]:
        copy.wait_send()

    def drain(k, carry):
        along_x(0, k).wait_send()
        along_x(1, k).wait_send()
        along_y_both(k).wait_send()
        along_y_mine(k).wait_send()

        @pl.when(k < 3)
        def sent_on():
            along_z_both(k).wait_send()
            along_z_mine(k).wait_send()

        return carry

    lax.fori_loop(0, 4, drain, 0)


def blocks_of(*lead):
    return pltpu.VMEM(lead + (BS, BS), LOW)


def reduce_grads(left_ids, right_ids, rows, lefts, rights, others):
    return pl.pallas_call(
        reduce_kernel,
        out_shape=(shape((6, BS, BS)), SHAPES["rows"]),
        in_specs=[SMEM_IN] * 2 + [VMEM_AT] + [ANY_AT] * 31,
        out_specs=(VMEM_AT, VMEM_AT),
        scratch_shapes=[
            pltpu.VMEM((N_LEFT, BS, 4 * TOKENS), LOW),
            pltpu.VMEM((N_RIGHT, 4 * TOKENS, BS), LOW),
            blocks_of(2, 4, QUART),
            blocks_of(2, 4, QUART),
            blocks_of(4, QUART),
            blocks_of(4, QUART),
            blocks_of(4, QUART),
            blocks_of(4, QUART),
            blocks_of(4, QUART),
            blocks_of(3, QUART),
            blocks_of(4, QUART),
            blocks_of(3, QUART),
            blocks_of(2, 2),
            blocks_of(2),
            pltpu.VMEM((20, D), FULL),
            pltpu.VMEM((20, D), FULL),
            pltpu.VMEM((20, D), FULL),
            pltpu.VMEM((3, 20, D), FULL),
            pltpu.VMEM((4, 20, D), FULL),
            pltpu.SemaphoreType.DMA((31,)),
            pltpu.SemaphoreType.DMA((1,)),
            pltpu.SemaphoreType.DMA((1,)),
            pltpu.SemaphoreType.DMA((7, 4)),
            pltpu.SemaphoreType.DMA((7, 4)),
            pltpu.SemaphoreType.DMA((6,)),
            pltpu.SemaphoreType.DMA((6,)),
        ],
        compiler_params=pltpu.CompilerParams(
            collective_id=5, has_side_effects=True, vmem_limit_bytes=VMEM_ASK
        ),
        cost_estimate=pl.CostEstimate(flops=6 << 30, bytes_accessed=40 << 20, transcendentals=0),
        name="reduce_grads",
    )(left_ids, right_ids, rows, *lefts, *rights, *others)


def halves(value):
    high = value.astype(LOW)
    return high, (value - high.astype(FULL)).astype(LOW)


def fine(left, right):
    return dot(
        jnp.concatenate([left[0], left[1], left[0]], axis=1),
        jnp.concatenate([right[0], right[0], right[1]], axis=0),
    )


def statistic(gram, shrink, diag, eye):
    return jnp.where(eye, 0.5 * diag, 0.0) + shrink * gram


def roots(stats, eye):
    scales = [jnp.sqrt(jnp.sum(jnp.sum(stat * stat, axis=1, keepdims=True), axis=0, keepdims=True)) for stat in stats]
    moving = [stat / scale for stat, scale in zip(stats, scales)]
    approx = [None] * len(stats)
    ahead = range(len(stats))
    for iteration in range(ITERS):
        factors = [(jnp.where(eye, 5.0, 0.0) - moving[i]) * 0.25 for i in ahead]
        parts = [halves(factor) for factor in factors]
        if iteration == 0:
            approx = [factors[i] * lax.rsqrt(jnp.sqrt(scales[i])) for i in ahead]
        else:
            approx = [fine(halves(approx[i]), parts[i]) for i in ahead]
        if iteration < ITERS - 1:
            squares = [halves(fine(parts[i], parts[i])) for i in ahead]
            fourths = [halves(fine(squares[i], squares[i])) for i in ahead]
            moving = [fine(fourths[i], halves(moving[i])) for i in ahead]
    return approx


def shampoo_kernel(
    own, left_diag, right_diag, grad_in, grads_out, moves_out, grad_out, staged, local_sems, send_sems, recv_sems,
    swap_local, swap_send, swap_recv,
):
    x, c, z, y = place()
    blk = 2 * z + y
    to_c = (2 * x + 1 - c, blk)
    to_x = (2 * (1 - x) + c, blk)
    meet_all()
    swap = Swap(swap_local, swap_send, swap_recv)
    swap.start(grad_in, grad_out)
    mine = c * HALF + x * 8
    both = c * HALF + QUART + 2 * x
    far_mine = c * HALF + (1 - x) * 8
    far_both = c * HALF + QUART + 2 * (1 - x)

    def link(kind, k, src, dst, to):
        return pltpu.make_async_remote_copy(
            src_ref=src, dst_ref=dst, send_sem=send_sems.at[kind, k], recv_sem=recv_sems.at[kind, k],
            device_id=to, device_id_type=MESH,
        )

    def grad_copy(kind, at, to):
        if at == 0:
            return link(kind, at, own.at[pl.ds(0, QUART)], grads_out.at[pl.ds(mine, QUART)], to)
        return link(kind, at, own.at[pl.ds(QUART, 2)], grads_out.at[pl.ds(both, 2)], to)

    def grad_on(at):
        where = grads_out.at[pl.ds(far_mine, QUART)] if at == 0 else grads_out.at[pl.ds(far_both, 2)]
        return link(2, at, where, where, to_c)

    grad_copies = [grad_copy(kind, at, to) for kind, to in ((0, to_x), (1, to_c)) for at in (0, 1)]
    for copy in grad_copies:
        copy.start()
    local = [
        pltpu.make_async_copy(own.at[pl.ds(0, QUART)], grads_out.at[pl.ds(mine, QUART)], local_sems.at[0]),
        pltpu.make_async_copy(own.at[pl.ds(QUART, 2)], grads_out.at[pl.ds(both, 2)], local_sems.at[1]),
    ]
    for copy in local:
        copy.start()
    eye = lax.broadcasted_iota(jnp.int32, (BS, BS), 0) == lax.broadcasted_iota(jnp.int32, (BS, BS), 1)

    def slot_of(i, far=False):
        first = (far_mine if far else mine) + i
        second = (far_both if far else both) + i - QUART
        return jnp.where(i < QUART, first, second)

    def move_copy(kind, i, to):
        return link(kind, i, staged.at[i], moves_out.at[slot_of(i)], to)

    def move_on(i):
        where = moves_out.at[slot_of(i, True)]
        return link(5, i, where, where, to_c)

    def kept(i):
        return pltpu.make_async_copy(staged.at[i], moves_out.at[slot_of(i)], local_sems.at[2 + i])

    def pair(at, carry):
        held = []
        stats = []
        for i in (2 * at, 2 * at + 1):
            low = own[i]
            grad = low.astype(FULL)
            mean = jnp.sum(jnp.sum(grad * grad, axis=1, keepdims=True), axis=0, keepdims=True) / (BS * BS)
            shrink = 0.5 / (mean + 1e-06)
            low_t = grad.T.astype(LOW)
            slot = slot_of(i)
            stats.append(statistic(dot(low, low_t), shrink, left_diag[pl.ds(slot, 1)], eye))
            stats.append(statistic(dot(low_t, low), shrink, right_diag[pl.ds(slot, 1)], eye))
            held.append((i, low, lax.rsqrt(mean + 1e-06)))
        sides = roots(stats, eye)
        for n, (i, low, rate) in enumerate(held):
            high, rest = halves(sides[2 * n])
            turned = dot(jnp.concatenate([high, rest], axis=1), jnp.concatenate([low, low], axis=0)) * rate
            staged[i] = fine(halves(turned), halves(sides[2 * n + 1])).astype(LOW)
            move_copy(3, i, to_x).start()
            move_copy(4, i, to_c).start()
            kept(i).start()
        return carry

    lax.fori_loop(0, 3, pair, 0)
    for at in (0, 1):
        grad_copies[at].wait_recv()
        grad_on(at).start()

    def pass_on(i, carry):
        move_copy(3, i, to_x).wait_recv()
        move_on(i).start()
        return carry

    lax.fori_loop(0, 6, pass_on, 0)
    for at in (0, 1):
        grad_copies[2 + at].wait_recv()
        grad_on(at).wait_recv()
        grad_on(at).wait_send()
        local[at].wait()
    for copy in grad_copies:
        copy.wait_send()

    def drain(i, carry):
        move_copy(4, i, to_c).wait_recv()
        move_on(i).wait_recv()
        move_copy(3, i, to_x).wait_send()
        move_copy(4, i, to_c).wait_send()
        move_on(i).wait_send()
        kept(i).wait()
        return carry

    lax.fori_loop(0, 6, drain, 0)
    swap.finish()


def shampoo(own, left_start, right_start, grad):
    return pl.pallas_call(
        shampoo_kernel,
        out_shape=(shape((GROUP, BS, BS)), shape((GROUP, BS, BS)), SHAPES["pred"]),
        in_specs=[VMEM_AT] * 3 + [ANY_AT],
        out_specs=(ANY_AT,) * 3,
        scratch_shapes=[
            blocks_of(6),
            pltpu.SemaphoreType.DMA((8,)),
            pltpu.SemaphoreType.DMA((6, 6)),
            pltpu.SemaphoreType.DMA((6, 6)),
        ]
        + swap_sems(1),
        compiler_params=pltpu.CompilerParams(
            collective_id=6, has_side_effects=True, vmem_limit_bytes=VMEM_ASK
        ),
        cost_estimate=pl.CostEstimate(flops=30 << 30, bytes_accessed=10 << 20, transcendentals=0),
        name="shampoo",
    )(own, left_start, right_start, grad)


def finish_kernel(grad, move, weight, left_diag, right_diag, grad_out, left_out, right_out, new_out, low_out):
    eye = lax.broadcasted_iota(jnp.int32, (BS, BS), 0) == lax.broadcasted_iota(jnp.int32, (BS, BS), 1)

    def mean(value):
        return jnp.sum(jnp.sum(value, axis=1, keepdims=True), axis=0, keepdims=True) / (BS * BS)

    for i in range(STEP):
        low = grad[i]
        full = low.astype(FULL)
        grad_out[i] = full
        shrink = 0.5 / (mean(full * full) + 1e-06)
        low_t = full.T.astype(LOW)
        left_out[i] = statistic(dot(low, low_t), shrink, left_diag[i], eye)
        right_out[i] = statistic(dot(low_t, low), shrink, right_diag[i], eye)
        step = move[i].astype(FULL)
        start = weight[i]
        ratio = jnp.sqrt(mean(start * start)) * lax.rsqrt(mean(step * step) + 1e-06)
        new = start - step_rate * ratio * step
        new_out[i] = new
        low_out[i] = new.astype(LOW)


STEP = 4


def finish_slots(grads, moves, masters, left_start, right_start):
    block = pl.BlockSpec((STEP, BS, BS), lambda i: (i, 0, 0))
    row = pl.BlockSpec((STEP, 1, BS), lambda i: (i, 0, 0))
    return pl.pallas_call(
        finish_kernel,
        grid=(GROUP // STEP,),
        compiler_params=pltpu.CompilerParams(vmem_limit_bytes=VMEM_ASK),
        out_shape=tuple(shape((GROUP, BS, BS), kind) for kind in (FULL, FULL, FULL, FULL, LOW)),
        in_specs=[block, block, block, row, row],
        out_specs=(block,) * 5,
        cost_estimate=pl.CostEstimate(flops=2 << 30, bytes_accessed=39 << 20, transcendentals=0),
        name="finish_slots",
    )(grads, moves, masters, left_start.reshape(GROUP, 1, BS), right_start.reshape(GROUP, 1, BS))


def layers(inputs, cot_first, cot_second, slots, leads, vectors, copies, notes):
    act_held = pltpu.VMEM((DEEP, TOKENS, BS), LOW)
    hidden_one, a_one, packed = plain(
        first_kernel, [SMEM_IN] * 2 + [VMEM_AT] * 2 + [ANY_AT], ("wide", "four_t", "packed"), ("qkv",), 1 << 30, "first"
    )(slots, leads, inputs, vectors, copies)
    o_msg, held_one, stats_one, turned_one, cot_second = attend(packed, notes, cot_second, 1, "attend_one")
    mid_one, u_one, o_one, n_one, act_one, pred_one, hidden_two, a_two, packed = plain(
        between_kernel,
        [SMEM_IN] * 2 + [VMEM_AT] * 3 + [ANY_AT],
        ("wide", "up", "four_t", "four_t", "sixteen_t", "pred", "wide", "four_t", "packed"),
        ("out", "up", "down", "qkv"),
        3 << 30,
        "between",
        [act_held],
    )(slots, leads, hidden_one, o_msg, vectors, copies)
    o_msg, held_two, stats_two, turned_two, cot_first = attend(packed, notes, cot_first, 1, "attend_two")
    o_two, n_two, act_two, pred_two, du_two, dz1_two, dz2_two, do_msg, dm_two, rows = plain(
        turn_kernel,
        [SMEM_IN] + [VMEM_AT] * 4 + [ANY_AT],
        ("four_t", "four_t", "sixteen_t", "pred", "sixteen", "four", "four", "pair", "wide", "rows"),
        ("out", "up", "down"),
        5 << 30,
        "turn",
        [pltpu.VMEM((DEEP, TOKENS, BS), FULL), act_held],
    )(slots, hidden_two, o_msg, cot_second, vectors, copies)
    dq_msg, dkv_msg, pred_one = attend_back(
        do_msg, held_two, notes, stats_two, turned_two, (), pred_one, 3, "attend_back_two"
    )
    dqkv_two, du_one, dz1_one, dz2_one, do_msg, dm_one, rows = plain(
        back_between_kernel,
        [SMEM_IN] * 2 + [VMEM_AT] * 9 + [ANY_AT],
        ("twelve", "sixteen", "four", "four", "pair", "wide", "rows"),
        ("out", "up", "down", "qkv"),
        3 << 30,
        "back_between",
    )(slots, leads, dm_two, hidden_two, dq_msg, dkv_msg, rows, cot_first, mid_one, u_one, vectors, copies)
    lefts = (a_one, o_one, n_one, act_one, a_two, o_two, n_two, act_two)
    rights = (dz1_one, du_one, dz2_one, dqkv_two, dz1_two, du_two, dz2_two)
    dq_msg, dkv_msg, *others, pred_two = attend_back(
        do_msg, held_one, notes, stats_one, turned_one, lefts + rights, pred_two, 4, "attend_back_one"
    )
    dqkv_one, input_grad, rows = plain(
        last_kernel,
        [SMEM_IN] * 2 + [VMEM_AT] * 6 + [ANY_AT],
        ("twelve", "pred", "rows"),
        ("qkv",),
        1 << 30,
        "last",
    )(slots, leads, dm_one, hidden_one, dq_msg, dkv_msg, rows, vectors, copies)
    return pred_one, pred_two, input_grad, lefts, (dqkv_one,) + rights, others, rows


def local_tuned(
    inputs,
    cot_first,
    cot_second,
    valid_flags,
    lead_steps,
    masters,
    assignment,
    left_start,
    right_start,
    vectors,
    vec_moment,
):
    notes = jnp.concatenate(
        [
            valid_flags.astype(FULL) - 1.0,
            jnp.pad(lead_steps.astype(FULL).T, ((0, 0), (0, TOKENS - 2))),
            jnp.zeros((6, TOKENS), FULL),
        ],
        axis=0,
    )
    copies, notes, rows_in = gather_weights(masters, notes, inputs)
    leads = notes[0, 1, :2].astype(jnp.int32).reshape(2, 1)
    pred_one, pred_two, input_grad, lefts, rights, others, rows = layers(
        rows_in, cot_first, cot_second, assignment, leads, vectors, copies, notes
    )
    position = jnp.arange(NB, dtype=jnp.int32)
    inverse = jnp.sum(
        jnp.where(assignment[None, :] == position[:, None], position[None, :], 0), axis=1
    )
    left_ids, right_ids = pools_of(inverse)
    own, vec_grads = reduce_grads(left_ids, right_ids, rows, lefts, rights, others)
    grads, moves, input_grad = shampoo(own, left_start, right_start, input_grad)
    input_grad = input_grad.astype(FULL)
    matrix_grads, left_stats, right_stats, new_masters, new_copies = finish_slots(
        grads, moves, masters, left_start, right_start
    )
    scaled_vec = vec_grads * lax.rsqrt(
        jnp.mean(vec_grads * vec_grads, axis=1, keepdims=True) + 1e-06
    )
    vec_moments = 0.5 * vec_moment + 0.5 * scaled_vec * scaled_vec
    new_vectors = vectors - vector_rate * scaled_vec * lax.rsqrt(vec_moments)
    return (
        pred_one,
        pred_two,
        input_grad,
        matrix_grads,
        left_stats,
        right_stats,
        new_masters,
        new_copies,
        vec_grads,
        vec_moments,
        new_vectors,
    )


def solution(mesh):
    placed = (
        P("samp", "blk", None),
        P("samp", "blk", None),
        P("samp", "blk", None),
        P("samp", "blk"),
        P(None, "samp"),
        P("blk", None, None),
        P(),
        P("blk", None),
        P("blk", None),
        P(),
        P(),
    )
    fits = mesh.shape["samp"] == 4 and mesh.shape["blk"] == 8
    return jax.shard_map(
        local_tuned if fits else local_any,
        mesh=mesh,
        in_specs=placed,
        out_specs=(
            P("samp", "blk", None),
            P("samp", "blk", None),
            P("samp", "blk", None),
            P("blk", None, None),
            P("blk", None, None),
            P("blk", None, None),
            P("blk", None, None),
            P("blk", None, None),
            P(),
            P(),
            P(),
        ),
        check_vma=False,
    )
```

```python
import functools
import math

import jax
import ml_dtypes
import jax.numpy as jnp
from jax import lax
from jax.experimental import pallas as pl
from jax.experimental.pallas import tpu as pltpu
from jax.sharding import PartitionSpec as P

D = 1024
HEADS = 16
FF = 4096
HD = 64
LEADS = 8
BS = 256
ITERS = 6
NB = 192


HIGH = lax.Precision.HIGHEST
step_rate = 0.5
vector_rate = 0.3
masked = 1000000000.0


def assemble(blocks, height, breadth):
    return (
        blocks.reshape(height // BS, breadth // BS, BS, BS)
        .transpose(0, 2, 1, 3)
        .reshape(height, breadth)
    )


def carve(matrix):
    height, breadth = matrix.shape
    return (
        matrix.reshape(height // BS, BS, breadth // BS, BS)
        .transpose(0, 2, 1, 3)
        .reshape(-1, BS, BS)
    )


def unpack(blocks):
    first_end = 3 * D * D // (BS * BS)
    second_end = first_end + D * D // (BS * BS)
    third_end = second_end + D * FF // (BS * BS)
    qkv_weight = assemble(blocks[:first_end], D, 3 * D)
    out_weight = assemble(blocks[first_end:second_end], D, D)
    up_weight = assemble(blocks[second_end:third_end], D, FF)
    down_weight = assemble(blocks[third_end:], FF, D)
    return (qkv_weight, out_weight, up_weight, down_weight)


def norm_layer(value, gain, shift):
    centred = value - jnp.mean(value, axis=-1, keepdims=True)
    spread = jnp.mean(centred * centred, axis=-1, keepdims=True)
    return centred * lax.rsqrt(spread + 1e-06) * gain + shift


def gelu_exact(value):
    return jax.nn.gelu(value, approximate=False)


def heads_of(tensor):
    return tensor.reshape(tensor.shape[0], tensor.shape[1], HEADS, HD)


def split_rows(member, count, width):
    shaped = member.reshape((member.shape[0], count, width) + member.shape[2:])
    return jnp.moveaxis(shaped, 1, 0)


def in_blocks(update, carry, members, length):
    width = math.gcd(length, 1024)
    count = length // width
    if count == 1:
        return update(carry, members, 0)
    stacked = tuple([split_rows(member, count, width) for member in members])
    offsets = jnp.arange(count, dtype=jnp.int32) * width

    def advance(state, item):
        return (update(state, item[0], item[1]), None)

    result, unused = lax.scan(advance, carry, (stacked, offsets))
    return result


def forward_update(query_heads, scaling):

    def update(carry, members, offset):
        running_max, running_sum, weighted = carry
        key_part, value_part, flag_part = members
        bias = (flag_part.astype(jnp.float32) - 1.0) * masked
        scores = (
            jnp.einsum(
                "sqhd,skhd->shqk",
                query_heads,
                heads_of(key_part),
                preferred_element_type=jnp.float32,
            )
            * scaling
            + bias[:, None, None, :]
        )
        new_max = jnp.maximum(running_max, jnp.max(scores, axis=-1))
        shrink = jnp.exp(running_max - new_max)
        expos = jnp.exp(scores - new_max[..., None])
        running_sum = running_sum * shrink + jnp.sum(expos, axis=-1)
        weighted = weighted * shrink[..., None] + jnp.einsum(
            "shqk,skhd->shqd",
            expos.astype(jnp.bfloat16),
            heads_of(value_part),
            preferred_element_type=jnp.float32,
        )
        return (new_max, running_sum, weighted)

    return update


def query_grad_update(query_heads, dout_heads, log_total, inner, scaling):

    def update(carry, members, offset):
        key_part, value_part, flag_part = members
        bias = (flag_part.astype(jnp.float32) - 1.0) * masked
        scores = (
            jnp.einsum(
                "sqhd,skhd->shqk",
                query_heads,
                heads_of(key_part),
                preferred_element_type=jnp.float32,
            )
            * scaling
            + bias[:, None, None, :]
        )
        probs = jnp.exp(scores - log_total[..., None])
        dprobs = jnp.einsum(
            "sqhd,skhd->shqk", dout_heads, heads_of(value_part), preferred_element_type=jnp.float32
        )
        dscores = (probs * (dprobs - inner[..., None])).astype(jnp.bfloat16)
        return (
            carry
            + jnp.einsum(
                "shqk,skhd->sqhd", dscores, heads_of(key_part), preferred_element_type=jnp.float32
            )
            * scaling
        )

    return update


def key_grad_update(key_heads, value_heads, key_bias, total_rows, inner_rows, scaling, anchor):

    def update(carry, members, offset):
        grad_keys, grad_values = carry
        query_part, dout_part = members
        length = query_part.shape[1]
        total_part = jnp.transpose(
            lax.dynamic_slice_in_dim(total_rows, anchor + offset, length, 1), (0, 2, 1)
        )
        inner_part = jnp.transpose(
            lax.dynamic_slice_in_dim(inner_rows, anchor + offset, length, 1), (0, 2, 1)
        )
        query_heads = heads_of(query_part)
        dout_heads = heads_of(dout_part)
        scores = (
            jnp.einsum(
                "sqhd,skhd->shqk", query_heads, key_heads, preferred_element_type=jnp.float32
            )
            * scaling
            + key_bias[:, None, None, :]
        )
        probs = jnp.exp(scores - total_part[..., None])
        dprobs = jnp.einsum(
            "sqhd,skhd->shqk", dout_heads, value_heads, preferred_element_type=jnp.float32
        )
        dscores = (probs * (dprobs - inner_part[..., None])).astype(jnp.bfloat16)
        grad_values = grad_values + jnp.einsum(
            "shqk,sqhd->skhd",
            probs.astype(jnp.bfloat16),
            dout_heads,
            preferred_element_type=jnp.float32,
        )
        grad_keys = (
            grad_keys
            + jnp.einsum(
                "shqk,sqhd->skhd", dscores, query_heads, preferred_element_type=jnp.float32
            )
            * scaling
        )
        return (grad_keys, grad_values)

    return update


def invert_root(stat):
    identity = jnp.eye(stat.shape[0], dtype=jnp.float32)
    frobenius = jnp.sqrt(jnp.sum(stat * stat))
    approx = identity * lax.rsqrt(jnp.sqrt(frobenius))
    moving = stat / frobenius
    for iteration in range(ITERS):
        factor = (5.0 * identity - moving) * 0.25
        approx = jnp.dot(approx, factor, precision=HIGH)
        square = jnp.dot(factor, factor, precision=HIGH)
        moving = jnp.dot(jnp.dot(square, square, precision=HIGH), moving, precision=HIGH)
    return approx


def precondition(gradient, left_diag, right_diag, weight):
    scaled = gradient * lax.rsqrt(jnp.mean(gradient * gradient) + 1e-06)
    identity = jnp.eye(BS, dtype=jnp.float32)
    left_new = 0.5 * identity * left_diag[None, :] + 0.5 * jnp.dot(scaled, scaled.T, precision=HIGH)
    right_new = 0.5 * identity * right_diag[None, :] + 0.5 * jnp.dot(
        scaled.T, scaled, precision=HIGH
    )
    direction = jnp.dot(
        jnp.dot(invert_root(left_new), scaled, precision=HIGH),
        invert_root(right_new),
        precision=HIGH,
    )
    ratio = jnp.sqrt(jnp.mean(weight * weight)) * lax.rsqrt(jnp.mean(direction * direction) + 1e-06)
    return (left_new, right_new, weight - step_rate * ratio * direction)


MESH = pl.DeviceIdType.MESH
LOW = jnp.bfloat16
FULL = jnp.float32
VMEM_ASK = 60 * 1024 * 1024
GROUP = 24
HALF = 12
QUART = 4


def place():
    samp = lax.axis_index("samp")
    blk = lax.axis_index("blk")
    return (lax.div(samp, 2), lax.rem(samp, 2), lax.div(blk, 2), lax.rem(blk, 2))


def meet(devices):
    barrier = pltpu.get_barrier_semaphore()
    for device in devices:
        pl.semaphore_signal(barrier, inc=1, device_id=device, device_id_type=MESH)
    pl.semaphore_wait(barrier, len(devices))


def meet_all():
    barrier = pltpu.get_barrier_semaphore()
    samp = lax.axis_index("samp")
    blk = lax.axis_index("blk")

    def tell(at, carry):
        to = lax.rem(samp * 8 + blk + at, 32)
        pl.semaphore_signal(
            barrier, inc=1, device_id=(lax.div(to, 8), lax.rem(to, 8)), device_id_type=MESH
        )
        return carry

    lax.fori_loop(1, 32, tell, 0)
    pl.semaphore_wait(barrier, 31)


def turned_pair(n):
    return 2 * lax.rem(n, 2) + lax.div(n, 2)


class Swap:
    def __init__(self, local_sems, send_sems, recv_sems, first=0):
        x, c, z, y = place()
        self.first = first
        self.stays = z == turned_pair(2 * x + c)
        self.to = (turned_pair(z), 2 * turned_pair(2 * x + c) + y)
        self.sems = (local_sems, send_sems, recv_sems)
        self.pairs = []

    def start(self, src, dst):
        at = self.first + len(self.pairs)
        local_sems, send_sems, recv_sems = self.sems
        local = pltpu.make_async_copy(src, dst, local_sems.at[at])
        away = pltpu.make_async_remote_copy(
            src_ref=src, dst_ref=dst, send_sem=send_sems.at[at], recv_sem=recv_sems.at[at],
            device_id=self.to, device_id_type=MESH,
        )
        self.pairs.append((local, away))

        @pl.when(self.stays)
        def keep():
            local.start()

        @pl.when(jnp.logical_not(self.stays))
        def send():
            away.start()

    def finish(self):
        @pl.when(self.stays)
        def kept():
            for local, away in self.pairs:
                local.wait()

        @pl.when(jnp.logical_not(self.stays))
        def sent():
            for local, away in self.pairs:
                away.wait()


def push(src, dst, send, recv, device):
    copy = pltpu.make_async_remote_copy(
        src_ref=src, dst_ref=dst, send_sem=send, recv_sem=recv, device_id=device, device_id_type=MESH
    )
    copy.start()
    return copy


FIRST, SECOND, BOTH, CROSS = range(4)
SIZES = (2, 2, 3, 1)


def gather_blocks(r, notes, while_last):
    x, c, z, y = place()
    samp = 2 * x + c
    blk = 2 * z + y
    to_y = (samp, 2 * z + 1 - y)
    to_x = (2 * (1 - x) + c, blk)
    to_c = (2 * x + 1 - c, blk)
    base = c * HALF
    out = r.weights
    starts = (base + x * 8, base + x * 8 + 2, base + QUART, base + QUART + 3)
    far_starts = (base + (1 - x) * 8, base + (1 - x) * 8 + 2)
    other = (1 - c) * HALF
    parts = [base + x * 8, base + QUART, base + (1 - x) * 8, other, other + QUART, other + 2 * QUART]
    notes_out, note_send, note_recv = r.notes_land, r.note_send, r.note_recv

    def load(at):
        return pltpu.make_async_copy(
            r.masters.at[pl.ds(parts[at], QUART)], r.wide.at[at % 2], r.load_sems.at[at]
        )

    def ready(at):
        load(at).wait()
        out[pl.ds(blk * GROUP + parts[at], QUART)] = r.wide[at % 2].astype(LOW)
        if at + 2 < len(parts):
            load(at + 2).start()

    def copy(group, start, size, sems, at, device):
        place_out = out.at[pl.ds(group * GROUP + start, size)]
        return pltpu.make_async_remote_copy(
            src_ref=place_out, dst_ref=place_out,
            send_sem=sems.at[(0,) + at], recv_sem=sems.at[(1,) + at], device_id=device, device_id_type=MESH,
        )

    def z_copy(kind, way, origin):
        to = (samp, blk + (2 if way == 0 else -2))
        return copy(2 * origin + y, starts[kind], SIZES[kind], r.z_sems, (kind, way, origin), to)

    def z_cross(way, origin, side):
        to = (samp, blk + (2 if way == 0 else -2))
        return copy(2 * origin + side, starts[CROSS], 1, r.z_sems, (CROSS + side, way, origin), to)

    def y_copy(kind, origin):
        return copy(2 * origin + y, starts[kind], SIZES[kind], r.y_sems, (kind, origin), to_y)

    def y_landed(kind, origin):
        return copy(2 * origin + 1 - y, starts[kind], SIZES[kind], r.y_sems, (kind, origin), to_y)

    def x_copy(kind, group):
        return copy(group, starts[kind], SIZES[kind], r.x_sems, (kind, group), to_x)

    def x_landed(kind, group):
        return copy(group, far_starts[kind], SIZES[kind], r.x_sems, (kind, group), to_x)

    def core_copy(kind, group):
        return copy(group, starts[kind], SIZES[kind], r.core_sems, (kind, group), to_c)

    def far_copy(kind, group):
        return copy(group, far_starts[kind], SIZES[kind], r.far_sems, (kind, group), to_c)

    def on_from_here(kind, group):
        if kind in (FIRST, SECOND):
            x_copy(kind, group).start()
        core_copy(kind, group).start()

    def begin(kind):
        @pl.when(z < 3)
        def up():
            z_copy(kind, 0, z).start()

        @pl.when(z > 0)
        def down():
            z_copy(kind, 1, z).start()

        y_copy(kind, z).start()

    def z_step(kind, distance):
        for way in (0, 1):
            origin = z - distance if way == 0 else z + distance

            @pl.when(origin >= 0 if way == 0 else origin <= 3)
            def arrived():
                z_copy(kind, way, origin).wait_recv()

                @pl.when(z < 3 if way == 0 else z > 0)
                def onward():
                    z_copy(kind, way, origin).start()

                y_copy(kind, origin).start()
                on_from_here(kind, 2 * origin + y)

    def y_step(kind, distance):
        for way in (0, 1):
            origin = z - distance if way == 0 else z + distance

            @pl.when(origin >= 0 if way == 0 else origin <= 3)
            def arrived():
                y_landed(kind, origin).wait_recv()
                on_from_here(kind, 2 * origin + 1 - y)

    def y_own(kind):
        y_landed(kind, z).wait_recv()
        on_from_here(kind, 2 * z + 1 - y)

    def cross_step(distance):
        for side in (0, 1):
            for way in (0, 1):
                origin = z - distance if way == 0 else z + distance

                @pl.when(origin >= 0 if way == 0 else origin <= 3)
                def arrived():
                    z_cross(way, origin, side).wait_recv()

                    @pl.when(z < 3 if way == 0 else z > 0)
                    def onward():
                        z_cross(way, origin, side).start()

                    core_copy(CROSS, 2 * origin + side).start()

    def x_step(kind, distance, same):
        for way in (0, 1):
            origin = z - distance if way == 0 else z + distance

            @pl.when(origin >= 0 if way == 0 else origin <= 3)
            def arrived():
                group = 2 * origin + (y if same else 1 - y)
                x_landed(kind, group).wait_recv()
                far_copy(kind, group).start()

    def x_own(kind):
        x_landed(kind, 2 * z + 1 - y).wait_recv()
        far_copy(kind, 2 * z + 1 - y).start()

    note_local = pltpu.make_async_copy(notes, notes_out.at[blk], r.load_sems.at[6])

    def note_copy(j, origin):
        return pltpu.make_async_remote_copy(
            src_ref=notes, dst_ref=notes_out.at[origin], send_sem=note_send.at[j], recv_sem=note_recv.at[origin],
            device_id=(j // 2, 2 * turned_pair(samp) + j % 2), device_id_type=MESH,
        )

    stays = z == turned_pair(samp)

    def is_me(j):
        return jnp.logical_and(stays, 2 * samp + y == j)

    def here_from(j):
        return jnp.logical_and(stays, blk == j)

    load(0).start()
    load(1).start()
    meet_all()
    r.swap_rows.start(r.rows_in, r.rows_land)
    ready(0)
    begin(FIRST)
    begin(SECOND)
    ready(1)
    y_copy(CROSS, z).start()
    for j in range(8):

        @pl.when(jnp.logical_not(is_me(j)))
        def send_note():
            note_copy(j, blk).start()

    @pl.when(stays)
    def keep_note():
        note_local.start()

    for at in range(2, len(parts)):
        ready(at)
    z_step(FIRST, 1)
    y_own(FIRST)
    z_step(SECOND, 1)
    y_own(SECOND)
    begin(BOTH)
    y_landed(CROSS, z).wait_recv()
    core_copy(CROSS, 2 * z + 1 - y).start()
    for way, there in ((0, z < 3), (1, z > 0)):
        for side in (0, 1):
            @pl.when(there)
            def both_sides():
                z_cross(way, z, side).start()

    z_step(FIRST, 2)
    y_step(FIRST, 1)
    z_step(SECOND, 2)
    y_step(SECOND, 1)
    x_own(FIRST)
    z_step(FIRST, 3)
    x_own(SECOND)
    y_step(FIRST, 2)
    z_step(SECOND, 3)
    x_step(FIRST, 1, True)
    y_step(SECOND, 2)
    x_step(SECOND, 1, True)
    y_step(FIRST, 3)
    y_step(SECOND, 3)
    z_step(BOTH, 1)
    x_step(FIRST, 1, False)
    x_step(FIRST, 2, True)
    y_own(BOTH)
    cross_step(1)
    x_step(SECOND, 1, False)
    x_step(SECOND, 2, True)
    z_step(BOTH, 2)
    x_step(FIRST, 3, True)
    y_step(BOTH, 1)
    cross_step(2)
    x_step(FIRST, 2, False)
    z_step(BOTH, 3)
    x_step(SECOND, 3, True)
    y_step(BOTH, 2)
    x_step(SECOND, 2, False)
    cross_step(3)
    x_step(FIRST, 3, False)
    y_step(BOTH, 3)
    x_step(SECOND, 3, False)

    while_last()
    other_starts = (other + x * 8, other + x * 8 + 2, other + QUART, other + QUART + 3)
    other_far = (other + (1 - x) * 8, other + (1 - x) * 8 + 2)

    def settle(group, carry):
        @pl.when(group != blk)
        def other_group():
            for kind in range(4):
                copy(group, other_starts[kind], SIZES[kind], r.core_sems, (kind, group), to_c).wait_recv()
                core_copy(kind, group).wait_send()
            for kind in (FIRST, SECOND):
                copy(group, other_far[kind], SIZES[kind], r.far_sems, (kind, group), to_c).wait_recv()
                far_copy(kind, group).wait_send()
                x_copy(kind, group).wait_send()

        return carry

    lax.fori_loop(0, 8, settle, 0)

    def sent_along(origin, carry):
        for kind in (FIRST, SECOND, BOTH):
            y_copy(kind, origin).wait_send()

            @pl.when(jnp.logical_and(origin <= z, z < 3))
            def up():
                z_copy(kind, 0, origin).wait_send()

            @pl.when(jnp.logical_and(origin >= z, z > 0))
            def down():
                z_copy(kind, 1, origin).wait_send()

        for side in (0, 1):
            @pl.when(jnp.logical_and(origin <= z, z < 3))
            def cross_up():
                z_cross(0, origin, side).wait_send()

            @pl.when(jnp.logical_and(origin >= z, z > 0))
            def cross_down():
                z_cross(1, origin, side).wait_send()

        return carry

    lax.fori_loop(0, 4, sent_along, 0)
    y_copy(CROSS, z).wait_send()
    for j in range(8):

        @pl.when(jnp.logical_not(is_me(j)))
        def sent_note():
            note_copy(j, blk).wait_send()

        @pl.when(jnp.logical_not(here_from(j)))
        def got_note():
            note_copy(j, j).wait_recv()

    @pl.when(stays)
    def kept_note():
        note_local.wait()


def local_any(
    inputs,
    cot_first,
    cot_second,
    valid_flags,
    lead_steps,
    masters,
    assignment,
    left_start,
    right_start,
    vectors,
    vec_moment,
):
    copies = lax.all_gather(masters.astype(jnp.bfloat16), "blk", axis=0, tiled=True)
    blocks = jnp.take(copies, assignment, axis=0)
    qkv_weight, out_weight, up_weight, down_weight = unpack(blocks)
    scaling = HD ** (-0.5)
    flags_low = valid_flags.astype(jnp.bfloat16)
    key_bias = (valid_flags.astype(jnp.float32) - 1.0) * masked
    lead_base = 8 + FF // D
    lead_table = vectors[lead_base:]
    samples = inputs.shape[0]
    patches = inputs.shape[1]

    def forward(hidden_in, lead_ids):
        chosen = (lead_ids[:, None] == jnp.arange(LEADS, dtype=jnp.int32)[None, :]).astype(
            jnp.float32
        )
        lead_rows = jnp.dot(chosen, lead_table, precision=HIGH)
        hidden = hidden_in + lead_rows[:, None, :]
        normed_low = norm_layer(hidden, vectors[0], vectors[1]).astype(jnp.bfloat16)
        packed = jnp.einsum(
            "spd,de->spe", normed_low, qkv_weight, preferred_element_type=jnp.float32
        )
        queries = (packed[..., :D] + vectors[2]).astype(jnp.bfloat16)
        keys_low = packed[..., D : 2 * D].astype(jnp.bfloat16)
        values_low = (packed[..., 2 * D :] + vectors[3]).astype(jnp.bfloat16)
        start_state = (
            jnp.full((samples, HEADS, patches), -1e30, jnp.float32),
            jnp.zeros((samples, HEADS, patches), jnp.float32),
            jnp.zeros((samples, HEADS, patches, HD), jnp.float32),
        )
        update = forward_update(heads_of(queries), scaling)
        gathered = None
        piece = (
            lax.all_gather(keys_low, "blk", axis=1, tiled=True),
            lax.all_gather(values_low, "blk", axis=1, tiled=True),
            lax.all_gather(flags_low, "blk", axis=1, tiled=True),
        )
        running_max, running_sum, weighted = in_blocks(
            update, start_state, piece, piece[0].shape[1]
        )
        attended = jnp.transpose(weighted / running_sum[..., None], (0, 2, 1, 3)).reshape(
            samples, patches, D
        )
        log_total = running_max + jnp.log(running_sum)
        attended_low = attended.astype(jnp.bfloat16)
        middle = (
            hidden
            + jnp.einsum(
                "spd,de->spe", attended_low, out_weight, preferred_element_type=jnp.float32
            )
            + vectors[4]
        )
        normed_two = norm_layer(middle, vectors[5], vectors[6]).astype(jnp.bfloat16)
        upward = jnp.einsum(
            "spd,df->spf", normed_two, up_weight, preferred_element_type=jnp.float32
        ) + vectors[8:lead_base].reshape(FF)
        activated = gelu_exact(upward).astype(jnp.bfloat16)
        result = (
            middle
            + jnp.einsum("spf,fd->spd", activated, down_weight, preferred_element_type=jnp.float32)
            + vectors[7]
        )
        saved = (
            hidden,
            normed_low,
            queries,
            keys_low,
            values_low,
            attended,
            attended_low,
            log_total,
            middle,
            normed_two,
            upward,
            activated,
            chosen,
            gathered,
        )
        return (result, saved)

    def backward(grad_out, saved):
        (
            hidden,
            normed_low,
            queries,
            keys_low,
            values_low,
            attended,
            attended_low,
            log_total,
            middle,
            normed_two,
            upward,
            activated,
            chosen,
            gathered,
        ) = saved
        grad_two = grad_out.astype(jnp.bfloat16)
        down_grad = jnp.einsum(
            "spf,spd->fd", activated, grad_two, preferred_element_type=jnp.float32
        )
        down_bias = jnp.sum(grad_two.astype(jnp.float32), axis=(0, 1))
        grad_act = jnp.einsum(
            "spd,fd->spf", grad_two, down_weight, preferred_element_type=jnp.float32
        )
        gelu_value, gelu_pull = jax.vjp(gelu_exact, upward)
        grad_up = gelu_pull(grad_act)[0].astype(jnp.bfloat16)
        up_grad = jnp.einsum("spd,spf->df", normed_two, grad_up, preferred_element_type=jnp.float32)
        up_bias = jnp.sum(grad_up.astype(jnp.float32), axis=(0, 1))
        grad_normed_two = jnp.einsum(
            "spf,df->spd", grad_up, up_weight, preferred_element_type=jnp.float32
        )
        norm_value, norm_pull = jax.vjp(norm_layer, middle, vectors[5], vectors[6])
        grad_middle_norm, gain_two, shift_two = norm_pull(grad_normed_two)
        grad_middle = grad_out + grad_middle_norm
        grad_one = grad_middle.astype(jnp.bfloat16)
        out_grad = jnp.einsum(
            "spd,spe->de", attended_low, grad_one, preferred_element_type=jnp.float32
        )
        out_bias = jnp.sum(grad_one.astype(jnp.float32), axis=(0, 1))
        grad_attended = jnp.einsum(
            "spe,de->spd", grad_one, out_weight, preferred_element_type=jnp.float32
        ).astype(jnp.bfloat16)
        inner = jnp.sum(
            (grad_attended.astype(jnp.float32) * attended).reshape(samples, patches, HEADS, HD),
            axis=-1,
        )
        inner_heads = jnp.transpose(inner, (0, 2, 1))
        zero_query = jnp.zeros((samples, patches, HEADS, HD), jnp.float32)
        update_query = query_grad_update(
            heads_of(queries), heads_of(grad_attended), log_total, inner_heads, scaling
        )
        piece = (
            lax.all_gather(keys_low, "blk", axis=1, tiled=True),
            lax.all_gather(values_low, "blk", axis=1, tiled=True),
            lax.all_gather(flags_low, "blk", axis=1, tiled=True),
        )
        grad_query = in_blocks(update_query, zero_query, piece, piece[0].shape[1])
        total_rows, inner_rows = (
            lax.all_gather(jnp.transpose(log_total, (0, 2, 1)), "blk", axis=1, tiled=True),
            lax.all_gather(inner, "blk", axis=1, tiled=True),
        )
        key_heads = heads_of(keys_low)
        value_heads = heads_of(values_low)
        zero_pair = (zero_query, zero_query)
        piece = (
            lax.all_gather(queries, "blk", axis=1, tiled=True),
            lax.all_gather(grad_attended, "blk", axis=1, tiled=True),
        )
        update_keys = key_grad_update(
            key_heads, value_heads, key_bias, total_rows, inner_rows, scaling, jnp.int32(0)
        )
        grad_keys, grad_values = in_blocks(update_keys, zero_pair, piece, piece[0].shape[1])
        grad_packed = jnp.concatenate(
            [
                grad_query.reshape(samples, patches, D),
                grad_keys.reshape(samples, patches, D),
                grad_values.reshape(samples, patches, D),
            ],
            axis=-1,
        ).astype(jnp.bfloat16)
        qkv_grad = jnp.einsum(
            "spd,spe->de", normed_low, grad_packed, preferred_element_type=jnp.float32
        )
        query_bias = jnp.sum(grad_packed[..., :D].astype(jnp.float32), axis=(0, 1))
        value_bias = jnp.sum(grad_packed[..., 2 * D :].astype(jnp.float32), axis=(0, 1))
        grad_normed = jnp.einsum(
            "spe,de->spd", grad_packed, qkv_weight, preferred_element_type=jnp.float32
        )
        first_value, first_pull = jax.vjp(norm_layer, hidden, vectors[0], vectors[1])
        grad_hidden_norm, gain_one, shift_one = first_pull(grad_normed)
        grad_hidden = grad_middle + grad_hidden_norm
        lead_grad = jnp.dot(chosen.T, jnp.sum(grad_hidden, axis=1), precision=HIGH)
        vec_rows = jnp.concatenate(
            [
                gain_one[None],
                shift_one[None],
                query_bias[None],
                value_bias[None],
                out_bias[None],
                gain_two[None],
                shift_two[None],
                down_bias[None],
                up_bias.reshape(FF // D, D),
                lead_grad,
            ],
            axis=0,
        )
        return (grad_hidden, (qkv_grad, out_grad, up_grad, down_grad), vec_rows)

    earlier, saved_one = forward(inputs.astype(jnp.float32), lead_steps[0])
    later, saved_two = forward(earlier, lead_steps[1])
    grad_between, mats_two, vec_two = backward(cot_second.astype(jnp.float32), saved_two)
    input_grad, mats_one, vec_one = backward(
        cot_first.astype(jnp.float32) + grad_between, saved_one
    )
    grad_blocks = jnp.concatenate(
        [
            carve(mats_one[0] + mats_two[0]),
            carve(mats_one[1] + mats_two[1]),
            carve(mats_one[2] + mats_two[2]),
            carve(mats_one[3] + mats_two[3]),
        ],
        axis=0,
    )
    position = jnp.arange(NB, dtype=jnp.int32)
    inverse = jnp.sum(
        jnp.where(assignment[None, :] == position[:, None], position[None, :], 0), axis=1
    )
    slotted = jnp.take(grad_blocks, inverse, axis=0)
    shared = lax.psum_scatter(slotted, "blk", scatter_dimension=0, tiled=True)
    matrix_grads = lax.psum(shared.astype(jnp.bfloat16), "samp").astype(jnp.float32)
    vec_grads = lax.psum(vec_one + vec_two, ("samp", "blk"))
    left_stats, right_stats, new_masters = jax.vmap(precondition)(
        matrix_grads, left_start, right_start, masters
    )
    scaled_vec = vec_grads * lax.rsqrt(
        jnp.mean(vec_grads * vec_grads, axis=1, keepdims=True) + 1e-06
    )
    vec_moments = 0.5 * vec_moment + 0.5 * scaled_vec * scaled_vec
    new_vectors = vectors - vector_rate * scaled_vec * lax.rsqrt(vec_moments)
    return (
        earlier.astype(jnp.bfloat16),
        later.astype(jnp.bfloat16),
        input_grad,
        matrix_grads,
        left_stats,
        right_stats,
        new_masters,
        new_masters.astype(jnp.bfloat16),
        vec_grads,
        vec_moments,
        new_vectors,
    )


TOKENS = 128
PAIR = 2 * HD
SEQ_ALL = 8 * TOKENS
QKV_AT, OUT_AT, UP_AT, DOWN_AT = 0, 48, 64, 128
WIDE = D // BS
DEEP = FF // BS
LEAD_AT = 8 + FF // D


def dot(left, right):
    return jnp.dot(left, right, preferred_element_type=FULL)


def dot_t(left, right):
    return lax.dot_general(left, right, (((1,), (1,)), ((), ())), preferred_element_type=FULL)


def normal(value):
    centred = value - jnp.mean(value, axis=-1, keepdims=True)
    rate = lax.rsqrt(jnp.mean(centred * centred, axis=-1, keepdims=True) + 1e-06)
    return (centred * rate, rate)


def normal_back(grad, unit, rate, gain):
    scaled = grad * gain
    return rate * (
        scaled
        - jnp.mean(scaled, axis=-1, keepdims=True)
        - unit * jnp.mean(scaled * unit, axis=-1, keepdims=True)
    )


def total(value):
    return jnp.sum(value, axis=0, keepdims=True)


def gelu_parts(value):
    phi = 0.5 + 0.5 * lax.erf(value * (0.5**0.5))
    return phi, value * phi


def gelu_slope(value):
    phi, unused = gelu_parts(value)
    return phi + value * jnp.exp(-0.5 * value * value) * ((2.0 * math.pi) ** -0.5)


class Weights:
    def __init__(self, slots, held):
        self.slots, self.held = slots, held

    def block(self, base, cols, row, col):
        return self.held[self.slots[base + row * cols + col]]

    def down_col(self, base, rows, cols, col):
        return jnp.concatenate([self.block(base, cols, row, col) for row in range(rows)], axis=0)

    def along_row(self, base, cols, row, first=0, last=None):
        return jnp.concatenate(
            [self.block(base, cols, row, col) for col in range(first, cols if last is None else last)], axis=1
        )


def lead_row(vecs, lead):
    row = jnp.zeros((1, D), FULL)
    for at in range(LEADS):
        row = row + jnp.where(lead == at, vecs[LEAD_AT + at : LEAD_AT + at + 1], 0.0)
    return row


def project(r, layer, hidden, vecs, weights):
    unit, unused = normal(hidden)
    normed = unit * vecs[0:1] + vecs[1:2]
    for k in range(WIDE):
        r.left_held[layer, k] = normed[:, k * BS : (k + 1) * BS].T.astype(LOW)
    give_pool(r, True, layer, 0)
    normed = normed.astype(LOW)
    for step in range(WIDE):
        within = lax.rem(step + lax.div(r.plane.me, 2), WIDE)
        cols = pl.ds(pl.multiple_of(within * BS, BS), BS)
        for kind in range(3):
            part = dot(normed, weights.down_col(QKV_AT, WIDE, 3 * WIDE, kind * WIDE + within))
            if kind != 1:
                row = 2 if kind == 0 else 3
                part = part + vecs[row : row + 1, cols]
            part = part.astype(LOW)
            for half in range(2):
                r.packed[2 * within + half, :, kind * PAIR : (kind + 1) * PAIR] = part[
                    :, half * PAIR : (half + 1) * PAIR
                ]
        for half in range(2):
            r.plane.send_or_keep(r.packed, r.held[layer], r.in_sems[layer], 2 * within + half)


def pool_at(left, kind):
    counts, bases = (LEFTS, LEFT_AT) if left else (RIGHTS, RIGHT_AT)
    return pl.ds(bases[kind], counts[kind])


def pool_copies(r, left, layer, kind):
    x, c, z, y = place()
    ids = pool_at(left, kind)
    at = (0 if left else 8) + 4 * layer + kind
    source = (r.left_held if left else r.right_held).at[layer, ids]

    def target(part):
        tokens = pl.ds((2 * part + layer) * TOKENS, TOKENS)
        return r.left_pool.at[ids, :, tokens] if left else r.right_pool.at[ids, tokens]

    here = pltpu.make_async_copy(source, target(0), r.pool_sems.at[0, at])
    there = pltpu.make_async_remote_copy(
        src_ref=source, dst_ref=target(1), send_sem=r.pool_sems.at[1, at], recv_sem=r.pool_sems.at[2, at],
        device_id=(2 * x + 1 - c, 2 * z + y), device_id_type=MESH,
    )
    return here, there


def give_pool(r, left, layer, kind):
    for copy in pool_copies(r, left, layer, kind):
        copy.start()


def feed(r, layer, hidden, vecs, weights, u_held):
    attended = jnp.concatenate([r.o_land[j] for j in range(8)], axis=1)
    for k in range(WIDE):
        r.left_held[layer, WIDE + k] = attended[:, k * BS : (k + 1) * BS].astype(FULL).T.astype(LOW)
    give_pool(r, True, layer, 1)
    branch = [dot(attended, weights.down_col(OUT_AT, WIDE, WIDE, n)) for n in range(WIDE)]
    middle = hidden + jnp.concatenate(branch, axis=1) + vecs[4:5]
    unit, unused = normal(middle)
    normed = unit * vecs[5:6] + vecs[6:7]
    for k in range(WIDE):
        r.left_held[layer, 2 * WIDE + k] = normed[:, k * BS : (k + 1) * BS].T.astype(LOW)
    give_pool(r, True, layer, 2)
    normed = normed.astype(LOW)
    per = D // BS
    for f in range(DEEP):
        bias = vecs[8 + f // per : 9 + f // per, (f % per) * BS : (f % per + 1) * BS]
        upward = dot(normed, weights.down_col(UP_AT, WIDE, DEEP, f)) + bias
        u_held[f] = upward
        activated = gelu_parts(upward)[1]
        r.act_held[:, f * BS : (f + 1) * BS] = activated.astype(LOW)
        r.left_held[layer, 3 * WIDE + f] = activated.T.astype(LOW)
    give_pool(r, True, layer, 3)
    branch = [dot(r.act_held[...], weights.down_col(DOWN_AT, DEEP, WIDE, n)) for n in range(WIDE)]
    return middle, middle + jnp.concatenate(branch, axis=1) + vecs[7:8]


def feed_back(r, layer, grad_out, middle, u_in, vecs, weights):
    rows = r.rows
    grad_two = grad_out.astype(LOW)
    for k in range(WIDE):
        r.right_held[layer, RIGHT_AT[3] + k] = grad_two[:, k * BS : (k + 1) * BS]
    give_pool(r, False, layer, 3)
    rows[7:8] += total(grad_two.astype(FULL))
    per = D // BS
    for f in range(DEEP):
        grad_act = dot_t(grad_two, weights.along_row(DOWN_AT, WIDE, f))
        grad_up = (grad_act * gelu_slope(u_in[f])).astype(LOW)
        r.right_held[layer, RIGHT_AT[2] + f] = grad_up
        rows[8 + f // per : 9 + f // per, (f % per) * BS : (f % per + 1) * BS] += total(grad_up.astype(FULL))
    give_pool(r, False, layer, 2)
    grad_up = jnp.concatenate([r.right_held[layer, RIGHT_AT[2] + f] for f in range(DEEP)], axis=1)
    grad_normed = jnp.concatenate(
        [dot_t(grad_up, weights.along_row(UP_AT, DEEP, k)) for k in range(WIDE)], axis=1
    )
    unit, rate = normal(middle)
    rows[5:6] += total(grad_normed * unit)
    rows[6:7] += total(grad_normed)
    grad_middle = grad_out + normal_back(grad_normed, unit, rate, vecs[5:6])
    grad_one = grad_middle.astype(LOW)
    for k in range(WIDE):
        r.right_held[layer, RIGHT_AT[1] + k] = grad_one[:, k * BS : (k + 1) * BS]
    give_pool(r, False, layer, 1)
    rows[4:5] += total(grad_one.astype(FULL))
    for k in range(WIDE):
        part = dot_t(grad_one, weights.along_row(OUT_AT, WIDE, k)).astype(LOW)
        for half in range(2):
            r.do_message[2 * k + half] = part[:, half * PAIR : (half + 1) * PAIR]
            r.plane.send_or_keep(r.do_message, r.do_land, r.do_sems[layer], 2 * k + half)
    return grad_middle


def project_back(r, layer, grad_middle, hidden, vecs, weights, lead):
    rows = r.rows

    def blocks_of_kind(kind):
        source, cols = (r.dq_land, slice(0, PAIR)) if kind == 0 else (r.dkv_land, slice((kind - 1) * PAIR, kind * PAIR))
        for within in range(WIDE):
            part = jnp.concatenate([source[2 * within, :, cols], source[2 * within + 1, :, cols]], axis=1)
            r.right_held[layer, kind * WIDE + within] = part
            if kind != 1:
                row = 2 if kind == 0 else 3
                rows[row : row + 1, within * BS : (within + 1) * BS] += total(part.astype(FULL))

    def back(first, last):
        part = jnp.concatenate([r.right_held[layer, n] for n in range(first, last)], axis=1)
        return jnp.concatenate(
            [dot_t(part, weights.along_row(QKV_AT, 3 * WIDE, k, first, last)) for k in range(WIDE)], axis=1
        )

    r.plane.received(r.dkv_land, r.dkv_sems[layer])
    blocks_of_kind(1)
    blocks_of_kind(2)
    grad_normed = back(WIDE, 3 * WIDE)
    r.plane.received(r.dq_land, r.dq_sems[layer])
    blocks_of_kind(0)
    give_pool(r, False, layer, 0)
    grad_normed = grad_normed + back(0, WIDE)
    unit, rate = normal(hidden)
    rows[0:1] += total(grad_normed * unit)
    rows[1:2] += total(grad_normed)
    grad_hidden = grad_middle + normal_back(grad_normed, unit, rate, vecs[0:1])
    sums = total(grad_hidden)
    for at in range(LEADS):
        rows[LEAD_AT + at : LEAD_AT + at + 1] += jnp.where(lead == at, sums, 0.0)
    return grad_hidden


def attend(r, layer):
    held, turned, stats = r.held[layer], r.turned[layer], r.stats[layer]
    plane = r.plane
    plane.received(held, r.in_sems[layer])
    both = held[...].reshape(SEQ_ALL, 3 * PAIR)
    queries = both[:, :PAIR].astype(FULL)
    keys = both[:, PAIR : 2 * PAIR].astype(FULL)
    values_t = both[:, 2 * PAIR :].astype(FULL).T.astype(LOW)
    for head in range(2):
        q_side, k_side, unused = head_sides(queries, keys, r.neg[...], head)
        r.query_side[head] = q_side.astype(LOW)
        r.key_side[head] = k_side.astype(LOW)

    def chunk(step, carry):
        at = lax.rem(step + lax.div(plane.me, 2), 4)
        first = pl.multiple_of(at * BS, BS)
        for head in range(2):
            scores = dot_t(r.key_side[head], r.query_side[head, pl.ds(first, BS)])
            most = jnp.max(scores, axis=0, keepdims=True)
            expos = jnp.exp(scores - most)
            sums = jnp.sum(expos, axis=0, keepdims=True)
            part = dot(values_t[head * HD : (head + 1) * HD], expos.astype(LOW)) / sums
            turned[at, head * HD : (head + 1) * HD] = part
            stats[head : head + 1, pl.ds(first, BS)] = most + jnp.log(sums)
        for half in range(2):
            to = 2 * at + half
            r.o_message[to] = turned[at, :, half * TOKENS : (half + 1) * TOKENS].T.astype(LOW)
            plane.send_or_keep(r.o_message, r.o_land, r.o_sems[layer], to)
        return carry

    lax.fori_loop(0, SEQ_ALL // BS, chunk, 0)
    plane.sent(r.packed, r.in_sems[layer])
    plane.received(r.o_land, r.o_sems[layer])
    plane.sent(r.o_message, r.o_sems[layer])


def attend_back(r, layer):
    held, turned, stats = r.held[layer], r.turned[layer], r.stats[layer]
    plane = r.plane
    both = held[...].reshape(SEQ_ALL, 3 * PAIR)
    queries = both[:, :PAIR].astype(FULL)
    keys = both[:, PAIR : 2 * PAIR].astype(FULL)
    keys_t = keys.T.astype(LOW)
    r.grad_q[...] = jnp.zeros_like(r.grad_q)
    for head in range(2):
        q_side, k_side, own = head_sides(queries, keys, r.neg[...], head)
        r.query_side[head] = q_side.astype(LOW)
        r.query_plain[head] = jnp.where(own, q_side, 0.0).astype(LOW)
        r.key_side[head] = k_side.astype(LOW)
    plane.received(r.do_land, r.do_sems[layer])
    grads = r.do_land[...].reshape(SEQ_ALL, PAIR).astype(FULL)
    lane = lax.broadcasted_iota(jnp.int32, grads.shape, 1)
    r.do_side[0] = jnp.where(lane < HD, grads, 0.0).astype(LOW)
    r.do_side[1] = jnp.where(lane >= HD, grads, 0.0).astype(LOW)
    grads_t = grads.T
    inner = []
    for head in range(2):
        side = slice(head * HD, (head + 1) * HD)
        inner.append(
            jnp.concatenate(
                [
                    jnp.sum(turned[at, side] * grads_t[side, at * BS : (at + 1) * BS], axis=0, keepdims=True)
                    for at in range(SEQ_ALL // BS)
                ],
                axis=1,
            )
        )
    left = lax.broadcasted_iota(jnp.int32, (BS, PAIR), 1) < HD
    keys_held = [keys_t[head * HD : (head + 1) * HD] for head in range(2)]
    for at in range(SEQ_ALL // BS):
        first = at * BS
        grad_k = []
        grad_v = None
        values = held[2 * at : 2 * at + 2, :, 2 * PAIR :].reshape(BS, PAIR)
        for head in range(2):
            scores = dot_t(r.key_side[head, first : first + BS], r.query_side[head])
            probs = jnp.exp(scores - stats[head : head + 1])
            dprobs = dot_t(values, r.do_side[head])
            dscores = (probs * (dprobs - inner[head])).astype(LOW)
            term = dot(probs.astype(LOW), r.do_side[head])
            grad_v = term if grad_v is None else grad_v + term
            grad_k.append(dot(dscores, r.query_plain[head]))
            r.grad_q[head * HD : (head + 1) * HD] += dot(keys_held[head][:, first : first + BS], dscores)
        grad_k = jnp.where(left, grad_k[0], grad_k[1]).astype(LOW)
        grad_v = grad_v.astype(LOW)
        for half in range(2):
            to = 2 * at + half
            rows = slice(half * TOKENS, (half + 1) * TOKENS)
            r.dkv_message[to, :, :PAIR] = grad_k[rows]
            r.dkv_message[to, :, PAIR:] = grad_v[rows]
            plane.send_or_keep(r.dkv_message, r.dkv_land, r.dkv_sems[layer], to)
    for j in range(8):
        r.dq_message[j] = (r.grad_q[:, j * TOKENS : (j + 1) * TOKENS].T * HD**-0.5).astype(LOW)
        plane.send_or_keep(r.dq_message, r.dq_land, r.dq_sems[layer], j)


class Refs:
    pass


SCRATCH = (
    ("weights", pltpu.VMEM((NB, BS, BS), LOW)),
    ("wide", pltpu.VMEM((2, QUART, BS, BS), FULL)),
    ("notes_land", pltpu.VMEM((8, 8, TOKENS), FULL)),
    ("rows_land", pltpu.VMEM((1, TOKENS, D), LOW)),
    ("first_land", pltpu.VMEM((1, TOKENS, D), LOW)),
    ("second_land", pltpu.VMEM((1, TOKENS, D), LOW)),
    ("pred_one", pltpu.VMEM((1, TOKENS, D), LOW)),
    ("pred_two", pltpu.VMEM((1, TOKENS, D), LOW)),
    ("hidden_one", pltpu.VMEM((TOKENS, D), FULL)),
    ("hidden_two", pltpu.VMEM((TOKENS, D), FULL)),
    ("middle_one", pltpu.VMEM((TOKENS, D), FULL)),
    ("u_one", pltpu.VMEM((DEEP, TOKENS, BS), FULL)),
    ("u_two", pltpu.VMEM((DEEP, TOKENS, BS), FULL)),
    ("act_held", pltpu.VMEM((TOKENS, FF), LOW)),
    ("left_held", pltpu.VMEM((2, 3 * WIDE + DEEP, BS, TOKENS), LOW)),
    ("right_held", pltpu.VMEM((2, 5 * WIDE + DEEP, TOKENS, BS), LOW)),
    ("packed", pltpu.VMEM((8, TOKENS, 3 * PAIR), LOW)),
    ("held", pltpu.VMEM((2, 8, TOKENS, 3 * PAIR), LOW)),
    ("turned", pltpu.VMEM((2, SEQ_ALL // BS, PAIR, BS), FULL)),
    ("stats", pltpu.VMEM((2, 8, SEQ_ALL), FULL)),
    ("o_message", pltpu.VMEM((8, TOKENS, PAIR), LOW)),
    ("o_land", pltpu.VMEM((8, TOKENS, PAIR), LOW)),
    ("do_message", pltpu.VMEM((8, TOKENS, PAIR), LOW)),
    ("do_land", pltpu.VMEM((8, TOKENS, PAIR), LOW)),
    ("dq_message", pltpu.VMEM((8, TOKENS, PAIR), LOW)),
    ("dq_land", pltpu.VMEM((8, TOKENS, PAIR), LOW)),
    ("dkv_message", pltpu.VMEM((8, TOKENS, 2 * PAIR), LOW)),
    ("dkv_land", pltpu.VMEM((8, TOKENS, 2 * PAIR), LOW)),
    ("neg", pltpu.VMEM((SEQ_ALL, PAIR), FULL)),
    ("query_side", pltpu.VMEM((2, SEQ_ALL, PAIR), LOW)),
    ("query_plain", pltpu.VMEM((2, SEQ_ALL, PAIR), LOW)),
    ("key_side", pltpu.VMEM((2, SEQ_ALL, PAIR), LOW)),
    ("do_side", pltpu.VMEM((2, SEQ_ALL, PAIR), LOW)),
    ("grad_q", pltpu.VMEM((PAIR, SEQ_ALL), FULL)),
    ("load_sems", pltpu.SemaphoreType.DMA((7,))),
    ("z_sems", pltpu.SemaphoreType.DMA((2, 5, 2, 4))),
    ("y_sems", pltpu.SemaphoreType.DMA((2, 4, 4))),
    ("x_sems", pltpu.SemaphoreType.DMA((2, 2, 8))),
    ("core_sems", pltpu.SemaphoreType.DMA((2, 4, 8))),
    ("far_sems", pltpu.SemaphoreType.DMA((2, 2, 8))),
    ("note_send", pltpu.SemaphoreType.DMA((8,))),
    ("note_recv", pltpu.SemaphoreType.DMA((8,))),
    ("swap_local", pltpu.SemaphoreType.DMA((5,))),
    ("swap_send", pltpu.SemaphoreType.DMA((5,))),
    ("swap_recv", pltpu.SemaphoreType.DMA((5,))),
    ("plane_sems", pltpu.SemaphoreType.DMA((5, 2, 2, 8))),
    ("pool_sems", pltpu.SemaphoreType.DMA((3, 16))),
)
INPUTS = ("slots", "masters", "notes", "rows_in", "first_in", "second_in", "vectors")
OUTPUTS = ("left_pool", "right_pool", "pred_one_out", "pred_two_out", "input_grad", "rows")


def model_kernel(*refs):
    r = Refs()
    for name, ref in zip(INPUTS + OUTPUTS + tuple(name for name, unused in SCRATCH), refs):
        setattr(r, name, ref)
    for name in ("held", "turned", "stats"):
        setattr(r, name, [getattr(r, name).at[layer] for layer in range(2)])
    for at, name in enumerate(("in_sems", "o_sems", "do_sems", "dq_sems", "dkv_sems")):
        setattr(r, name, [r.plane_sems.at[at, layer] for layer in range(2)])
    swaps = [Swap(r.swap_local, r.swap_send, r.swap_recv, at) for at in range(5)]
    r.swap_rows = swaps[0]
    r.plane = Plane()
    vecs = r.vectors
    weights = Weights(r.slots, r.weights)

    def while_last():
        swaps[1].start(r.second_in, r.second_land)
        swaps[2].start(r.first_in, r.first_land)
        swaps[0].finish()
        r.rows[...] = jnp.zeros_like(r.rows)
        for layer in range(2):
            r.stats[layer][...] = jnp.zeros((8, SEQ_ALL), FULL)

    gather_blocks(r, r.notes, while_last)
    mask_columns(r.notes_land, r.neg)
    leads = [r.notes_land[0, 1:2, at : at + 1] for at in range(2)]
    r.hidden_one[...] = r.rows_land[0].astype(FULL) + lead_row(vecs, leads[0])
    project(r, 0, r.hidden_one[...], vecs, weights)
    attend(r, 0)
    middle, result = feed(r, 0, r.hidden_one[...], vecs, weights, r.u_one)
    r.middle_one[...] = middle
    r.pred_one[0] = result.astype(LOW)
    swaps[3].start(r.pred_one, r.pred_one_out)
    r.hidden_two[...] = result + lead_row(vecs, leads[1])
    project(r, 1, r.hidden_two[...], vecs, weights)
    attend(r, 1)
    middle, result = feed(r, 1, r.hidden_two[...], vecs, weights, r.u_two)
    r.pred_two[0] = result.astype(LOW)
    swaps[4].start(r.pred_two, r.pred_two_out)
    swaps[1].finish()
    grad_middle = feed_back(r, 1, r.second_land[0].astype(FULL), middle, r.u_two, vecs, weights)
    attend_back(r, 1)
    grad = project_back(r, 1, grad_middle, r.hidden_two[...], vecs, weights, leads[1])
    for source, sems in ((r.do_message, r.do_sems), (r.dkv_message, r.dkv_sems), (r.dq_message, r.dq_sems)):
        r.plane.sent(source, sems[1])
    swaps[2].finish()
    grad = grad + r.first_land[0].astype(FULL)
    grad_middle = feed_back(r, 0, grad, r.middle_one[...], r.u_one, vecs, weights)
    attend_back(r, 0)
    grad = project_back(r, 0, grad_middle, r.hidden_one[...], vecs, weights, leads[0])
    r.input_grad[0] = grad.astype(LOW)
    for source, sems in ((r.do_message, r.do_sems), (r.dkv_message, r.dkv_sems), (r.dq_message, r.dq_sems)):
        r.plane.sent(source, sems[0])
    for left in (True, False):
        for layer in range(2):
            for kind in range(4):
                for copy in pool_copies(r, left, layer, kind):
                    copy.wait()
    swaps[3].finish()
    swaps[4].finish()


def model(slots, masters, notes, rows, first, second, vectors):
    return pl.pallas_call(
        model_kernel,
        out_shape=(
            shape((N_LEFT, BS, 4 * TOKENS)),
            shape((N_RIGHT, 4 * TOKENS, BS)),
            SHAPES["pred"],
            SHAPES["pred"],
            SHAPES["pred"],
            SHAPES["rows"],
        ),
        in_specs=[SMEM_IN] + [ANY_AT] * 5 + [VMEM_AT],
        out_specs=(ANY_AT,) * 4 + (VMEM_AT,) * 2,
        scratch_shapes=[spec for unused, spec in SCRATCH],
        compiler_params=pltpu.CompilerParams(
            collective_id=0, has_side_effects=True, vmem_limit_bytes=63 * 1024 * 1024
        ),
        cost_estimate=pl.CostEstimate(flops=24 << 30, bytes_accessed=60 << 20, transcendentals=1 << 23),
        name="model",
    )(slots, masters, notes, rows, first, second, vectors)


SMEM_IN = pl.BlockSpec(memory_space=pltpu.SMEM)
VMEM_AT = pl.BlockSpec(memory_space=pltpu.VMEM)
ANY_AT = pl.BlockSpec(memory_space=pl.ANY)


def shape(dims, kind=LOW):
    return jax.ShapeDtypeStruct(dims, kind)


SHAPES = {"pred": shape((1, TOKENS, D)), "rows": shape((20, D), FULL)}


def bias_pieces():
    left = masked
    pieces = []
    for unused in range(3):
        piece = float(ml_dtypes.bfloat16(left))
        pieces.append(piece)
        left -= piece
    assert left == 0.0
    return pieces


MASK_PIECES = bias_pieces()


def head_sides(queries, keys, neg, head):
    lane = lax.broadcasted_iota(jnp.int32, queries.shape, 1)
    own = (lane < HD) if head == 0 else (lane >= HD)
    spot = lane - (HD if head == 0 else 0)
    key_side = jnp.zeros_like(keys)
    for at, piece in enumerate(MASK_PIECES):
        key_side = jnp.where(spot == at, neg * piece, key_side)
    key_side = jnp.where(own, keys, key_side)
    ones = jnp.where((spot >= 0) & (spot < 3), 1.0, 0.0)
    query_side = jnp.where(own, queries * HD**-0.5, ones)
    return query_side, key_side, own


class Plane:
    def __init__(self):
        x, c, z, y = place()
        self.z = z
        self.me = 4 * c + 2 * x + y

    def device(self, j):
        return (turned_pair(lax.div(j, 2)), 2 * self.z + lax.rem(j, 2))

    def other(self, step):
        return lax.rem(self.me + step, 8)

    def others(self):
        return [self.device(self.other(step)) for step in range(1, 8)]

    def copy(self, src, dst, sems, send_at, recv_at, to):
        return pltpu.make_async_remote_copy(
            src_ref=src, dst_ref=dst, send_sem=sems.at[0, send_at], recv_sem=sems.at[1, recv_at],
            device_id=self.device(to), device_id_type=MESH,
        )

    def send(self, source, target, sems, to):
        self.copy(source.at[to], target.at[self.me], sems, to, self.me, to).start()

    def send_or_keep(self, source, target, sems, to):
        @pl.when(to != self.me)
        def away():
            self.send(source, target, sems, to)

        @pl.when(to == self.me)
        def keep():
            target[to] = source[to]

    def received(self, target, sems):
        for step in range(1, 8):
            j = self.other(step)
            self.copy(target.at[j], target.at[j], sems, j, j, j).wait_recv()

    def sent(self, source, sems):
        for step in range(1, 8):
            j = self.other(step)
            self.copy(source.at[j], source.at[j], sems, j, j, j).wait_send()


def mask_columns(notes, neg):
    for j in range(8):
        neg[j * TOKENS : (j + 1) * TOKENS] = jnp.broadcast_to(notes[j, 0:1], (TOKENS, TOKENS)).T


LEFTS = (WIDE, WIDE, WIDE, DEEP)
RIGHTS = (3 * WIDE, WIDE, DEEP, WIDE)
LEFT_AT = (0, WIDE, 2 * WIDE, 3 * WIDE)
RIGHT_AT = (0, 3 * WIDE, 4 * WIDE, 4 * WIDE + DEEP)
N_LEFT = 3 * WIDE + DEEP
N_RIGHT = 5 * WIDE + DEEP


def pools_of(block):
    left = jnp.zeros_like(block)
    right = jnp.zeros_like(block)
    for at, base in enumerate((QKV_AT, OUT_AT, UP_AT, DOWN_AT)):
        inside = block >= base
        cols = RIGHTS[at]
        left = jnp.where(inside, LEFT_AT[at] + (block - base) // cols, left)
        right = jnp.where(inside, RIGHT_AT[at] + (block - base) % cols, right)
    return left, right


def halves(value):
    high = value.astype(LOW)
    return high, (value - high.astype(FULL)).astype(LOW)


def fine(left, right):
    return dot(
        jnp.concatenate([left[0], left[1], left[0]], axis=1),
        jnp.concatenate([right[0], right[0], right[1]], axis=0),
    )


def statistic(gram, shrink, diag, eye):
    return jnp.where(eye, 0.5 * diag, 0.0) + shrink * gram


def roots(stats, eye):
    scales = [jnp.sqrt(jnp.sum(jnp.sum(stat * stat, axis=1, keepdims=True), axis=0, keepdims=True)) for stat in stats]
    moving = [stat / scale for stat, scale in zip(stats, scales)]
    approx = [None] * len(stats)
    ahead = range(len(stats))
    for iteration in range(ITERS):
        factors = [(jnp.where(eye, 5.0, 0.0) - moving[i]) * 0.25 for i in ahead]
        parts = [halves(factor) for factor in factors]
        if iteration == 0:
            approx = [factors[i] * lax.rsqrt(jnp.sqrt(scales[i])) for i in ahead]
        else:
            approx = [fine(halves(approx[i]), parts[i]) for i in ahead]
        if iteration < ITERS - 1:
            squares = [halves(fine(parts[i], parts[i])) for i in ahead]
            fourths = [halves(fine(squares[i], squares[i])) for i in ahead]
            moving = [fine(fourths[i], halves(moving[i])) for i in ahead]
    return approx


PAIRED = 2
SUM_SCRATCH = (
    ("left_t", pltpu.VMEM((N_LEFT, BS, 4 * TOKENS), LOW)),
    ("right_pool", pltpu.VMEM((N_RIGHT, 4 * TOKENS, BS), LOW)),
    ("x_stage", pltpu.VMEM((2, 2, 4, PAIRED, BS, BS), LOW)),
    ("x_land", pltpu.VMEM((2, 2, 4, PAIRED, BS, BS), LOW)),
    ("yb_stage", pltpu.VMEM((4, QUART, BS, BS), LOW)),
    ("yb_land", pltpu.VMEM((4, QUART, BS, BS), LOW)),
    ("ym_stage", pltpu.VMEM((2, 4, PAIRED, BS, BS), LOW)),
    ("ym_land", pltpu.VMEM((2, 4, PAIRED, BS, BS), LOW)),
    ("zb_stage", pltpu.VMEM((4, QUART, BS, BS), LOW)),
    ("zb_land", pltpu.VMEM((3, QUART, BS, BS), LOW)),
    ("zm_stage", pltpu.VMEM((2, 4, PAIRED, BS, BS), LOW)),
    ("zm_land", pltpu.VMEM((2, 3, PAIRED, BS, BS), LOW)),
    ("both_stage", pltpu.VMEM((2, PAIRED, BS, BS), LOW)),
    ("both_land", pltpu.VMEM((PAIRED, BS, BS), LOW)),
    ("own", pltpu.VMEM((6, BS, BS), LOW)),
    ("staged", pltpu.VMEM((6, BS, BS), LOW)),
    ("pair_rows", pltpu.VMEM((20, D), FULL)),
    ("chip_rows", pltpu.VMEM((20, D), FULL)),
    ("plane_rows", pltpu.VMEM((20, D), FULL)),
    ("row_land", pltpu.VMEM((3, 20, D), FULL)),
    ("row_z", pltpu.VMEM((4, 20, D), FULL)),
    ("pool_sems", pltpu.SemaphoreType.DMA((2,))),
    ("send_sems", pltpu.SemaphoreType.DMA((11, 4))),
    ("recv_sems", pltpu.SemaphoreType.DMA((11, 4))),
    ("row_send", pltpu.SemaphoreType.DMA((6,))),
    ("row_recv", pltpu.SemaphoreType.DMA((6,))),
    ("share_send", pltpu.SemaphoreType.DMA((6, 6))),
    ("share_recv", pltpu.SemaphoreType.DMA((6, 6))),
    ("local_sems", pltpu.SemaphoreType.DMA((9,))),
    ("swap_local", pltpu.SemaphoreType.DMA((1,))),
    ("swap_send", pltpu.SemaphoreType.DMA((1,))),
    ("swap_recv", pltpu.SemaphoreType.DMA((1,))),
)
SUM_INPUTS = ("left_ids", "right_ids", "rows_in", "left_diag", "right_diag", "grad_in", "left_in", "right_in")
SUM_OUTPUTS = ("rows_out", "grads_out", "moves_out", "grad_out")


def update_kernel(*refs):
    r = Refs()
    for name, ref in zip(SUM_INPUTS + SUM_OUTPUTS + tuple(name for name, unused in SUM_SCRATCH), refs):
        setattr(r, name, ref)
    here = [
        pltpu.make_async_copy(r.right_in, r.right_pool, r.pool_sems.at[0]),
        pltpu.make_async_copy(r.left_in, r.left_t, r.pool_sems.at[1]),
    ]
    for copy in here:
        copy.start()
    x, c, z, y = place()
    samp = 2 * x + c
    blk = 2 * z + y
    to_c = (2 * x + 1 - c, blk)
    to_x = (2 * (1 - x) + c, blk)
    to_y = (samp, 2 * z + 1 - y)
    to_z = [(samp, 2 * lax.rem(z + step, 4) + y) for step in (1, 2, 3)]
    meet_all()
    swap = Swap(r.swap_local, r.swap_send, r.swap_recv)
    swap.start(r.grad_in, r.grad_out)
    row_copies = [push(r.rows_in, r.row_land.at[0], r.row_send.at[0], r.row_recv.at[0], to_c)]
    eye = lax.broadcasted_iota(jnp.int32, (BS, BS), 0) == lax.broadcasted_iota(jnp.int32, (BS, BS), 1)

    def group(half, k):
        return 2 * lax.rem(z + 1 + k, 4) + (1 - y if half == 0 else y)

    def part(half, k, offset, count=PAIRED):
        slot = group(half, k) * GROUP + c * HALF + offset
        return [dot(r.left_t[r.left_ids[slot + i]], r.right_pool[r.right_ids[slot + i]]) for i in range(count)]

    def mine(batch):
        return x * 8 + PAIRED * batch

    def other(batch):
        return (1 - x) * 8 + PAIRED * batch

    both = QUART

    def link(kind, k, stage, land, to):
        return pltpu.make_async_remote_copy(
            src_ref=stage, dst_ref=land, send_sem=r.send_sems.at[kind, k], recv_sem=r.recv_sems.at[kind, k],
            device_id=to, device_id_type=MESH,
        )

    def along_x(batch, half, k):
        return link(2 * batch + half, k, r.x_stage.at[batch, half, k], r.x_land.at[batch, half, k], to_x)

    def along_y_both(k):
        return link(4, k, r.yb_stage.at[k], r.yb_land.at[k], to_y)

    def along_y(batch, k):
        return link(5 + batch, k, r.ym_stage.at[batch, k], r.ym_land.at[batch, k], to_y)

    def along_z_both(k):
        return link(7, k, r.zb_stage.at[k], r.zb_land.at[k], (samp, group(1, k)))

    def along_z(batch, k):
        return link(8 + batch, k, r.zm_stage.at[batch, k], r.zm_land.at[batch, k], (samp, group(1, k)))

    def last():
        return link(10, 0, r.both_stage.at[1 - x], r.both_land, to_x)

    def send_x(batch, half, k):
        for i, value in enumerate(part(half, k, other(batch))):
            r.x_stage[batch, half, k, i] = value.astype(LOW)
        along_x(batch, half, k).start()

    def add_x_send_y(batch, k):
        values = part(0, k, mine(batch))
        along_x(batch, 0, k).wait_recv()
        for i, value in enumerate(values):
            r.ym_stage[batch, k, i] = (value + r.x_land[batch, 0, k, i].astype(FULL)).astype(LOW)
        along_y(batch, k).start()

    def add_both_send_z(batch, k):
        values = part(1, k, mine(batch))
        along_x(batch, 1, k).wait_recv()
        values = [value + r.x_land[batch, 1, k, i].astype(FULL) for i, value in enumerate(values)]
        along_y(batch, k).wait_recv()
        for i, value in enumerate(values):
            r.zm_stage[batch, k, i] = (value + r.ym_land[batch, k, i].astype(FULL)).astype(LOW)

        @pl.when(k < 3)
        def send_on():
            along_z(batch, k).start()

    def each(step):
        def body(k, carry):
            step(k)
            return carry

        lax.fori_loop(0, 4, body, 0)

    def slot_of(i, far=False):
        side = (1 - x) if far else x
        return c * HALF + (side * 8 + i if i < QUART else QUART + 2 * side + i - QUART)

    def share(kind, k, src, dst, to):
        return pltpu.make_async_remote_copy(
            src_ref=src, dst_ref=dst, send_sem=r.share_send.at[kind, k], recv_sem=r.share_recv.at[kind, k],
            device_id=to, device_id_type=MESH,
        )

    def grad_to(kind, pair, to):
        place_out = r.grads_out.at[pl.ds(slot_of(PAIRED * pair), PAIRED)]
        return share(kind, pair, r.own.at[pl.ds(PAIRED * pair, PAIRED)], place_out, to)

    def grad_on(pair):
        place_out = r.grads_out.at[pl.ds(slot_of(PAIRED * pair, True), PAIRED)]
        return share(2, pair, place_out, place_out, to_c)

    def grad_kept(pair):
        place_out = r.grads_out.at[pl.ds(slot_of(PAIRED * pair), PAIRED)]
        return pltpu.make_async_copy(r.own.at[pl.ds(PAIRED * pair, PAIRED)], place_out, r.local_sems.at[6 + pair])

    def move_to(kind, i, to):
        return share(kind, i, r.staged.at[i], r.moves_out.at[slot_of(i)], to)

    def move_on(i):
        place_out = r.moves_out.at[slot_of(i, True)]
        return share(5, i, place_out, place_out, to_c)

    def move_kept(i):
        return pltpu.make_async_copy(r.staged.at[i], r.moves_out.at[slot_of(i)], r.local_sems.at[i])

    def share_grads(pair):
        grad_to(0, pair, to_x).start()
        grad_to(1, pair, to_c).start()
        grad_kept(pair).start()

    def directions(pair):
        held = []
        stats = []
        for i in range(PAIRED * pair, PAIRED * pair + PAIRED):
            low = r.own[i]
            grad = low.astype(FULL)
            mean = jnp.sum(jnp.sum(grad * grad, axis=1, keepdims=True), axis=0, keepdims=True) / (BS * BS)
            shrink = 0.5 / (mean + 1e-06)
            low_t = grad.T.astype(LOW)
            slot = slot_of(i)
            stats.append(statistic(dot(low, low_t), shrink, r.left_diag[pl.ds(slot, 1)], eye))
            stats.append(statistic(dot(low_t, low), shrink, r.right_diag[pl.ds(slot, 1)], eye))
            held.append((i, low, lax.rsqrt(mean + 1e-06)))
        sides = roots(stats, eye)
        for n, (i, low, rate) in enumerate(held):
            high, rest = halves(sides[2 * n])
            turned = dot(jnp.concatenate([high, rest], axis=1), jnp.concatenate([low, low], axis=0)) * rate
            r.staged[i] = fine(halves(turned), halves(sides[2 * n + 1])).astype(LOW)
            move_to(3, i, to_x).start()
            move_to(4, i, to_c).start()
            move_kept(i).start()

    def finish_batch(batch):
        for k in range(3):
            along_z(batch, k).wait_recv()
        for i in range(PAIRED):
            value = r.zm_stage[batch, 3, i].astype(FULL)
            for k in range(3):
                value = value + r.zm_land[batch, k, i].astype(FULL)
            r.own[PAIRED * batch + i] = value.astype(LOW)
        share_grads(batch)

    def pass_on(pair):
        grad_to(0, pair, to_x).wait_recv()
        grad_on(pair).start()
        for i in range(PAIRED * pair, PAIRED * pair + PAIRED):
            move_to(3, i, to_x).wait_recv()
            move_on(i).start()

    for copy in here:
        copy.wait()

    @each
    def begin(k):
        for i, value in enumerate(part(0, k, both, QUART)):
            r.yb_stage[k, i] = value.astype(LOW)
        along_y_both(k).start()
        send_x(0, 0, k)

    @each
    def more(k):
        send_x(0, 1, k)

    row_copies[0].wait_recv()
    r.pair_rows[...] = r.rows_in[...] + r.row_land[0]
    row_copies.append(push(r.pair_rows, r.row_land.at[1], r.row_send.at[1], r.row_recv.at[1], to_x))

    @each
    def middle(k):
        add_x_send_y(0, k)
        values = part(1, k, both, QUART)
        along_y_both(k).wait_recv()
        for i, value in enumerate(values):
            r.zb_stage[k, i] = (value + r.yb_land[k, i].astype(FULL)).astype(LOW)

        @pl.when(k < 3)
        def send_on():
            along_z_both(k).start()

        send_x(1, 0, k)

    row_copies[1].wait_recv()
    r.chip_rows[...] = r.pair_rows[...] + r.row_land[1]
    row_copies.append(push(r.chip_rows, r.row_land.at[2], r.row_send.at[2], r.row_recv.at[2], to_y))

    @each
    def late(k):
        add_both_send_z(0, k)

    for k in range(3):
        along_z_both(k).wait_recv()
    for i in range(QUART):
        value = r.zb_stage[3, i].astype(FULL)
        for k in range(3):
            value = value + r.zb_land[k, i].astype(FULL)
        r.both_stage[i // 2, i % 2] = value.astype(LOW)
    last().start()

    @each
    def more_again(k):
        send_x(1, 1, k)

    @each
    def middle_again(k):
        add_x_send_y(1, k)

    row_copies[2].wait_recv()
    r.plane_rows[...] = r.chip_rows[...] + r.row_land[2]
    for step in range(3):
        row_copies.append(
            push(r.plane_rows, r.row_z.at[z], r.row_send.at[3 + step], r.row_recv.at[3 + step], to_z[step])
        )
    r.row_z[z] = r.plane_rows[...]
    last().wait_recv()
    for i in range(PAIRED):
        r.own[QUART + i] = (r.both_stage[x, i].astype(FULL) + r.both_land[i].astype(FULL)).astype(LOW)
    share_grads(2)
    directions(2)

    @each
    def late_again(k):
        add_both_send_z(1, k)

    finish_batch(0)
    directions(0)
    for step in range(3):
        row_copies[3 + step].wait_recv()
    r.rows_out[...] = (r.row_z[0] + r.row_z[1]) + (r.row_z[2] + r.row_z[3])
    finish_batch(1)
    pass_on(2)
    directions(1)
    pass_on(0)
    pass_on(1)
    for pair in range(3):
        grad_to(1, pair, to_c).wait_recv()
        grad_on(pair).wait_recv()
        grad_to(0, pair, to_x).wait_send()
        grad_to(1, pair, to_c).wait_send()
        grad_on(pair).wait_send()
        grad_kept(pair).wait()
    for i in range(6):
        move_to(4, i, to_c).wait_recv()
        move_on(i).wait_recv()
        move_to(3, i, to_x).wait_send()
        move_to(4, i, to_c).wait_send()
        move_on(i).wait_send()
        move_kept(i).wait()
    for copy in row_copies:
        copy.wait_send()
    last().wait_send()

    @each
    def drain(k):
        along_y_both(k).wait_send()
        for batch in range(2):
            along_x(batch, 0, k).wait_send()
            along_x(batch, 1, k).wait_send()
            along_y(batch, k).wait_send()

        @pl.when(k < 3)
        def sent_on():
            along_z_both(k).wait_send()
            for batch in range(2):
                along_z(batch, k).wait_send()

    swap.finish()


def update(left_ids, right_ids, rows, left_start, right_start, grad, left_pool, right_pool):
    return pl.pallas_call(
        update_kernel,
        out_shape=(SHAPES["rows"], shape((GROUP, BS, BS)), shape((GROUP, BS, BS)), SHAPES["pred"]),
        in_specs=[SMEM_IN] * 2 + [VMEM_AT] * 3 + [ANY_AT] * 3,
        out_specs=(VMEM_AT,) + (ANY_AT,) * 3,
        scratch_shapes=[spec for unused, spec in SUM_SCRATCH],
        compiler_params=pltpu.CompilerParams(
            collective_id=1, has_side_effects=True, vmem_limit_bytes=VMEM_ASK
        ),
        cost_estimate=pl.CostEstimate(flops=36 << 30, bytes_accessed=40 << 20, transcendentals=0),
        name="update",
    )(left_ids, right_ids, rows, left_start, right_start, grad, left_pool, right_pool)


def finish_kernel(grad, move, weight, left_diag, right_diag, grad_out, left_out, right_out, new_out, low_out):
    eye = lax.broadcasted_iota(jnp.int32, (BS, BS), 0) == lax.broadcasted_iota(jnp.int32, (BS, BS), 1)

    def mean(value):
        return jnp.sum(jnp.sum(value, axis=1, keepdims=True), axis=0, keepdims=True) / (BS * BS)

    for i in range(STEP):
        low = grad[i]
        full = low.astype(FULL)
        grad_out[i] = full
        shrink = 0.5 / (mean(full * full) + 1e-06)
        low_t = full.T.astype(LOW)
        left_out[i] = statistic(dot(low, low_t), shrink, left_diag[i], eye)
        right_out[i] = statistic(dot(low_t, low), shrink, right_diag[i], eye)
        step = move[i].astype(FULL)
        start = weight[i]
        ratio = jnp.sqrt(mean(start * start)) * lax.rsqrt(mean(step * step) + 1e-06)
        new = start - step_rate * ratio * step
        new_out[i] = new
        low_out[i] = new.astype(LOW)


STEP = 4


def finish_slots(grads, moves, masters, left_start, right_start):
    block = pl.BlockSpec((STEP, BS, BS), lambda i: (i, 0, 0))
    row = pl.BlockSpec((STEP, 1, BS), lambda i: (i, 0, 0))
    return pl.pallas_call(
        finish_kernel,
        grid=(GROUP // STEP,),
        compiler_params=pltpu.CompilerParams(vmem_limit_bytes=VMEM_ASK),
        out_shape=tuple(shape((GROUP, BS, BS), kind) for kind in (FULL, FULL, FULL, FULL, LOW)),
        in_specs=[block, block, block, row, row],
        out_specs=(block,) * 5,
        cost_estimate=pl.CostEstimate(flops=2 << 30, bytes_accessed=39 << 20, transcendentals=0),
        name="finish_slots",
    )(grads, moves, masters, left_start.reshape(GROUP, 1, BS), right_start.reshape(GROUP, 1, BS))


def local_tuned(
    inputs,
    cot_first,
    cot_second,
    valid_flags,
    lead_steps,
    masters,
    assignment,
    left_start,
    right_start,
    vectors,
    vec_moment,
):
    notes = jnp.concatenate(
        [
            valid_flags.astype(FULL) - 1.0,
            jnp.pad(lead_steps.astype(FULL).T, ((0, 0), (0, TOKENS - 2))),
            jnp.zeros((6, TOKENS), FULL),
        ],
        axis=0,
    )
    left_pool, right_pool, pred_one, pred_two, input_grad, rows = model(
        assignment, masters, notes, inputs, cot_first, cot_second, vectors
    )
    position = jnp.arange(NB, dtype=jnp.int32)
    inverse = jnp.sum(
        jnp.where(assignment[None, :] == position[:, None], position[None, :], 0), axis=1
    )
    left_ids, right_ids = pools_of(inverse)
    vec_grads, grads, moves, input_grad = update(
        left_ids, right_ids, rows, left_start, right_start, input_grad, left_pool, right_pool
    )
    input_grad = input_grad.astype(FULL)
    matrix_grads, left_stats, right_stats, new_masters, new_copies = finish_slots(
        grads, moves, masters, left_start, right_start
    )
    scaled_vec = vec_grads * lax.rsqrt(
        jnp.mean(vec_grads * vec_grads, axis=1, keepdims=True) + 1e-06
    )
    vec_moments = 0.5 * vec_moment + 0.5 * scaled_vec * scaled_vec
    new_vectors = vectors - vector_rate * scaled_vec * lax.rsqrt(vec_moments)
    return (
        pred_one,
        pred_two,
        input_grad,
        matrix_grads,
        left_stats,
        right_stats,
        new_masters,
        new_copies,
        vec_grads,
        vec_moments,
        new_vectors,
    )


def solution(mesh):
    placed = (
        P("samp", "blk", None),
        P("samp", "blk", None),
        P("samp", "blk", None),
        P("samp", "blk"),
        P(None, "samp"),
        P("blk", None, None),
        P(),
        P("blk", None),
        P("blk", None),
        P(),
        P(),
    )
    fits = mesh.shape["samp"] == 4 and mesh.shape["blk"] == 8
    return jax.shard_map(
        local_tuned if fits else local_any,
        mesh=mesh,
        in_specs=placed,
        out_specs=(
            P("samp", "blk", None),
            P("samp", "blk", None),
            P("samp", "blk", None),
            P("blk", None, None),
            P("blk", None, None),
            P("blk", None, None),
            P("blk", None, None),
            P("blk", None, None),
            P(),
            P(),
            P(),
        ),
        check_vma=False,
    )
```

```python
import functools
import math

import jax
import ml_dtypes
import jax.numpy as jnp
from jax import lax
from jax.experimental import pallas as pl
from jax.experimental.pallas import tpu as pltpu
from jax.sharding import PartitionSpec as P

D = 1024
HEADS = 16
FF = 4096
HD = 64
LEADS = 8
BS = 256
ITERS = 6
NB = 192


HIGH = lax.Precision.HIGHEST
step_rate = 0.5
vector_rate = 0.3
masked = 1000000000.0


def assemble(blocks, height, breadth):
    return (
        blocks.reshape(height // BS, breadth // BS, BS, BS)
        .transpose(0, 2, 1, 3)
        .reshape(height, breadth)
    )


def carve(matrix):
    height, breadth = matrix.shape
    return (
        matrix.reshape(height // BS, BS, breadth // BS, BS)
        .transpose(0, 2, 1, 3)
        .reshape(-1, BS, BS)
    )


def unpack(blocks):
    first_end = 3 * D * D // (BS * BS)
    second_end = first_end + D * D // (BS * BS)
    third_end = second_end + D * FF // (BS * BS)
    qkv_weight = assemble(blocks[:first_end], D, 3 * D)
    out_weight = assemble(blocks[first_end:second_end], D, D)
    up_weight = assemble(blocks[second_end:third_end], D, FF)
    down_weight = assemble(blocks[third_end:], FF, D)
    return (qkv_weight, out_weight, up_weight, down_weight)


def norm_layer(value, gain, shift):
    centred = value - jnp.mean(value, axis=-1, keepdims=True)
    spread = jnp.mean(centred * centred, axis=-1, keepdims=True)
    return centred * lax.rsqrt(spread + 1e-06) * gain + shift


def gelu_exact(value):
    return jax.nn.gelu(value, approximate=False)


def heads_of(tensor):
    return tensor.reshape(tensor.shape[0], tensor.shape[1], HEADS, HD)


def split_rows(member, count, width):
    shaped = member.reshape((member.shape[0], count, width) + member.shape[2:])
    return jnp.moveaxis(shaped, 1, 0)


def in_blocks(update, carry, members, length):
    width = math.gcd(length, 1024)
    count = length // width
    if count == 1:
        return update(carry, members, 0)
    stacked = tuple([split_rows(member, count, width) for member in members])
    offsets = jnp.arange(count, dtype=jnp.int32) * width

    def advance(state, item):
        return (update(state, item[0], item[1]), None)

    result, unused = lax.scan(advance, carry, (stacked, offsets))
    return result


def forward_update(query_heads, scaling):

    def update(carry, members, offset):
        running_max, running_sum, weighted = carry
        key_part, value_part, flag_part = members
        bias = (flag_part.astype(jnp.float32) - 1.0) * masked
        scores = (
            jnp.einsum(
                "sqhd,skhd->shqk",
                query_heads,
                heads_of(key_part),
                preferred_element_type=jnp.float32,
            )
            * scaling
            + bias[:, None, None, :]
        )
        new_max = jnp.maximum(running_max, jnp.max(scores, axis=-1))
        shrink = jnp.exp(running_max - new_max)
        expos = jnp.exp(scores - new_max[..., None])
        running_sum = running_sum * shrink + jnp.sum(expos, axis=-1)
        weighted = weighted * shrink[..., None] + jnp.einsum(
            "shqk,skhd->shqd",
            expos.astype(jnp.bfloat16),
            heads_of(value_part),
            preferred_element_type=jnp.float32,
        )
        return (new_max, running_sum, weighted)

    return update


def query_grad_update(query_heads, dout_heads, log_total, inner, scaling):

    def update(carry, members, offset):
        key_part, value_part, flag_part = members
        bias = (flag_part.astype(jnp.float32) - 1.0) * masked
        scores = (
            jnp.einsum(
                "sqhd,skhd->shqk",
                query_heads,
                heads_of(key_part),
                preferred_element_type=jnp.float32,
            )
            * scaling
            + bias[:, None, None, :]
        )
        probs = jnp.exp(scores - log_total[..., None])
        dprobs = jnp.einsum(
            "sqhd,skhd->shqk", dout_heads, heads_of(value_part), preferred_element_type=jnp.float32
        )
        dscores = (probs * (dprobs - inner[..., None])).astype(jnp.bfloat16)
        return (
            carry
            + jnp.einsum(
                "shqk,skhd->sqhd", dscores, heads_of(key_part), preferred_element_type=jnp.float32
            )
            * scaling
        )

    return update


def key_grad_update(key_heads, value_heads, key_bias, total_rows, inner_rows, scaling, anchor):

    def update(carry, members, offset):
        grad_keys, grad_values = carry
        query_part, dout_part = members
        length = query_part.shape[1]
        total_part = jnp.transpose(
            lax.dynamic_slice_in_dim(total_rows, anchor + offset, length, 1), (0, 2, 1)
        )
        inner_part = jnp.transpose(
            lax.dynamic_slice_in_dim(inner_rows, anchor + offset, length, 1), (0, 2, 1)
        )
        query_heads = heads_of(query_part)
        dout_heads = heads_of(dout_part)
        scores = (
            jnp.einsum(
                "sqhd,skhd->shqk", query_heads, key_heads, preferred_element_type=jnp.float32
            )
            * scaling
            + key_bias[:, None, None, :]
        )
        probs = jnp.exp(scores - total_part[..., None])
        dprobs = jnp.einsum(
            "sqhd,skhd->shqk", dout_heads, value_heads, preferred_element_type=jnp.float32
        )
        dscores = (probs * (dprobs - inner_part[..., None])).astype(jnp.bfloat16)
        grad_values = grad_values + jnp.einsum(
            "shqk,sqhd->skhd",
            probs.astype(jnp.bfloat16),
            dout_heads,
            preferred_element_type=jnp.float32,
        )
        grad_keys = (
            grad_keys
            + jnp.einsum(
                "shqk,sqhd->skhd", dscores, query_heads, preferred_element_type=jnp.float32
            )
            * scaling
        )
        return (grad_keys, grad_values)

    return update


def invert_root(stat):
    identity = jnp.eye(stat.shape[0], dtype=jnp.float32)
    frobenius = jnp.sqrt(jnp.sum(stat * stat))
    approx = identity * lax.rsqrt(jnp.sqrt(frobenius))
    moving = stat / frobenius
    for iteration in range(ITERS):
        factor = (5.0 * identity - moving) * 0.25
        approx = jnp.dot(approx, factor, precision=HIGH)
        square = jnp.dot(factor, factor, precision=HIGH)
        moving = jnp.dot(jnp.dot(square, square, precision=HIGH), moving, precision=HIGH)
    return approx


def precondition(gradient, left_diag, right_diag, weight):
    scaled = gradient * lax.rsqrt(jnp.mean(gradient * gradient) + 1e-06)
    identity = jnp.eye(BS, dtype=jnp.float32)
    left_new = 0.5 * identity * left_diag[None, :] + 0.5 * jnp.dot(scaled, scaled.T, precision=HIGH)
    right_new = 0.5 * identity * right_diag[None, :] + 0.5 * jnp.dot(
        scaled.T, scaled, precision=HIGH
    )
    direction = jnp.dot(
        jnp.dot(invert_root(left_new), scaled, precision=HIGH),
        invert_root(right_new),
        precision=HIGH,
    )
    ratio = jnp.sqrt(jnp.mean(weight * weight)) * lax.rsqrt(jnp.mean(direction * direction) + 1e-06)
    return (left_new, right_new, weight - step_rate * ratio * direction)


MESH = pl.DeviceIdType.MESH
LOW = jnp.bfloat16
FULL = jnp.float32
VMEM_ASK = 60 * 1024 * 1024
GROUP = 24
HALF = 12
QUART = 4


def place():
    samp = lax.axis_index("samp")
    blk = lax.axis_index("blk")
    return (lax.div(samp, 2), lax.rem(samp, 2), lax.div(blk, 2), lax.rem(blk, 2))


def meet(devices):
    barrier = pltpu.get_barrier_semaphore()
    for device in devices:
        pl.semaphore_signal(barrier, inc=1, device_id=device, device_id_type=MESH)
    pl.semaphore_wait(barrier, len(devices))


def meet_all():
    barrier = pltpu.get_barrier_semaphore()
    samp = lax.axis_index("samp")
    blk = lax.axis_index("blk")

    def tell(at, carry):
        to = lax.rem(samp * 8 + blk + at, 32)
        pl.semaphore_signal(
            barrier, inc=1, device_id=(lax.div(to, 8), lax.rem(to, 8)), device_id_type=MESH
        )
        return carry

    lax.fori_loop(1, 32, tell, 0)
    pl.semaphore_wait(barrier, 31)


def turned_pair(n):
    return 2 * lax.rem(n, 2) + lax.div(n, 2)


class Swap:
    def __init__(self, local_sems, send_sems, recv_sems, first=0):
        x, c, z, y = place()
        self.first = first
        self.stays = z == turned_pair(2 * x + c)
        self.to = (turned_pair(z), 2 * turned_pair(2 * x + c) + y)
        self.sems = (local_sems, send_sems, recv_sems)
        self.pairs = []

    def start(self, src, dst):
        at = self.first + len(self.pairs)
        local_sems, send_sems, recv_sems = self.sems
        local = pltpu.make_async_copy(src, dst, local_sems.at[at])
        away = pltpu.make_async_remote_copy(
            src_ref=src, dst_ref=dst, send_sem=send_sems.at[at], recv_sem=recv_sems.at[at],
            device_id=self.to, device_id_type=MESH,
        )
        self.pairs.append((local, away))

        @pl.when(self.stays)
        def keep():
            local.start()

        @pl.when(jnp.logical_not(self.stays))
        def send():
            away.start()

    def finish(self):
        @pl.when(self.stays)
        def kept():
            for local, away in self.pairs:
                local.wait()

        @pl.when(jnp.logical_not(self.stays))
        def sent():
            for local, away in self.pairs:
                away.wait()


def push(src, dst, send, recv, device):
    copy = pltpu.make_async_remote_copy(
        src_ref=src, dst_ref=dst, send_sem=send, recv_sem=recv, device_id=device, device_id_type=MESH
    )
    copy.start()
    return copy


FIRST, SECOND, BOTH, CROSS = range(4)
SIZES = (2, 2, 3, 1)


def gather_blocks(r, notes, while_last):
    x, c, z, y = place()
    samp = 2 * x + c
    blk = 2 * z + y
    to_y = (samp, 2 * z + 1 - y)
    to_x = (2 * (1 - x) + c, blk)
    to_c = (2 * x + 1 - c, blk)
    base = c * HALF
    out = r.weights
    starts = (base + x * 8, base + x * 8 + 2, base + QUART, base + QUART + 3)
    far_starts = (base + (1 - x) * 8, base + (1 - x) * 8 + 2)
    other = (1 - c) * HALF
    parts = [base + x * 8, base + QUART, base + (1 - x) * 8, other, other + QUART, other + 2 * QUART]
    notes_out, note_send, note_recv = r.notes_land, r.note_send, r.note_recv

    def load(at):
        return pltpu.make_async_copy(
            r.masters.at[pl.ds(parts[at], QUART)], r.wide.at[at % 2], r.load_sems.at[at]
        )

    def ready(at):
        load(at).wait()
        out[pl.ds(blk * GROUP + parts[at], QUART)] = r.wide[at % 2].astype(LOW)
        if at + 2 < len(parts):
            load(at + 2).start()

    def copy(group, start, size, sems, at, device):
        place_out = out.at[pl.ds(group * GROUP + start, size)]
        return pltpu.make_async_remote_copy(
            src_ref=place_out, dst_ref=place_out,
            send_sem=sems.at[(0,) + at], recv_sem=sems.at[(1,) + at], device_id=device, device_id_type=MESH,
        )

    def z_copy(kind, way, origin):
        to = (samp, blk + (2 if way == 0 else -2))
        return copy(2 * origin + y, starts[kind], SIZES[kind], r.z_sems, (kind, way, origin), to)

    def z_cross(way, origin, side):
        to = (samp, blk + (2 if way == 0 else -2))
        return copy(2 * origin + side, starts[CROSS], 1, r.z_sems, (CROSS + side, way, origin), to)

    def y_copy(kind, origin):
        return copy(2 * origin + y, starts[kind], SIZES[kind], r.y_sems, (kind, origin), to_y)

    def y_landed(kind, origin):
        return copy(2 * origin + 1 - y, starts[kind], SIZES[kind], r.y_sems, (kind, origin), to_y)

    def x_copy(kind, group):
        return copy(group, starts[kind], SIZES[kind], r.x_sems, (kind, group), to_x)

    def x_landed(kind, group):
        return copy(group, far_starts[kind], SIZES[kind], r.x_sems, (kind, group), to_x)

    def core_copy(kind, group):
        return copy(group, starts[kind], SIZES[kind], r.core_sems, (kind, group), to_c)

    def far_copy(kind, group):
        return copy(group, far_starts[kind], SIZES[kind], r.far_sems, (kind, group), to_c)

    def on_from_here(kind, group):
        if kind in (FIRST, SECOND):
            x_copy(kind, group).start()
        core_copy(kind, group).start()

    def begin(kind):
        @pl.when(z < 3)
        def up():
            z_copy(kind, 0, z).start()

        @pl.when(z > 0)
        def down():
            z_copy(kind, 1, z).start()

        y_copy(kind, z).start()

    def z_step(kind, distance):
        for way in (0, 1):
            origin = z - distance if way == 0 else z + distance

            @pl.when(origin >= 0 if way == 0 else origin <= 3)
            def arrived():
                z_copy(kind, way, origin).wait_recv()

                @pl.when(z < 3 if way == 0 else z > 0)
                def onward():
                    z_copy(kind, way, origin).start()

                y_copy(kind, origin).start()
                on_from_here(kind, 2 * origin + y)

    def y_step(kind, distance):
        for way in (0, 1):
            origin = z - distance if way == 0 else z + distance

            @pl.when(origin >= 0 if way == 0 else origin <= 3)
            def arrived():
                y_landed(kind, origin).wait_recv()
                on_from_here(kind, 2 * origin + 1 - y)

    def y_own(kind):
        y_landed(kind, z).wait_recv()
        on_from_here(kind, 2 * z + 1 - y)

    def cross_step(distance):
        for side in (0, 1):
            for way in (0, 1):
                origin = z - distance if way == 0 else z + distance

                @pl.when(origin >= 0 if way == 0 else origin <= 3)
                def arrived():
                    z_cross(way, origin, side).wait_recv()

                    @pl.when(z < 3 if way == 0 else z > 0)
                    def onward():
                        z_cross(way, origin, side).start()

                    core_copy(CROSS, 2 * origin + side).start()

    def x_step(kind, distance, same):
        for way in (0, 1):
            origin = z - distance if way == 0 else z + distance

            @pl.when(origin >= 0 if way == 0 else origin <= 3)
            def arrived():
                group = 2 * origin + (y if same else 1 - y)
                x_landed(kind, group).wait_recv()
                far_copy(kind, group).start()

    def x_own(kind):
        x_landed(kind, 2 * z + 1 - y).wait_recv()
        far_copy(kind, 2 * z + 1 - y).start()

    note_local = pltpu.make_async_copy(notes, notes_out.at[blk], r.load_sems.at[6])

    def note_copy(j, origin):
        return pltpu.make_async_remote_copy(
            src_ref=notes, dst_ref=notes_out.at[origin], send_sem=note_send.at[j], recv_sem=note_recv.at[origin],
            device_id=(j // 2, 2 * turned_pair(samp) + j % 2), device_id_type=MESH,
        )

    stays = z == turned_pair(samp)

    def is_me(j):
        return jnp.logical_and(stays, 2 * samp + y == j)

    def here_from(j):
        return jnp.logical_and(stays, blk == j)

    load(0).start()
    load(1).start()
    meet_all()
    r.swap_rows.start(r.rows_in, r.rows_land)
    ready(0)
    begin(FIRST)
    begin(SECOND)
    ready(1)
    y_copy(CROSS, z).start()
    for j in range(8):

        @pl.when(jnp.logical_not(is_me(j)))
        def send_note():
            note_copy(j, blk).start()

    @pl.when(stays)
    def keep_note():
        note_local.start()

    for at in range(2, len(parts)):
        ready(at)
    z_step(FIRST, 1)
    y_own(FIRST)
    z_step(SECOND, 1)
    y_own(SECOND)
    begin(BOTH)
    y_landed(CROSS, z).wait_recv()
    core_copy(CROSS, 2 * z + 1 - y).start()
    for way, there in ((0, z < 3), (1, z > 0)):
        for side in (0, 1):
            @pl.when(there)
            def both_sides():
                z_cross(way, z, side).start()

    z_step(FIRST, 2)
    y_step(FIRST, 1)
    z_step(SECOND, 2)
    y_step(SECOND, 1)
    x_own(FIRST)
    z_step(FIRST, 3)
    x_own(SECOND)
    y_step(FIRST, 2)
    z_step(SECOND, 3)
    x_step(FIRST, 1, True)
    y_step(SECOND, 2)
    x_step(SECOND, 1, True)
    y_step(FIRST, 3)
    y_step(SECOND, 3)
    z_step(BOTH, 1)
    x_step(FIRST, 1, False)
    x_step(FIRST, 2, True)
    y_own(BOTH)
    cross_step(1)
    x_step(SECOND, 1, False)
    x_step(SECOND, 2, True)
    z_step(BOTH, 2)
    x_step(FIRST, 3, True)
    y_step(BOTH, 1)
    cross_step(2)
    x_step(FIRST, 2, False)
    z_step(BOTH, 3)
    x_step(SECOND, 3, True)
    y_step(BOTH, 2)
    x_step(SECOND, 2, False)
    cross_step(3)
    x_step(FIRST, 3, False)
    y_step(BOTH, 3)
    x_step(SECOND, 3, False)

    while_last()
    other_starts = (other + x * 8, other + x * 8 + 2, other + QUART, other + QUART + 3)
    other_far = (other + (1 - x) * 8, other + (1 - x) * 8 + 2)

    def settle(group, carry):
        @pl.when(group != blk)
        def other_group():
            for kind in range(4):
                copy(group, other_starts[kind], SIZES[kind], r.core_sems, (kind, group), to_c).wait_recv()
                core_copy(kind, group).wait_send()
            for kind in (FIRST, SECOND):
                copy(group, other_far[kind], SIZES[kind], r.far_sems, (kind, group), to_c).wait_recv()
                far_copy(kind, group).wait_send()
                x_copy(kind, group).wait_send()

        return carry

    lax.fori_loop(0, 8, settle, 0)

    def sent_along(origin, carry):
        for kind in (FIRST, SECOND, BOTH):
            y_copy(kind, origin).wait_send()

            @pl.when(jnp.logical_and(origin <= z, z < 3))
            def up():
                z_copy(kind, 0, origin).wait_send()

            @pl.when(jnp.logical_and(origin >= z, z > 0))
            def down():
                z_copy(kind, 1, origin).wait_send()

        for side in (0, 1):
            @pl.when(jnp.logical_and(origin <= z, z < 3))
            def cross_up():
                z_cross(0, origin, side).wait_send()

            @pl.when(jnp.logical_and(origin >= z, z > 0))
            def cross_down():
                z_cross(1, origin, side).wait_send()

        return carry

    lax.fori_loop(0, 4, sent_along, 0)
    y_copy(CROSS, z).wait_send()
    for j in range(8):

        @pl.when(jnp.logical_not(is_me(j)))
        def sent_note():
            note_copy(j, blk).wait_send()

        @pl.when(jnp.logical_not(here_from(j)))
        def got_note():
            note_copy(j, j).wait_recv()

    @pl.when(stays)
    def kept_note():
        note_local.wait()


def local_any(
    inputs,
    cot_first,
    cot_second,
    valid_flags,
    lead_steps,
    masters,
    assignment,
    left_start,
    right_start,
    vectors,
    vec_moment,
):
    copies = lax.all_gather(masters.astype(jnp.bfloat16), "blk", axis=0, tiled=True)
    blocks = jnp.take(copies, assignment, axis=0)
    qkv_weight, out_weight, up_weight, down_weight = unpack(blocks)
    scaling = HD ** (-0.5)
    flags_low = valid_flags.astype(jnp.bfloat16)
    key_bias = (valid_flags.astype(jnp.float32) - 1.0) * masked
    lead_base = 8 + FF // D
    lead_table = vectors[lead_base:]
    samples = inputs.shape[0]
    patches = inputs.shape[1]

    def forward(hidden_in, lead_ids):
        chosen = (lead_ids[:, None] == jnp.arange(LEADS, dtype=jnp.int32)[None, :]).astype(
            jnp.float32
        )
        lead_rows = jnp.dot(chosen, lead_table, precision=HIGH)
        hidden = hidden_in + lead_rows[:, None, :]
        normed_low = norm_layer(hidden, vectors[0], vectors[1]).astype(jnp.bfloat16)
        packed = jnp.einsum(
            "spd,de->spe", normed_low, qkv_weight, preferred_element_type=jnp.float32
        )
        queries = (packed[..., :D] + vectors[2]).astype(jnp.bfloat16)
        keys_low = packed[..., D : 2 * D].astype(jnp.bfloat16)
        values_low = (packed[..., 2 * D :] + vectors[3]).astype(jnp.bfloat16)
        start_state = (
            jnp.full((samples, HEADS, patches), -1e30, jnp.float32),
            jnp.zeros((samples, HEADS, patches), jnp.float32),
            jnp.zeros((samples, HEADS, patches, HD), jnp.float32),
        )
        update = forward_update(heads_of(queries), scaling)
        gathered = None
        piece = (
            lax.all_gather(keys_low, "blk", axis=1, tiled=True),
            lax.all_gather(values_low, "blk", axis=1, tiled=True),
            lax.all_gather(flags_low, "blk", axis=1, tiled=True),
        )
        running_max, running_sum, weighted = in_blocks(
            update, start_state, piece, piece[0].shape[1]
        )
        attended = jnp.transpose(weighted / running_sum[..., None], (0, 2, 1, 3)).reshape(
            samples, patches, D
        )
        log_total = running_max + jnp.log(running_sum)
        attended_low = attended.astype(jnp.bfloat16)
        middle = (
            hidden
            + jnp.einsum(
                "spd,de->spe", attended_low, out_weight, preferred_element_type=jnp.float32
            )
            + vectors[4]
        )
        normed_two = norm_layer(middle, vectors[5], vectors[6]).astype(jnp.bfloat16)
        upward = jnp.einsum(
            "spd,df->spf", normed_two, up_weight, preferred_element_type=jnp.float32
        ) + vectors[8:lead_base].reshape(FF)
        activated = gelu_exact(upward).astype(jnp.bfloat16)
        result = (
            middle
            + jnp.einsum("spf,fd->spd", activated, down_weight, preferred_element_type=jnp.float32)
            + vectors[7]
        )
        saved = (
            hidden,
            normed_low,
            queries,
            keys_low,
            values_low,
            attended,
            attended_low,
            log_total,
            middle,
            normed_two,
            upward,
            activated,
            chosen,
            gathered,
        )
        return (result, saved)

    def backward(grad_out, saved):
        (
            hidden,
            normed_low,
            queries,
            keys_low,
            values_low,
            attended,
            attended_low,
            log_total,
            middle,
            normed_two,
            upward,
            activated,
            chosen,
            gathered,
        ) = saved
        grad_two = grad_out.astype(jnp.bfloat16)
        down_grad = jnp.einsum(
            "spf,spd->fd", activated, grad_two, preferred_element_type=jnp.float32
        )
        down_bias = jnp.sum(grad_two.astype(jnp.float32), axis=(0, 1))
        grad_act = jnp.einsum(
            "spd,fd->spf", grad_two, down_weight, preferred_element_type=jnp.float32
        )
        gelu_value, gelu_pull = jax.vjp(gelu_exact, upward)
        grad_up = gelu_pull(grad_act)[0].astype(jnp.bfloat16)
        up_grad = jnp.einsum("spd,spf->df", normed_two, grad_up, preferred_element_type=jnp.float32)
        up_bias = jnp.sum(grad_up.astype(jnp.float32), axis=(0, 1))
        grad_normed_two = jnp.einsum(
            "spf,df->spd", grad_up, up_weight, preferred_element_type=jnp.float32
        )
        norm_value, norm_pull = jax.vjp(norm_layer, middle, vectors[5], vectors[6])
        grad_middle_norm, gain_two, shift_two = norm_pull(grad_normed_two)
        grad_middle = grad_out + grad_middle_norm
        grad_one = grad_middle.astype(jnp.bfloat16)
        out_grad = jnp.einsum(
            "spd,spe->de", attended_low, grad_one, preferred_element_type=jnp.float32
        )
        out_bias = jnp.sum(grad_one.astype(jnp.float32), axis=(0, 1))
        grad_attended = jnp.einsum(
            "spe,de->spd", grad_one, out_weight, preferred_element_type=jnp.float32
        ).astype(jnp.bfloat16)
        inner = jnp.sum(
            (grad_attended.astype(jnp.float32) * attended).reshape(samples, patches, HEADS, HD),
            axis=-1,
        )
        inner_heads = jnp.transpose(inner, (0, 2, 1))
        zero_query = jnp.zeros((samples, patches, HEADS, HD), jnp.float32)
        update_query = query_grad_update(
            heads_of(queries), heads_of(grad_attended), log_total, inner_heads, scaling
        )
        piece = (
            lax.all_gather(keys_low, "blk", axis=1, tiled=True),
            lax.all_gather(values_low, "blk", axis=1, tiled=True),
            lax.all_gather(flags_low, "blk", axis=1, tiled=True),
        )
        grad_query = in_blocks(update_query, zero_query, piece, piece[0].shape[1])
        total_rows, inner_rows = (
            lax.all_gather(jnp.transpose(log_total, (0, 2, 1)), "blk", axis=1, tiled=True),
            lax.all_gather(inner, "blk", axis=1, tiled=True),
        )
        key_heads = heads_of(keys_low)
        value_heads = heads_of(values_low)
        zero_pair = (zero_query, zero_query)
        piece = (
            lax.all_gather(queries, "blk", axis=1, tiled=True),
            lax.all_gather(grad_attended, "blk", axis=1, tiled=True),
        )
        update_keys = key_grad_update(
            key_heads, value_heads, key_bias, total_rows, inner_rows, scaling, jnp.int32(0)
        )
        grad_keys, grad_values = in_blocks(update_keys, zero_pair, piece, piece[0].shape[1])
        grad_packed = jnp.concatenate(
            [
                grad_query.reshape(samples, patches, D),
                grad_keys.reshape(samples, patches, D),
                grad_values.reshape(samples, patches, D),
            ],
            axis=-1,
        ).astype(jnp.bfloat16)
        qkv_grad = jnp.einsum(
            "spd,spe->de", normed_low, grad_packed, preferred_element_type=jnp.float32
        )
        query_bias = jnp.sum(grad_packed[..., :D].astype(jnp.float32), axis=(0, 1))
        value_bias = jnp.sum(grad_packed[..., 2 * D :].astype(jnp.float32), axis=(0, 1))
        grad_normed = jnp.einsum(
            "spe,de->spd", grad_packed, qkv_weight, preferred_element_type=jnp.float32
        )
        first_value, first_pull = jax.vjp(norm_layer, hidden, vectors[0], vectors[1])
        grad_hidden_norm, gain_one, shift_one = first_pull(grad_normed)
        grad_hidden = grad_middle + grad_hidden_norm
        lead_grad = jnp.dot(chosen.T, jnp.sum(grad_hidden, axis=1), precision=HIGH)
        vec_rows = jnp.concatenate(
            [
                gain_one[None],
                shift_one[None],
                query_bias[None],
                value_bias[None],
                out_bias[None],
                gain_two[None],
                shift_two[None],
                down_bias[None],
                up_bias.reshape(FF // D, D),
                lead_grad,
            ],
            axis=0,
        )
        return (grad_hidden, (qkv_grad, out_grad, up_grad, down_grad), vec_rows)

    earlier, saved_one = forward(inputs.astype(jnp.float32), lead_steps[0])
    later, saved_two = forward(earlier, lead_steps[1])
    grad_between, mats_two, vec_two = backward(cot_second.astype(jnp.float32), saved_two)
    input_grad, mats_one, vec_one = backward(
        cot_first.astype(jnp.float32) + grad_between, saved_one
    )
    grad_blocks = jnp.concatenate(
        [
            carve(mats_one[0] + mats_two[0]),
            carve(mats_one[1] + mats_two[1]),
            carve(mats_one[2] + mats_two[2]),
            carve(mats_one[3] + mats_two[3]),
        ],
        axis=0,
    )
    position = jnp.arange(NB, dtype=jnp.int32)
    inverse = jnp.sum(
        jnp.where(assignment[None, :] == position[:, None], position[None, :], 0), axis=1
    )
    slotted = jnp.take(grad_blocks, inverse, axis=0)
    shared = lax.psum_scatter(slotted, "blk", scatter_dimension=0, tiled=True)
    matrix_grads = lax.psum(shared.astype(jnp.bfloat16), "samp").astype(jnp.float32)
    vec_grads = lax.psum(vec_one + vec_two, ("samp", "blk"))
    left_stats, right_stats, new_masters = jax.vmap(precondition)(
        matrix_grads, left_start, right_start, masters
    )
    scaled_vec = vec_grads * lax.rsqrt(
        jnp.mean(vec_grads * vec_grads, axis=1, keepdims=True) + 1e-06
    )
    vec_moments = 0.5 * vec_moment + 0.5 * scaled_vec * scaled_vec
    new_vectors = vectors - vector_rate * scaled_vec * lax.rsqrt(vec_moments)
    return (
        earlier.astype(jnp.bfloat16),
        later.astype(jnp.bfloat16),
        input_grad,
        matrix_grads,
        left_stats,
        right_stats,
        new_masters,
        new_masters.astype(jnp.bfloat16),
        vec_grads,
        vec_moments,
        new_vectors,
    )


TOKENS = 128
PAIR = 2 * HD
SEQ_ALL = 8 * TOKENS
QKV_AT, OUT_AT, UP_AT, DOWN_AT = 0, 48, 64, 128
WIDE = D // BS
DEEP = FF // BS
LEAD_AT = 8 + FF // D


def dot(left, right):
    return jnp.dot(left, right, preferred_element_type=FULL)


def dot_t(left, right):
    return lax.dot_general(left, right, (((1,), (1,)), ((), ())), preferred_element_type=FULL)


def normal(value):
    centred = value - jnp.mean(value, axis=-1, keepdims=True)
    rate = lax.rsqrt(jnp.mean(centred * centred, axis=-1, keepdims=True) + 1e-06)
    return (centred * rate, rate)


def normal_back(grad, unit, rate, gain):
    scaled = grad * gain
    return rate * (
        scaled
        - jnp.mean(scaled, axis=-1, keepdims=True)
        - unit * jnp.mean(scaled * unit, axis=-1, keepdims=True)
    )


def total(value):
    return jnp.sum(value, axis=0, keepdims=True)


def gelu_parts(value):
    phi = 0.5 + 0.5 * lax.erf(value * (0.5**0.5))
    return phi, value * phi


def gelu_slope(value, phi):
    return phi + value * jnp.exp(-0.5 * value * value) * ((2.0 * math.pi) ** -0.5)


class Weights:
    def __init__(self, slots, held):
        self.slots, self.held = slots, held

    def block(self, base, cols, row, col):
        return self.held[self.slots[base + row * cols + col]]

    def down_col(self, base, rows, cols, col):
        return jnp.concatenate([self.block(base, cols, row, col) for row in range(rows)], axis=0)

    def along_row(self, base, cols, row, first=0, last=None):
        return jnp.concatenate(
            [self.block(base, cols, row, col) for col in range(first, cols if last is None else last)], axis=1
        )


def lead_row(vecs, lead):
    row = jnp.zeros((1, D), FULL)
    for at in range(LEADS):
        row = row + jnp.where(lead == at, vecs[LEAD_AT + at : LEAD_AT + at + 1], 0.0)
    return row


def project(r, layer, hidden, vecs, weights):
    unit, unused = normal(hidden)
    normed = unit * vecs[0:1] + vecs[1:2]
    for k in range(WIDE):
        r.left_held[layer, k] = normed[:, k * BS : (k + 1) * BS].T.astype(LOW)
    give_pool(r, True, layer, 0)
    normed = normed.astype(LOW)
    for kind in (1, 0, 2):
        for step in range(WIDE):
            within = lax.rem(step + lax.div(r.plane.me, 2), WIDE)
            part = dot(normed, weights.down_col(QKV_AT, WIDE, 3 * WIDE, kind * WIDE + within))
            if kind != 1:
                row = 2 if kind == 0 else 3
                part = part + vecs[row : row + 1, pl.ds(pl.multiple_of(within * BS, BS), BS)]
            part = part.astype(LOW)
            for half in range(2):
                r.packed[kind, 2 * within + half] = part[:, half * PAIR : (half + 1) * PAIR]
                r.plane.send_or_keep(
                    r.packed.at[kind], r.held[layer].at[kind], r.in_sems[layer].at[kind], 2 * within + half
                )


def pool_at(left, kind):
    counts, bases = (LEFTS, LEFT_AT) if left else (RIGHTS, RIGHT_AT)
    return pl.ds(bases[kind], counts[kind])


def pool_copies(r, left, layer, kind):
    x, c, z, y = place()
    ids = pool_at(left, kind)
    at = (0 if left else 8) + 4 * layer + kind
    source = (r.left_held if left else r.right_held).at[layer, ids]

    def target(part):
        tokens = pl.ds((2 * part + layer) * TOKENS, TOKENS)
        return r.left_pool.at[ids, :, tokens] if left else r.right_pool.at[ids, tokens]

    here = pltpu.make_async_copy(source, target(0), r.pool_sems.at[0, at])
    there = pltpu.make_async_remote_copy(
        src_ref=source, dst_ref=target(1), send_sem=r.pool_sems.at[1, at], recv_sem=r.pool_sems.at[2, at],
        device_id=(2 * x + 1 - c, 2 * z + y), device_id_type=MESH,
    )
    return here, there


def give_pool(r, left, layer, kind):
    for copy in pool_copies(r, left, layer, kind):
        copy.start()


def feed(r, layer, hidden, vecs, weights, slope_held):
    attended = jnp.concatenate([r.o_land[j] for j in range(8)], axis=1)
    for k in range(WIDE):
        r.left_held[layer, WIDE + k] = attended[:, k * BS : (k + 1) * BS].astype(FULL).T.astype(LOW)
    give_pool(r, True, layer, 1)
    branch = [dot(attended, weights.down_col(OUT_AT, WIDE, WIDE, n)) for n in range(WIDE)]
    middle = hidden + jnp.concatenate(branch, axis=1) + vecs[4:5]
    unit, unused = normal(middle)
    normed = unit * vecs[5:6] + vecs[6:7]
    for k in range(WIDE):
        r.left_held[layer, 2 * WIDE + k] = normed[:, k * BS : (k + 1) * BS].T.astype(LOW)
    give_pool(r, True, layer, 2)
    normed = normed.astype(LOW)
    per = D // BS
    for f in range(DEEP):
        bias = vecs[8 + f // per : 9 + f // per, (f % per) * BS : (f % per + 1) * BS]
        upward = dot(normed, weights.down_col(UP_AT, WIDE, DEEP, f)) + bias
        phi, activated = gelu_parts(upward)
        slope_held[f] = gelu_slope(upward, phi)
        r.act_held[:, f * BS : (f + 1) * BS] = activated.astype(LOW)
        r.left_held[layer, 3 * WIDE + f] = activated.T.astype(LOW)
    give_pool(r, True, layer, 3)
    branch = [dot(r.act_held[...], weights.down_col(DOWN_AT, DEEP, WIDE, n)) for n in range(WIDE)]
    return middle, middle + jnp.concatenate(branch, axis=1) + vecs[7:8]


def feed_back(r, layer, grad_out, middle, slope_in, vecs, weights):
    rows = r.rows
    grad_two = grad_out.astype(LOW)
    for k in range(WIDE):
        r.right_held[layer, RIGHT_AT[3] + k] = grad_two[:, k * BS : (k + 1) * BS]
    give_pool(r, False, layer, 3)
    rows[7:8] += total(grad_two.astype(FULL))
    per = D // BS
    for f in range(DEEP):
        grad_act = dot_t(grad_two, weights.along_row(DOWN_AT, WIDE, f))
        grad_up = (grad_act * slope_in[f]).astype(LOW)
        r.right_held[layer, RIGHT_AT[2] + f] = grad_up
        rows[8 + f // per : 9 + f // per, (f % per) * BS : (f % per + 1) * BS] += total(grad_up.astype(FULL))
    give_pool(r, False, layer, 2)
    grad_up = jnp.concatenate([r.right_held[layer, RIGHT_AT[2] + f] for f in range(DEEP)], axis=1)
    grad_normed = jnp.concatenate(
        [dot_t(grad_up, weights.along_row(UP_AT, DEEP, k)) for k in range(WIDE)], axis=1
    )
    unit, rate = normal(middle)
    rows[5:6] += total(grad_normed * unit)
    rows[6:7] += total(grad_normed)
    grad_middle = grad_out + normal_back(grad_normed, unit, rate, vecs[5:6])
    grad_one = grad_middle.astype(LOW)
    for k in range(WIDE):
        r.right_held[layer, RIGHT_AT[1] + k] = grad_one[:, k * BS : (k + 1) * BS]
    give_pool(r, False, layer, 1)
    rows[4:5] += total(grad_one.astype(FULL))
    for k in range(WIDE):
        part = dot_t(grad_one, weights.along_row(OUT_AT, WIDE, k)).astype(LOW)
        for half in range(2):
            r.do_message[2 * k + half] = part[:, half * PAIR : (half + 1) * PAIR]
            r.plane.send_or_keep(r.do_message, r.do_land, r.do_sems[layer], 2 * k + half)
    return grad_middle


def project_back(r, layer, grad_middle, hidden, vecs, weights, lead):
    rows = r.rows

    def blocks_of_kind(kind):
        source, cols = (r.dq_land, slice(0, PAIR)) if kind == 0 else (r.dkv_land, slice((kind - 1) * PAIR, kind * PAIR))
        for within in range(WIDE):
            part = jnp.concatenate([source[2 * within, :, cols], source[2 * within + 1, :, cols]], axis=1)
            r.right_held[layer, kind * WIDE + within] = part
            if kind != 1:
                row = 2 if kind == 0 else 3
                rows[row : row + 1, within * BS : (within + 1) * BS] += total(part.astype(FULL))

    def back(first, last):
        part = jnp.concatenate([r.right_held[layer, n] for n in range(first, last)], axis=1)
        return jnp.concatenate(
            [dot_t(part, weights.along_row(QKV_AT, 3 * WIDE, k, first, last)) for k in range(WIDE)], axis=1
        )

    r.plane.received(r.dkv_land, r.dkv_sems[layer])
    blocks_of_kind(1)
    blocks_of_kind(2)
    grad_normed = back(WIDE, 3 * WIDE)
    r.plane.received(r.dq_land, r.dq_sems[layer])
    blocks_of_kind(0)
    give_pool(r, False, layer, 0)
    grad_normed = grad_normed + back(0, WIDE)
    unit, rate = normal(hidden)
    rows[0:1] += total(grad_normed * unit)
    rows[1:2] += total(grad_normed)
    grad_hidden = grad_middle + normal_back(grad_normed, unit, rate, vecs[0:1])
    sums = total(grad_hidden)
    for at in range(LEADS):
        rows[LEAD_AT + at : LEAD_AT + at + 1] += jnp.where(lead == at, sums, 0.0)
    return grad_hidden


def attend(r, layer):
    held, turned, stats, sems = r.held[layer], r.turned[layer], r.stats[layer], r.in_sems[layer]
    plane = r.plane
    plane.received(held.at[1], sems.at[1])
    keys = held[1].reshape(SEQ_ALL, PAIR).astype(FULL)
    for head in range(2):
        r.key_side[head] = key_columns(keys, r.neg[...], head).astype(LOW)

    def chunk(step, carry):
        at = lax.rem(step + lax.div(plane.me, 2), 4)
        first = pl.multiple_of(at * BS, BS)
        for half in range(2):
            plane.received_from(held.at[0], sems.at[0], 2 * at + half)
        queries = held[0, pl.ds(2 * at, 2)].reshape(BS, PAIR).astype(FULL)
        scales = []
        for head in range(2):
            scores = dot_t(r.key_side[head], query_columns(queries, head).astype(LOW))
            most = jnp.max(scores, axis=0, keepdims=True)
            expos = jnp.exp(scores - most)
            sums = jnp.sum(expos, axis=0, keepdims=True)
            r.expos[head] = expos.astype(LOW)
            stats[head : head + 1, pl.ds(first, BS)] = most + jnp.log(sums)
            scales.append(1.0 / sums)

        @pl.when(step == 0)
        def values_in():
            plane.received(held.at[2], sems.at[2])
            r.values_t[...] = held[2].reshape(SEQ_ALL, PAIR).astype(FULL).T.astype(LOW)

        for head in range(2):
            side = slice(head * HD, (head + 1) * HD)
            turned[at, side] = dot(r.values_t[side], r.expos[head]) * scales[head]
        for half in range(2):
            to = 2 * at + half
            r.o_message[to] = turned[at, :, half * TOKENS : (half + 1) * TOKENS].T.astype(LOW)
            plane.send_or_keep(r.o_message, r.o_land, r.o_sems[layer], to)
        return carry

    lax.fori_loop(0, SEQ_ALL // BS, chunk, 0)
    for kind in range(3):
        plane.sent(r.packed.at[kind], sems.at[kind])
    plane.received(r.o_land, r.o_sems[layer])
    plane.sent(r.o_message, r.o_sems[layer])


def attend_back(r, layer):
    held, turned, stats = r.held[layer], r.turned[layer], r.stats[layer]
    plane = r.plane
    queries = held[0].reshape(SEQ_ALL, PAIR).astype(FULL)
    keys = held[1].reshape(SEQ_ALL, PAIR).astype(FULL)
    keys_t = keys.T.astype(LOW)
    r.grad_q[...] = jnp.zeros_like(r.grad_q)
    for head in range(2):
        side = query_columns(queries, head)
        r.query_side[head] = side.astype(LOW)
        r.query_plain[head] = jnp.where(own_columns(queries, head)[0], side, 0.0).astype(LOW)
        r.key_side[head] = key_columns(keys, r.neg[...], head).astype(LOW)
    plane.received(r.do_land, r.do_sems[layer])
    grads = r.do_land[...].reshape(SEQ_ALL, PAIR).astype(FULL)
    lane = lax.broadcasted_iota(jnp.int32, grads.shape, 1)
    r.do_side[0] = jnp.where(lane < HD, grads, 0.0).astype(LOW)
    r.do_side[1] = jnp.where(lane >= HD, grads, 0.0).astype(LOW)
    grads_t = grads.T
    inner = []
    for head in range(2):
        side = slice(head * HD, (head + 1) * HD)
        inner.append(
            jnp.concatenate(
                [
                    jnp.sum(turned[at, side] * grads_t[side, at * BS : (at + 1) * BS], axis=0, keepdims=True)
                    for at in range(SEQ_ALL // BS)
                ],
                axis=1,
            )
        )
    left = lax.broadcasted_iota(jnp.int32, (BS, PAIR), 1) < HD
    keys_held = [keys_t[head * HD : (head + 1) * HD] for head in range(2)]
    for at in range(SEQ_ALL // BS):
        first = at * BS
        grad_k = []
        grad_v = None
        values = held[2, 2 * at : 2 * at + 2].reshape(BS, PAIR)
        for head in range(2):
            scores = dot_t(r.key_side[head, first : first + BS], r.query_side[head])
            probs = jnp.exp(scores - stats[head : head + 1])
            dprobs = dot_t(values, r.do_side[head])
            dscores = (probs * (dprobs - inner[head])).astype(LOW)
            term = dot(probs.astype(LOW), r.do_side[head])
            grad_v = term if grad_v is None else grad_v + term
            grad_k.append(dot(dscores, r.query_plain[head]))
            r.grad_q[head * HD : (head + 1) * HD] += dot(keys_held[head][:, first : first + BS], dscores)
        grad_k = jnp.where(left, grad_k[0], grad_k[1]).astype(LOW)
        grad_v = grad_v.astype(LOW)
        for half in range(2):
            to = 2 * at + half
            rows = slice(half * TOKENS, (half + 1) * TOKENS)
            r.dkv_message[to, :, :PAIR] = grad_k[rows]
            r.dkv_message[to, :, PAIR:] = grad_v[rows]
            plane.send_or_keep(r.dkv_message, r.dkv_land, r.dkv_sems[layer], to)
    for j in range(8):
        r.dq_message[j] = (r.grad_q[:, j * TOKENS : (j + 1) * TOKENS].T * HD**-0.5).astype(LOW)
        plane.send_or_keep(r.dq_message, r.dq_land, r.dq_sems[layer], j)


class Refs:
    pass


def names(**given):
    return tuple(given)


SCRATCH = dict(
    weights=pltpu.VMEM((NB, BS, BS), LOW),
    wide=pltpu.VMEM((2, QUART, BS, BS), FULL),
    notes=pltpu.VMEM((8, TOKENS), FULL),
    notes_land=pltpu.VMEM((8, 8, TOKENS), FULL),
    rows_land=pltpu.VMEM((1, TOKENS, D), LOW),
    first_land=pltpu.VMEM((1, TOKENS, D), LOW),
    second_land=pltpu.VMEM((1, TOKENS, D), LOW),
    pred_one=pltpu.VMEM((1, TOKENS, D), LOW),
    pred_two=pltpu.VMEM((1, TOKENS, D), LOW),
    hidden_one=pltpu.VMEM((TOKENS, D), FULL),
    hidden_two=pltpu.VMEM((TOKENS, D), FULL),
    middle_one=pltpu.VMEM((TOKENS, D), FULL),
    slope_one=pltpu.VMEM((DEEP, TOKENS, BS), FULL),
    slope_two=pltpu.VMEM((DEEP, TOKENS, BS), FULL),
    act_held=pltpu.VMEM((TOKENS, FF), LOW),
    left_held=pltpu.VMEM((2, 3 * WIDE + DEEP, BS, TOKENS), LOW),
    right_held=pltpu.VMEM((2, 5 * WIDE + DEEP, TOKENS, BS), LOW),
    packed=pltpu.VMEM((3, 8, TOKENS, PAIR), LOW),
    held=pltpu.VMEM((2, 3, 8, TOKENS, PAIR), LOW),
    values_t=pltpu.VMEM((PAIR, SEQ_ALL), LOW),
    expos=pltpu.VMEM((2, SEQ_ALL, BS), LOW),
    turned=pltpu.VMEM((2, SEQ_ALL // BS, PAIR, BS), FULL),
    stats=pltpu.VMEM((2, 8, SEQ_ALL), FULL),
    o_message=pltpu.VMEM((8, TOKENS, PAIR), LOW),
    o_land=pltpu.VMEM((8, TOKENS, PAIR), LOW),
    do_message=pltpu.VMEM((8, TOKENS, PAIR), LOW),
    do_land=pltpu.VMEM((8, TOKENS, PAIR), LOW),
    dq_message=pltpu.VMEM((8, TOKENS, PAIR), LOW),
    dq_land=pltpu.VMEM((8, TOKENS, PAIR), LOW),
    dkv_message=pltpu.VMEM((8, TOKENS, 2 * PAIR), LOW),
    dkv_land=pltpu.VMEM((8, TOKENS, 2 * PAIR), LOW),
    neg=pltpu.VMEM((SEQ_ALL, PAIR), FULL),
    query_side=pltpu.VMEM((2, SEQ_ALL, PAIR), LOW),
    query_plain=pltpu.VMEM((2, SEQ_ALL, PAIR), LOW),
    key_side=pltpu.VMEM((2, SEQ_ALL, PAIR), LOW),
    do_side=pltpu.VMEM((2, SEQ_ALL, PAIR), LOW),
    grad_q=pltpu.VMEM((PAIR, SEQ_ALL), FULL),
    load_sems=pltpu.SemaphoreType.DMA((7,)),
    z_sems=pltpu.SemaphoreType.DMA((2, 5, 2, 4)),
    y_sems=pltpu.SemaphoreType.DMA((2, 4, 4)),
    x_sems=pltpu.SemaphoreType.DMA((2, 2, 8)),
    core_sems=pltpu.SemaphoreType.DMA((2, 4, 8)),
    far_sems=pltpu.SemaphoreType.DMA((2, 2, 8)),
    note_send=pltpu.SemaphoreType.DMA((8,)),
    note_recv=pltpu.SemaphoreType.DMA((8,)),
    swap_local=pltpu.SemaphoreType.DMA((5,)),
    swap_send=pltpu.SemaphoreType.DMA((5,)),
    swap_recv=pltpu.SemaphoreType.DMA((5,)),
    plane_sems=pltpu.SemaphoreType.DMA((2, 7, 2, 8)),
    pool_sems=pltpu.SemaphoreType.DMA((3, 16)),
)
INPUTS = names(slots=0, lead_steps=0, flags=0, masters=0, rows_in=0, first_in=0, second_in=0, vectors=0)
OUTPUTS = names(left_pool=0, right_pool=0, pred_one_out=0, pred_two_out=0, input_grad=0, rows=0)


def model_kernel(*refs):
    r = Refs()
    for name, ref in zip(INPUTS + OUTPUTS + tuple(SCRATCH), refs):
        setattr(r, name, ref)
    for name in ("held", "turned", "stats"):
        setattr(r, name, [getattr(r, name).at[layer] for layer in range(2)])
    r.in_sems = [r.plane_sems.at[layer, pl.ds(0, 3)] for layer in range(2)]
    for at, name in enumerate(("o_sems", "do_sems", "dq_sems", "dkv_sems")):
        setattr(r, name, [r.plane_sems.at[layer, 3 + at] for layer in range(2)])
    swaps = [Swap(r.swap_local, r.swap_send, r.swap_recv, at) for at in range(5)]
    r.swap_rows = swaps[0]
    r.plane = Plane()
    vecs = r.vectors
    weights = Weights(r.slots, r.weights)

    def while_last():
        swaps[1].start(r.second_in, r.second_land)
        swaps[2].start(r.first_in, r.first_land)
        swaps[0].finish()
        r.rows[...] = jnp.zeros_like(r.rows)
        for layer in range(2):
            r.stats[layer][...] = jnp.zeros((8, SEQ_ALL), FULL)

    lane = lax.broadcasted_iota(jnp.int32, (1, TOKENS), 1)
    r.notes[...] = jnp.zeros_like(r.notes)
    r.notes[0:1] = r.flags[...].astype(FULL) - 1.0
    for at in range(2):
        r.notes[1:2] += jnp.where(lane == at, r.lead_steps[at, 0].astype(FULL), 0.0)
    gather_blocks(r, r.notes, while_last)
    mask_columns(r.notes_land, r.neg)
    leads = [r.notes_land[0, 1:2, at : at + 1] for at in range(2)]
    r.hidden_one[...] = r.rows_land[0].astype(FULL) + lead_row(vecs, leads[0])
    project(r, 0, r.hidden_one[...], vecs, weights)
    attend(r, 0)
    middle, result = feed(r, 0, r.hidden_one[...], vecs, weights, r.slope_one)
    r.middle_one[...] = middle
    r.pred_one[0] = result.astype(LOW)
    swaps[3].start(r.pred_one, r.pred_one_out)
    r.hidden_two[...] = result + lead_row(vecs, leads[1])
    project(r, 1, r.hidden_two[...], vecs, weights)
    attend(r, 1)
    middle, result = feed(r, 1, r.hidden_two[...], vecs, weights, r.slope_two)
    r.pred_two[0] = result.astype(LOW)
    swaps[4].start(r.pred_two, r.pred_two_out)
    swaps[1].finish()
    grad_middle = feed_back(r, 1, r.second_land[0].astype(FULL), middle, r.slope_two, vecs, weights)
    attend_back(r, 1)
    grad = project_back(r, 1, grad_middle, r.hidden_two[...], vecs, weights, leads[1])
    for source, sems in ((r.do_message, r.do_sems), (r.dkv_message, r.dkv_sems), (r.dq_message, r.dq_sems)):
        r.plane.sent(source, sems[1])
    swaps[2].finish()
    grad = grad + r.first_land[0].astype(FULL)
    grad_middle = feed_back(r, 0, grad, r.middle_one[...], r.slope_one, vecs, weights)
    attend_back(r, 0)
    grad = project_back(r, 0, grad_middle, r.hidden_one[...], vecs, weights, leads[0])
    r.input_grad[0] = grad.astype(LOW)
    for source, sems in ((r.do_message, r.do_sems), (r.dkv_message, r.dkv_sems), (r.dq_message, r.dq_sems)):
        r.plane.sent(source, sems[0])
    for left in (True, False):
        for layer in range(2):
            for kind in range(4):
                for copy in pool_copies(r, left, layer, kind):
                    copy.wait()
    swaps[3].finish()
    swaps[4].finish()


def model(slots, lead_steps, flags, masters, rows, first, second, vectors):
    return pl.pallas_call(
        model_kernel,
        out_shape=(
            shape((N_LEFT, BS, 4 * TOKENS)),
            shape((N_RIGHT, 4 * TOKENS, BS)),
            SHAPES["pred"],
            SHAPES["pred"],
            SHAPES["pred"],
            SHAPES["rows"],
        ),
        in_specs=[SMEM_IN] * 2 + [VMEM_AT] + [ANY_AT] * 4 + [VMEM_AT],
        out_specs=(ANY_AT,) * 4 + (VMEM_AT,) * 2,
        scratch_shapes=list(SCRATCH.values()),
        compiler_params=pltpu.CompilerParams(
            collective_id=0, has_side_effects=True, vmem_limit_bytes=63 * 1024 * 1024
        ),
        cost_estimate=pl.CostEstimate(flops=24 << 30, bytes_accessed=60 << 20, transcendentals=1 << 23),
        name="model",
    )(slots, lead_steps, flags, masters, rows, first, second, vectors)


SMEM_IN = pl.BlockSpec(memory_space=pltpu.SMEM)
VMEM_AT = pl.BlockSpec(memory_space=pltpu.VMEM)
ANY_AT = pl.BlockSpec(memory_space=pl.ANY)


def shape(dims, kind=LOW):
    return jax.ShapeDtypeStruct(dims, kind)


SHAPES = {"pred": shape((1, TOKENS, D)), "rows": shape((20, D), FULL)}


def bias_pieces():
    left = masked
    pieces = []
    for unused in range(3):
        piece = float(ml_dtypes.bfloat16(left))
        pieces.append(piece)
        left -= piece
    assert left == 0.0
    return pieces


MASK_PIECES = bias_pieces()


def own_columns(like, head):
    lane = lax.broadcasted_iota(jnp.int32, like.shape, 1)
    return (lane < HD) if head == 0 else (lane >= HD), lane - (HD if head == 0 else 0)


def key_columns(keys, neg, head):
    own, spot = own_columns(keys, head)
    side = jnp.zeros_like(keys)
    for at, piece in enumerate(MASK_PIECES):
        side = jnp.where(spot == at, neg * piece, side)
    return jnp.where(own, keys, side)


def query_columns(queries, head):
    own, spot = own_columns(queries, head)
    return jnp.where(own, queries * HD**-0.5, jnp.where((spot >= 0) & (spot < 3), 1.0, 0.0))


class Plane:
    def __init__(self):
        x, c, z, y = place()
        self.z = z
        self.me = 4 * c + 2 * x + y

    def device(self, j):
        return (turned_pair(lax.div(j, 2)), 2 * self.z + lax.rem(j, 2))

    def other(self, step):
        return lax.rem(self.me + step, 8)

    def others(self):
        return [self.device(self.other(step)) for step in range(1, 8)]

    def copy(self, src, dst, sems, send_at, recv_at, to):
        return pltpu.make_async_remote_copy(
            src_ref=src, dst_ref=dst, send_sem=sems.at[0, send_at], recv_sem=sems.at[1, recv_at],
            device_id=self.device(to), device_id_type=MESH,
        )

    def send(self, source, target, sems, to):
        self.copy(source.at[to], target.at[self.me], sems, to, self.me, to).start()

    def send_or_keep(self, source, target, sems, to):
        @pl.when(to != self.me)
        def away():
            self.send(source, target, sems, to)

        @pl.when(to == self.me)
        def keep():
            target[to] = source[to]

    def received(self, target, sems):
        for step in range(1, 8):
            j = self.other(step)
            self.copy(target.at[j], target.at[j], sems, j, j, j).wait_recv()

    def received_from(self, target, sems, j):
        @pl.when(j != self.me)
        def arrived():
            self.copy(target.at[j], target.at[j], sems, j, j, j).wait_recv()

    def sent(self, source, sems):
        for step in range(1, 8):
            j = self.other(step)
            self.copy(source.at[j], source.at[j], sems, j, j, j).wait_send()


def mask_columns(notes, neg):
    for j in range(8):
        neg[j * TOKENS : (j + 1) * TOKENS] = jnp.broadcast_to(notes[j, 0:1], (TOKENS, TOKENS)).T


LEFTS = (WIDE, WIDE, WIDE, DEEP)
RIGHTS = (3 * WIDE, WIDE, DEEP, WIDE)
LEFT_AT = (0, WIDE, 2 * WIDE, 3 * WIDE)
RIGHT_AT = (0, 3 * WIDE, 4 * WIDE, 4 * WIDE + DEEP)
N_LEFT = 3 * WIDE + DEEP
N_RIGHT = 5 * WIDE + DEEP


def pools_of(block):
    left = jnp.zeros_like(block)
    right = jnp.zeros_like(block)
    for at, base in enumerate((QKV_AT, OUT_AT, UP_AT, DOWN_AT)):
        inside = block >= base
        cols = RIGHTS[at]
        left = jnp.where(inside, LEFT_AT[at] + (block - base) // cols, left)
        right = jnp.where(inside, RIGHT_AT[at] + (block - base) % cols, right)
    return left, right


def halves(value):
    high = value.astype(LOW)
    return high, (value - high.astype(FULL)).astype(LOW)


def fine(left, right):
    return dot(
        jnp.concatenate([left[0], left[1], left[0]], axis=1),
        jnp.concatenate([right[0], right[0], right[1]], axis=0),
    )


def statistic(gram, shrink, diag, eye):
    return jnp.where(eye, 0.5 * diag, 0.0) + shrink * gram


def roots(stats, eye):
    scales = [jnp.sqrt(jnp.sum(jnp.sum(stat * stat, axis=1, keepdims=True), axis=0, keepdims=True)) for stat in stats]
    moving = [stat / scale for stat, scale in zip(stats, scales)]
    approx = [None] * len(stats)
    ahead = range(len(stats))
    for iteration in range(ITERS):
        factors = [(jnp.where(eye, 5.0, 0.0) - moving[i]) * 0.25 for i in ahead]
        parts = [halves(factor) for factor in factors]
        if iteration == 0:
            approx = [factors[i] * lax.rsqrt(jnp.sqrt(scales[i])) for i in ahead]
        else:
            approx = [fine(halves(approx[i]), parts[i]) for i in ahead]
        if iteration < ITERS - 1:
            squares = [halves(fine(parts[i], parts[i])) for i in ahead]
            fourths = [halves(fine(squares[i], squares[i])) for i in ahead]
            moving = [fine(fourths[i], halves(moving[i])) for i in ahead]
    return approx


PAIRED = 2
SUM_SCRATCH = dict(
    left_t=pltpu.VMEM((N_LEFT, BS, 4 * TOKENS), LOW),
    right_pool=pltpu.VMEM((N_RIGHT, 4 * TOKENS, BS), LOW),
    x_stage=pltpu.VMEM((2, 2, 4, PAIRED, BS, BS), LOW),
    x_land=pltpu.VMEM((2, 2, 4, PAIRED, BS, BS), LOW),
    yb_stage=pltpu.VMEM((4, QUART, BS, BS), LOW),
    yb_land=pltpu.VMEM((4, QUART, BS, BS), LOW),
    ym_stage=pltpu.VMEM((2, 4, PAIRED, BS, BS), LOW),
    ym_land=pltpu.VMEM((2, 4, PAIRED, BS, BS), LOW),
    zb_stage=pltpu.VMEM((4, QUART, BS, BS), LOW),
    zb_land=pltpu.VMEM((3, QUART, BS, BS), LOW),
    zm_stage=pltpu.VMEM((2, 4, PAIRED, BS, BS), LOW),
    zm_land=pltpu.VMEM((2, 3, PAIRED, BS, BS), LOW),
    both_stage=pltpu.VMEM((2, PAIRED, BS, BS), LOW),
    both_land=pltpu.VMEM((PAIRED, BS, BS), LOW),
    own=pltpu.VMEM((6, BS, BS), LOW),
    staged=pltpu.VMEM((6, BS, BS), LOW),
    pair_rows=pltpu.VMEM((20, D), FULL),
    chip_rows=pltpu.VMEM((20, D), FULL),
    plane_rows=pltpu.VMEM((20, D), FULL),
    row_land=pltpu.VMEM((3, 20, D), FULL),
    row_z=pltpu.VMEM((4, 20, D), FULL),
    pool_sems=pltpu.SemaphoreType.DMA((2,)),
    send_sems=pltpu.SemaphoreType.DMA((11, 4)),
    recv_sems=pltpu.SemaphoreType.DMA((11, 4)),
    row_send=pltpu.SemaphoreType.DMA((6,)),
    row_recv=pltpu.SemaphoreType.DMA((6,)),
    share_send=pltpu.SemaphoreType.DMA((6, 6)),
    share_recv=pltpu.SemaphoreType.DMA((6, 6)),
    local_sems=pltpu.SemaphoreType.DMA((9,)),
    swap_local=pltpu.SemaphoreType.DMA((1,)),
    swap_send=pltpu.SemaphoreType.DMA((1,)),
    swap_recv=pltpu.SemaphoreType.DMA((1,)),
)
SUM_INPUTS = names(left_ids=0, right_ids=0, rows_in=0, left_diag=0, right_diag=0, grad_in=0, left_in=0, right_in=0)
SUM_OUTPUTS = names(rows_out=0, grads_out=0, moves_out=0, grad_out=0)


def update_kernel(*refs):
    r = Refs()
    for name, ref in zip(SUM_INPUTS + SUM_OUTPUTS + tuple(SUM_SCRATCH), refs):
        setattr(r, name, ref)
    here = [
        pltpu.make_async_copy(r.right_in, r.right_pool, r.pool_sems.at[0]),
        pltpu.make_async_copy(r.left_in, r.left_t, r.pool_sems.at[1]),
    ]
    for copy in here:
        copy.start()
    x, c, z, y = place()
    samp = 2 * x + c
    blk = 2 * z + y
    to_c = (2 * x + 1 - c, blk)
    to_x = (2 * (1 - x) + c, blk)
    to_y = (samp, 2 * z + 1 - y)
    to_z = [(samp, 2 * lax.rem(z + step, 4) + y) for step in (1, 2, 3)]
    meet_all()
    swap = Swap(r.swap_local, r.swap_send, r.swap_recv)
    swap.start(r.grad_in, r.grad_out)
    row_copies = [push(r.rows_in, r.row_land.at[0], r.row_send.at[0], r.row_recv.at[0], to_c)]
    eye = lax.broadcasted_iota(jnp.int32, (BS, BS), 0) == lax.broadcasted_iota(jnp.int32, (BS, BS), 1)

    def group(half, k):
        return 2 * lax.rem(z + 1 + k, 4) + (1 - y if half == 0 else y)

    def part(half, k, offset, count=PAIRED):
        slot = group(half, k) * GROUP + c * HALF + offset
        return [dot(r.left_t[r.left_ids[slot + i]], r.right_pool[r.right_ids[slot + i]]) for i in range(count)]

    def mine(batch):
        return x * 8 + PAIRED * batch

    def other(batch):
        return (1 - x) * 8 + PAIRED * batch

    both = QUART

    def link(kind, k, stage, land, to):
        return pltpu.make_async_remote_copy(
            src_ref=stage, dst_ref=land, send_sem=r.send_sems.at[kind, k], recv_sem=r.recv_sems.at[kind, k],
            device_id=to, device_id_type=MESH,
        )

    def along_x(batch, half, k):
        return link(2 * batch + half, k, r.x_stage.at[batch, half, k], r.x_land.at[batch, half, k], to_x)

    def along_y_both(k):
        return link(4, k, r.yb_stage.at[k], r.yb_land.at[k], to_y)

    def along_y(batch, k):
        return link(5 + batch, k, r.ym_stage.at[batch, k], r.ym_land.at[batch, k], to_y)

    def along_z_both(k):
        return link(7, k, r.zb_stage.at[k], r.zb_land.at[k], (samp, group(1, k)))

    def along_z(batch, k):
        return link(8 + batch, k, r.zm_stage.at[batch, k], r.zm_land.at[batch, k], (samp, group(1, k)))

    def last():
        return link(10, 0, r.both_stage.at[1 - x], r.both_land, to_x)

    def send_x(batch, half, k):
        for i, value in enumerate(part(half, k, other(batch))):
            r.x_stage[batch, half, k, i] = value.astype(LOW)
        along_x(batch, half, k).start()

    def add_x_send_y(batch, k):
        values = part(0, k, mine(batch))
        along_x(batch, 0, k).wait_recv()
        for i, value in enumerate(values):
            r.ym_stage[batch, k, i] = (value + r.x_land[batch, 0, k, i].astype(FULL)).astype(LOW)
        along_y(batch, k).start()

    def add_both_send_z(batch, k):
        values = part(1, k, mine(batch))
        along_x(batch, 1, k).wait_recv()
        values = [value + r.x_land[batch, 1, k, i].astype(FULL) for i, value in enumerate(values)]
        along_y(batch, k).wait_recv()
        for i, value in enumerate(values):
            r.zm_stage[batch, k, i] = (value + r.ym_land[batch, k, i].astype(FULL)).astype(LOW)

        @pl.when(k < 3)
        def send_on():
            along_z(batch, k).start()

    def each(step):
        def body(k, carry):
            step(k)
            return carry

        lax.fori_loop(0, 4, body, 0)

    def slot_of(i, far=False):
        side = (1 - x) if far else x
        return c * HALF + (side * 8 + i if i < QUART else QUART + 2 * side + i - QUART)

    def share(kind, k, src, dst, to):
        return pltpu.make_async_remote_copy(
            src_ref=src, dst_ref=dst, send_sem=r.share_send.at[kind, k], recv_sem=r.share_recv.at[kind, k],
            device_id=to, device_id_type=MESH,
        )

    def grad_to(kind, pair, to):
        place_out = r.grads_out.at[pl.ds(slot_of(PAIRED * pair), PAIRED)]
        return share(kind, pair, r.own.at[pl.ds(PAIRED * pair, PAIRED)], place_out, to)

    def grad_on(pair):
        place_out = r.grads_out.at[pl.ds(slot_of(PAIRED * pair, True), PAIRED)]
        return share(2, pair, place_out, place_out, to_c)

    def grad_kept(pair):
        place_out = r.grads_out.at[pl.ds(slot_of(PAIRED * pair), PAIRED)]
        return pltpu.make_async_copy(r.own.at[pl.ds(PAIRED * pair, PAIRED)], place_out, r.local_sems.at[6 + pair])

    def move_to(kind, i, to):
        return share(kind, i, r.staged.at[i], r.moves_out.at[slot_of(i)], to)

    def move_on(i):
        place_out = r.moves_out.at[slot_of(i, True)]
        return share(5, i, place_out, place_out, to_c)

    def move_kept(i):
        return pltpu.make_async_copy(r.staged.at[i], r.moves_out.at[slot_of(i)], r.local_sems.at[i])

    def share_grads(pair):
        grad_to(0, pair, to_x).start()
        grad_to(1, pair, to_c).start()
        grad_kept(pair).start()

    def directions(pair):
        held = []
        stats = []
        for i in range(PAIRED * pair, PAIRED * pair + PAIRED):
            low = r.own[i]
            grad = low.astype(FULL)
            mean = jnp.sum(jnp.sum(grad * grad, axis=1, keepdims=True), axis=0, keepdims=True) / (BS * BS)
            shrink = 0.5 / (mean + 1e-06)
            low_t = grad.T.astype(LOW)
            slot = slot_of(i)
            stats.append(statistic(dot(low, low_t), shrink, r.left_diag[pl.ds(slot, 1)], eye))
            stats.append(statistic(dot(low_t, low), shrink, r.right_diag[pl.ds(slot, 1)], eye))
            held.append((i, low, lax.rsqrt(mean + 1e-06)))
        sides = roots(stats, eye)
        for n, (i, low, rate) in enumerate(held):
            high, rest = halves(sides[2 * n])
            turned = dot(jnp.concatenate([high, rest], axis=1), jnp.concatenate([low, low], axis=0)) * rate
            r.staged[i] = fine(halves(turned), halves(sides[2 * n + 1])).astype(LOW)
            move_to(3, i, to_x).start()
            move_to(4, i, to_c).start()
            move_kept(i).start()

    def finish_batch(batch):
        for k in range(3):
            along_z(batch, k).wait_recv()
        for i in range(PAIRED):
            value = r.zm_stage[batch, 3, i].astype(FULL)
            for k in range(3):
                value = value + r.zm_land[batch, k, i].astype(FULL)
            r.own[PAIRED * batch + i] = value.astype(LOW)
        share_grads(batch)

    def pass_on(pair):
        grad_to(0, pair, to_x).wait_recv()
        grad_on(pair).start()
        for i in range(PAIRED * pair, PAIRED * pair + PAIRED):
            move_to(3, i, to_x).wait_recv()
            move_on(i).start()

    for copy in here:
        copy.wait()

    @each
    def begin(k):
        for i, value in enumerate(part(0, k, both, QUART)):
            r.yb_stage[k, i] = value.astype(LOW)
        along_y_both(k).start()
        send_x(0, 0, k)

    @each
    def more(k):
        send_x(0, 1, k)

    row_copies[0].wait_recv()
    r.pair_rows[...] = r.rows_in[...] + r.row_land[0]
    row_copies.append(push(r.pair_rows, r.row_land.at[1], r.row_send.at[1], r.row_recv.at[1], to_x))

    @each
    def middle(k):
        add_x_send_y(0, k)
        values = part(1, k, both, QUART)
        along_y_both(k).wait_recv()
        for i, value in enumerate(values):
            r.zb_stage[k, i] = (value + r.yb_land[k, i].astype(FULL)).astype(LOW)

        @pl.when(k < 3)
        def send_on():
            along_z_both(k).start()

        send_x(1, 0, k)

    row_copies[1].wait_recv()
    r.chip_rows[...] = r.pair_rows[...] + r.row_land[1]
    row_copies.append(push(r.chip_rows, r.row_land.at[2], r.row_send.at[2], r.row_recv.at[2], to_y))

    @each
    def late(k):
        add_both_send_z(0, k)

    for k in range(3):
        along_z_both(k).wait_recv()
    for i in range(QUART):
        value = r.zb_stage[3, i].astype(FULL)
        for k in range(3):
            value = value + r.zb_land[k, i].astype(FULL)
        r.both_stage[i // 2, i % 2] = value.astype(LOW)
    last().start()

    @each
    def more_again(k):
        send_x(1, 1, k)

    @each
    def middle_again(k):
        add_x_send_y(1, k)

    row_copies[2].wait_recv()
    r.plane_rows[...] = r.chip_rows[...] + r.row_land[2]
    for step in range(3):
        row_copies.append(
            push(r.plane_rows, r.row_z.at[z], r.row_send.at[3 + step], r.row_recv.at[3 + step], to_z[step])
        )
    r.row_z[z] = r.plane_rows[...]
    last().wait_recv()
    for i in range(PAIRED):
        r.own[QUART + i] = (r.both_stage[x, i].astype(FULL) + r.both_land[i].astype(FULL)).astype(LOW)
    share_grads(2)
    directions(2)

    @each
    def late_again(k):
        add_both_send_z(1, k)

    finish_batch(0)
    directions(0)
    for step in range(3):
        row_copies[3 + step].wait_recv()
    r.rows_out[...] = (r.row_z[0] + r.row_z[1]) + (r.row_z[2] + r.row_z[3])
    finish_batch(1)
    pass_on(2)
    directions(1)
    pass_on(0)
    pass_on(1)
    for pair in range(3):
        grad_to(1, pair, to_c).wait_recv()
        grad_on(pair).wait_recv()
        grad_to(0, pair, to_x).wait_send()
        grad_to(1, pair, to_c).wait_send()
        grad_on(pair).wait_send()
        grad_kept(pair).wait()
    for i in range(6):
        move_to(4, i, to_c).wait_recv()
        move_on(i).wait_recv()
        move_to(3, i, to_x).wait_send()
        move_to(4, i, to_c).wait_send()
        move_on(i).wait_send()
        move_kept(i).wait()
    for copy in row_copies:
        copy.wait_send()
    last().wait_send()

    @each
    def drain(k):
        along_y_both(k).wait_send()
        for batch in range(2):
            along_x(batch, 0, k).wait_send()
            along_x(batch, 1, k).wait_send()
            along_y(batch, k).wait_send()

        @pl.when(k < 3)
        def sent_on():
            along_z_both(k).wait_send()
            for batch in range(2):
                along_z(batch, k).wait_send()

    swap.finish()


def update(left_ids, right_ids, rows, left_start, right_start, grad, left_pool, right_pool):
    return pl.pallas_call(
        update_kernel,
        out_shape=(SHAPES["rows"], shape((GROUP, BS, BS)), shape((GROUP, BS, BS)), SHAPES["pred"]),
        in_specs=[SMEM_IN] * 2 + [VMEM_AT] * 3 + [ANY_AT] * 3,
        out_specs=(VMEM_AT,) + (ANY_AT,) * 3,
        scratch_shapes=list(SUM_SCRATCH.values()),
        compiler_params=pltpu.CompilerParams(
            collective_id=1, has_side_effects=True, vmem_limit_bytes=VMEM_ASK
        ),
        cost_estimate=pl.CostEstimate(flops=36 << 30, bytes_accessed=40 << 20, transcendentals=0),
        name="update",
    )(left_ids, right_ids, rows, left_start, right_start, grad, left_pool, right_pool)


STEP = 4


def finish_kernel(
    grad, move, weight, left_diag, right_diag, rows, vecs, moment, input_grad, pred_one, pred_two,
    grad_out, left_out, right_out, new_out, low_out,
    rows_out, moment_out, vecs_out, input_out, pred_one_out, pred_two_out,
):
    eye = lax.broadcasted_iota(jnp.int32, (BS, BS), 0) == lax.broadcasted_iota(jnp.int32, (BS, BS), 1)
    at = pl.program_id(0)

    def mean(value):
        return jnp.sum(jnp.sum(value, axis=1, keepdims=True), axis=0, keepdims=True) / (BS * BS)

    for i in range(STEP):
        low = grad[i]
        full = low.astype(FULL)
        grad_out[i] = full
        shrink = 0.5 / (mean(full * full) + 1e-06)
        low_t = full.T.astype(LOW)
        left_out[i] = statistic(dot(low, low_t), shrink, left_diag[pl.ds(at * STEP + i, 1)], eye)
        right_out[i] = statistic(dot(low_t, low), shrink, right_diag[pl.ds(at * STEP + i, 1)], eye)
        step = move[i].astype(FULL)
        start = weight[i]
        ratio = jnp.sqrt(mean(start * start)) * lax.rsqrt(mean(step * step) + 1e-06)
        new = start - step_rate * ratio * step
        new_out[i] = new
        low_out[i] = new.astype(LOW)

    @pl.when(at == 0)
    def small():
        value = rows[...]
        scaled = value * lax.rsqrt(jnp.mean(value * value, axis=1, keepdims=True) + 1e-06)
        moments = 0.5 * moment[...] + 0.5 * scaled * scaled
        rows_out[...] = value
        moment_out[...] = moments
        vecs_out[...] = vecs[...] - vector_rate * scaled * lax.rsqrt(moments)
        input_out[...] = input_grad[...].astype(FULL)
        pred_one_out[...] = pred_one[...]
        pred_two_out[...] = pred_two[...]


def finish_slots(grads, moves, masters, left_start, right_start, rows, vecs, moment, input_grad, pred_one, pred_two):
    block = pl.BlockSpec((STEP, BS, BS), lambda i: (i, 0, 0))
    diag = pl.BlockSpec((GROUP, BS), lambda i: (0, 0))
    row = pl.BlockSpec((20, D), lambda i: (0, 0))
    wide = pl.BlockSpec((1, TOKENS, D), lambda i: (0, 0, 0))
    return pl.pallas_call(
        finish_kernel,
        grid=(GROUP // STEP,),
        compiler_params=pltpu.CompilerParams(vmem_limit_bytes=VMEM_ASK),
        out_shape=tuple(shape((GROUP, BS, BS), kind) for kind in (FULL, FULL, FULL, FULL, LOW))
        + (SHAPES["rows"],) * 3
        + (shape((1, TOKENS, D), FULL),)
        + (SHAPES["pred"],) * 2,
        in_specs=[block, block, block, diag, diag, row, row, row, wide, wide, wide],
        out_specs=(block,) * 5 + (row,) * 3 + (wide,) * 3,
        cost_estimate=pl.CostEstimate(flops=2 << 30, bytes_accessed=41 << 20, transcendentals=0),
        name="finish_slots",
    )(grads, moves, masters, left_start, right_start, rows, vecs, moment, input_grad, pred_one, pred_two)


def local_tuned(
    inputs,
    cot_first,
    cot_second,
    valid_flags,
    lead_steps,
    masters,
    assignment,
    left_start,
    right_start,
    vectors,
    vec_moment,
):
    left_pool, right_pool, pred_one, pred_two, input_grad, rows = model(
        assignment, lead_steps, valid_flags, masters, inputs, cot_first, cot_second, vectors
    )
    position = jnp.arange(NB, dtype=jnp.int32)
    inverse = jnp.sum(
        jnp.where(assignment[None, :] == position[:, None], position[None, :], 0), axis=1
    )
    left_ids, right_ids = pools_of(inverse)
    vec_grads, grads, moves, input_grad = update(
        left_ids, right_ids, rows, left_start, right_start, input_grad, left_pool, right_pool
    )
    (
        matrix_grads, left_stats, right_stats, new_masters, new_copies,
        vec_grads, vec_moments, new_vectors, input_grad, pred_one, pred_two,
    ) = finish_slots(
        grads, moves, masters, left_start, right_start, vec_grads, vectors, vec_moment, input_grad, pred_one, pred_two
    )
    return (
        pred_one,
        pred_two,
        input_grad,
        matrix_grads,
        left_stats,
        right_stats,
        new_masters,
        new_copies,
        vec_grads,
        vec_moments,
        new_vectors,
    )


def solution(mesh):
    placed = (
        P("samp", "blk", None),
        P("samp", "blk", None),
        P("samp", "blk", None),
        P("samp", "blk"),
        P(None, "samp"),
        P("blk", None, None),
        P(),
        P("blk", None),
        P("blk", None),
        P(),
        P(),
    )
    fits = mesh.shape["samp"] == 4 and mesh.shape["blk"] == 8
    return jax.shard_map(
        local_tuned if fits else local_any,
        mesh=mesh,
        in_specs=placed,
        out_specs=(
            P("samp", "blk", None),
            P("samp", "blk", None),
            P("samp", "blk", None),
            P("blk", None, None),
            P("blk", None, None),
            P("blk", None, None),
            P("blk", None, None),
            P("blk", None, None),
            P(),
            P(),
            P(),
        ),
        check_vma=False,
    )
```

```python
import functools
import math

import jax
import ml_dtypes
import jax.numpy as jnp
from jax import lax
from jax.experimental import pallas as pl
from jax.experimental.pallas import tpu as pltpu
from jax.sharding import PartitionSpec as P

D = 1024
HEADS = 16
FF = 4096
HD = 64
LEADS = 8
BS = 256
ITERS = 6
NB = 192


HIGH = lax.Precision.HIGHEST
step_rate = 0.5
vector_rate = 0.3
masked = 1000000000.0


def assemble(blocks, height, breadth):
    return (
        blocks.reshape(height // BS, breadth // BS, BS, BS)
        .transpose(0, 2, 1, 3)
        .reshape(height, breadth)
    )


def carve(matrix):
    height, breadth = matrix.shape
    return (
        matrix.reshape(height // BS, BS, breadth // BS, BS)
        .transpose(0, 2, 1, 3)
        .reshape(-1, BS, BS)
    )


def unpack(blocks):
    first_end = 3 * D * D // (BS * BS)
    second_end = first_end + D * D // (BS * BS)
    third_end = second_end + D * FF // (BS * BS)
    qkv_weight = assemble(blocks[:first_end], D, 3 * D)
    out_weight = assemble(blocks[first_end:second_end], D, D)
    up_weight = assemble(blocks[second_end:third_end], D, FF)
    down_weight = assemble(blocks[third_end:], FF, D)
    return (qkv_weight, out_weight, up_weight, down_weight)


def norm_layer(value, gain, shift):
    centred = value - jnp.mean(value, axis=-1, keepdims=True)
    spread = jnp.mean(centred * centred, axis=-1, keepdims=True)
    return centred * lax.rsqrt(spread + 1e-06) * gain + shift


def gelu_exact(value):
    return jax.nn.gelu(value, approximate=False)


def heads_of(tensor):
    return tensor.reshape(tensor.shape[0], tensor.shape[1], HEADS, HD)


def split_rows(member, count, width):
    shaped = member.reshape((member.shape[0], count, width) + member.shape[2:])
    return jnp.moveaxis(shaped, 1, 0)


def in_blocks(update, carry, members, length):
    width = math.gcd(length, 1024)
    count = length // width
    if count == 1:
        return update(carry, members, 0)
    stacked = tuple([split_rows(member, count, width) for member in members])
    offsets = jnp.arange(count, dtype=jnp.int32) * width

    def advance(state, item):
        return (update(state, item[0], item[1]), None)

    result, unused = lax.scan(advance, carry, (stacked, offsets))
    return result


def forward_update(query_heads, scaling):

    def update(carry, members, offset):
        running_max, running_sum, weighted = carry
        key_part, value_part, flag_part = members
        bias = (flag_part.astype(jnp.float32) - 1.0) * masked
        scores = (
            jnp.einsum(
                "sqhd,skhd->shqk",
                query_heads,
                heads_of(key_part),
                preferred_element_type=jnp.float32,
            )
            * scaling
            + bias[:, None, None, :]
        )
        new_max = jnp.maximum(running_max, jnp.max(scores, axis=-1))
        shrink = jnp.exp(running_max - new_max)
        expos = jnp.exp(scores - new_max[..., None])
        running_sum = running_sum * shrink + jnp.sum(expos, axis=-1)
        weighted = weighted * shrink[..., None] + jnp.einsum(
            "shqk,skhd->shqd",
            expos.astype(jnp.bfloat16),
            heads_of(value_part),
            preferred_element_type=jnp.float32,
        )
        return (new_max, running_sum, weighted)

    return update


def query_grad_update(query_heads, dout_heads, log_total, inner, scaling):

    def update(carry, members, offset):
        key_part, value_part, flag_part = members
        bias = (flag_part.astype(jnp.float32) - 1.0) * masked
        scores = (
            jnp.einsum(
                "sqhd,skhd->shqk",
                query_heads,
                heads_of(key_part),
                preferred_element_type=jnp.float32,
            )
            * scaling
            + bias[:, None, None, :]
        )
        probs = jnp.exp(scores - log_total[..., None])
        dprobs = jnp.einsum(
            "sqhd,skhd->shqk", dout_heads, heads_of(value_part), preferred_element_type=jnp.float32
        )
        dscores = (probs * (dprobs - inner[..., None])).astype(jnp.bfloat16)
        return (
            carry
            + jnp.einsum(
                "shqk,skhd->sqhd", dscores, heads_of(key_part), preferred_element_type=jnp.float32
            )
            * scaling
        )

    return update


def key_grad_update(key_heads, value_heads, key_bias, total_rows, inner_rows, scaling, anchor):

    def update(carry, members, offset):
        grad_keys, grad_values = carry
        query_part, dout_part = members
        length = query_part.shape[1]
        total_part = jnp.transpose(
            lax.dynamic_slice_in_dim(total_rows, anchor + offset, length, 1), (0, 2, 1)
        )
        inner_part = jnp.transpose(
            lax.dynamic_slice_in_dim(inner_rows, anchor + offset, length, 1), (0, 2, 1)
        )
        query_heads = heads_of(query_part)
        dout_heads = heads_of(dout_part)
        scores = (
            jnp.einsum(
                "sqhd,skhd->shqk", query_heads, key_heads, preferred_element_type=jnp.float32
            )
            * scaling
            + key_bias[:, None, None, :]
        )
        probs = jnp.exp(scores - total_part[..., None])
        dprobs = jnp.einsum(
            "sqhd,skhd->shqk", dout_heads, value_heads, preferred_element_type=jnp.float32
        )
        dscores = (probs * (dprobs - inner_part[..., None])).astype(jnp.bfloat16)
        grad_values = grad_values + jnp.einsum(
            "shqk,sqhd->skhd",
            probs.astype(jnp.bfloat16),
            dout_heads,
            preferred_element_type=jnp.float32,
        )
        grad_keys = (
            grad_keys
            + jnp.einsum(
                "shqk,sqhd->skhd", dscores, query_heads, preferred_element_type=jnp.float32
            )
            * scaling
        )
        return (grad_keys, grad_values)

    return update


def invert_root(stat):
    identity = jnp.eye(stat.shape[0], dtype=jnp.float32)
    frobenius = jnp.sqrt(jnp.sum(stat * stat))
    approx = identity * lax.rsqrt(jnp.sqrt(frobenius))
    moving = stat / frobenius
    for iteration in range(ITERS):
        factor = (5.0 * identity - moving) * 0.25
        approx = jnp.dot(approx, factor, precision=HIGH)
        square = jnp.dot(factor, factor, precision=HIGH)
        moving = jnp.dot(jnp.dot(square, square, precision=HIGH), moving, precision=HIGH)
    return approx


def precondition(gradient, left_diag, right_diag, weight):
    scaled = gradient * lax.rsqrt(jnp.mean(gradient * gradient) + 1e-06)
    identity = jnp.eye(BS, dtype=jnp.float32)
    left_new = 0.5 * identity * left_diag[None, :] + 0.5 * jnp.dot(scaled, scaled.T, precision=HIGH)
    right_new = 0.5 * identity * right_diag[None, :] + 0.5 * jnp.dot(
        scaled.T, scaled, precision=HIGH
    )
    direction = jnp.dot(
        jnp.dot(invert_root(left_new), scaled, precision=HIGH),
        invert_root(right_new),
        precision=HIGH,
    )
    ratio = jnp.sqrt(jnp.mean(weight * weight)) * lax.rsqrt(jnp.mean(direction * direction) + 1e-06)
    return (left_new, right_new, weight - step_rate * ratio * direction)


MESH = pl.DeviceIdType.MESH
LOW = jnp.bfloat16
FULL = jnp.float32
VMEM_ASK = 60 * 1024 * 1024
GROUP = 24
HALF = 12
QUART = 4


def place():
    samp = lax.axis_index("samp")
    blk = lax.axis_index("blk")
    return (lax.div(samp, 2), lax.rem(samp, 2), lax.div(blk, 2), lax.rem(blk, 2))


def meet(devices):
    barrier = pltpu.get_barrier_semaphore()
    for device in devices:
        pl.semaphore_signal(barrier, inc=1, device_id=device, device_id_type=MESH)
    pl.semaphore_wait(barrier, len(devices))


def meet_all():
    barrier = pltpu.get_barrier_semaphore()
    samp = lax.axis_index("samp")
    blk = lax.axis_index("blk")

    def tell(at, carry):
        to = lax.rem(samp * 8 + blk + at, 32)
        pl.semaphore_signal(
            barrier, inc=1, device_id=(lax.div(to, 8), lax.rem(to, 8)), device_id_type=MESH
        )
        return carry

    lax.fori_loop(1, 32, tell, 0)
    pl.semaphore_wait(barrier, 31)


def turned_pair(n):
    return 2 * lax.rem(n, 2) + lax.div(n, 2)


class Swap:
    def __init__(self, local_sems, send_sems, recv_sems, first=0):
        x, c, z, y = place()
        self.first = first
        self.stays = z == turned_pair(2 * x + c)
        self.to = (turned_pair(z), 2 * turned_pair(2 * x + c) + y)
        self.sems = (local_sems, send_sems, recv_sems)
        self.pairs = []

    def start(self, src, dst):
        at = self.first + len(self.pairs)
        local_sems, send_sems, recv_sems = self.sems
        local = pltpu.make_async_copy(src, dst, local_sems.at[at])
        away = pltpu.make_async_remote_copy(
            src_ref=src, dst_ref=dst, send_sem=send_sems.at[at], recv_sem=recv_sems.at[at],
            device_id=self.to, device_id_type=MESH,
        )
        self.pairs.append((local, away))

        @pl.when(self.stays)
        def keep():
            local.start()

        @pl.when(jnp.logical_not(self.stays))
        def send():
            away.start()

    def finish(self):
        @pl.when(self.stays)
        def kept():
            for local, away in self.pairs:
                local.wait()

        @pl.when(jnp.logical_not(self.stays))
        def sent():
            for local, away in self.pairs:
                away.wait()


def push(src, dst, send, recv, device):
    copy = pltpu.make_async_remote_copy(
        src_ref=src, dst_ref=dst, send_sem=send, recv_sem=recv, device_id=device, device_id_type=MESH
    )
    copy.start()
    return copy


FIRST, SECOND, BOTH, CROSS = range(4)
SIZES = (2, 2, 3, 1)


def gather_blocks(r, notes, while_last):
    x, c, z, y = place()
    samp = 2 * x + c
    blk = 2 * z + y
    to_y = (samp, 2 * z + 1 - y)
    to_x = (2 * (1 - x) + c, blk)
    to_c = (2 * x + 1 - c, blk)
    base = c * HALF
    out = r.weights
    starts = (base + x * 8, base + x * 8 + 2, base + QUART, base + QUART + 3)
    far_starts = (base + (1 - x) * 8, base + (1 - x) * 8 + 2)
    other = (1 - c) * HALF
    parts = [base + x * 8, base + QUART, base + (1 - x) * 8, other, other + QUART, other + 2 * QUART]
    notes_out, note_send, note_recv = r.notes_land, r.note_send, r.note_recv

    def load(at):
        return pltpu.make_async_copy(
            r.masters.at[pl.ds(parts[at], QUART)], r.wide.at[at % 2], r.load_sems.at[at]
        )

    def ready(at):
        load(at).wait()
        out[pl.ds(blk * GROUP + parts[at], QUART)] = r.wide[at % 2].astype(LOW)
        if at + 2 < len(parts):
            load(at + 2).start()

    def copy(group, start, size, sems, at, device):
        place_out = out.at[pl.ds(group * GROUP + start, size)]
        return pltpu.make_async_remote_copy(
            src_ref=place_out, dst_ref=place_out,
            send_sem=sems.at[(0,) + at], recv_sem=sems.at[(1,) + at], device_id=device, device_id_type=MESH,
        )

    def z_copy(kind, way, origin):
        to = (samp, blk + (2 if way == 0 else -2))
        return copy(2 * origin + y, starts[kind], SIZES[kind], r.z_sems, (kind, way, origin), to)

    def z_cross(way, origin, side):
        to = (samp, blk + (2 if way == 0 else -2))
        return copy(2 * origin + side, starts[CROSS], 1, r.z_sems, (CROSS + side, way, origin), to)

    def y_copy(kind, origin):
        return copy(2 * origin + y, starts[kind], SIZES[kind], r.y_sems, (kind, origin), to_y)

    def y_landed(kind, origin):
        return copy(2 * origin + 1 - y, starts[kind], SIZES[kind], r.y_sems, (kind, origin), to_y)

    def x_copy(kind, group):
        return copy(group, starts[kind], SIZES[kind], r.x_sems, (kind, group), to_x)

    def x_landed(kind, group):
        return copy(group, far_starts[kind], SIZES[kind], r.x_sems, (kind, group), to_x)

    def core_copy(kind, group):
        return copy(group, starts[kind], SIZES[kind], r.core_sems, (kind, group), to_c)

    def far_copy(kind, group):
        return copy(group, far_starts[kind], SIZES[kind], r.far_sems, (kind, group), to_c)

    def on_from_here(kind, group):
        if kind in (FIRST, SECOND):
            x_copy(kind, group).start()
        core_copy(kind, group).start()

    def begin(kind):
        @pl.when(z < 3)
        def up():
            z_copy(kind, 0, z).start()

        @pl.when(z > 0)
        def down():
            z_copy(kind, 1, z).start()

        y_copy(kind, z).start()

    def z_step(kind, distance):
        for way in (0, 1):
            origin = z - distance if way == 0 else z + distance

            @pl.when(origin >= 0 if way == 0 else origin <= 3)
            def arrived():
                z_copy(kind, way, origin).wait_recv()

                @pl.when(z < 3 if way == 0 else z > 0)
                def onward():
                    z_copy(kind, way, origin).start()

                y_copy(kind, origin).start()
                on_from_here(kind, 2 * origin + y)

    def y_step(kind, distance):
        for way in (0, 1):
            origin = z - distance if way == 0 else z + distance

            @pl.when(origin >= 0 if way == 0 else origin <= 3)
            def arrived():
                y_landed(kind, origin).wait_recv()
                on_from_here(kind, 2 * origin + 1 - y)

    def y_own(kind):
        y_landed(kind, z).wait_recv()
        on_from_here(kind, 2 * z + 1 - y)

    def cross_step(distance):
        for side in (0, 1):
            for way in (0, 1):
                origin = z - distance if way == 0 else z + distance

                @pl.when(origin >= 0 if way == 0 else origin <= 3)
                def arrived():
                    z_cross(way, origin, side).wait_recv()

                    @pl.when(z < 3 if way == 0 else z > 0)
                    def onward():
                        z_cross(way, origin, side).start()

                    core_copy(CROSS, 2 * origin + side).start()

    def x_step(kind, distance, same):
        for way in (0, 1):
            origin = z - distance if way == 0 else z + distance

            @pl.when(origin >= 0 if way == 0 else origin <= 3)
            def arrived():
                group = 2 * origin + (y if same else 1 - y)
                x_landed(kind, group).wait_recv()
                far_copy(kind, group).start()

    def x_own(kind):
        x_landed(kind, 2 * z + 1 - y).wait_recv()
        far_copy(kind, 2 * z + 1 - y).start()

    note_local = pltpu.make_async_copy(notes, notes_out.at[blk], r.load_sems.at[6])

    def note_copy(j, origin):
        return pltpu.make_async_remote_copy(
            src_ref=notes, dst_ref=notes_out.at[origin], send_sem=note_send.at[j], recv_sem=note_recv.at[origin],
            device_id=(j // 2, 2 * turned_pair(samp) + j % 2), device_id_type=MESH,
        )

    stays = z == turned_pair(samp)

    def is_me(j):
        return jnp.logical_and(stays, 2 * samp + y == j)

    def here_from(j):
        return jnp.logical_and(stays, blk == j)

    load(0).start()
    load(1).start()
    meet_all()
    r.swap_rows.start(r.rows_in, r.rows_land)
    def cross_begin():
        y_landed(CROSS, z).wait_recv()
        core_copy(CROSS, 2 * z + 1 - y).start()
        for way, there in ((0, z < 3), (1, z > 0)):
            for side in (0, 1):
                @pl.when(there)
                def both_sides():
                    z_cross(way, z, side).start()

    ready(0)
    begin(FIRST)
    begin(SECOND)
    ready(1)
    y_copy(CROSS, z).start()
    for j in range(8):

        @pl.when(jnp.logical_not(is_me(j)))
        def send_note():
            note_copy(j, blk).start()

    @pl.when(stays)
    def keep_note():
        note_local.start()

    for at in range(2, len(parts)):
        ready(at)
    z_step(FIRST, 1)
    z_step(SECOND, 1)
    y_own(SECOND)
    z_step(FIRST, 2)
    begin(BOTH)
    z_step(SECOND, 2)
    y_step(FIRST, 1)
    y_own(FIRST)
    y_own(BOTH)
    z_step(SECOND, 3)
    x_step(FIRST, 1, True)
    y_step(SECOND, 1)
    x_own(SECOND)
    z_step(BOTH, 1)
    cross_begin()
    x_step(FIRST, 2, True)
    z_step(FIRST, 3)
    y_step(FIRST, 2)
    cross_step(1)
    x_step(SECOND, 1, True)
    x_own(FIRST)
    y_step(SECOND, 2)
    y_step(SECOND, 3)
    x_step(FIRST, 1, False)
    z_step(BOTH, 2)
    x_step(SECOND, 1, False)
    y_step(BOTH, 1)
    x_step(FIRST, 2, False)
    z_step(BOTH, 3)
    x_step(SECOND, 2, True)
    y_step(FIRST, 3)
    x_step(FIRST, 3, True)
    cross_step(2)
    y_step(BOTH, 2)
    x_step(SECOND, 3, False)
    x_step(SECOND, 2, False)
    x_step(SECOND, 3, True)
    cross_step(3)
    y_step(BOTH, 3)
    x_step(FIRST, 3, False)

    while_last()
    other_starts = (other + x * 8, other + x * 8 + 2, other + QUART, other + QUART + 3)
    other_far = (other + (1 - x) * 8, other + (1 - x) * 8 + 2)

    def settle(group, carry):
        @pl.when(group != blk)
        def other_group():
            for kind in range(4):
                copy(group, other_starts[kind], SIZES[kind], r.core_sems, (kind, group), to_c).wait_recv()
                core_copy(kind, group).wait_send()
            for kind in (FIRST, SECOND):
                copy(group, other_far[kind], SIZES[kind], r.far_sems, (kind, group), to_c).wait_recv()
                far_copy(kind, group).wait_send()
                x_copy(kind, group).wait_send()

        return carry

    lax.fori_loop(0, 8, settle, 0)

    def sent_along(origin, carry):
        for kind in (FIRST, SECOND, BOTH):
            y_copy(kind, origin).wait_send()

            @pl.when(jnp.logical_and(origin <= z, z < 3))
            def up():
                z_copy(kind, 0, origin).wait_send()

            @pl.when(jnp.logical_and(origin >= z, z > 0))
            def down():
                z_copy(kind, 1, origin).wait_send()

        for side in (0, 1):
            @pl.when(jnp.logical_and(origin <= z, z < 3))
            def cross_up():
                z_cross(0, origin, side).wait_send()

            @pl.when(jnp.logical_and(origin >= z, z > 0))
            def cross_down():
                z_cross(1, origin, side).wait_send()

        return carry

    lax.fori_loop(0, 4, sent_along, 0)
    y_copy(CROSS, z).wait_send()
    for j in range(8):

        @pl.when(jnp.logical_not(is_me(j)))
        def sent_note():
            note_copy(j, blk).wait_send()

        @pl.when(jnp.logical_not(here_from(j)))
        def got_note():
            note_copy(j, j).wait_recv()

    @pl.when(stays)
    def kept_note():
        note_local.wait()


def local_any(
    inputs,
    cot_first,
    cot_second,
    valid_flags,
    lead_steps,
    masters,
    assignment,
    left_start,
    right_start,
    vectors,
    vec_moment,
):
    copies = lax.all_gather(masters.astype(jnp.bfloat16), "blk", axis=0, tiled=True)
    blocks = jnp.take(copies, assignment, axis=0)
    qkv_weight, out_weight, up_weight, down_weight = unpack(blocks)
    scaling = HD ** (-0.5)
    flags_low = valid_flags.astype(jnp.bfloat16)
    key_bias = (valid_flags.astype(jnp.float32) - 1.0) * masked
    lead_base = 8 + FF // D
    lead_table = vectors[lead_base:]
    samples = inputs.shape[0]
    patches = inputs.shape[1]

    def forward(hidden_in, lead_ids):
        chosen = (lead_ids[:, None] == jnp.arange(LEADS, dtype=jnp.int32)[None, :]).astype(
            jnp.float32
        )
        lead_rows = jnp.dot(chosen, lead_table, precision=HIGH)
        hidden = hidden_in + lead_rows[:, None, :]
        normed_low = norm_layer(hidden, vectors[0], vectors[1]).astype(jnp.bfloat16)
        packed = jnp.einsum(
            "spd,de->spe", normed_low, qkv_weight, preferred_element_type=jnp.float32
        )
        queries = (packed[..., :D] + vectors[2]).astype(jnp.bfloat16)
        keys_low = packed[..., D : 2 * D].astype(jnp.bfloat16)
        values_low = (packed[..., 2 * D :] + vectors[3]).astype(jnp.bfloat16)
        start_state = (
            jnp.full((samples, HEADS, patches), -1e30, jnp.float32),
            jnp.zeros((samples, HEADS, patches), jnp.float32),
            jnp.zeros((samples, HEADS, patches, HD), jnp.float32),
        )
        update = forward_update(heads_of(queries), scaling)
        gathered = None
        piece = (
            lax.all_gather(keys_low, "blk", axis=1, tiled=True),
            lax.all_gather(values_low, "blk", axis=1, tiled=True),
            lax.all_gather(flags_low, "blk", axis=1, tiled=True),
        )
        running_max, running_sum, weighted = in_blocks(
            update, start_state, piece, piece[0].shape[1]
        )
        attended = jnp.transpose(weighted / running_sum[..., None], (0, 2, 1, 3)).reshape(
            samples, patches, D
        )
        log_total = running_max + jnp.log(running_sum)
        attended_low = attended.astype(jnp.bfloat16)
        middle = (
            hidden
            + jnp.einsum(
                "spd,de->spe", attended_low, out_weight, preferred_element_type=jnp.float32
            )
            + vectors[4]
        )
        normed_two = norm_layer(middle, vectors[5], vectors[6]).astype(jnp.bfloat16)
        upward = jnp.einsum(
            "spd,df->spf", normed_two, up_weight, preferred_element_type=jnp.float32
        ) + vectors[8:lead_base].reshape(FF)
        activated = gelu_exact(upward).astype(jnp.bfloat16)
        result = (
            middle
            + jnp.einsum("spf,fd->spd", activated, down_weight, preferred_element_type=jnp.float32)
            + vectors[7]
        )
        saved = (
            hidden,
            normed_low,
            queries,
            keys_low,
            values_low,
            attended,
            attended_low,
            log_total,
            middle,
            normed_two,
            upward,
            activated,
            chosen,
            gathered,
        )
        return (result, saved)

    def backward(grad_out, saved):
        (
            hidden,
            normed_low,
            queries,
            keys_low,
            values_low,
            attended,
            attended_low,
            log_total,
            middle,
            normed_two,
            upward,
            activated,
            chosen,
            gathered,
        ) = saved
        grad_two = grad_out.astype(jnp.bfloat16)
        down_grad = jnp.einsum(
            "spf,spd->fd", activated, grad_two, preferred_element_type=jnp.float32
        )
        down_bias = jnp.sum(grad_two.astype(jnp.float32), axis=(0, 1))
        grad_act = jnp.einsum(
            "spd,fd->spf", grad_two, down_weight, preferred_element_type=jnp.float32
        )
        gelu_value, gelu_pull = jax.vjp(gelu_exact, upward)
        grad_up = gelu_pull(grad_act)[0].astype(jnp.bfloat16)
        up_grad = jnp.einsum("spd,spf->df", normed_two, grad_up, preferred_element_type=jnp.float32)
        up_bias = jnp.sum(grad_up.astype(jnp.float32), axis=(0, 1))
        grad_normed_two = jnp.einsum(
            "spf,df->spd", grad_up, up_weight, preferred_element_type=jnp.float32
        )
        norm_value, norm_pull = jax.vjp(norm_layer, middle, vectors[5], vectors[6])
        grad_middle_norm, gain_two, shift_two = norm_pull(grad_normed_two)
        grad_middle = grad_out + grad_middle_norm
        grad_one = grad_middle.astype(jnp.bfloat16)
        out_grad = jnp.einsum(
            "spd,spe->de", attended_low, grad_one, preferred_element_type=jnp.float32
        )
        out_bias = jnp.sum(grad_one.astype(jnp.float32), axis=(0, 1))
        grad_attended = jnp.einsum(
            "spe,de->spd", grad_one, out_weight, preferred_element_type=jnp.float32
        ).astype(jnp.bfloat16)
        inner = jnp.sum(
            (grad_attended.astype(jnp.float32) * attended).reshape(samples, patches, HEADS, HD),
            axis=-1,
        )
        inner_heads = jnp.transpose(inner, (0, 2, 1))
        zero_query = jnp.zeros((samples, patches, HEADS, HD), jnp.float32)
        update_query = query_grad_update(
            heads_of(queries), heads_of(grad_attended), log_total, inner_heads, scaling
        )
        piece = (
            lax.all_gather(keys_low, "blk", axis=1, tiled=True),
            lax.all_gather(values_low, "blk", axis=1, tiled=True),
            lax.all_gather(flags_low, "blk", axis=1, tiled=True),
        )
        grad_query = in_blocks(update_query, zero_query, piece, piece[0].shape[1])
        total_rows, inner_rows = (
            lax.all_gather(jnp.transpose(log_total, (0, 2, 1)), "blk", axis=1, tiled=True),
            lax.all_gather(inner, "blk", axis=1, tiled=True),
        )
        key_heads = heads_of(keys_low)
        value_heads = heads_of(values_low)
        zero_pair = (zero_query, zero_query)
        piece = (
            lax.all_gather(queries, "blk", axis=1, tiled=True),
            lax.all_gather(grad_attended, "blk", axis=1, tiled=True),
        )
        update_keys = key_grad_update(
            key_heads, value_heads, key_bias, total_rows, inner_rows, scaling, jnp.int32(0)
        )
        grad_keys, grad_values = in_blocks(update_keys, zero_pair, piece, piece[0].shape[1])
        grad_packed = jnp.concatenate(
            [
                grad_query.reshape(samples, patches, D),
                grad_keys.reshape(samples, patches, D),
                grad_values.reshape(samples, patches, D),
            ],
            axis=-1,
        ).astype(jnp.bfloat16)
        qkv_grad = jnp.einsum(
            "spd,spe->de", normed_low, grad_packed, preferred_element_type=jnp.float32
        )
        query_bias = jnp.sum(grad_packed[..., :D].astype(jnp.float32), axis=(0, 1))
        value_bias = jnp.sum(grad_packed[..., 2 * D :].astype(jnp.float32), axis=(0, 1))
        grad_normed = jnp.einsum(
            "spe,de->spd", grad_packed, qkv_weight, preferred_element_type=jnp.float32
        )
        first_value, first_pull = jax.vjp(norm_layer, hidden, vectors[0], vectors[1])
        grad_hidden_norm, gain_one, shift_one = first_pull(grad_normed)
        grad_hidden = grad_middle + grad_hidden_norm
        lead_grad = jnp.dot(chosen.T, jnp.sum(grad_hidden, axis=1), precision=HIGH)
        vec_rows = jnp.concatenate(
            [
                gain_one[None],
                shift_one[None],
                query_bias[None],
                value_bias[None],
                out_bias[None],
                gain_two[None],
                shift_two[None],
                down_bias[None],
                up_bias.reshape(FF // D, D),
                lead_grad,
            ],
            axis=0,
        )
        return (grad_hidden, (qkv_grad, out_grad, up_grad, down_grad), vec_rows)

    earlier, saved_one = forward(inputs.astype(jnp.float32), lead_steps[0])
    later, saved_two = forward(earlier, lead_steps[1])
    grad_between, mats_two, vec_two = backward(cot_second.astype(jnp.float32), saved_two)
    input_grad, mats_one, vec_one = backward(
        cot_first.astype(jnp.float32) + grad_between, saved_one
    )
    grad_blocks = jnp.concatenate(
        [
            carve(mats_one[0] + mats_two[0]),
            carve(mats_one[1] + mats_two[1]),
            carve(mats_one[2] + mats_two[2]),
            carve(mats_one[3] + mats_two[3]),
        ],
        axis=0,
    )
    position = jnp.arange(NB, dtype=jnp.int32)
    inverse = jnp.sum(
        jnp.where(assignment[None, :] == position[:, None], position[None, :], 0), axis=1
    )
    slotted = jnp.take(grad_blocks, inverse, axis=0)
    shared = lax.psum_scatter(slotted, "blk", scatter_dimension=0, tiled=True)
    matrix_grads = lax.psum(shared.astype(jnp.bfloat16), "samp").astype(jnp.float32)
    vec_grads = lax.psum(vec_one + vec_two, ("samp", "blk"))
    left_stats, right_stats, new_masters = jax.vmap(precondition)(
        matrix_grads, left_start, right_start, masters
    )
    scaled_vec = vec_grads * lax.rsqrt(
        jnp.mean(vec_grads * vec_grads, axis=1, keepdims=True) + 1e-06
    )
    vec_moments = 0.5 * vec_moment + 0.5 * scaled_vec * scaled_vec
    new_vectors = vectors - vector_rate * scaled_vec * lax.rsqrt(vec_moments)
    return (
        earlier.astype(jnp.bfloat16),
        later.astype(jnp.bfloat16),
        input_grad,
        matrix_grads,
        left_stats,
        right_stats,
        new_masters,
        new_masters.astype(jnp.bfloat16),
        vec_grads,
        vec_moments,
        new_vectors,
    )


TOKENS = 128
PAIR = 2 * HD
SEQ_ALL = 8 * TOKENS
QKV_AT, OUT_AT, UP_AT, DOWN_AT = 0, 48, 64, 128
WIDE = D // BS
DEEP = FF // BS
LEAD_AT = 8 + FF // D


def dot(left, right):
    return jnp.dot(left, right, preferred_element_type=FULL)


def dot_t(left, right):
    return lax.dot_general(left, right, (((1,), (1,)), ((), ())), preferred_element_type=FULL)


def normal(value):
    centred = value - jnp.mean(value, axis=-1, keepdims=True)
    rate = lax.rsqrt(jnp.mean(centred * centred, axis=-1, keepdims=True) + 1e-06)
    return (centred * rate, rate)


def normal_back(grad, unit, rate, gain):
    scaled = grad * gain
    return rate * (
        scaled
        - jnp.mean(scaled, axis=-1, keepdims=True)
        - unit * jnp.mean(scaled * unit, axis=-1, keepdims=True)
    )


def total(value):
    return jnp.sum(value, axis=0, keepdims=True)


def gelu_parts(value):
    phi = 0.5 + 0.5 * lax.erf(value * (0.5**0.5))
    return phi, value * phi


def gelu_slope(value, phi):
    return phi + value * jnp.exp(-0.5 * value * value) * ((2.0 * math.pi) ** -0.5)


class Weights:
    def __init__(self, slots, held):
        self.slots, self.held = slots, held

    def block(self, base, cols, row, col):
        return self.held[self.slots[base + row * cols + col]]

    def down_col(self, base, rows, cols, col):
        return jnp.concatenate([self.block(base, cols, row, col) for row in range(rows)], axis=0)

    def along_row(self, base, cols, row, first=0, last=None):
        return jnp.concatenate(
            [self.block(base, cols, row, col) for col in range(first, cols if last is None else last)], axis=1
        )


def lead_row(vecs, lead):
    row = jnp.zeros((1, D), FULL)
    for at in range(LEADS):
        row = row + jnp.where(lead == at, vecs[LEAD_AT + at : LEAD_AT + at + 1], 0.0)
    return row


def project(r, layer, hidden, vecs, weights):
    unit, unused = normal(hidden)
    normed = (unit * vecs[0:1] + vecs[1:2]).astype(LOW)
    for k in range(WIDE):
        r.left_held[layer, k] = normed[:, k * BS : (k + 1) * BS].T
    give_pool(r, True, layer, 0)
    for kind in (1, 0, 2):
        for step in range(WIDE):
            within = lax.rem(step + lax.div(r.plane.me, 2), WIDE)
            part = dot(normed, weights.down_col(QKV_AT, WIDE, 3 * WIDE, kind * WIDE + within))
            if kind != 1:
                row = 2 if kind == 0 else 3
                part = part + vecs[row : row + 1, pl.ds(pl.multiple_of(within * BS, BS), BS)]
            part = part.astype(LOW)
            for half in range(2):
                r.packed[kind, 2 * within + half] = part[:, half * PAIR : (half + 1) * PAIR]
                r.plane.send_or_keep(
                    r.packed.at[kind], r.held[layer].at[kind], r.in_sems[layer].at[kind], 2 * within + half
                )


def pool_at(left, kind):
    counts, bases = (LEFTS, LEFT_AT) if left else (RIGHTS, RIGHT_AT)
    return pl.ds(bases[kind], counts[kind])


def pool_copies(r, left, layer, kind):
    x, c, z, y = place()
    ids = pool_at(left, kind)
    at = (0 if left else 8) + 4 * layer + kind
    source = (r.left_held if left else r.right_held).at[layer, ids]

    def target(part):
        tokens = pl.ds((2 * part + layer) * TOKENS, TOKENS)
        return r.left_pool.at[ids, :, tokens] if left else r.right_pool.at[ids, tokens]

    here = pltpu.make_async_copy(source, target(0), r.pool_sems.at[0, at])
    there = pltpu.make_async_remote_copy(
        src_ref=source, dst_ref=target(1), send_sem=r.pool_sems.at[1, at], recv_sem=r.pool_sems.at[2, at],
        device_id=(2 * x + 1 - c, 2 * z + y), device_id_type=MESH,
    )
    return here, there


def give_pool(r, left, layer, kind):
    for copy in pool_copies(r, left, layer, kind):
        copy.start()


def feed(r, layer, hidden, vecs, weights, slope_held):
    attended = jnp.concatenate([r.o_land[j] for j in range(8)], axis=1)
    for k in range(WIDE):
        r.left_held[layer, WIDE + k] = attended[:, k * BS : (k + 1) * BS].T
    give_pool(r, True, layer, 1)
    branch = [dot(attended, weights.down_col(OUT_AT, WIDE, WIDE, n)) for n in range(WIDE)]
    middle = hidden + jnp.concatenate(branch, axis=1) + vecs[4:5]
    unit, unused = normal(middle)
    normed = (unit * vecs[5:6] + vecs[6:7]).astype(LOW)
    for k in range(WIDE):
        r.left_held[layer, 2 * WIDE + k] = normed[:, k * BS : (k + 1) * BS].T
    give_pool(r, True, layer, 2)
    per = D // BS
    for f in range(DEEP):
        bias = vecs[8 + f // per : 9 + f // per, (f % per) * BS : (f % per + 1) * BS]
        upward = dot(normed, weights.down_col(UP_AT, WIDE, DEEP, f)) + bias
        phi, activated = gelu_parts(upward)
        slope_held[f] = gelu_slope(upward, phi)
        activated = activated.astype(LOW)
        r.act_held[:, f * BS : (f + 1) * BS] = activated
        r.left_held[layer, 3 * WIDE + f] = activated.T
    give_pool(r, True, layer, 3)
    branch = [dot(r.act_held[...], weights.down_col(DOWN_AT, DEEP, WIDE, n)) for n in range(WIDE)]
    return middle, middle + jnp.concatenate(branch, axis=1) + vecs[7:8]


def feed_back(r, layer, grad_out, middle, slope_in, vecs, weights):
    rows = r.rows
    grad_two = grad_out.astype(LOW)
    for k in range(WIDE):
        r.right_held[layer, RIGHT_AT[3] + k] = grad_two[:, k * BS : (k + 1) * BS]
    give_pool(r, False, layer, 3)
    rows[7:8] += total(grad_two.astype(FULL))
    per = D // BS
    for f in range(DEEP):
        grad_act = dot_t(grad_two, weights.along_row(DOWN_AT, WIDE, f))
        grad_up = (grad_act * slope_in[f]).astype(LOW)
        r.right_held[layer, RIGHT_AT[2] + f] = grad_up
        rows[8 + f // per : 9 + f // per, (f % per) * BS : (f % per + 1) * BS] += total(grad_up.astype(FULL))
    give_pool(r, False, layer, 2)
    grad_up = jnp.concatenate([r.right_held[layer, RIGHT_AT[2] + f] for f in range(DEEP)], axis=1)
    grad_normed = jnp.concatenate(
        [dot_t(grad_up, weights.along_row(UP_AT, DEEP, k)) for k in range(WIDE)], axis=1
    )
    unit, rate = normal(middle)
    rows[5:6] += total(grad_normed * unit)
    rows[6:7] += total(grad_normed)
    grad_middle = grad_out + normal_back(grad_normed, unit, rate, vecs[5:6])
    grad_one = grad_middle.astype(LOW)
    for k in range(WIDE):
        r.right_held[layer, RIGHT_AT[1] + k] = grad_one[:, k * BS : (k + 1) * BS]
    give_pool(r, False, layer, 1)
    rows[4:5] += total(grad_one.astype(FULL))
    for k in range(WIDE):
        part = dot_t(grad_one, weights.along_row(OUT_AT, WIDE, k)).astype(LOW)
        for half in range(2):
            r.do_message[2 * k + half] = part[:, half * PAIR : (half + 1) * PAIR]
            r.plane.send_or_keep(r.do_message, r.do_land, r.do_sems[layer], 2 * k + half)
    return grad_middle


def project_back(r, layer, grad_middle, hidden, vecs, weights, lead):
    rows = r.rows

    def blocks_of_kind(kind):
        source, cols = (r.dq_land, slice(0, PAIR)) if kind == 0 else (r.dkv_land, slice((kind - 1) * PAIR, kind * PAIR))
        for within in range(WIDE):
            part = jnp.concatenate([source[2 * within, :, cols], source[2 * within + 1, :, cols]], axis=1)
            r.right_held[layer, kind * WIDE + within] = part
            if kind != 1:
                row = 2 if kind == 0 else 3
                rows[row : row + 1, within * BS : (within + 1) * BS] += total(part.astype(FULL))

    def back(first, last):
        part = jnp.concatenate([r.right_held[layer, n] for n in range(first, last)], axis=1)
        return jnp.concatenate(
            [dot_t(part, weights.along_row(QKV_AT, 3 * WIDE, k, first, last)) for k in range(WIDE)], axis=1
        )

    r.plane.received(r.dkv_land, r.dkv_sems[layer])
    blocks_of_kind(1)
    blocks_of_kind(2)
    grad_normed = back(WIDE, 3 * WIDE)
    r.plane.received(r.dq_land, r.dq_sems[layer])
    blocks_of_kind(0)
    give_pool(r, False, layer, 0)
    grad_normed = grad_normed + back(0, WIDE)
    unit, rate = normal(hidden)
    rows[0:1] += total(grad_normed * unit)
    rows[1:2] += total(grad_normed)
    grad_hidden = grad_middle + normal_back(grad_normed, unit, rate, vecs[0:1])
    sums = total(grad_hidden)
    for at in range(LEADS):
        rows[LEAD_AT + at : LEAD_AT + at + 1] += jnp.where(lead == at, sums, 0.0)
    return grad_hidden


def attend(r, layer):
    held, turned, stats, sems = r.held[layer], r.turned[layer], r.stats[layer], r.in_sems[layer]
    plane = r.plane
    plane.received(held.at[1], sems.at[1])
    keys = held[1].reshape(SEQ_ALL, PAIR).astype(FULL)
    for head in range(2):
        r.key_side[head] = key_columns(keys, r.neg[...], head).astype(LOW)

    def chunk(step, carry):
        at = lax.rem(step + lax.div(plane.me, 2), 4)
        first = pl.multiple_of(at * BS, BS)
        for half in range(2):
            plane.received_from(held.at[0], sems.at[0], 2 * at + half)
        queries = held[0, pl.ds(2 * at, 2)].reshape(BS, PAIR).astype(FULL)
        scales = []
        for head in range(2):
            scores = dot_t(r.key_side[head], query_columns(queries, head).astype(LOW))
            most = jnp.max(scores, axis=0, keepdims=True)
            expos = jnp.exp(scores - most)
            sums = jnp.sum(expos, axis=0, keepdims=True)
            r.expos[head] = expos.astype(LOW)
            stats[head : head + 1, pl.ds(first, BS)] = most + jnp.log(sums)
            scales.append(1.0 / sums)

        @pl.when(step == 0)
        def values_in():
            plane.received(held.at[2], sems.at[2])
            r.values_t[...] = held[2].reshape(SEQ_ALL, PAIR).T

        for head in range(2):
            side = slice(head * HD, (head + 1) * HD)
            turned[at, side] = dot(r.values_t[side], r.expos[head]) * scales[head]
        for half in range(2):
            to = 2 * at + half
            r.o_message[to] = turned[at, :, half * TOKENS : (half + 1) * TOKENS].astype(LOW).T
            plane.send_or_keep(r.o_message, r.o_land, r.o_sems[layer], to)
        return carry

    lax.fori_loop(0, SEQ_ALL // BS, chunk, 0)
    for kind in range(3):
        plane.sent(r.packed.at[kind], sems.at[kind])
    plane.received(r.o_land, r.o_sems[layer])
    plane.sent(r.o_message, r.o_sems[layer])


def attend_back(r, layer):
    held, turned, stats = r.held[layer], r.turned[layer], r.stats[layer]
    plane = r.plane
    queries = held[0].reshape(SEQ_ALL, PAIR).astype(FULL)
    keys = held[1].reshape(SEQ_ALL, PAIR).astype(FULL)
    keys_t = held[1].reshape(SEQ_ALL, PAIR).T
    r.grad_q[...] = jnp.zeros_like(r.grad_q)
    for head in range(2):
        side = query_columns(queries, head)
        r.query_side[head] = side.astype(LOW)
        r.query_plain[head] = jnp.where(own_columns(queries, head)[0], side, 0.0).astype(LOW)
        r.key_side[head] = key_columns(keys, r.neg[...], head).astype(LOW)
    plane.received(r.do_land, r.do_sems[layer])
    grads = r.do_land[...].reshape(SEQ_ALL, PAIR).astype(FULL)
    lane = lax.broadcasted_iota(jnp.int32, grads.shape, 1)
    r.do_side[0] = jnp.where(lane < HD, grads, 0.0).astype(LOW)
    r.do_side[1] = jnp.where(lane >= HD, grads, 0.0).astype(LOW)
    grads_t = r.do_land[...].reshape(SEQ_ALL, PAIR).T.astype(FULL)
    inner = []
    for head in range(2):
        side = slice(head * HD, (head + 1) * HD)
        inner.append(
            jnp.concatenate(
                [
                    jnp.sum(turned[at, side] * grads_t[side, at * BS : (at + 1) * BS], axis=0, keepdims=True)
                    for at in range(SEQ_ALL // BS)
                ],
                axis=1,
            )
        )
    left = lax.broadcasted_iota(jnp.int32, (BS, PAIR), 1) < HD
    keys_held = [keys_t[head * HD : (head + 1) * HD] for head in range(2)]
    for at in range(SEQ_ALL // BS):
        first = at * BS
        grad_k = []
        grad_v = None
        values = held[2, 2 * at : 2 * at + 2].reshape(BS, PAIR)
        for head in range(2):
            scores = dot_t(r.key_side[head, first : first + BS], r.query_side[head])
            probs = jnp.exp(scores - stats[head : head + 1])
            dprobs = dot_t(values, r.do_side[head])
            dscores = (probs * (dprobs - inner[head])).astype(LOW)
            term = dot(probs.astype(LOW), r.do_side[head])
            grad_v = term if grad_v is None else grad_v + term
            grad_k.append(dot(dscores, r.query_plain[head]))
            r.grad_q[head * HD : (head + 1) * HD] += dot(keys_held[head][:, first : first + BS], dscores)
        grad_k = jnp.where(left, grad_k[0], grad_k[1]).astype(LOW)
        grad_v = grad_v.astype(LOW)
        for half in range(2):
            to = 2 * at + half
            rows = slice(half * TOKENS, (half + 1) * TOKENS)
            r.dkv_message[to, :, :PAIR] = grad_k[rows]
            r.dkv_message[to, :, PAIR:] = grad_v[rows]
            plane.send_or_keep(r.dkv_message, r.dkv_land, r.dkv_sems[layer], to)
    for j in range(8):
        r.dq_message[j] = (r.grad_q[:, j * TOKENS : (j + 1) * TOKENS] * HD**-0.5).astype(LOW).T
        plane.send_or_keep(r.dq_message, r.dq_land, r.dq_sems[layer], j)


class Refs:
    pass


def names(**given):
    return tuple(given)


SCRATCH = dict(
    weights=pltpu.VMEM((NB, BS, BS), LOW),
    wide=pltpu.VMEM((2, QUART, BS, BS), FULL),
    notes=pltpu.VMEM((8, TOKENS), FULL),
    notes_land=pltpu.VMEM((8, 8, TOKENS), FULL),
    rows_land=pltpu.VMEM((1, TOKENS, D), LOW),
    first_land=pltpu.VMEM((1, TOKENS, D), LOW),
    second_land=pltpu.VMEM((1, TOKENS, D), LOW),
    pred_one=pltpu.VMEM((1, TOKENS, D), LOW),
    pred_two=pltpu.VMEM((1, TOKENS, D), LOW),
    hidden_one=pltpu.VMEM((TOKENS, D), FULL),
    hidden_two=pltpu.VMEM((TOKENS, D), FULL),
    middle_one=pltpu.VMEM((TOKENS, D), FULL),
    slope_one=pltpu.VMEM((DEEP, TOKENS, BS), FULL),
    slope_two=pltpu.VMEM((DEEP, TOKENS, BS), FULL),
    act_held=pltpu.VMEM((TOKENS, FF), LOW),
    left_held=pltpu.VMEM((2, 3 * WIDE + DEEP, BS, TOKENS), LOW),
    right_held=pltpu.VMEM((2, 5 * WIDE + DEEP, TOKENS, BS), LOW),
    packed=pltpu.VMEM((3, 8, TOKENS, PAIR), LOW),
    held=pltpu.VMEM((2, 3, 8, TOKENS, PAIR), LOW),
    values_t=pltpu.VMEM((PAIR, SEQ_ALL), LOW),
    expos=pltpu.VMEM((2, SEQ_ALL, BS), LOW),
    turned=pltpu.VMEM((2, SEQ_ALL // BS, PAIR, BS), FULL),
    stats=pltpu.VMEM((2, 8, SEQ_ALL), FULL),
    o_message=pltpu.VMEM((8, TOKENS, PAIR), LOW),
    o_land=pltpu.VMEM((8, TOKENS, PAIR), LOW),
    do_message=pltpu.VMEM((8, TOKENS, PAIR), LOW),
    do_land=pltpu.VMEM((8, TOKENS, PAIR), LOW),
    dq_message=pltpu.VMEM((8, TOKENS, PAIR), LOW),
    dq_land=pltpu.VMEM((8, TOKENS, PAIR), LOW),
    dkv_message=pltpu.VMEM((8, TOKENS, 2 * PAIR), LOW),
    dkv_land=pltpu.VMEM((8, TOKENS, 2 * PAIR), LOW),
    neg=pltpu.VMEM((SEQ_ALL, PAIR), FULL),
    query_side=pltpu.VMEM((2, SEQ_ALL, PAIR), LOW),
    query_plain=pltpu.VMEM((2, SEQ_ALL, PAIR), LOW),
    key_side=pltpu.VMEM((2, SEQ_ALL, PAIR), LOW),
    do_side=pltpu.VMEM((2, SEQ_ALL, PAIR), LOW),
    grad_q=pltpu.VMEM((PAIR, SEQ_ALL), FULL),
    load_sems=pltpu.SemaphoreType.DMA((7,)),
    z_sems=pltpu.SemaphoreType.DMA((2, 5, 2, 4)),
    y_sems=pltpu.SemaphoreType.DMA((2, 4, 4)),
    x_sems=pltpu.SemaphoreType.DMA((2, 2, 8)),
    core_sems=pltpu.SemaphoreType.DMA((2, 4, 8)),
    far_sems=pltpu.SemaphoreType.DMA((2, 2, 8)),
    note_send=pltpu.SemaphoreType.DMA((8,)),
    note_recv=pltpu.SemaphoreType.DMA((8,)),
    swap_local=pltpu.SemaphoreType.DMA((5,)),
    swap_send=pltpu.SemaphoreType.DMA((5,)),
    swap_recv=pltpu.SemaphoreType.DMA((5,)),
    plane_sems=pltpu.SemaphoreType.DMA((2, 7, 2, 8)),
    pool_sems=pltpu.SemaphoreType.DMA((3, 16)),
)
INPUTS = names(slots=0, lead_steps=0, flags=0, masters=0, rows_in=0, first_in=0, second_in=0, vectors=0)
OUTPUTS = names(left_pool=0, right_pool=0, pred_one_out=0, pred_two_out=0, input_grad=0, rows=0)


def model_kernel(*refs):
    r = Refs()
    for name, ref in zip(INPUTS + OUTPUTS + tuple(SCRATCH), refs):
        setattr(r, name, ref)
    for name in ("held", "turned", "stats"):
        setattr(r, name, [getattr(r, name).at[layer] for layer in range(2)])
    r.in_sems = [r.plane_sems.at[layer, pl.ds(0, 3)] for layer in range(2)]
    for at, name in enumerate(("o_sems", "do_sems", "dq_sems", "dkv_sems")):
        setattr(r, name, [r.plane_sems.at[layer, 3 + at] for layer in range(2)])
    swaps = [Swap(r.swap_local, r.swap_send, r.swap_recv, at) for at in range(5)]
    r.swap_rows = swaps[0]
    r.plane = Plane()
    vecs = r.vectors
    weights = Weights(r.slots, r.weights)

    def while_last():
        swaps[0].finish()
        r.rows[...] = jnp.zeros_like(r.rows)
        for layer in range(2):
            r.stats[layer][...] = jnp.zeros((8, SEQ_ALL), FULL)

    lane = lax.broadcasted_iota(jnp.int32, (1, TOKENS), 1)
    r.notes[...] = jnp.zeros_like(r.notes)
    r.notes[0:1] = r.flags[...].astype(FULL) - 1.0
    for at in range(2):
        r.notes[1:2] += jnp.where(lane == at, r.lead_steps[at, 0].astype(FULL), 0.0)
    gather_blocks(r, r.notes, while_last)
    mask_columns(r.notes_land, r.neg)
    leads = [r.notes_land[0, 1:2, at : at + 1] for at in range(2)]
    r.hidden_one[...] = r.rows_land[0].astype(FULL) + lead_row(vecs, leads[0])
    project(r, 0, r.hidden_one[...], vecs, weights)
    attend(r, 0)
    swaps[1].start(r.second_in, r.second_land)
    middle, result = feed(r, 0, r.hidden_one[...], vecs, weights, r.slope_one)
    r.middle_one[...] = middle
    r.pred_one[0] = result.astype(LOW)
    r.hidden_two[...] = result + lead_row(vecs, leads[1])
    project(r, 1, r.hidden_two[...], vecs, weights)
    attend(r, 1)
    swaps[3].start(r.pred_one, r.pred_one_out)
    middle, result = feed(r, 1, r.hidden_two[...], vecs, weights, r.slope_two)
    r.pred_two[0] = result.astype(LOW)
    swaps[2].start(r.first_in, r.first_land)
    swaps[1].finish()
    grad_middle = feed_back(r, 1, r.second_land[0].astype(FULL), middle, r.slope_two, vecs, weights)
    attend_back(r, 1)
    grad = project_back(r, 1, grad_middle, r.hidden_two[...], vecs, weights, leads[1])
    for source, sems in ((r.do_message, r.do_sems), (r.dkv_message, r.dkv_sems), (r.dq_message, r.dq_sems)):
        r.plane.sent(source, sems[1])
    swaps[2].finish()
    swaps[4].start(r.pred_two, r.pred_two_out)
    grad = grad + r.first_land[0].astype(FULL)
    grad_middle = feed_back(r, 0, grad, r.middle_one[...], r.slope_one, vecs, weights)
    attend_back(r, 0)
    grad = project_back(r, 0, grad_middle, r.hidden_one[...], vecs, weights, leads[0])
    r.input_grad[0] = grad.astype(LOW)
    for source, sems in ((r.do_message, r.do_sems), (r.dkv_message, r.dkv_sems), (r.dq_message, r.dq_sems)):
        r.plane.sent(source, sems[0])
    for left in (True, False):
        for layer in range(2):
            for kind in range(4):
                for copy in pool_copies(r, left, layer, kind):
                    copy.wait()
    swaps[3].finish()
    swaps[4].finish()


def model(slots, lead_steps, flags, masters, rows, first, second, vectors):
    return pl.pallas_call(
        model_kernel,
        out_shape=(
            shape((N_LEFT, BS, 4 * TOKENS)),
            shape((N_RIGHT, 4 * TOKENS, BS)),
            SHAPES["pred"],
            SHAPES["pred"],
            SHAPES["pred"],
            SHAPES["rows"],
        ),
        in_specs=[SMEM_IN] * 2 + [VMEM_AT] + [ANY_AT] * 4 + [VMEM_AT],
        out_specs=(ANY_AT,) * 4 + (VMEM_AT,) * 2,
        scratch_shapes=list(SCRATCH.values()),
        compiler_params=pltpu.CompilerParams(
            collective_id=0, has_side_effects=True, vmem_limit_bytes=63 * 1024 * 1024
        ),
        cost_estimate=pl.CostEstimate(flops=24 << 30, bytes_accessed=60 << 20, transcendentals=1 << 23),
        name="model",
    )(slots, lead_steps, flags, masters, rows, first, second, vectors)


SMEM_IN = pl.BlockSpec(memory_space=pltpu.SMEM)
VMEM_AT = pl.BlockSpec(memory_space=pltpu.VMEM)
ANY_AT = pl.BlockSpec(memory_space=pl.ANY)


def shape(dims, kind=LOW):
    return jax.ShapeDtypeStruct(dims, kind)


SHAPES = {"pred": shape((1, TOKENS, D)), "rows": shape((20, D), FULL)}


def bias_pieces():
    left = masked
    pieces = []
    for unused in range(3):
        piece = float(ml_dtypes.bfloat16(left))
        pieces.append(piece)
        left -= piece
    assert left == 0.0
    return pieces


MASK_PIECES = bias_pieces()


def own_columns(like, head):
    lane = lax.broadcasted_iota(jnp.int32, like.shape, 1)
    return (lane < HD) if head == 0 else (lane >= HD), lane - (HD if head == 0 else 0)


def key_columns(keys, neg, head):
    own, spot = own_columns(keys, head)
    side = jnp.zeros_like(keys)
    for at, piece in enumerate(MASK_PIECES):
        side = jnp.where(spot == at, neg * piece, side)
    return jnp.where(own, keys, side)


def query_columns(queries, head):
    own, spot = own_columns(queries, head)
    return jnp.where(own, queries * HD**-0.5, jnp.where((spot >= 0) & (spot < 3), 1.0, 0.0))


class Plane:
    def __init__(self):
        x, c, z, y = place()
        self.z = z
        self.me = 4 * c + 2 * x + y

    def device(self, j):
        return (turned_pair(lax.div(j, 2)), 2 * self.z + lax.rem(j, 2))

    def other(self, step):
        return lax.rem(self.me + step, 8)

    def others(self):
        return [self.device(self.other(step)) for step in range(1, 8)]

    def copy(self, src, dst, sems, send_at, recv_at, to):
        return pltpu.make_async_remote_copy(
            src_ref=src, dst_ref=dst, send_sem=sems.at[0, send_at], recv_sem=sems.at[1, recv_at],
            device_id=self.device(to), device_id_type=MESH,
        )

    def send(self, source, target, sems, to):
        self.copy(source.at[to], target.at[self.me], sems, to, self.me, to).start()

    def send_or_keep(self, source, target, sems, to):
        @pl.when(to != self.me)
        def away():
            self.send(source, target, sems, to)

        @pl.when(to == self.me)
        def keep():
            target[to] = source[to]

    def received(self, target, sems):
        for step in range(1, 8):
            j = self.other(step)
            self.copy(target.at[j], target.at[j], sems, j, j, j).wait_recv()

    def received_from(self, target, sems, j):
        @pl.when(j != self.me)
        def arrived():
            self.copy(target.at[j], target.at[j], sems, j, j, j).wait_recv()

    def sent(self, source, sems):
        for step in range(1, 8):
            j = self.other(step)
            self.copy(source.at[j], source.at[j], sems, j, j, j).wait_send()


def mask_columns(notes, neg):
    for j in range(8):
        neg[j * TOKENS : (j + 1) * TOKENS] = jnp.broadcast_to(notes[j, 0:1], (TOKENS, TOKENS)).T


LEFTS = (WIDE, WIDE, WIDE, DEEP)
RIGHTS = (3 * WIDE, WIDE, DEEP, WIDE)
LEFT_AT = (0, WIDE, 2 * WIDE, 3 * WIDE)
RIGHT_AT = (0, 3 * WIDE, 4 * WIDE, 4 * WIDE + DEEP)
N_LEFT = 3 * WIDE + DEEP
N_RIGHT = 5 * WIDE + DEEP


def pools_of(block):
    left = jnp.zeros_like(block)
    right = jnp.zeros_like(block)
    for at, base in enumerate((QKV_AT, OUT_AT, UP_AT, DOWN_AT)):
        inside = block >= base
        cols = RIGHTS[at]
        left = jnp.where(inside, LEFT_AT[at] + (block - base) // cols, left)
        right = jnp.where(inside, RIGHT_AT[at] + (block - base) % cols, right)
    return left, right


def halves(value):
    high = value.astype(LOW)
    return high, (value - high.astype(FULL)).astype(LOW)


def fine(left, right):
    return dot(
        jnp.concatenate([left[0], left[1], left[0]], axis=1),
        jnp.concatenate([right[0], right[0], right[1]], axis=0),
    )


def statistic(gram, shrink, diag, eye):
    return jnp.where(eye, 0.5 * diag, 0.0) + shrink * gram


def roots(stats, eye):
    scales = [jnp.sqrt(jnp.sum(jnp.sum(stat * stat, axis=1, keepdims=True), axis=0, keepdims=True)) for stat in stats]
    moving = [stat / scale for stat, scale in zip(stats, scales)]
    approx = [None] * len(stats)
    ahead = range(len(stats))
    for iteration in range(ITERS):
        factors = [(jnp.where(eye, 5.0, 0.0) - moving[i]) * 0.25 for i in ahead]
        parts = [halves(factor) for factor in factors]
        if iteration == 0:
            approx = [factors[i] * lax.rsqrt(jnp.sqrt(scales[i])) for i in ahead]
        else:
            approx = [fine(halves(approx[i]), parts[i]) for i in ahead]
        if iteration < ITERS - 1:
            squares = [halves(fine(parts[i], parts[i])) for i in ahead]
            fourths = [halves(fine(squares[i], squares[i])) for i in ahead]
            moving = [fine(fourths[i], halves(moving[i])) for i in ahead]
    return approx


PAIRED = 2
SUM_SCRATCH = dict(
    left_t=pltpu.VMEM((N_LEFT, BS, 4 * TOKENS), LOW),
    right_pool=pltpu.VMEM((N_RIGHT, 4 * TOKENS, BS), LOW),
    x_stage=pltpu.VMEM((2, 2, 4, PAIRED, BS, BS), LOW),
    x_land=pltpu.VMEM((2, 2, 4, PAIRED, BS, BS), LOW),
    yb_stage=pltpu.VMEM((4, QUART, BS, BS), LOW),
    yb_land=pltpu.VMEM((4, QUART, BS, BS), LOW),
    ym_stage=pltpu.VMEM((2, 4, PAIRED, BS, BS), LOW),
    ym_land=pltpu.VMEM((2, 4, PAIRED, BS, BS), LOW),
    zb_stage=pltpu.VMEM((4, QUART, BS, BS), LOW),
    zb_land=pltpu.VMEM((3, QUART, BS, BS), LOW),
    zm_stage=pltpu.VMEM((2, 4, PAIRED, BS, BS), LOW),
    zm_land=pltpu.VMEM((2, 3, PAIRED, BS, BS), LOW),
    both_stage=pltpu.VMEM((2, PAIRED, BS, BS), LOW),
    both_land=pltpu.VMEM((PAIRED, BS, BS), LOW),
    own=pltpu.VMEM((6, BS, BS), LOW),
    staged=pltpu.VMEM((6, BS, BS), LOW),
    pair_rows=pltpu.VMEM((20, D), FULL),
    chip_rows=pltpu.VMEM((20, D), FULL),
    plane_rows=pltpu.VMEM((20, D), FULL),
    row_land=pltpu.VMEM((3, 20, D), FULL),
    row_z=pltpu.VMEM((4, 20, D), FULL),
    pool_sems=pltpu.SemaphoreType.DMA((2,)),
    send_sems=pltpu.SemaphoreType.DMA((11, 4)),
    recv_sems=pltpu.SemaphoreType.DMA((11, 4)),
    row_send=pltpu.SemaphoreType.DMA((6,)),
    row_recv=pltpu.SemaphoreType.DMA((6,)),
    share_send=pltpu.SemaphoreType.DMA((6, 6)),
    share_recv=pltpu.SemaphoreType.DMA((6, 6)),
    local_sems=pltpu.SemaphoreType.DMA((9,)),
    swap_local=pltpu.SemaphoreType.DMA((1,)),
    swap_send=pltpu.SemaphoreType.DMA((1,)),
    swap_recv=pltpu.SemaphoreType.DMA((1,)),
)
SUM_INPUTS = names(left_ids=0, right_ids=0, rows_in=0, left_diag=0, right_diag=0, grad_in=0, left_in=0, right_in=0)
SUM_OUTPUTS = names(rows_out=0, grads_out=0, moves_out=0, grad_out=0)


def update_kernel(*refs):
    r = Refs()
    for name, ref in zip(SUM_INPUTS + SUM_OUTPUTS + tuple(SUM_SCRATCH), refs):
        setattr(r, name, ref)
    here = [
        pltpu.make_async_copy(r.right_in, r.right_pool, r.pool_sems.at[0]),
        pltpu.make_async_copy(r.left_in, r.left_t, r.pool_sems.at[1]),
    ]
    for copy in here:
        copy.start()
    x, c, z, y = place()
    samp = 2 * x + c
    blk = 2 * z + y
    to_c = (2 * x + 1 - c, blk)
    to_x = (2 * (1 - x) + c, blk)
    to_y = (samp, 2 * z + 1 - y)
    to_z = [(samp, 2 * lax.rem(z + step, 4) + y) for step in (1, 2, 3)]
    meet_all()
    swap = Swap(r.swap_local, r.swap_send, r.swap_recv)
    swap.start(r.grad_in, r.grad_out)
    row_copies = [push(r.rows_in, r.row_land.at[0], r.row_send.at[0], r.row_recv.at[0], to_c)]
    eye = lax.broadcasted_iota(jnp.int32, (BS, BS), 0) == lax.broadcasted_iota(jnp.int32, (BS, BS), 1)

    def group(half, k):
        return 2 * lax.rem(z + 1 + k, 4) + (1 - y if half == 0 else y)

    def part(half, k, offset, count=PAIRED):
        slot = group(half, k) * GROUP + c * HALF + offset
        return [dot(r.left_t[r.left_ids[slot + i]], r.right_pool[r.right_ids[slot + i]]) for i in range(count)]

    def mine(batch):
        return x * 8 + PAIRED * batch

    def other(batch):
        return (1 - x) * 8 + PAIRED * batch

    both = QUART

    def link(kind, k, stage, land, to):
        return pltpu.make_async_remote_copy(
            src_ref=stage, dst_ref=land, send_sem=r.send_sems.at[kind, k], recv_sem=r.recv_sems.at[kind, k],
            device_id=to, device_id_type=MESH,
        )

    def along_x(batch, half, k):
        return link(2 * batch + half, k, r.x_stage.at[batch, half, k], r.x_land.at[batch, half, k], to_x)

    def along_y_both(k):
        return link(4, k, r.yb_stage.at[k], r.yb_land.at[k], to_y)

    def along_y(batch, k):
        return link(5 + batch, k, r.ym_stage.at[batch, k], r.ym_land.at[batch, k], to_y)

    def along_z_both(k):
        return link(7, k, r.zb_stage.at[k], r.zb_land.at[k], (samp, group(1, k)))

    def along_z(batch, k):
        return link(8 + batch, k, r.zm_stage.at[batch, k], r.zm_land.at[batch, k], (samp, group(1, k)))

    def last():
        return link(10, 0, r.both_stage.at[1 - x], r.both_land, to_x)

    def send_x(batch, half, k):
        for i, value in enumerate(part(half, k, other(batch))):
            r.x_stage[batch, half, k, i] = value.astype(LOW)
        along_x(batch, half, k).start()

    def add_x_send_y(batch, k):
        values = part(0, k, mine(batch))
        along_x(batch, 0, k).wait_recv()
        for i, value in enumerate(values):
            r.ym_stage[batch, k, i] = (value + r.x_land[batch, 0, k, i].astype(FULL)).astype(LOW)
        along_y(batch, k).start()

    def add_both_send_z(batch, k):
        values = part(1, k, mine(batch))
        along_x(batch, 1, k).wait_recv()
        values = [value + r.x_land[batch, 1, k, i].astype(FULL) for i, value in enumerate(values)]
        along_y(batch, k).wait_recv()
        for i, value in enumerate(values):
            r.zm_stage[batch, k, i] = (value + r.ym_land[batch, k, i].astype(FULL)).astype(LOW)

        @pl.when(k < 3)
        def send_on():
            along_z(batch, k).start()

    def each(step):
        def body(k, carry):
            step(k)
            return carry

        lax.fori_loop(0, 4, body, 0)

    def slot_of(i, far=False):
        side = (1 - x) if far else x
        return c * HALF + (side * 8 + i if i < QUART else QUART + 2 * side + i - QUART)

    def share(kind, k, src, dst, to):
        return pltpu.make_async_remote_copy(
            src_ref=src, dst_ref=dst, send_sem=r.share_send.at[kind, k], recv_sem=r.share_recv.at[kind, k],
            device_id=to, device_id_type=MESH,
        )

    def grad_to(kind, pair, to):
        place_out = r.grads_out.at[pl.ds(slot_of(PAIRED * pair), PAIRED)]
        return share(kind, pair, r.own.at[pl.ds(PAIRED * pair, PAIRED)], place_out, to)

    def grad_on(pair):
        place_out = r.grads_out.at[pl.ds(slot_of(PAIRED * pair, True), PAIRED)]
        return share(2, pair, place_out, place_out, to_c)

    def grad_kept(pair):
        place_out = r.grads_out.at[pl.ds(slot_of(PAIRED * pair), PAIRED)]
        return pltpu.make_async_copy(r.own.at[pl.ds(PAIRED * pair, PAIRED)], place_out, r.local_sems.at[6 + pair])

    def move_to(kind, i, to):
        return share(kind, i, r.staged.at[i], r.moves_out.at[slot_of(i)], to)

    def move_on(i):
        place_out = r.moves_out.at[slot_of(i, True)]
        return share(5, i, place_out, place_out, to_c)

    def move_kept(i):
        return pltpu.make_async_copy(r.staged.at[i], r.moves_out.at[slot_of(i)], r.local_sems.at[i])

    def share_grads(pair):
        grad_to(0, pair, to_x).start()
        grad_to(1, pair, to_c).start()
        grad_kept(pair).start()

    def directions(pair):
        held = []
        stats = []
        for i in range(PAIRED * pair, PAIRED * pair + PAIRED):
            low = r.own[i]
            grad = low.astype(FULL)
            mean = jnp.sum(jnp.sum(grad * grad, axis=1, keepdims=True), axis=0, keepdims=True) / (BS * BS)
            shrink = 0.5 / (mean + 1e-06)
            low_t = grad.T.astype(LOW)
            slot = slot_of(i)
            stats.append(statistic(dot(low, low_t), shrink, r.left_diag[pl.ds(slot, 1)], eye))
            stats.append(statistic(dot(low_t, low), shrink, r.right_diag[pl.ds(slot, 1)], eye))
            held.append((i, low, lax.rsqrt(mean + 1e-06)))
        sides = roots(stats, eye)
        for n, (i, low, rate) in enumerate(held):
            high, rest = halves(sides[2 * n])
            turned = dot(jnp.concatenate([high, rest], axis=1), jnp.concatenate([low, low], axis=0)) * rate
            r.staged[i] = fine(halves(turned), halves(sides[2 * n + 1])).astype(LOW)
            move_to(3, i, to_x).start()
            move_to(4, i, to_c).start()
            move_kept(i).start()

    def finish_batch(batch):
        for k in range(3):
            along_z(batch, k).wait_recv()
        for i in range(PAIRED):
            value = r.zm_stage[batch, 3, i].astype(FULL)
            for k in range(3):
                value = value + r.zm_land[batch, k, i].astype(FULL)
            r.own[PAIRED * batch + i] = value.astype(LOW)
        share_grads(batch)

    def pass_on(pair):
        grad_to(0, pair, to_x).wait_recv()
        grad_on(pair).start()
        for i in range(PAIRED * pair, PAIRED * pair + PAIRED):
            move_to(3, i, to_x).wait_recv()
            move_on(i).start()

    for copy in here:
        copy.wait()

    @each
    def begin(k):
        send_x(0, 0, k)

    @each
    def begin_both(k):
        for i, value in enumerate(part(0, k, both, QUART)):
            r.yb_stage[k, i] = value.astype(LOW)
        along_y_both(k).start()
        send_x(1, 0, k)

    @each
    def more(k):
        send_x(0, 1, k)

    row_copies[0].wait_recv()
    r.pair_rows[...] = r.rows_in[...] + r.row_land[0]
    row_copies.append(push(r.pair_rows, r.row_land.at[1], r.row_send.at[1], r.row_recv.at[1], to_x))

    @each
    def middle(k):
        add_x_send_y(0, k)
        values = part(1, k, both, QUART)
        along_y_both(k).wait_recv()
        for i, value in enumerate(values):
            r.zb_stage[k, i] = (value + r.yb_land[k, i].astype(FULL)).astype(LOW)

        @pl.when(k < 3)
        def send_on():
            along_z_both(k).start()

    row_copies[1].wait_recv()
    r.chip_rows[...] = r.pair_rows[...] + r.row_land[1]
    row_copies.append(push(r.chip_rows, r.row_land.at[2], r.row_send.at[2], r.row_recv.at[2], to_y))
    for k in range(3):
        along_z_both(k).wait_recv()
    for i in range(QUART):
        value = r.zb_stage[3, i].astype(FULL)
        for k in range(3):
            value = value + r.zb_land[k, i].astype(FULL)
        r.both_stage[i // 2, i % 2] = value.astype(LOW)
    last().start()

    @each
    def middle_again(k):
        add_x_send_y(1, k)

    @each
    def late(k):
        add_both_send_z(0, k)

    @each
    def more_again(k):
        send_x(1, 1, k)

    row_copies[2].wait_recv()
    r.plane_rows[...] = r.chip_rows[...] + r.row_land[2]
    for step in range(3):
        row_copies.append(
            push(r.plane_rows, r.row_z.at[z], r.row_send.at[3 + step], r.row_recv.at[3 + step], to_z[step])
        )
    r.row_z[z] = r.plane_rows[...]
    last().wait_recv()
    for i in range(PAIRED):
        r.own[QUART + i] = (r.both_stage[x, i].astype(FULL) + r.both_land[i].astype(FULL)).astype(LOW)
    share_grads(2)
    directions(2)
    finish_batch(0)

    @each
    def late_again(k):
        add_both_send_z(1, k)

    directions(0)
    for step in range(3):
        row_copies[3 + step].wait_recv()
    r.rows_out[...] = (r.row_z[0] + r.row_z[1]) + (r.row_z[2] + r.row_z[3])
    finish_batch(1)
    pass_on(2)
    directions(1)
    pass_on(0)
    pass_on(1)
    for pair in range(3):
        grad_to(1, pair, to_c).wait_recv()
        grad_on(pair).wait_recv()
        grad_to(0, pair, to_x).wait_send()
        grad_to(1, pair, to_c).wait_send()
        grad_on(pair).wait_send()
        grad_kept(pair).wait()
    for i in range(6):
        move_to(4, i, to_c).wait_recv()
        move_on(i).wait_recv()
        move_to(3, i, to_x).wait_send()
        move_to(4, i, to_c).wait_send()
        move_on(i).wait_send()
        move_kept(i).wait()
    for copy in row_copies:
        copy.wait_send()
    last().wait_send()

    @each
    def drain(k):
        along_y_both(k).wait_send()
        for batch in range(2):
            along_x(batch, 0, k).wait_send()
            along_x(batch, 1, k).wait_send()
            along_y(batch, k).wait_send()

        @pl.when(k < 3)
        def sent_on():
            along_z_both(k).wait_send()
            for batch in range(2):
                along_z(batch, k).wait_send()

    swap.finish()


def update(left_ids, right_ids, rows, left_start, right_start, grad, left_pool, right_pool):
    return pl.pallas_call(
        update_kernel,
        out_shape=(SHAPES["rows"], shape((GROUP, BS, BS)), shape((GROUP, BS, BS)), SHAPES["pred"]),
        in_specs=[SMEM_IN] * 2 + [VMEM_AT] * 3 + [ANY_AT] * 3,
        out_specs=(VMEM_AT,) + (ANY_AT,) * 3,
        scratch_shapes=list(SUM_SCRATCH.values()),
        compiler_params=pltpu.CompilerParams(
            collective_id=1, has_side_effects=True, vmem_limit_bytes=VMEM_ASK
        ),
        cost_estimate=pl.CostEstimate(flops=36 << 30, bytes_accessed=40 << 20, transcendentals=0),
        name="update",
    )(left_ids, right_ids, rows, left_start, right_start, grad, left_pool, right_pool)


STEP = 8


def finish_kernel(
    grad, move, weight, left_diag, right_diag, rows, vecs, moment, input_grad, pred_one, pred_two,
    grad_out, left_out, right_out, new_out, low_out,
    rows_out, moment_out, vecs_out, input_out, pred_one_out, pred_two_out,
):
    eye = lax.broadcasted_iota(jnp.int32, (BS, BS), 0) == lax.broadcasted_iota(jnp.int32, (BS, BS), 1)
    at = pl.program_id(0)

    def mean(value):
        return jnp.sum(jnp.sum(value, axis=1, keepdims=True), axis=0, keepdims=True) / (BS * BS)

    for i in range(STEP):
        low = grad[i]
        full = low.astype(FULL)
        grad_out[i] = full
        shrink = 0.5 / (mean(full * full) + 1e-06)
        low_t = full.T.astype(LOW)
        left_out[i] = statistic(dot(low, low_t), shrink, left_diag[pl.ds(at * STEP + i, 1)], eye)
        right_out[i] = statistic(dot(low_t, low), shrink, right_diag[pl.ds(at * STEP + i, 1)], eye)
        step = move[i].astype(FULL)
        start = weight[i]
        ratio = jnp.sqrt(mean(start * start)) * lax.rsqrt(mean(step * step) + 1e-06)
        new = start - step_rate * ratio * step
        new_out[i] = new
        low_out[i] = new.astype(LOW)

    @pl.when(at == 0)
    def small():
        value = rows[...]
        scaled = value * lax.rsqrt(jnp.mean(value * value, axis=1, keepdims=True) + 1e-06)
        moments = 0.5 * moment[...] + 0.5 * scaled * scaled
        rows_out[...] = value
        moment_out[...] = moments
        vecs_out[...] = vecs[...] - vector_rate * scaled * lax.rsqrt(moments)
        input_out[...] = input_grad[...].astype(FULL)
        pred_one_out[...] = pred_one[...]
        pred_two_out[...] = pred_two[...]


def finish_slots(grads, moves, masters, left_start, right_start, rows, vecs, moment, input_grad, pred_one, pred_two):
    block = pl.BlockSpec((STEP, BS, BS), lambda i: (i, 0, 0))
    diag = pl.BlockSpec((GROUP, BS), lambda i: (0, 0))
    row = pl.BlockSpec((20, D), lambda i: (0, 0))
    wide = pl.BlockSpec((1, TOKENS, D), lambda i: (0, 0, 0))
    return pl.pallas_call(
        finish_kernel,
        grid=(GROUP // STEP,),
        compiler_params=pltpu.CompilerParams(vmem_limit_bytes=VMEM_ASK),
        out_shape=tuple(shape((GROUP, BS, BS), kind) for kind in (FULL, FULL, FULL, FULL, LOW))
        + (SHAPES["rows"],) * 3
        + (shape((1, TOKENS, D), FULL),)
        + (SHAPES["pred"],) * 2,
        in_specs=[block, block, block, diag, diag, row, row, row, wide, wide, wide],
        out_specs=(block,) * 5 + (row,) * 3 + (wide,) * 3,
        cost_estimate=pl.CostEstimate(flops=2 << 30, bytes_accessed=41 << 20, transcendentals=0),
        name="finish_slots",
    )(grads, moves, masters, left_start, right_start, rows, vecs, moment, input_grad, pred_one, pred_two)


def local_tuned(
    inputs,
    cot_first,
    cot_second,
    valid_flags,
    lead_steps,
    masters,
    assignment,
    left_start,
    right_start,
    vectors,
    vec_moment,
):
    left_pool, right_pool, pred_one, pred_two, input_grad, rows = model(
        assignment, lead_steps, valid_flags, masters, inputs, cot_first, cot_second, vectors
    )
    position = jnp.arange(NB, dtype=jnp.int32)
    inverse = jnp.sum(
        jnp.where(assignment[None, :] == position[:, None], position[None, :], 0), axis=1
    )
    left_ids, right_ids = pools_of(inverse)
    vec_grads, grads, moves, input_grad = update(
        left_ids, right_ids, rows, left_start, right_start, input_grad, left_pool, right_pool
    )
    (
        matrix_grads, left_stats, right_stats, new_masters, new_copies,
        vec_grads, vec_moments, new_vectors, input_grad, pred_one, pred_two,
    ) = finish_slots(
        grads, moves, masters, left_start, right_start, vec_grads, vectors, vec_moment, input_grad, pred_one, pred_two
    )
    return (
        pred_one,
        pred_two,
        input_grad,
        matrix_grads,
        left_stats,
        right_stats,
        new_masters,
        new_copies,
        vec_grads,
        vec_moments,
        new_vectors,
    )


def solution(mesh):
    placed = (
        P("samp", "blk", None),
        P("samp", "blk", None),
        P("samp", "blk", None),
        P("samp", "blk"),
        P(None, "samp"),
        P("blk", None, None),
        P(),
        P("blk", None),
        P("blk", None),
        P(),
        P(),
    )
    fits = mesh.shape["samp"] == 4 and mesh.shape["blk"] == 8
    return jax.shard_map(
        local_tuned if fits else local_any,
        mesh=mesh,
        in_specs=placed,
        out_specs=(
            P("samp", "blk", None),
            P("samp", "blk", None),
            P("samp", "blk", None),
            P("blk", None, None),
            P("blk", None, None),
            P("blk", None, None),
            P("blk", None, None),
            P("blk", None, None),
            P(),
            P(),
            P(),
        ),
        check_vma=False,
    )
```

```python
import functools
import math

import jax
import ml_dtypes
import jax.numpy as jnp
from jax import lax
from jax.experimental import pallas as pl
from jax.experimental.pallas import tpu as pltpu
from jax.sharding import PartitionSpec as P

D = 1024
HEADS = 16
FF = 4096
HD = 64
LEADS = 8
BS = 256
ITERS = 6
NB = 192


HIGH = lax.Precision.HIGHEST
step_rate = 0.5
vector_rate = 0.3
masked = 1000000000.0


def assemble(blocks, height, breadth):
    return (
        blocks.reshape(height // BS, breadth // BS, BS, BS)
        .transpose(0, 2, 1, 3)
        .reshape(height, breadth)
    )


def carve(matrix):
    height, breadth = matrix.shape
    return (
        matrix.reshape(height // BS, BS, breadth // BS, BS)
        .transpose(0, 2, 1, 3)
        .reshape(-1, BS, BS)
    )


def unpack(blocks):
    first_end = 3 * D * D // (BS * BS)
    second_end = first_end + D * D // (BS * BS)
    third_end = second_end + D * FF // (BS * BS)
    qkv_weight = assemble(blocks[:first_end], D, 3 * D)
    out_weight = assemble(blocks[first_end:second_end], D, D)
    up_weight = assemble(blocks[second_end:third_end], D, FF)
    down_weight = assemble(blocks[third_end:], FF, D)
    return (qkv_weight, out_weight, up_weight, down_weight)


def norm_layer(value, gain, shift):
    centred = value - jnp.mean(value, axis=-1, keepdims=True)
    spread = jnp.mean(centred * centred, axis=-1, keepdims=True)
    return centred * lax.rsqrt(spread + 1e-06) * gain + shift


def gelu_exact(value):
    return jax.nn.gelu(value, approximate=False)


def heads_of(tensor):
    return tensor.reshape(tensor.shape[0], tensor.shape[1], HEADS, HD)


def split_rows(member, count, width):
    shaped = member.reshape((member.shape[0], count, width) + member.shape[2:])
    return jnp.moveaxis(shaped, 1, 0)


def in_blocks(update, carry, members, length):
    width = math.gcd(length, 1024)
    count = length // width
    if count == 1:
        return update(carry, members, 0)
    stacked = tuple([split_rows(member, count, width) for member in members])
    offsets = jnp.arange(count, dtype=jnp.int32) * width

    def advance(state, item):
        return (update(state, item[0], item[1]), None)

    result, unused = lax.scan(advance, carry, (stacked, offsets))
    return result


def forward_update(query_heads, scaling):

    def update(carry, members, offset):
        running_max, running_sum, weighted = carry
        key_part, value_part, flag_part = members
        bias = (flag_part.astype(jnp.float32) - 1.0) * masked
        scores = (
            jnp.einsum(
                "sqhd,skhd->shqk",
                query_heads,
                heads_of(key_part),
                preferred_element_type=jnp.float32,
            )
            * scaling
            + bias[:, None, None, :]
        )
        new_max = jnp.maximum(running_max, jnp.max(scores, axis=-1))
        shrink = jnp.exp(running_max - new_max)
        expos = jnp.exp(scores - new_max[..., None])
        running_sum = running_sum * shrink + jnp.sum(expos, axis=-1)
        weighted = weighted * shrink[..., None] + jnp.einsum(
            "shqk,skhd->shqd",
            expos.astype(jnp.bfloat16),
            heads_of(value_part),
            preferred_element_type=jnp.float32,
        )
        return (new_max, running_sum, weighted)

    return update


def query_grad_update(query_heads, dout_heads, log_total, inner, scaling):

    def update(carry, members, offset):
        key_part, value_part, flag_part = members
        bias = (flag_part.astype(jnp.float32) - 1.0) * masked
        scores = (
            jnp.einsum(
                "sqhd,skhd->shqk",
                query_heads,
                heads_of(key_part),
                preferred_element_type=jnp.float32,
            )
            * scaling
            + bias[:, None, None, :]
        )
        probs = jnp.exp(scores - log_total[..., None])
        dprobs = jnp.einsum(
            "sqhd,skhd->shqk", dout_heads, heads_of(value_part), preferred_element_type=jnp.float32
        )
        dscores = (probs * (dprobs - inner[..., None])).astype(jnp.bfloat16)
        return (
            carry
            + jnp.einsum(
                "shqk,skhd->sqhd", dscores, heads_of(key_part), preferred_element_type=jnp.float32
            )
            * scaling
        )

    return update


def key_grad_update(key_heads, value_heads, key_bias, total_rows, inner_rows, scaling, anchor):

    def update(carry, members, offset):
        grad_keys, grad_values = carry
        query_part, dout_part = members
        length = query_part.shape[1]
        total_part = jnp.transpose(
            lax.dynamic_slice_in_dim(total_rows, anchor + offset, length, 1), (0, 2, 1)
        )
        inner_part = jnp.transpose(
            lax.dynamic_slice_in_dim(inner_rows, anchor + offset, length, 1), (0, 2, 1)
        )
        query_heads = heads_of(query_part)
        dout_heads = heads_of(dout_part)
        scores = (
            jnp.einsum(
                "sqhd,skhd->shqk", query_heads, key_heads, preferred_element_type=jnp.float32
            )
            * scaling
            + key_bias[:, None, None, :]
        )
        probs = jnp.exp(scores - total_part[..., None])
        dprobs = jnp.einsum(
            "sqhd,skhd->shqk", dout_heads, value_heads, preferred_element_type=jnp.float32
        )
        dscores = (probs * (dprobs - inner_part[..., None])).astype(jnp.bfloat16)
        grad_values = grad_values + jnp.einsum(
            "shqk,sqhd->skhd",
            probs.astype(jnp.bfloat16),
            dout_heads,
            preferred_element_type=jnp.float32,
        )
        grad_keys = (
            grad_keys
            + jnp.einsum(
                "shqk,sqhd->skhd", dscores, query_heads, preferred_element_type=jnp.float32
            )
            * scaling
        )
        return (grad_keys, grad_values)

    return update


def invert_root(stat):
    identity = jnp.eye(stat.shape[0], dtype=jnp.float32)
    frobenius = jnp.sqrt(jnp.sum(stat * stat))
    approx = identity * lax.rsqrt(jnp.sqrt(frobenius))
    moving = stat / frobenius
    for iteration in range(ITERS):
        factor = (5.0 * identity - moving) * 0.25
        approx = jnp.dot(approx, factor, precision=HIGH)
        square = jnp.dot(factor, factor, precision=HIGH)
        moving = jnp.dot(jnp.dot(square, square, precision=HIGH), moving, precision=HIGH)
    return approx


def precondition(gradient, left_diag, right_diag, weight):
    scaled = gradient * lax.rsqrt(jnp.mean(gradient * gradient) + 1e-06)
    identity = jnp.eye(BS, dtype=jnp.float32)
    left_new = 0.5 * identity * left_diag[None, :] + 0.5 * jnp.dot(scaled, scaled.T, precision=HIGH)
    right_new = 0.5 * identity * right_diag[None, :] + 0.5 * jnp.dot(
        scaled.T, scaled, precision=HIGH
    )
    direction = jnp.dot(
        jnp.dot(invert_root(left_new), scaled, precision=HIGH),
        invert_root(right_new),
        precision=HIGH,
    )
    ratio = jnp.sqrt(jnp.mean(weight * weight)) * lax.rsqrt(jnp.mean(direction * direction) + 1e-06)
    return (left_new, right_new, weight - step_rate * ratio * direction)


MESH = pl.DeviceIdType.MESH
LOW = jnp.bfloat16
FULL = jnp.float32
VMEM_ASK = 60 * 1024 * 1024
GROUP = 24
HALF = 12
QUART = 4


def place():
    samp = lax.axis_index("samp")
    blk = lax.axis_index("blk")
    return (lax.div(samp, 2), lax.rem(samp, 2), lax.div(blk, 2), lax.rem(blk, 2))


def meet(devices):
    barrier = pltpu.get_barrier_semaphore()
    for device in devices:
        pl.semaphore_signal(barrier, inc=1, device_id=device, device_id_type=MESH)
    pl.semaphore_wait(barrier, len(devices))


def meet_all():
    barrier = pltpu.get_barrier_semaphore()
    samp = lax.axis_index("samp")
    blk = lax.axis_index("blk")

    def tell(at, carry):
        to = lax.rem(samp * 8 + blk + at, 32)
        pl.semaphore_signal(
            barrier, inc=1, device_id=(lax.div(to, 8), lax.rem(to, 8)), device_id_type=MESH
        )
        return carry

    lax.fori_loop(1, 32, tell, 0)
    pl.semaphore_wait(barrier, 31)


def turned_pair(n):
    return 2 * lax.rem(n, 2) + lax.div(n, 2)


class Swap:
    def __init__(self, local_sems, send_sems, recv_sems, first=0):
        x, c, z, y = place()
        self.first = first
        self.stays = z == turned_pair(2 * x + c)
        self.to = (turned_pair(z), 2 * turned_pair(2 * x + c) + y)
        self.sems = (local_sems, send_sems, recv_sems)
        self.pairs = []

    def start(self, src, dst):
        at = self.first + len(self.pairs)
        local_sems, send_sems, recv_sems = self.sems
        local = pltpu.make_async_copy(src, dst, local_sems.at[at])
        away = pltpu.make_async_remote_copy(
            src_ref=src, dst_ref=dst, send_sem=send_sems.at[at], recv_sem=recv_sems.at[at],
            device_id=self.to, device_id_type=MESH,
        )
        self.pairs.append((local, away))

        @pl.when(self.stays)
        def keep():
            local.start()

        @pl.when(jnp.logical_not(self.stays))
        def send():
            away.start()

    def finish(self):
        @pl.when(self.stays)
        def kept():
            for local, away in self.pairs:
                local.wait()

        @pl.when(jnp.logical_not(self.stays))
        def sent():
            for local, away in self.pairs:
                away.wait()


def push(src, dst, send, recv, device):
    copy = pltpu.make_async_remote_copy(
        src_ref=src, dst_ref=dst, send_sem=send, recv_sem=recv, device_id=device, device_id_type=MESH
    )
    copy.start()
    return copy


FIRST, SECOND, BOTH, CROSS = range(4)
SIZES = (2, 2, 3, 1)


def gather_blocks(r, notes, while_last):
    x, c, z, y = place()
    samp = 2 * x + c
    blk = 2 * z + y
    to_y = (samp, 2 * z + 1 - y)
    to_x = (2 * (1 - x) + c, blk)
    to_c = (2 * x + 1 - c, blk)
    base = c * HALF
    out = r.weights
    starts = (base + x * 8, base + x * 8 + 2, base + QUART, base + QUART + 3)
    far_starts = (base + (1 - x) * 8, base + (1 - x) * 8 + 2)
    other = (1 - c) * HALF
    parts = [base + x * 8, base + QUART, base + (1 - x) * 8, other, other + QUART, other + 2 * QUART]
    notes_out, note_send, note_recv = r.notes_land, r.note_send, r.note_recv

    def load(at):
        return pltpu.make_async_copy(
            r.masters.at[pl.ds(parts[at], QUART)], r.wide.at[at % 2], r.load_sems.at[at]
        )

    def ready(at):
        load(at).wait()
        out[pl.ds(blk * GROUP + parts[at], QUART)] = r.wide[at % 2].astype(LOW)
        if at + 2 < len(parts):
            load(at + 2).start()

    def copy(group, start, size, sems, at, device):
        place_out = out.at[pl.ds(group * GROUP + start, size)]
        return pltpu.make_async_remote_copy(
            src_ref=place_out, dst_ref=place_out,
            send_sem=sems.at[(0,) + at], recv_sem=sems.at[(1,) + at], device_id=device, device_id_type=MESH,
        )

    def z_copy(kind, way, origin):
        to = (samp, blk + (2 if way == 0 else -2))
        return copy(2 * origin + y, starts[kind], SIZES[kind], r.z_sems, (kind, way, origin), to)

    def z_cross(way, origin, side):
        to = (samp, blk + (2 if way == 0 else -2))
        return copy(2 * origin + side, starts[CROSS], 1, r.z_sems, (CROSS + side, way, origin), to)

    def y_copy(kind, origin):
        return copy(2 * origin + y, starts[kind], SIZES[kind], r.y_sems, (kind, origin), to_y)

    def y_landed(kind, origin):
        return copy(2 * origin + 1 - y, starts[kind], SIZES[kind], r.y_sems, (kind, origin), to_y)

    def x_copy(kind, group):
        return copy(group, starts[kind], SIZES[kind], r.x_sems, (kind, group), to_x)

    def x_landed(kind, group):
        return copy(group, far_starts[kind], SIZES[kind], r.x_sems, (kind, group), to_x)

    def core_copy(kind, group):
        return copy(group, starts[kind], SIZES[kind], r.core_sems, (kind, group), to_c)

    def far_copy(kind, group):
        return copy(group, far_starts[kind], SIZES[kind], r.far_sems, (kind, group), to_c)

    def on_from_here(kind, group):
        if kind in (FIRST, SECOND):
            x_copy(kind, group).start()
        core_copy(kind, group).start()

    def begin(kind):
        @pl.when(z < 3)
        def up():
            z_copy(kind, 0, z).start()

        @pl.when(z > 0)
        def down():
            z_copy(kind, 1, z).start()

        y_copy(kind, z).start()

    def z_step(kind, distance):
        for way in (0, 1):
            origin = z - distance if way == 0 else z + distance

            @pl.when(origin >= 0 if way == 0 else origin <= 3)
            def arrived():
                z_copy(kind, way, origin).wait_recv()

                @pl.when(z < 3 if way == 0 else z > 0)
                def onward():
                    z_copy(kind, way, origin).start()

                y_copy(kind, origin).start()
                on_from_here(kind, 2 * origin + y)

    def y_step(kind, distance):
        for way in (0, 1):
            origin = z - distance if way == 0 else z + distance

            @pl.when(origin >= 0 if way == 0 else origin <= 3)
            def arrived():
                y_landed(kind, origin).wait_recv()
                on_from_here(kind, 2 * origin + 1 - y)

    def y_own(kind):
        y_landed(kind, z).wait_recv()
        on_from_here(kind, 2 * z + 1 - y)

    def cross_step(distance):
        for side in (0, 1):
            for way in (0, 1):
                origin = z - distance if way == 0 else z + distance

                @pl.when(origin >= 0 if way == 0 else origin <= 3)
                def arrived():
                    z_cross(way, origin, side).wait_recv()

                    @pl.when(z < 3 if way == 0 else z > 0)
                    def onward():
                        z_cross(way, origin, side).start()

                    core_copy(CROSS, 2 * origin + side).start()

    def x_step(kind, distance, same):
        for way in (0, 1):
            origin = z - distance if way == 0 else z + distance

            @pl.when(origin >= 0 if way == 0 else origin <= 3)
            def arrived():
                group = 2 * origin + (y if same else 1 - y)
                x_landed(kind, group).wait_recv()
                far_copy(kind, group).start()

    def x_own(kind):
        x_landed(kind, 2 * z + 1 - y).wait_recv()
        far_copy(kind, 2 * z + 1 - y).start()

    note_local = pltpu.make_async_copy(notes, notes_out.at[blk], r.load_sems.at[6])

    def note_copy(j, origin):
        return pltpu.make_async_remote_copy(
            src_ref=notes, dst_ref=notes_out.at[origin], send_sem=note_send.at[j], recv_sem=note_recv.at[origin],
            device_id=(j // 2, 2 * turned_pair(samp) + j % 2), device_id_type=MESH,
        )

    stays = z == turned_pair(samp)

    def is_me(j):
        return jnp.logical_and(stays, 2 * samp + y == j)

    def here_from(j):
        return jnp.logical_and(stays, blk == j)

    load(0).start()
    load(1).start()
    meet_all()
    r.swap_rows.start(r.rows_in, r.rows_land)
    def cross_begin():
        y_landed(CROSS, z).wait_recv()
        core_copy(CROSS, 2 * z + 1 - y).start()
        for way, there in ((0, z < 3), (1, z > 0)):
            for side in (0, 1):
                @pl.when(there)
                def both_sides():
                    z_cross(way, z, side).start()

    ready(0)
    begin(FIRST)
    begin(SECOND)
    ready(1)
    y_copy(CROSS, z).start()
    for j in range(8):

        @pl.when(jnp.logical_not(is_me(j)))
        def send_note():
            note_copy(j, blk).start()

    @pl.when(stays)
    def keep_note():
        note_local.start()

    for at in range(2, len(parts)):
        ready(at)
    z_step(FIRST, 1)
    z_step(SECOND, 1)
    y_own(SECOND)
    z_step(FIRST, 2)
    begin(BOTH)
    z_step(SECOND, 2)
    y_step(FIRST, 1)
    y_own(FIRST)
    y_own(BOTH)
    z_step(SECOND, 3)
    x_step(FIRST, 1, True)
    y_step(SECOND, 1)
    x_own(SECOND)
    z_step(BOTH, 1)
    cross_begin()
    x_step(FIRST, 2, True)
    z_step(FIRST, 3)
    y_step(FIRST, 2)
    cross_step(1)
    x_step(SECOND, 1, True)
    x_own(FIRST)
    y_step(SECOND, 2)
    y_step(SECOND, 3)
    x_step(FIRST, 1, False)
    z_step(BOTH, 2)
    x_step(SECOND, 1, False)
    y_step(BOTH, 1)
    x_step(FIRST, 2, False)
    z_step(BOTH, 3)
    x_step(SECOND, 2, True)
    y_step(FIRST, 3)
    x_step(FIRST, 3, True)
    cross_step(2)
    y_step(BOTH, 2)
    x_step(SECOND, 3, False)
    x_step(SECOND, 2, False)
    x_step(SECOND, 3, True)
    cross_step(3)
    y_step(BOTH, 3)
    x_step(FIRST, 3, False)

    while_last()
    other_starts = (other + x * 8, other + x * 8 + 2, other + QUART, other + QUART + 3)
    other_far = (other + (1 - x) * 8, other + (1 - x) * 8 + 2)

    def settle(group, carry):
        @pl.when(group != blk)
        def other_group():
            for kind in range(4):
                copy(group, other_starts[kind], SIZES[kind], r.core_sems, (kind, group), to_c).wait_recv()
                core_copy(kind, group).wait_send()
            for kind in (FIRST, SECOND):
                copy(group, other_far[kind], SIZES[kind], r.far_sems, (kind, group), to_c).wait_recv()
                far_copy(kind, group).wait_send()
                x_copy(kind, group).wait_send()

        return carry

    lax.fori_loop(0, 8, settle, 0)

    def sent_along(origin, carry):
        for kind in (FIRST, SECOND, BOTH):
            y_copy(kind, origin).wait_send()

            @pl.when(jnp.logical_and(origin <= z, z < 3))
            def up():
                z_copy(kind, 0, origin).wait_send()

            @pl.when(jnp.logical_and(origin >= z, z > 0))
            def down():
                z_copy(kind, 1, origin).wait_send()

        for side in (0, 1):
            @pl.when(jnp.logical_and(origin <= z, z < 3))
            def cross_up():
                z_cross(0, origin, side).wait_send()

            @pl.when(jnp.logical_and(origin >= z, z > 0))
            def cross_down():
                z_cross(1, origin, side).wait_send()

        return carry

    lax.fori_loop(0, 4, sent_along, 0)
    y_copy(CROSS, z).wait_send()
    for j in range(8):

        @pl.when(jnp.logical_not(is_me(j)))
        def sent_note():
            note_copy(j, blk).wait_send()

        @pl.when(jnp.logical_not(here_from(j)))
        def got_note():
            note_copy(j, j).wait_recv()

    @pl.when(stays)
    def kept_note():
        note_local.wait()


def local_any(
    inputs,
    cot_first,
    cot_second,
    valid_flags,
    lead_steps,
    masters,
    assignment,
    left_start,
    right_start,
    vectors,
    vec_moment,
):
    copies = lax.all_gather(masters.astype(jnp.bfloat16), "blk", axis=0, tiled=True)
    blocks = jnp.take(copies, assignment, axis=0)
    qkv_weight, out_weight, up_weight, down_weight = unpack(blocks)
    scaling = HD ** (-0.5)
    flags_low = valid_flags.astype(jnp.bfloat16)
    key_bias = (valid_flags.astype(jnp.float32) - 1.0) * masked
    lead_base = 8 + FF // D
    lead_table = vectors[lead_base:]
    samples = inputs.shape[0]
    patches = inputs.shape[1]

    def forward(hidden_in, lead_ids):
        chosen = (lead_ids[:, None] == jnp.arange(LEADS, dtype=jnp.int32)[None, :]).astype(
            jnp.float32
        )
        lead_rows = jnp.dot(chosen, lead_table, precision=HIGH)
        hidden = hidden_in + lead_rows[:, None, :]
        normed_low = norm_layer(hidden, vectors[0], vectors[1]).astype(jnp.bfloat16)
        packed = jnp.einsum(
            "spd,de->spe", normed_low, qkv_weight, preferred_element_type=jnp.float32
        )
        queries = (packed[..., :D] + vectors[2]).astype(jnp.bfloat16)
        keys_low = packed[..., D : 2 * D].astype(jnp.bfloat16)
        values_low = (packed[..., 2 * D :] + vectors[3]).astype(jnp.bfloat16)
        start_state = (
            jnp.full((samples, HEADS, patches), -1e30, jnp.float32),
            jnp.zeros((samples, HEADS, patches), jnp.float32),
            jnp.zeros((samples, HEADS, patches, HD), jnp.float32),
        )
        update = forward_update(heads_of(queries), scaling)
        gathered = None
        piece = (
            lax.all_gather(keys_low, "blk", axis=1, tiled=True),
            lax.all_gather(values_low, "blk", axis=1, tiled=True),
            lax.all_gather(flags_low, "blk", axis=1, tiled=True),
        )
        running_max, running_sum, weighted = in_blocks(
            update, start_state, piece, piece[0].shape[1]
        )
        attended = jnp.transpose(weighted / running_sum[..., None], (0, 2, 1, 3)).reshape(
            samples, patches, D
        )
        log_total = running_max + jnp.log(running_sum)
        attended_low = attended.astype(jnp.bfloat16)
        middle = (
            hidden
            + jnp.einsum(
                "spd,de->spe", attended_low, out_weight, preferred_element_type=jnp.float32
            )
            + vectors[4]
        )
        normed_two = norm_layer(middle, vectors[5], vectors[6]).astype(jnp.bfloat16)
        upward = jnp.einsum(
            "spd,df->spf", normed_two, up_weight, preferred_element_type=jnp.float32
        ) + vectors[8:lead_base].reshape(FF)
        activated = gelu_exact(upward).astype(jnp.bfloat16)
        result = (
            middle
            + jnp.einsum("spf,fd->spd", activated, down_weight, preferred_element_type=jnp.float32)
            + vectors[7]
        )
        saved = (
            hidden,
            normed_low,
            queries,
            keys_low,
            values_low,
            attended,
            attended_low,
            log_total,
            middle,
            normed_two,
            upward,
            activated,
            chosen,
            gathered,
        )
        return (result, saved)

    def backward(grad_out, saved):
        (
            hidden,
            normed_low,
            queries,
            keys_low,
            values_low,
            attended,
            attended_low,
            log_total,
            middle,
            normed_two,
            upward,
            activated,
            chosen,
            gathered,
        ) = saved
        grad_two = grad_out.astype(jnp.bfloat16)
        down_grad = jnp.einsum(
            "spf,spd->fd", activated, grad_two, preferred_element_type=jnp.float32
        )
        down_bias = jnp.sum(grad_two.astype(jnp.float32), axis=(0, 1))
        grad_act = jnp.einsum(
            "spd,fd->spf", grad_two, down_weight, preferred_element_type=jnp.float32
        )
        gelu_value, gelu_pull = jax.vjp(gelu_exact, upward)
        grad_up = gelu_pull(grad_act)[0].astype(jnp.bfloat16)
        up_grad = jnp.einsum("spd,spf->df", normed_two, grad_up, preferred_element_type=jnp.float32)
        up_bias = jnp.sum(grad_up.astype(jnp.float32), axis=(0, 1))
        grad_normed_two = jnp.einsum(
            "spf,df->spd", grad_up, up_weight, preferred_element_type=jnp.float32
        )
        norm_value, norm_pull = jax.vjp(norm_layer, middle, vectors[5], vectors[6])
        grad_middle_norm, gain_two, shift_two = norm_pull(grad_normed_two)
        grad_middle = grad_out + grad_middle_norm
        grad_one = grad_middle.astype(jnp.bfloat16)
        out_grad = jnp.einsum(
            "spd,spe->de", attended_low, grad_one, preferred_element_type=jnp.float32
        )
        out_bias = jnp.sum(grad_one.astype(jnp.float32), axis=(0, 1))
        grad_attended = jnp.einsum(
            "spe,de->spd", grad_one, out_weight, preferred_element_type=jnp.float32
        ).astype(jnp.bfloat16)
        inner = jnp.sum(
            (grad_attended.astype(jnp.float32) * attended).reshape(samples, patches, HEADS, HD),
            axis=-1,
        )
        inner_heads = jnp.transpose(inner, (0, 2, 1))
        zero_query = jnp.zeros((samples, patches, HEADS, HD), jnp.float32)
        update_query = query_grad_update(
            heads_of(queries), heads_of(grad_attended), log_total, inner_heads, scaling
        )
        piece = (
            lax.all_gather(keys_low, "blk", axis=1, tiled=True),
            lax.all_gather(values_low, "blk", axis=1, tiled=True),
            lax.all_gather(flags_low, "blk", axis=1, tiled=True),
        )
        grad_query = in_blocks(update_query, zero_query, piece, piece[0].shape[1])
        total_rows, inner_rows = (
            lax.all_gather(jnp.transpose(log_total, (0, 2, 1)), "blk", axis=1, tiled=True),
            lax.all_gather(inner, "blk", axis=1, tiled=True),
        )
        key_heads = heads_of(keys_low)
        value_heads = heads_of(values_low)
        zero_pair = (zero_query, zero_query)
        piece = (
            lax.all_gather(queries, "blk", axis=1, tiled=True),
            lax.all_gather(grad_attended, "blk", axis=1, tiled=True),
        )
        update_keys = key_grad_update(
            key_heads, value_heads, key_bias, total_rows, inner_rows, scaling, jnp.int32(0)
        )
        grad_keys, grad_values = in_blocks(update_keys, zero_pair, piece, piece[0].shape[1])
        grad_packed = jnp.concatenate(
            [
                grad_query.reshape(samples, patches, D),
                grad_keys.reshape(samples, patches, D),
                grad_values.reshape(samples, patches, D),
            ],
            axis=-1,
        ).astype(jnp.bfloat16)
        qkv_grad = jnp.einsum(
            "spd,spe->de", normed_low, grad_packed, preferred_element_type=jnp.float32
        )
        query_bias = jnp.sum(grad_packed[..., :D].astype(jnp.float32), axis=(0, 1))
        value_bias = jnp.sum(grad_packed[..., 2 * D :].astype(jnp.float32), axis=(0, 1))
        grad_normed = jnp.einsum(
            "spe,de->spd", grad_packed, qkv_weight, preferred_element_type=jnp.float32
        )
        first_value, first_pull = jax.vjp(norm_layer, hidden, vectors[0], vectors[1])
        grad_hidden_norm, gain_one, shift_one = first_pull(grad_normed)
        grad_hidden = grad_middle + grad_hidden_norm
        lead_grad = jnp.dot(chosen.T, jnp.sum(grad_hidden, axis=1), precision=HIGH)
        vec_rows = jnp.concatenate(
            [
                gain_one[None],
                shift_one[None],
                query_bias[None],
                value_bias[None],
                out_bias[None],
                gain_two[None],
                shift_two[None],
                down_bias[None],
                up_bias.reshape(FF // D, D),
                lead_grad,
            ],
            axis=0,
        )
        return (grad_hidden, (qkv_grad, out_grad, up_grad, down_grad), vec_rows)

    earlier, saved_one = forward(inputs.astype(jnp.float32), lead_steps[0])
    later, saved_two = forward(earlier, lead_steps[1])
    grad_between, mats_two, vec_two = backward(cot_second.astype(jnp.float32), saved_two)
    input_grad, mats_one, vec_one = backward(
        cot_first.astype(jnp.float32) + grad_between, saved_one
    )
    grad_blocks = jnp.concatenate(
        [
            carve(mats_one[0] + mats_two[0]),
            carve(mats_one[1] + mats_two[1]),
            carve(mats_one[2] + mats_two[2]),
            carve(mats_one[3] + mats_two[3]),
        ],
        axis=0,
    )
    position = jnp.arange(NB, dtype=jnp.int32)
    inverse = jnp.sum(
        jnp.where(assignment[None, :] == position[:, None], position[None, :], 0), axis=1
    )
    slotted = jnp.take(grad_blocks, inverse, axis=0)
    shared = lax.psum_scatter(slotted, "blk", scatter_dimension=0, tiled=True)
    matrix_grads = lax.psum(shared.astype(jnp.bfloat16), "samp").astype(jnp.float32)
    vec_grads = lax.psum(vec_one + vec_two, ("samp", "blk"))
    left_stats, right_stats, new_masters = jax.vmap(precondition)(
        matrix_grads, left_start, right_start, masters
    )
    scaled_vec = vec_grads * lax.rsqrt(
        jnp.mean(vec_grads * vec_grads, axis=1, keepdims=True) + 1e-06
    )
    vec_moments = 0.5 * vec_moment + 0.5 * scaled_vec * scaled_vec
    new_vectors = vectors - vector_rate * scaled_vec * lax.rsqrt(vec_moments)
    return (
        earlier.astype(jnp.bfloat16),
        later.astype(jnp.bfloat16),
        input_grad,
        matrix_grads,
        left_stats,
        right_stats,
        new_masters,
        new_masters.astype(jnp.bfloat16),
        vec_grads,
        vec_moments,
        new_vectors,
    )


TOKENS = 128
PAIR = 2 * HD
SEQ_ALL = 8 * TOKENS
QKV_AT, OUT_AT, UP_AT, DOWN_AT = 0, 48, 64, 128
WIDE = D // BS
DEEP = FF // BS
LEAD_AT = 8 + FF // D


def dot(left, right):
    return jnp.dot(left, right, preferred_element_type=FULL)


def dot_t(left, right):
    return lax.dot_general(left, right, (((1,), (1,)), ((), ())), preferred_element_type=FULL)


def normal(value):
    centred = value - jnp.mean(value, axis=-1, keepdims=True)
    rate = lax.rsqrt(jnp.mean(centred * centred, axis=-1, keepdims=True) + 1e-06)
    return (centred * rate, rate)


def normal_back(grad, unit, rate, gain):
    scaled = grad * gain
    return rate * (
        scaled
        - jnp.mean(scaled, axis=-1, keepdims=True)
        - unit * jnp.mean(scaled * unit, axis=-1, keepdims=True)
    )


def total(value):
    return jnp.sum(value, axis=0, keepdims=True)


def gelu_parts(value):
    phi = 0.5 + 0.5 * lax.erf(value * (0.5**0.5))
    return phi, value * phi


def gelu_slope(value, phi):
    return phi + value * jnp.exp(-0.5 * value * value) * ((2.0 * math.pi) ** -0.5)


class Weights:
    def __init__(self, slots, held):
        self.slots, self.held = slots, held

    def block(self, base, cols, row, col):
        return self.held[self.slots[base + row * cols + col]]

    def down_col(self, base, rows, cols, col):
        return jnp.concatenate([self.block(base, cols, row, col) for row in range(rows)], axis=0)

    def along_row(self, base, cols, row, first=0, last=None):
        return jnp.concatenate(
            [self.block(base, cols, row, col) for col in range(first, cols if last is None else last)], axis=1
        )


def lead_row(vecs, lead):
    row = jnp.zeros((1, D), FULL)
    for at in range(LEADS):
        row = row + jnp.where(lead == at, vecs[LEAD_AT + at : LEAD_AT + at + 1], 0.0)
    return row


def project(r, layer, hidden, vecs, weights):
    unit, unused = normal(hidden)
    normed = (unit * vecs[0:1] + vecs[1:2]).astype(LOW)
    for k in range(WIDE):
        r.left_held[layer, k] = normed[:, k * BS : (k + 1) * BS].T
    give_pool(r, True, layer, 0)
    for kind in (1, 0, 2):
        for step in range(WIDE):
            within = lax.rem(step + lax.div(r.plane.me, 2), WIDE)
            part = dot(normed, weights.down_col(QKV_AT, WIDE, 3 * WIDE, kind * WIDE + within))
            if kind != 1:
                row = 2 if kind == 0 else 3
                part = part + vecs[row : row + 1, pl.ds(pl.multiple_of(within * BS, BS), BS)]
            part = part.astype(LOW)
            for half in range(2):
                r.packed[kind, 2 * within + half] = part[:, half * PAIR : (half + 1) * PAIR]
                r.plane.send_or_keep(
                    r.packed.at[kind], r.held[layer].at[kind], r.in_sems[layer].at[kind], 2 * within + half
                )


def pool_at(left, kind):
    counts, bases = (LEFTS, LEFT_AT) if left else (RIGHTS, RIGHT_AT)
    return pl.ds(bases[kind], counts[kind])


def pool_copies(r, left, layer, kind):
    x, c, z, y = place()
    ids = pool_at(left, kind)
    at = (0 if left else 8) + 4 * layer + kind
    source = (r.left_held if left else r.right_held).at[layer, ids]

    def target(part):
        tokens = pl.ds((2 * part + layer) * TOKENS, TOKENS)
        return r.left_pool.at[ids, :, tokens] if left else r.right_pool.at[ids, tokens]

    here = pltpu.make_async_copy(source, target(0), r.pool_sems.at[0, at])
    there = pltpu.make_async_remote_copy(
        src_ref=source, dst_ref=target(1), send_sem=r.pool_sems.at[1, at], recv_sem=r.pool_sems.at[2, at],
        device_id=(2 * x + 1 - c, 2 * z + y), device_id_type=MESH,
    )
    return here, there


def give_pool(r, left, layer, kind):
    for copy in pool_copies(r, left, layer, kind):
        copy.start()


def feed(r, layer, hidden, vecs, weights, slope_held):
    attended = jnp.concatenate([r.o_land[j] for j in range(8)], axis=1)
    for k in range(WIDE):
        r.left_held[layer, WIDE + k] = attended[:, k * BS : (k + 1) * BS].T
    give_pool(r, True, layer, 1)
    branch = [dot(attended, weights.down_col(OUT_AT, WIDE, WIDE, n)) for n in range(WIDE)]
    middle = hidden + jnp.concatenate(branch, axis=1) + vecs[4:5]
    unit, unused = normal(middle)
    normed = (unit * vecs[5:6] + vecs[6:7]).astype(LOW)
    for k in range(WIDE):
        r.left_held[layer, 2 * WIDE + k] = normed[:, k * BS : (k + 1) * BS].T
    give_pool(r, True, layer, 2)
    per = D // BS
    for f in range(DEEP):
        bias = vecs[8 + f // per : 9 + f // per, (f % per) * BS : (f % per + 1) * BS]
        upward = dot(normed, weights.down_col(UP_AT, WIDE, DEEP, f)) + bias
        phi, activated = gelu_parts(upward)
        slope_held[f] = gelu_slope(upward, phi)
        activated = activated.astype(LOW)
        r.act_held[:, f * BS : (f + 1) * BS] = activated
        r.left_held[layer, 3 * WIDE + f] = activated.T
    give_pool(r, True, layer, 3)
    branch = [dot(r.act_held[...], weights.down_col(DOWN_AT, DEEP, WIDE, n)) for n in range(WIDE)]
    return middle, middle + jnp.concatenate(branch, axis=1) + vecs[7:8]


def feed_back(r, layer, grad_out, middle, slope_in, vecs, weights):
    rows = r.rows
    grad_two = grad_out.astype(LOW)
    for k in range(WIDE):
        r.right_held[layer, RIGHT_AT[3] + k] = grad_two[:, k * BS : (k + 1) * BS]
    give_pool(r, False, layer, 3)
    rows[7:8] += total(grad_two.astype(FULL))
    per = D // BS
    for f in range(DEEP):
        grad_act = dot_t(grad_two, weights.along_row(DOWN_AT, WIDE, f))
        grad_up = (grad_act * slope_in[f]).astype(LOW)
        r.right_held[layer, RIGHT_AT[2] + f] = grad_up
        rows[8 + f // per : 9 + f // per, (f % per) * BS : (f % per + 1) * BS] += total(grad_up.astype(FULL))
    give_pool(r, False, layer, 2)
    grad_up = jnp.concatenate([r.right_held[layer, RIGHT_AT[2] + f] for f in range(DEEP)], axis=1)
    grad_normed = jnp.concatenate(
        [dot_t(grad_up, weights.along_row(UP_AT, DEEP, k)) for k in range(WIDE)], axis=1
    )
    unit, rate = normal(middle)
    rows[5:6] += total(grad_normed * unit)
    rows[6:7] += total(grad_normed)
    grad_middle = grad_out + normal_back(grad_normed, unit, rate, vecs[5:6])
    grad_one = grad_middle.astype(LOW)
    for k in range(WIDE):
        r.right_held[layer, RIGHT_AT[1] + k] = grad_one[:, k * BS : (k + 1) * BS]
    give_pool(r, False, layer, 1)
    rows[4:5] += total(grad_one.astype(FULL))
    for k in range(WIDE):
        part = dot_t(grad_one, weights.along_row(OUT_AT, WIDE, k)).astype(LOW)
        for half in range(2):
            r.do_message[2 * k + half] = part[:, half * PAIR : (half + 1) * PAIR]
            r.plane.send_or_keep(r.do_message, r.do_land, r.do_sems[layer], 2 * k + half)
    return grad_middle


def project_back(r, layer, grad_middle, hidden, vecs, weights, lead):
    rows = r.rows

    def blocks_of_kind(kind):
        source, cols = (r.dq_land, slice(0, PAIR)) if kind == 0 else (r.dkv_land, slice((kind - 1) * PAIR, kind * PAIR))
        for within in range(WIDE):
            part = jnp.concatenate([source[2 * within, :, cols], source[2 * within + 1, :, cols]], axis=1)
            r.right_held[layer, kind * WIDE + within] = part
            if kind != 1:
                row = 2 if kind == 0 else 3
                rows[row : row + 1, within * BS : (within + 1) * BS] += total(part.astype(FULL))

    def back(first, last):
        part = jnp.concatenate([r.right_held[layer, n] for n in range(first, last)], axis=1)
        return jnp.concatenate(
            [dot_t(part, weights.along_row(QKV_AT, 3 * WIDE, k, first, last)) for k in range(WIDE)], axis=1
        )

    r.plane.received(r.dkv_land, r.dkv_sems[layer])
    blocks_of_kind(1)
    blocks_of_kind(2)
    grad_normed = back(WIDE, 3 * WIDE)
    r.plane.received(r.dq_land, r.dq_sems[layer])
    blocks_of_kind(0)
    give_pool(r, False, layer, 0)
    grad_normed = grad_normed + back(0, WIDE)
    unit, rate = normal(hidden)
    rows[0:1] += total(grad_normed * unit)
    rows[1:2] += total(grad_normed)
    grad_hidden = grad_middle + normal_back(grad_normed, unit, rate, vecs[0:1])
    sums = total(grad_hidden)
    for at in range(LEADS):
        rows[LEAD_AT + at : LEAD_AT + at + 1] += jnp.where(lead == at, sums, 0.0)
    return grad_hidden


def attend(r, layer):
    held, turned, stats, sems = r.held[layer], r.turned[layer], r.stats[layer], r.in_sems[layer]
    plane = r.plane
    plane.received(held.at[1], sems.at[1])
    keys = held[1].reshape(SEQ_ALL, PAIR).astype(FULL)
    for head in range(2):
        r.key_side[head] = key_columns(keys, r.neg[...], head).astype(LOW)

    def chunk(step, carry):
        at = lax.rem(step + lax.div(plane.me, 2), 4)
        first = pl.multiple_of(at * BS, BS)
        for half in range(2):
            plane.received_from(held.at[0], sems.at[0], 2 * at + half)
        queries = held[0, pl.ds(2 * at, 2)].reshape(BS, PAIR).astype(FULL)
        scales = []
        for head in range(2):
            scores = dot_t(r.key_side[head], query_columns(queries, head).astype(LOW))
            most = jnp.max(scores, axis=0, keepdims=True)
            expos = jnp.exp(scores - most)
            sums = jnp.sum(expos, axis=0, keepdims=True)
            r.expos[head] = expos.astype(LOW)
            stats[head : head + 1, pl.ds(first, BS)] = most + jnp.log(sums)
            scales.append(1.0 / sums)

        @pl.when(step == 0)
        def values_in():
            plane.received(held.at[2], sems.at[2])
            r.values_t[...] = held[2].reshape(SEQ_ALL, PAIR).T

        for head in range(2):
            side = slice(head * HD, (head + 1) * HD)
            turned[at, side] = dot(r.values_t[side], r.expos[head]) * scales[head]
        for half in range(2):
            to = 2 * at + half
            r.o_message[to] = turned[at, :, half * TOKENS : (half + 1) * TOKENS].astype(LOW).T
            plane.send_or_keep(r.o_message, r.o_land, r.o_sems[layer], to)
        return carry

    lax.fori_loop(0, SEQ_ALL // BS, chunk, 0)
    for kind in range(3):
        plane.sent(r.packed.at[kind], sems.at[kind])
    plane.received(r.o_land, r.o_sems[layer])
    plane.sent(r.o_message, r.o_sems[layer])


def attend_back(r, layer):
    held, turned, stats = r.held[layer], r.turned[layer], r.stats[layer]
    plane = r.plane
    queries = held[0].reshape(SEQ_ALL, PAIR).astype(FULL)
    keys = held[1].reshape(SEQ_ALL, PAIR).astype(FULL)
    keys_t = held[1].reshape(SEQ_ALL, PAIR).T
    r.grad_q[...] = jnp.zeros_like(r.grad_q)
    for head in range(2):
        side = query_columns(queries, head)
        r.query_side[head] = side.astype(LOW)
        r.query_plain[head] = jnp.where(own_columns(queries, head)[0], side, 0.0).astype(LOW)
        r.key_side[head] = key_columns(keys, r.neg[...], head).astype(LOW)
    plane.received(r.do_land, r.do_sems[layer])
    grads = r.do_land[...].reshape(SEQ_ALL, PAIR).astype(FULL)
    lane = lax.broadcasted_iota(jnp.int32, grads.shape, 1)
    r.do_side[0] = jnp.where(lane < HD, grads, 0.0).astype(LOW)
    r.do_side[1] = jnp.where(lane >= HD, grads, 0.0).astype(LOW)
    grads_t = r.do_land[...].reshape(SEQ_ALL, PAIR).T.astype(FULL)
    inner = []
    for head in range(2):
        side = slice(head * HD, (head + 1) * HD)
        inner.append(
            jnp.concatenate(
                [
                    jnp.sum(turned[at, side] * grads_t[side, at * BS : (at + 1) * BS], axis=0, keepdims=True)
                    for at in range(SEQ_ALL // BS)
                ],
                axis=1,
            )
        )
    left = lax.broadcasted_iota(jnp.int32, (BS, PAIR), 1) < HD
    keys_held = [keys_t[head * HD : (head + 1) * HD] for head in range(2)]
    for at in range(SEQ_ALL // BS):
        first = at * BS
        grad_k = []
        grad_v = None
        values = held[2, 2 * at : 2 * at + 2].reshape(BS, PAIR)
        for head in range(2):
            scores = dot_t(r.key_side[head, first : first + BS], r.query_side[head])
            probs = jnp.exp(scores - stats[head : head + 1])
            dprobs = dot_t(values, r.do_side[head])
            dscores = (probs * (dprobs - inner[head])).astype(LOW)
            term = dot(probs.astype(LOW), r.do_side[head])
            grad_v = term if grad_v is None else grad_v + term
            grad_k.append(dot(dscores, r.query_plain[head]))
            r.grad_q[head * HD : (head + 1) * HD] += dot(keys_held[head][:, first : first + BS], dscores)
        grad_k = jnp.where(left, grad_k[0], grad_k[1]).astype(LOW)
        grad_v = grad_v.astype(LOW)
        for half in range(2):
            to = 2 * at + half
            rows = slice(half * TOKENS, (half + 1) * TOKENS)
            r.dkv_message[to, :, :PAIR] = grad_k[rows]
            r.dkv_message[to, :, PAIR:] = grad_v[rows]
            plane.send_or_keep(r.dkv_message, r.dkv_land, r.dkv_sems[layer], to)
    for j in range(8):
        r.dq_message[j] = (r.grad_q[:, j * TOKENS : (j + 1) * TOKENS] * HD**-0.5).astype(LOW).T
        plane.send_or_keep(r.dq_message, r.dq_land, r.dq_sems[layer], j)


class Refs:
    pass


def names(**given):
    return tuple(given)


SCRATCH = dict(
    weights=pltpu.VMEM((NB, BS, BS), LOW),
    wide=pltpu.VMEM((2, QUART, BS, BS), FULL),
    notes=pltpu.VMEM((8, TOKENS), FULL),
    notes_land=pltpu.VMEM((8, 8, TOKENS), FULL),
    rows_land=pltpu.VMEM((1, TOKENS, D), LOW),
    first_land=pltpu.VMEM((1, TOKENS, D), LOW),
    second_land=pltpu.VMEM((1, TOKENS, D), LOW),
    pred_one=pltpu.VMEM((1, TOKENS, D), LOW),
    pred_two=pltpu.VMEM((1, TOKENS, D), LOW),
    hidden_one=pltpu.VMEM((TOKENS, D), FULL),
    hidden_two=pltpu.VMEM((TOKENS, D), FULL),
    middle_one=pltpu.VMEM((TOKENS, D), FULL),
    slope_one=pltpu.VMEM((DEEP, TOKENS, BS), FULL),
    slope_two=pltpu.VMEM((DEEP, TOKENS, BS), FULL),
    act_held=pltpu.VMEM((TOKENS, FF), LOW),
    left_held=pltpu.VMEM((2, 3 * WIDE + DEEP, BS, TOKENS), LOW),
    right_held=pltpu.VMEM((2, 5 * WIDE + DEEP, TOKENS, BS), LOW),
    packed=pltpu.VMEM((3, 8, TOKENS, PAIR), LOW),
    held=pltpu.VMEM((2, 3, 8, TOKENS, PAIR), LOW),
    values_t=pltpu.VMEM((PAIR, SEQ_ALL), LOW),
    expos=pltpu.VMEM((2, SEQ_ALL, BS), LOW),
    turned=pltpu.VMEM((2, SEQ_ALL // BS, PAIR, BS), FULL),
    stats=pltpu.VMEM((2, 8, SEQ_ALL), FULL),
    o_message=pltpu.VMEM((8, TOKENS, PAIR), LOW),
    o_land=pltpu.VMEM((8, TOKENS, PAIR), LOW),
    do_message=pltpu.VMEM((8, TOKENS, PAIR), LOW),
    do_land=pltpu.VMEM((8, TOKENS, PAIR), LOW),
    dq_message=pltpu.VMEM((8, TOKENS, PAIR), LOW),
    dq_land=pltpu.VMEM((8, TOKENS, PAIR), LOW),
    dkv_message=pltpu.VMEM((8, TOKENS, 2 * PAIR), LOW),
    dkv_land=pltpu.VMEM((8, TOKENS, 2 * PAIR), LOW),
    neg=pltpu.VMEM((SEQ_ALL, PAIR), FULL),
    query_side=pltpu.VMEM((2, SEQ_ALL, PAIR), LOW),
    query_plain=pltpu.VMEM((2, SEQ_ALL, PAIR), LOW),
    key_side=pltpu.VMEM((2, SEQ_ALL, PAIR), LOW),
    do_side=pltpu.VMEM((2, SEQ_ALL, PAIR), LOW),
    grad_q=pltpu.VMEM((PAIR, SEQ_ALL), FULL),
    load_sems=pltpu.SemaphoreType.DMA((7,)),
    z_sems=pltpu.SemaphoreType.DMA((2, 5, 2, 4)),
    y_sems=pltpu.SemaphoreType.DMA((2, 4, 4)),
    x_sems=pltpu.SemaphoreType.DMA((2, 2, 8)),
    core_sems=pltpu.SemaphoreType.DMA((2, 4, 8)),
    far_sems=pltpu.SemaphoreType.DMA((2, 2, 8)),
    note_send=pltpu.SemaphoreType.DMA((8,)),
    note_recv=pltpu.SemaphoreType.DMA((8,)),
    swap_local=pltpu.SemaphoreType.DMA((5,)),
    swap_send=pltpu.SemaphoreType.DMA((5,)),
    swap_recv=pltpu.SemaphoreType.DMA((5,)),
    plane_sems=pltpu.SemaphoreType.DMA((2, 7, 2, 8)),
    pool_sems=pltpu.SemaphoreType.DMA((3, 16)),
)
INPUTS = names(slots=0, lead_steps=0, flags=0, masters=0, rows_in=0, first_in=0, second_in=0, vectors=0)
OUTPUTS = names(left_pool=0, right_pool=0, pred_one_out=0, pred_two_out=0, input_grad=0, rows=0)


def model_kernel(*refs):
    r = Refs()
    for name, ref in zip(INPUTS + OUTPUTS + tuple(SCRATCH), refs):
        setattr(r, name, ref)
    for name in ("held", "turned", "stats"):
        setattr(r, name, [getattr(r, name).at[layer] for layer in range(2)])
    r.in_sems = [r.plane_sems.at[layer, pl.ds(0, 3)] for layer in range(2)]
    for at, name in enumerate(("o_sems", "do_sems", "dq_sems", "dkv_sems")):
        setattr(r, name, [r.plane_sems.at[layer, 3 + at] for layer in range(2)])
    swaps = [Swap(r.swap_local, r.swap_send, r.swap_recv, at) for at in range(5)]
    r.swap_rows = swaps[0]
    r.plane = Plane()
    vecs = r.vectors
    weights = Weights(r.slots, r.weights)

    def while_last():
        swaps[0].finish()
        r.rows[...] = jnp.zeros_like(r.rows)
        for layer in range(2):
            r.stats[layer][...] = jnp.zeros((8, SEQ_ALL), FULL)

    lane = lax.broadcasted_iota(jnp.int32, (1, TOKENS), 1)
    r.notes[...] = jnp.zeros_like(r.notes)
    r.notes[0:1] = r.flags[...].astype(FULL) - 1.0
    for at in range(2):
        r.notes[1:2] += jnp.where(lane == at, r.lead_steps[at, 0].astype(FULL), 0.0)
    gather_blocks(r, r.notes, while_last)
    mask_columns(r.notes_land, r.neg)
    leads = [r.notes_land[0, 1:2, at : at + 1] for at in range(2)]
    r.hidden_one[...] = r.rows_land[0].astype(FULL) + lead_row(vecs, leads[0])
    project(r, 0, r.hidden_one[...], vecs, weights)
    attend(r, 0)
    swaps[1].start(r.second_in, r.second_land)
    middle, result = feed(r, 0, r.hidden_one[...], vecs, weights, r.slope_one)
    r.middle_one[...] = middle
    r.pred_one[0] = result.astype(LOW)
    r.hidden_two[...] = result + lead_row(vecs, leads[1])
    project(r, 1, r.hidden_two[...], vecs, weights)
    attend(r, 1)
    swaps[3].start(r.pred_one, r.pred_one_out)
    middle, result = feed(r, 1, r.hidden_two[...], vecs, weights, r.slope_two)
    r.pred_two[0] = result.astype(LOW)
    swaps[2].start(r.first_in, r.first_land)
    swaps[1].finish()
    grad_middle = feed_back(r, 1, r.second_land[0].astype(FULL), middle, r.slope_two, vecs, weights)
    attend_back(r, 1)
    grad = project_back(r, 1, grad_middle, r.hidden_two[...], vecs, weights, leads[1])
    for source, sems in ((r.do_message, r.do_sems), (r.dkv_message, r.dkv_sems), (r.dq_message, r.dq_sems)):
        r.plane.sent(source, sems[1])
    swaps[2].finish()
    swaps[4].start(r.pred_two, r.pred_two_out)
    grad = grad + r.first_land[0].astype(FULL)
    grad_middle = feed_back(r, 0, grad, r.middle_one[...], r.slope_one, vecs, weights)
    attend_back(r, 0)
    grad = project_back(r, 0, grad_middle, r.hidden_one[...], vecs, weights, leads[0])
    r.input_grad[0] = grad.astype(LOW)
    for source, sems in ((r.do_message, r.do_sems), (r.dkv_message, r.dkv_sems), (r.dq_message, r.dq_sems)):
        r.plane.sent(source, sems[0])
    for left in (True, False):
        for layer in range(2):
            for kind in range(4):
                for copy in pool_copies(r, left, layer, kind):
                    copy.wait()
    swaps[3].finish()
    swaps[4].finish()


def model(slots, lead_steps, flags, masters, rows, first, second, vectors):
    return pl.pallas_call(
        model_kernel,
        out_shape=(
            shape((N_LEFT, BS, 4 * TOKENS)),
            shape((N_RIGHT, 4 * TOKENS, BS)),
            SHAPES["pred"],
            SHAPES["pred"],
            SHAPES["pred"],
            SHAPES["rows"],
        ),
        in_specs=[SMEM_IN] * 2 + [VMEM_AT] + [ANY_AT] * 4 + [VMEM_AT],
        out_specs=(ANY_AT,) * 4 + (VMEM_AT,) * 2,
        scratch_shapes=list(SCRATCH.values()),
        compiler_params=pltpu.CompilerParams(
            collective_id=0, has_side_effects=True, vmem_limit_bytes=63 * 1024 * 1024
        ),
        cost_estimate=pl.CostEstimate(flops=24 << 30, bytes_accessed=60 << 20, transcendentals=1 << 23),
        name="model",
    )(slots, lead_steps, flags, masters, rows, first, second, vectors)


SMEM_IN = pl.BlockSpec(memory_space=pltpu.SMEM)
VMEM_AT = pl.BlockSpec(memory_space=pltpu.VMEM)
ANY_AT = pl.BlockSpec(memory_space=pl.ANY)


def shape(dims, kind=LOW):
    return jax.ShapeDtypeStruct(dims, kind)


SHAPES = {"pred": shape((1, TOKENS, D)), "rows": shape((20, D), FULL)}


def bias_pieces():
    left = masked
    pieces = []
    for unused in range(3):
        piece = float(ml_dtypes.bfloat16(left))
        pieces.append(piece)
        left -= piece
    assert left == 0.0
    return pieces


MASK_PIECES = bias_pieces()


def own_columns(like, head):
    lane = lax.broadcasted_iota(jnp.int32, like.shape, 1)
    return (lane < HD) if head == 0 else (lane >= HD), lane - (HD if head == 0 else 0)


def key_columns(keys, neg, head):
    own, spot = own_columns(keys, head)
    side = jnp.zeros_like(keys)
    for at, piece in enumerate(MASK_PIECES):
        side = jnp.where(spot == at, neg * piece, side)
    return jnp.where(own, keys, side)


def query_columns(queries, head):
    own, spot = own_columns(queries, head)
    return jnp.where(own, queries * HD**-0.5, jnp.where((spot >= 0) & (spot < 3), 1.0, 0.0))


class Plane:
    def __init__(self):
        x, c, z, y = place()
        self.z = z
        self.me = 4 * c + 2 * x + y

    def device(self, j):
        return (turned_pair(lax.div(j, 2)), 2 * self.z + lax.rem(j, 2))

    def other(self, step):
        return lax.rem(self.me + step, 8)

    def others(self):
        return [self.device(self.other(step)) for step in range(1, 8)]

    def copy(self, src, dst, sems, send_at, recv_at, to):
        return pltpu.make_async_remote_copy(
            src_ref=src, dst_ref=dst, send_sem=sems.at[0, send_at], recv_sem=sems.at[1, recv_at],
            device_id=self.device(to), device_id_type=MESH,
        )

    def send(self, source, target, sems, to):
        self.copy(source.at[to], target.at[self.me], sems, to, self.me, to).start()

    def send_or_keep(self, source, target, sems, to):
        @pl.when(to != self.me)
        def away():
            self.send(source, target, sems, to)

        @pl.when(to == self.me)
        def keep():
            target[to] = source[to]

    def received(self, target, sems):
        for step in range(1, 8):
            j = self.other(step)
            self.copy(target.at[j], target.at[j], sems, j, j, j).wait_recv()

    def received_from(self, target, sems, j):
        @pl.when(j != self.me)
        def arrived():
            self.copy(target.at[j], target.at[j], sems, j, j, j).wait_recv()

    def sent(self, source, sems):
        for step in range(1, 8):
            j = self.other(step)
            self.copy(source.at[j], source.at[j], sems, j, j, j).wait_send()


def mask_columns(notes, neg):
    for j in range(8):
        neg[j * TOKENS : (j + 1) * TOKENS] = jnp.broadcast_to(notes[j, 0:1], (TOKENS, TOKENS)).T


LEFTS = (WIDE, WIDE, WIDE, DEEP)
RIGHTS = (3 * WIDE, WIDE, DEEP, WIDE)
LEFT_AT = (0, WIDE, 2 * WIDE, 3 * WIDE)
RIGHT_AT = (0, 3 * WIDE, 4 * WIDE, 4 * WIDE + DEEP)
N_LEFT = 3 * WIDE + DEEP
N_RIGHT = 5 * WIDE + DEEP


def pools_of(block):
    left = jnp.zeros_like(block)
    right = jnp.zeros_like(block)
    for at, base in enumerate((QKV_AT, OUT_AT, UP_AT, DOWN_AT)):
        inside = block >= base
        cols = RIGHTS[at]
        left = jnp.where(inside, LEFT_AT[at] + (block - base) // cols, left)
        right = jnp.where(inside, RIGHT_AT[at] + (block - base) % cols, right)
    return left, right


def halves(value):
    high = value.astype(LOW)
    return high, (value - high.astype(FULL)).astype(LOW)


def fine(left, right):
    return dot(
        jnp.concatenate([left[0], left[1], left[0]], axis=1),
        jnp.concatenate([right[0], right[0], right[1]], axis=0),
    )


def statistic(gram, shrink, diag, eye):
    return jnp.where(eye, 0.5 * diag, 0.0) + shrink * gram


def roots(stats, eye):
    scales = [jnp.sqrt(jnp.sum(jnp.sum(stat * stat, axis=1, keepdims=True), axis=0, keepdims=True)) for stat in stats]
    moving = [stat / scale for stat, scale in zip(stats, scales)]
    approx = [None] * len(stats)
    ahead = range(len(stats))
    for iteration in range(ITERS):
        factors = [(jnp.where(eye, 5.0, 0.0) - moving[i]) * 0.25 for i in ahead]
        parts = [halves(factor) for factor in factors]
        if iteration == 0:
            approx = [factors[i] * lax.rsqrt(jnp.sqrt(scales[i])) for i in ahead]
        else:
            approx = [fine(halves(approx[i]), parts[i]) for i in ahead]
        if iteration < ITERS - 1:
            squares = [halves(fine(parts[i], parts[i])) for i in ahead]
            fourths = [halves(fine(squares[i], squares[i])) for i in ahead]
            moving = [fine(fourths[i], halves(moving[i])) for i in ahead]
    return approx


PAIRED = 2
SUM_SCRATCH = dict(
    left_t=pltpu.VMEM((N_LEFT, BS, 4 * TOKENS), LOW),
    right_pool=pltpu.VMEM((N_RIGHT, 4 * TOKENS, BS), LOW),
    x_stage=pltpu.VMEM((2, 2, 4, PAIRED, BS, BS), LOW),
    x_land=pltpu.VMEM((2, 2, 4, PAIRED, BS, BS), LOW),
    yb_stage=pltpu.VMEM((4, QUART, BS, BS), LOW),
    yb_land=pltpu.VMEM((4, QUART, BS, BS), LOW),
    ym_stage=pltpu.VMEM((2, 4, PAIRED, BS, BS), LOW),
    ym_land=pltpu.VMEM((2, 4, PAIRED, BS, BS), LOW),
    zb_stage=pltpu.VMEM((4, QUART, BS, BS), LOW),
    zb_land=pltpu.VMEM((3, QUART, BS, BS), LOW),
    zm_stage=pltpu.VMEM((2, 4, PAIRED, BS, BS), LOW),
    zm_land=pltpu.VMEM((2, 3, PAIRED, BS, BS), LOW),
    both_stage=pltpu.VMEM((2, PAIRED, BS, BS), LOW),
    both_land=pltpu.VMEM((PAIRED, BS, BS), LOW),
    own=pltpu.VMEM((6, BS, BS), LOW),
    staged=pltpu.VMEM((6, BS, BS), LOW),
    pair_rows=pltpu.VMEM((20, D), FULL),
    chip_rows=pltpu.VMEM((20, D), FULL),
    plane_rows=pltpu.VMEM((20, D), FULL),
    row_land=pltpu.VMEM((3, 20, D), FULL),
    row_z=pltpu.VMEM((4, 20, D), FULL),
    pool_sems=pltpu.SemaphoreType.DMA((2,)),
    send_sems=pltpu.SemaphoreType.DMA((11, 4)),
    recv_sems=pltpu.SemaphoreType.DMA((11, 4)),
    row_send=pltpu.SemaphoreType.DMA((6,)),
    row_recv=pltpu.SemaphoreType.DMA((6,)),
    share_send=pltpu.SemaphoreType.DMA((6, 6)),
    share_recv=pltpu.SemaphoreType.DMA((6, 6)),
    local_sems=pltpu.SemaphoreType.DMA((9,)),
    swap_local=pltpu.SemaphoreType.DMA((1,)),
    swap_send=pltpu.SemaphoreType.DMA((1,)),
    swap_recv=pltpu.SemaphoreType.DMA((1,)),
)
SUM_INPUTS = names(left_ids=0, right_ids=0, rows_in=0, left_diag=0, right_diag=0, grad_in=0, left_in=0, right_in=0)
SUM_OUTPUTS = names(rows_out=0, grads_out=0, moves_out=0, grad_out=0)


def update_kernel(*refs):
    r = Refs()
    for name, ref in zip(SUM_INPUTS + SUM_OUTPUTS + tuple(SUM_SCRATCH), refs):
        setattr(r, name, ref)
    here = [
        pltpu.make_async_copy(r.right_in, r.right_pool, r.pool_sems.at[0]),
        pltpu.make_async_copy(r.left_in, r.left_t, r.pool_sems.at[1]),
    ]
    for copy in here:
        copy.start()
    x, c, z, y = place()
    samp = 2 * x + c
    blk = 2 * z + y
    to_c = (2 * x + 1 - c, blk)
    to_x = (2 * (1 - x) + c, blk)
    to_y = (samp, 2 * z + 1 - y)
    to_z = [(samp, 2 * lax.rem(z + step, 4) + y) for step in (1, 2, 3)]
    meet_all()
    swap = Swap(r.swap_local, r.swap_send, r.swap_recv)
    swap.start(r.grad_in, r.grad_out)
    row_copies = [push(r.rows_in, r.row_land.at[0], r.row_send.at[0], r.row_recv.at[0], to_c)]
    eye = lax.broadcasted_iota(jnp.int32, (BS, BS), 0) == lax.broadcasted_iota(jnp.int32, (BS, BS), 1)

    def group(half, k):
        return 2 * lax.rem(z + 1 + k, 4) + (1 - y if half == 0 else y)

    def part(half, k, offset, count=PAIRED):
        slot = group(half, k) * GROUP + c * HALF + offset
        return [dot(r.left_t[r.left_ids[slot + i]], r.right_pool[r.right_ids[slot + i]]) for i in range(count)]

    def mine(batch):
        return x * 8 + PAIRED * batch

    def other(batch):
        return (1 - x) * 8 + PAIRED * batch

    both = QUART

    def link(kind, k, stage, land, to):
        return pltpu.make_async_remote_copy(
            src_ref=stage, dst_ref=land, send_sem=r.send_sems.at[kind, k], recv_sem=r.recv_sems.at[kind, k],
            device_id=to, device_id_type=MESH,
        )

    def along_x(batch, half, k):
        return link(2 * batch + half, k, r.x_stage.at[batch, half, k], r.x_land.at[batch, half, k], to_x)

    def along_y_both(k):
        return link(4, k, r.yb_stage.at[k], r.yb_land.at[k], to_y)

    def along_y(batch, k):
        return link(5 + batch, k, r.ym_stage.at[batch, k], r.ym_land.at[batch, k], to_y)

    def along_z_both(k):
        return link(7, k, r.zb_stage.at[k], r.zb_land.at[k], (samp, group(1, k)))

    def along_z(batch, k):
        return link(8 + batch, k, r.zm_stage.at[batch, k], r.zm_land.at[batch, k], (samp, group(1, k)))

    def last():
        return link(10, 0, r.both_stage.at[1 - x], r.both_land, to_x)

    def send_x(batch, half, k):
        for i, value in enumerate(part(half, k, other(batch))):
            r.x_stage[batch, half, k, i] = value.astype(LOW)
        along_x(batch, half, k).start()

    def add_x_send_y(batch, k):
        values = part(0, k, mine(batch))
        along_x(batch, 0, k).wait_recv()
        for i, value in enumerate(values):
            r.ym_stage[batch, k, i] = (value + r.x_land[batch, 0, k, i].astype(FULL)).astype(LOW)
        along_y(batch, k).start()

    def add_both_send_z(batch, k):
        values = part(1, k, mine(batch))
        along_x(batch, 1, k).wait_recv()
        values = [value + r.x_land[batch, 1, k, i].astype(FULL) for i, value in enumerate(values)]
        along_y(batch, k).wait_recv()
        for i, value in enumerate(values):
            r.zm_stage[batch, k, i] = (value + r.ym_land[batch, k, i].astype(FULL)).astype(LOW)

        @pl.when(k < 3)
        def send_on():
            along_z(batch, k).start()

    def each(step):
        def body(k, carry):
            step(k)
            return carry

        lax.fori_loop(0, 4, body, 0)

    def slot_of(i, far=False):
        side = (1 - x) if far else x
        return c * HALF + (side * 8 + i if i < QUART else QUART + 2 * side + i - QUART)

    def share(kind, k, src, dst, to):
        return pltpu.make_async_remote_copy(
            src_ref=src, dst_ref=dst, send_sem=r.share_send.at[kind, k], recv_sem=r.share_recv.at[kind, k],
            device_id=to, device_id_type=MESH,
        )

    def grad_to(kind, pair, to):
        place_out = r.grads_out.at[pl.ds(slot_of(PAIRED * pair), PAIRED)]
        return share(kind, pair, r.own.at[pl.ds(PAIRED * pair, PAIRED)], place_out, to)

    def grad_on(pair):
        place_out = r.grads_out.at[pl.ds(slot_of(PAIRED * pair, True), PAIRED)]
        return share(2, pair, place_out, place_out, to_c)

    def grad_kept(pair):
        place_out = r.grads_out.at[pl.ds(slot_of(PAIRED * pair), PAIRED)]
        return pltpu.make_async_copy(r.own.at[pl.ds(PAIRED * pair, PAIRED)], place_out, r.local_sems.at[6 + pair])

    def move_to(kind, i, to):
        return share(kind, i, r.staged.at[i], r.moves_out.at[slot_of(i)], to)

    def move_on(i):
        place_out = r.moves_out.at[slot_of(i, True)]
        return share(5, i, place_out, place_out, to_c)

    def move_kept(i):
        return pltpu.make_async_copy(r.staged.at[i], r.moves_out.at[slot_of(i)], r.local_sems.at[i])

    def share_grads(pair):
        grad_to(0, pair, to_x).start()
        grad_to(1, pair, to_c).start()
        grad_kept(pair).start()

    def directions(pair):
        held = []
        stats = []
        for i in range(PAIRED * pair, PAIRED * pair + PAIRED):
            low = r.own[i]
            grad = low.astype(FULL)
            mean = jnp.sum(jnp.sum(grad * grad, axis=1, keepdims=True), axis=0, keepdims=True) / (BS * BS)
            shrink = 0.5 / (mean + 1e-06)
            low_t = grad.T.astype(LOW)
            slot = slot_of(i)
            stats.append(statistic(dot(low, low_t), shrink, r.left_diag[pl.ds(slot, 1)], eye))
            stats.append(statistic(dot(low_t, low), shrink, r.right_diag[pl.ds(slot, 1)], eye))
            held.append((i, low, lax.rsqrt(mean + 1e-06)))
        sides = roots(stats, eye)
        for n, (i, low, rate) in enumerate(held):
            high, rest = halves(sides[2 * n])
            turned = dot(jnp.concatenate([high, rest], axis=1), jnp.concatenate([low, low], axis=0)) * rate
            r.staged[i] = fine(halves(turned), halves(sides[2 * n + 1])).astype(LOW)
            move_to(3, i, to_x).start()
            move_to(4, i, to_c).start()
            move_kept(i).start()

    def finish_batch(batch):
        for k in range(3):
            along_z(batch, k).wait_recv()
        for i in range(PAIRED):
            value = r.zm_stage[batch, 3, i].astype(FULL)
            for k in range(3):
                value = value + r.zm_land[batch, k, i].astype(FULL)
            r.own[PAIRED * batch + i] = value.astype(LOW)
        share_grads(batch)

    def pass_on(pair):
        grad_to(0, pair, to_x).wait_recv()
        grad_on(pair).start()
        for i in range(PAIRED * pair, PAIRED * pair + PAIRED):
            move_to(3, i, to_x).wait_recv()
            move_on(i).start()

    for copy in here:
        copy.wait()

    @each
    def begin(k):
        for i, value in enumerate(part(0, k, both, QUART)):
            r.yb_stage[k, i] = value.astype(LOW)
        along_y_both(k).start()
        send_x(0, 0, k)

    @each
    def more(k):
        send_x(0, 1, k)

    row_copies[0].wait_recv()
    r.pair_rows[...] = r.rows_in[...] + r.row_land[0]
    row_copies.append(push(r.pair_rows, r.row_land.at[1], r.row_send.at[1], r.row_recv.at[1], to_x))

    @each
    def middle(k):
        add_x_send_y(0, k)
        values = part(1, k, both, QUART)
        along_y_both(k).wait_recv()
        for i, value in enumerate(values):
            r.zb_stage[k, i] = (value + r.yb_land[k, i].astype(FULL)).astype(LOW)

        @pl.when(k < 3)
        def send_on():
            along_z_both(k).start()

        send_x(1, 0, k)

    row_copies[1].wait_recv()
    r.chip_rows[...] = r.pair_rows[...] + r.row_land[1]
    row_copies.append(push(r.chip_rows, r.row_land.at[2], r.row_send.at[2], r.row_recv.at[2], to_y))

    @each
    def late(k):
        add_both_send_z(0, k)

    for k in range(3):
        along_z_both(k).wait_recv()
    for i in range(QUART):
        value = r.zb_stage[3, i].astype(FULL)
        for k in range(3):
            value = value + r.zb_land[k, i].astype(FULL)
        r.both_stage[i // 2, i % 2] = value.astype(LOW)
    last().start()

    @each
    def more_again(k):
        send_x(1, 1, k)

    @each
    def middle_again(k):
        add_x_send_y(1, k)

    row_copies[2].wait_recv()
    r.plane_rows[...] = r.chip_rows[...] + r.row_land[2]
    for step in range(3):
        row_copies.append(
            push(r.plane_rows, r.row_z.at[z], r.row_send.at[3 + step], r.row_recv.at[3 + step], to_z[step])
        )
    r.row_z[z] = r.plane_rows[...]
    last().wait_recv()
    for i in range(PAIRED):
        r.own[QUART + i] = (r.both_stage[x, i].astype(FULL) + r.both_land[i].astype(FULL)).astype(LOW)
    share_grads(2)
    directions(2)

    @each
    def late_again(k):
        add_both_send_z(1, k)

    finish_batch(0)
    directions(0)
    for step in range(3):
        row_copies[3 + step].wait_recv()
    r.rows_out[...] = (r.row_z[0] + r.row_z[1]) + (r.row_z[2] + r.row_z[3])
    finish_batch(1)
    pass_on(2)
    directions(1)
    pass_on(0)
    pass_on(1)
    for pair in range(3):
        grad_to(1, pair, to_c).wait_recv()
        grad_on(pair).wait_recv()
        grad_to(0, pair, to_x).wait_send()
        grad_to(1, pair, to_c).wait_send()
        grad_on(pair).wait_send()
        grad_kept(pair).wait()
    for i in range(6):
        move_to(4, i, to_c).wait_recv()
        move_on(i).wait_recv()
        move_to(3, i, to_x).wait_send()
        move_to(4, i, to_c).wait_send()
        move_on(i).wait_send()
        move_kept(i).wait()
    for copy in row_copies:
        copy.wait_send()
    last().wait_send()

    @each
    def drain(k):
        along_y_both(k).wait_send()
        for batch in range(2):
            along_x(batch, 0, k).wait_send()
            along_x(batch, 1, k).wait_send()
            along_y(batch, k).wait_send()

        @pl.when(k < 3)
        def sent_on():
            along_z_both(k).wait_send()
            for batch in range(2):
                along_z(batch, k).wait_send()

    swap.finish()


def update(left_ids, right_ids, rows, left_start, right_start, grad, left_pool, right_pool):
    return pl.pallas_call(
        update_kernel,
        out_shape=(SHAPES["rows"], shape((GROUP, BS, BS)), shape((GROUP, BS, BS)), SHAPES["pred"]),
        in_specs=[SMEM_IN] * 2 + [VMEM_AT] * 3 + [ANY_AT] * 3,
        out_specs=(VMEM_AT,) + (ANY_AT,) * 3,
        scratch_shapes=list(SUM_SCRATCH.values()),
        compiler_params=pltpu.CompilerParams(
            collective_id=1, has_side_effects=True, vmem_limit_bytes=VMEM_ASK
        ),
        cost_estimate=pl.CostEstimate(flops=36 << 30, bytes_accessed=40 << 20, transcendentals=0),
        name="update",
    )(left_ids, right_ids, rows, left_start, right_start, grad, left_pool, right_pool)


STEP = 8


def finish_kernel(
    grad, move, weight, left_diag, right_diag, rows, vecs, moment, input_grad, pred_one, pred_two,
    grad_out, left_out, right_out, new_out, low_out,
    rows_out, moment_out, vecs_out, input_out, pred_one_out, pred_two_out,
):
    eye = lax.broadcasted_iota(jnp.int32, (BS, BS), 0) == lax.broadcasted_iota(jnp.int32, (BS, BS), 1)
    at = pl.program_id(0)

    def mean(value):
        return jnp.sum(jnp.sum(value, axis=1, keepdims=True), axis=0, keepdims=True) / (BS * BS)

    for i in range(STEP):
        low = grad[i]
        full = low.astype(FULL)
        grad_out[i] = full
        shrink = 0.5 / (mean(full * full) + 1e-06)
        low_t = full.T.astype(LOW)
        left_out[i] = statistic(dot(low, low_t), shrink, left_diag[pl.ds(at * STEP + i, 1)], eye)
        right_out[i] = statistic(dot(low_t, low), shrink, right_diag[pl.ds(at * STEP + i, 1)], eye)
        step = move[i].astype(FULL)
        start = weight[i]
        ratio = jnp.sqrt(mean(start * start)) * lax.rsqrt(mean(step * step) + 1e-06)
        new = start - step_rate * ratio * step
        new_out[i] = new
        low_out[i] = new.astype(LOW)

    @pl.when(at == 0)
    def small():
        value = rows[...]
        scaled = value * lax.rsqrt(jnp.mean(value * value, axis=1, keepdims=True) + 1e-06)
        moments = 0.5 * moment[...] + 0.5 * scaled * scaled
        rows_out[...] = value
        moment_out[...] = moments
        vecs_out[...] = vecs[...] - vector_rate * scaled * lax.rsqrt(moments)
        input_out[...] = input_grad[...].astype(FULL)
        pred_one_out[...] = pred_one[...]
        pred_two_out[...] = pred_two[...]


def finish_slots(grads, moves, masters, left_start, right_start, rows, vecs, moment, input_grad, pred_one, pred_two):
    block = pl.BlockSpec((STEP, BS, BS), lambda i: (i, 0, 0))
    diag = pl.BlockSpec((GROUP, BS), lambda i: (0, 0))
    row = pl.BlockSpec((20, D), lambda i: (0, 0))
    wide = pl.BlockSpec((1, TOKENS, D), lambda i: (0, 0, 0))
    return pl.pallas_call(
        finish_kernel,
        grid=(GROUP // STEP,),
        compiler_params=pltpu.CompilerParams(vmem_limit_bytes=VMEM_ASK),
        out_shape=tuple(shape((GROUP, BS, BS), kind) for kind in (FULL, FULL, FULL, FULL, LOW))
        + (SHAPES["rows"],) * 3
        + (shape((1, TOKENS, D), FULL),)
        + (SHAPES["pred"],) * 2,
        in_specs=[block, block, block, diag, diag, row, row, row, wide, wide, wide],
        out_specs=(block,) * 5 + (row,) * 3 + (wide,) * 3,
        cost_estimate=pl.CostEstimate(flops=2 << 30, bytes_accessed=41 << 20, transcendentals=0),
        name="finish_slots",
    )(grads, moves, masters, left_start, right_start, rows, vecs, moment, input_grad, pred_one, pred_two)


def local_tuned(
    inputs,
    cot_first,
    cot_second,
    valid_flags,
    lead_steps,
    masters,
    assignment,
    left_start,
    right_start,
    vectors,
    vec_moment,
):
    left_pool, right_pool, pred_one, pred_two, input_grad, rows = model(
        assignment, lead_steps, valid_flags, masters, inputs, cot_first, cot_second, vectors
    )
    position = jnp.arange(NB, dtype=jnp.int32)
    inverse = jnp.sum(
        jnp.where(assignment[None, :] == position[:, None], position[None, :], 0), axis=1
    )
    left_ids, right_ids = pools_of(inverse)
    vec_grads, grads, moves, input_grad = update(
        left_ids, right_ids, rows, left_start, right_start, input_grad, left_pool, right_pool
    )
    (
        matrix_grads, left_stats, right_stats, new_masters, new_copies,
        vec_grads, vec_moments, new_vectors, input_grad, pred_one, pred_two,
    ) = finish_slots(
        grads, moves, masters, left_start, right_start, vec_grads, vectors, vec_moment, input_grad, pred_one, pred_two
    )
    return (
        pred_one,
        pred_two,
        input_grad,
        matrix_grads,
        left_stats,
        right_stats,
        new_masters,
        new_copies,
        vec_grads,
        vec_moments,
        new_vectors,
    )


def solution(mesh):
    placed = (
        P("samp", "blk", None),
        P("samp", "blk", None),
        P("samp", "blk", None),
        P("samp", "blk"),
        P(None, "samp"),
        P("blk", None, None),
        P(),
        P("blk", None),
        P("blk", None),
        P(),
        P(),
    )
    fits = mesh.shape["samp"] == 4 and mesh.shape["blk"] == 8
    return jax.shard_map(
        local_tuned if fits else local_any,
        mesh=mesh,
        in_specs=placed,
        out_specs=(
            P("samp", "blk", None),
            P("samp", "blk", None),
            P("samp", "blk", None),
            P("blk", None, None),
            P("blk", None, None),
            P("blk", None, None),
            P("blk", None, None),
            P("blk", None, None),
            P(),
            P(),
            P(),
        ),
        check_vma=False,
    )
```

```python
import functools
import math

import jax
import ml_dtypes
import jax.numpy as jnp
from jax import lax
from jax.experimental import pallas as pl
from jax.experimental.pallas import tpu as pltpu
from jax.sharding import PartitionSpec as P

D = 1024
HEADS = 16
FF = 4096
HD = 64
LEADS = 8
BS = 256
ITERS = 6
NB = 192


HIGH = lax.Precision.HIGHEST
step_rate = 0.5
vector_rate = 0.3
masked = 1000000000.0


def assemble(blocks, height, breadth):
    return (
        blocks.reshape(height // BS, breadth // BS, BS, BS)
        .transpose(0, 2, 1, 3)
        .reshape(height, breadth)
    )


def carve(matrix):
    height, breadth = matrix.shape
    return (
        matrix.reshape(height // BS, BS, breadth // BS, BS)
        .transpose(0, 2, 1, 3)
        .reshape(-1, BS, BS)
    )


def unpack(blocks):
    first_end = 3 * D * D // (BS * BS)
    second_end = first_end + D * D // (BS * BS)
    third_end = second_end + D * FF // (BS * BS)
    qkv_weight = assemble(blocks[:first_end], D, 3 * D)
    out_weight = assemble(blocks[first_end:second_end], D, D)
    up_weight = assemble(blocks[second_end:third_end], D, FF)
    down_weight = assemble(blocks[third_end:], FF, D)
    return (qkv_weight, out_weight, up_weight, down_weight)


def norm_layer(value, gain, shift):
    centred = value - jnp.mean(value, axis=-1, keepdims=True)
    spread = jnp.mean(centred * centred, axis=-1, keepdims=True)
    return centred * lax.rsqrt(spread + 1e-06) * gain + shift


def gelu_exact(value):
    return jax.nn.gelu(value, approximate=False)


def heads_of(tensor):
    return tensor.reshape(tensor.shape[0], tensor.shape[1], HEADS, HD)


def split_rows(member, count, width):
    shaped = member.reshape((member.shape[0], count, width) + member.shape[2:])
    return jnp.moveaxis(shaped, 1, 0)


def in_blocks(update, carry, members, length):
    width = math.gcd(length, 1024)
    count = length // width
    if count == 1:
        return update(carry, members, 0)
    stacked = tuple([split_rows(member, count, width) for member in members])
    offsets = jnp.arange(count, dtype=jnp.int32) * width

    def advance(state, item):
        return (update(state, item[0], item[1]), None)

    result, unused = lax.scan(advance, carry, (stacked, offsets))
    return result


def forward_update(query_heads, scaling):

    def update(carry, members, offset):
        running_max, running_sum, weighted = carry
        key_part, value_part, flag_part = members
        bias = (flag_part.astype(jnp.float32) - 1.0) * masked
        scores = (
            jnp.einsum(
                "sqhd,skhd->shqk",
                query_heads,
                heads_of(key_part),
                preferred_element_type=jnp.float32,
            )
            * scaling
            + bias[:, None, None, :]
        )
        new_max = jnp.maximum(running_max, jnp.max(scores, axis=-1))
        shrink = jnp.exp(running_max - new_max)
        expos = jnp.exp(scores - new_max[..., None])
        running_sum = running_sum * shrink + jnp.sum(expos, axis=-1)
        weighted = weighted * shrink[..., None] + jnp.einsum(
            "shqk,skhd->shqd",
            expos.astype(jnp.bfloat16),
            heads_of(value_part),
            preferred_element_type=jnp.float32,
        )
        return (new_max, running_sum, weighted)

    return update


def query_grad_update(query_heads, dout_heads, log_total, inner, scaling):

    def update(carry, members, offset):
        key_part, value_part, flag_part = members
        bias = (flag_part.astype(jnp.float32) - 1.0) * masked
        scores = (
            jnp.einsum(
                "sqhd,skhd->shqk",
                query_heads,
                heads_of(key_part),
                preferred_element_type=jnp.float32,
            )
            * scaling
            + bias[:, None, None, :]
        )
        probs = jnp.exp(scores - log_total[..., None])
        dprobs = jnp.einsum(
            "sqhd,skhd->shqk", dout_heads, heads_of(value_part), preferred_element_type=jnp.float32
        )
        dscores = (probs * (dprobs - inner[..., None])).astype(jnp.bfloat16)
        return (
            carry
            + jnp.einsum(
                "shqk,skhd->sqhd", dscores, heads_of(key_part), preferred_element_type=jnp.float32
            )
            * scaling
        )

    return update


def key_grad_update(key_heads, value_heads, key_bias, total_rows, inner_rows, scaling, anchor):

    def update(carry, members, offset):
        grad_keys, grad_values = carry
        query_part, dout_part = members
        length = query_part.shape[1]
        total_part = jnp.transpose(
            lax.dynamic_slice_in_dim(total_rows, anchor + offset, length, 1), (0, 2, 1)
        )
        inner_part = jnp.transpose(
            lax.dynamic_slice_in_dim(inner_rows, anchor + offset, length, 1), (0, 2, 1)
        )
        query_heads = heads_of(query_part)
        dout_heads = heads_of(dout_part)
        scores = (
            jnp.einsum(
                "sqhd,skhd->shqk", query_heads, key_heads, preferred_element_type=jnp.float32
            )
            * scaling
            + key_bias[:, None, None, :]
        )
        probs = jnp.exp(scores - total_part[..., None])
        dprobs = jnp.einsum(
            "sqhd,skhd->shqk", dout_heads, value_heads, preferred_element_type=jnp.float32
        )
        dscores = (probs * (dprobs - inner_part[..., None])).astype(jnp.bfloat16)
        grad_values = grad_values + jnp.einsum(
            "shqk,sqhd->skhd",
            probs.astype(jnp.bfloat16),
            dout_heads,
            preferred_element_type=jnp.float32,
        )
        grad_keys = (
            grad_keys
            + jnp.einsum(
                "shqk,sqhd->skhd", dscores, query_heads, preferred_element_type=jnp.float32
            )
            * scaling
        )
        return (grad_keys, grad_values)

    return update


def invert_root(stat):
    identity = jnp.eye(stat.shape[0], dtype=jnp.float32)
    frobenius = jnp.sqrt(jnp.sum(stat * stat))
    approx = identity * lax.rsqrt(jnp.sqrt(frobenius))
    moving = stat / frobenius
    for iteration in range(ITERS):
        factor = (5.0 * identity - moving) * 0.25
        approx = jnp.dot(approx, factor, precision=HIGH)
        square = jnp.dot(factor, factor, precision=HIGH)
        moving = jnp.dot(jnp.dot(square, square, precision=HIGH), moving, precision=HIGH)
    return approx


def precondition(gradient, left_diag, right_diag, weight):
    scaled = gradient * lax.rsqrt(jnp.mean(gradient * gradient) + 1e-06)
    identity = jnp.eye(BS, dtype=jnp.float32)
    left_new = 0.5 * identity * left_diag[None, :] + 0.5 * jnp.dot(scaled, scaled.T, precision=HIGH)
    right_new = 0.5 * identity * right_diag[None, :] + 0.5 * jnp.dot(
        scaled.T, scaled, precision=HIGH
    )
    direction = jnp.dot(
        jnp.dot(invert_root(left_new), scaled, precision=HIGH),
        invert_root(right_new),
        precision=HIGH,
    )
    ratio = jnp.sqrt(jnp.mean(weight * weight)) * lax.rsqrt(jnp.mean(direction * direction) + 1e-06)
    return (left_new, right_new, weight - step_rate * ratio * direction)


MESH = pl.DeviceIdType.MESH
LOW = jnp.bfloat16
FULL = jnp.float32
VMEM_ASK = 60 * 1024 * 1024
GROUP = 24
HALF = 12
QUART = 4


def place():
    samp = lax.axis_index("samp")
    blk = lax.axis_index("blk")
    return (lax.div(samp, 2), lax.rem(samp, 2), lax.div(blk, 2), lax.rem(blk, 2))


def meet(devices):
    barrier = pltpu.get_barrier_semaphore()
    for device in devices:
        pl.semaphore_signal(barrier, inc=1, device_id=device, device_id_type=MESH)
    pl.semaphore_wait(barrier, len(devices))


def meet_all():
    barrier = pltpu.get_barrier_semaphore()
    samp = lax.axis_index("samp")
    blk = lax.axis_index("blk")

    def tell(at, carry):
        to = lax.rem(samp * 8 + blk + at, 32)
        pl.semaphore_signal(
            barrier, inc=1, device_id=(lax.div(to, 8), lax.rem(to, 8)), device_id_type=MESH
        )
        return carry

    lax.fori_loop(1, 32, tell, 0)
    pl.semaphore_wait(barrier, 31)


def turned_pair(n):
    return 2 * lax.rem(n, 2) + lax.div(n, 2)


class Swap:
    def __init__(self, local_sems, send_sems, recv_sems, first=0):
        x, c, z, y = place()
        self.first = first
        self.stays = z == turned_pair(2 * x + c)
        self.to = (turned_pair(z), 2 * turned_pair(2 * x + c) + y)
        self.sems = (local_sems, send_sems, recv_sems)
        self.pairs = []

    def start(self, src, dst):
        at = self.first + len(self.pairs)
        local_sems, send_sems, recv_sems = self.sems
        local = pltpu.make_async_copy(src, dst, local_sems.at[at])
        away = pltpu.make_async_remote_copy(
            src_ref=src, dst_ref=dst, send_sem=send_sems.at[at], recv_sem=recv_sems.at[at],
            device_id=self.to, device_id_type=MESH,
        )
        self.pairs.append((local, away))

        @pl.when(self.stays)
        def keep():
            local.start()

        @pl.when(jnp.logical_not(self.stays))
        def send():
            away.start()

    def finish(self):
        @pl.when(self.stays)
        def kept():
            for local, away in self.pairs:
                local.wait()

        @pl.when(jnp.logical_not(self.stays))
        def sent():
            for local, away in self.pairs:
                away.wait()


def push(src, dst, send, recv, device):
    copy = pltpu.make_async_remote_copy(
        src_ref=src, dst_ref=dst, send_sem=send, recv_sem=recv, device_id=device, device_id_type=MESH
    )
    copy.start()
    return copy


FIRST, SECOND, BOTH, CROSS = range(4)
SIZES = (2, 2, 3, 1)


def gather_blocks(r, notes, while_last):
    x, c, z, y = place()
    samp = 2 * x + c
    blk = 2 * z + y
    to_y = (samp, 2 * z + 1 - y)
    to_x = (2 * (1 - x) + c, blk)
    to_c = (2 * x + 1 - c, blk)
    base = c * HALF
    out = r.weights
    starts = (base + x * 8, base + x * 8 + 2, base + QUART, base + QUART + 3)
    far_starts = (base + (1 - x) * 8, base + (1 - x) * 8 + 2)
    other = (1 - c) * HALF
    parts = [base + x * 8, base + QUART, base + (1 - x) * 8, other, other + QUART, other + 2 * QUART]
    notes_out, note_send, note_recv = r.notes_land, r.note_send, r.note_recv

    def load(at):
        return pltpu.make_async_copy(
            r.masters.at[pl.ds(parts[at], QUART)], r.wide.at[at % 2], r.load_sems.at[at]
        )

    def ready(at):
        load(at).wait()
        out[pl.ds(blk * GROUP + parts[at], QUART)] = r.wide[at % 2].astype(LOW)
        if at + 2 < len(parts):
            load(at + 2).start()

    def copy(group, start, size, sems, at, device):
        place_out = out.at[pl.ds(group * GROUP + start, size)]
        return pltpu.make_async_remote_copy(
            src_ref=place_out, dst_ref=place_out,
            send_sem=sems.at[(0,) + at], recv_sem=sems.at[(1,) + at], device_id=device, device_id_type=MESH,
        )

    def z_copy(kind, way, origin):
        to = (samp, blk + (2 if way == 0 else -2))
        return copy(2 * origin + y, starts[kind], SIZES[kind], r.z_sems, (kind, way, origin), to)

    def z_cross(way, origin, side):
        to = (samp, blk + (2 if way == 0 else -2))
        return copy(2 * origin + side, starts[CROSS], 1, r.z_sems, (CROSS + side, way, origin), to)

    def y_copy(kind, origin):
        return copy(2 * origin + y, starts[kind], SIZES[kind], r.y_sems, (kind, origin), to_y)

    def y_landed(kind, origin):
        return copy(2 * origin + 1 - y, starts[kind], SIZES[kind], r.y_sems, (kind, origin), to_y)

    def x_copy(kind, group):
        return copy(group, starts[kind], SIZES[kind], r.x_sems, (kind, group), to_x)

    def x_landed(kind, group):
        return copy(group, far_starts[kind], SIZES[kind], r.x_sems, (kind, group), to_x)

    def core_copy(kind, group):
        return copy(group, starts[kind], SIZES[kind], r.core_sems, (kind, group), to_c)

    def far_copy(kind, group):
        return copy(group, far_starts[kind], SIZES[kind], r.far_sems, (kind, group), to_c)

    def on_from_here(kind, group):
        if kind in (FIRST, SECOND):
            x_copy(kind, group).start()
        core_copy(kind, group).start()

    def begin(kind):
        @pl.when(z < 3)
        def up():
            z_copy(kind, 0, z).start()

        @pl.when(z > 0)
        def down():
            z_copy(kind, 1, z).start()

        y_copy(kind, z).start()

    def z_step(kind, distance):
        for way in (0, 1):
            origin = z - distance if way == 0 else z + distance

            @pl.when(origin >= 0 if way == 0 else origin <= 3)
            def arrived():
                z_copy(kind, way, origin).wait_recv()

                @pl.when(z < 3 if way == 0 else z > 0)
                def onward():
                    z_copy(kind, way, origin).start()

                y_copy(kind, origin).start()
                on_from_here(kind, 2 * origin + y)

    def y_step(kind, distance):
        for way in (0, 1):
            origin = z - distance if way == 0 else z + distance

            @pl.when(origin >= 0 if way == 0 else origin <= 3)
            def arrived():
                y_landed(kind, origin).wait_recv()
                on_from_here(kind, 2 * origin + 1 - y)

    def y_own(kind):
        y_landed(kind, z).wait_recv()
        on_from_here(kind, 2 * z + 1 - y)

    def cross_step(distance):
        for side in (0, 1):
            for way in (0, 1):
                origin = z - distance if way == 0 else z + distance

                @pl.when(origin >= 0 if way == 0 else origin <= 3)
                def arrived():
                    z_cross(way, origin, side).wait_recv()

                    @pl.when(z < 3 if way == 0 else z > 0)
                    def onward():
                        z_cross(way, origin, side).start()

                    core_copy(CROSS, 2 * origin + side).start()

    def x_step(kind, distance, same):
        for way in (0, 1):
            origin = z - distance if way == 0 else z + distance

            @pl.when(origin >= 0 if way == 0 else origin <= 3)
            def arrived():
                group = 2 * origin + (y if same else 1 - y)
                x_landed(kind, group).wait_recv()
                far_copy(kind, group).start()

    def x_own(kind):
        x_landed(kind, 2 * z + 1 - y).wait_recv()
        far_copy(kind, 2 * z + 1 - y).start()

    note_local = pltpu.make_async_copy(notes, notes_out.at[blk], r.load_sems.at[6])

    def note_copy(j, origin):
        return pltpu.make_async_remote_copy(
            src_ref=notes, dst_ref=notes_out.at[origin], send_sem=note_send.at[j], recv_sem=note_recv.at[origin],
            device_id=(j // 2, 2 * turned_pair(samp) + j % 2), device_id_type=MESH,
        )

    stays = z == turned_pair(samp)

    def is_me(j):
        return jnp.logical_and(stays, 2 * samp + y == j)

    def here_from(j):
        return jnp.logical_and(stays, blk == j)

    load(0).start()
    load(1).start()
    meet_all()
    r.swap_rows.start(r.rows_in, r.rows_land)
    def cross_begin():
        y_landed(CROSS, z).wait_recv()
        core_copy(CROSS, 2 * z + 1 - y).start()
        for way, there in ((0, z < 3), (1, z > 0)):
            for side in (0, 1):
                @pl.when(there)
                def both_sides():
                    z_cross(way, z, side).start()

    ready(0)
    begin(FIRST)
    begin(SECOND)
    ready(1)
    y_copy(CROSS, z).start()
    for j in range(8):

        @pl.when(jnp.logical_not(is_me(j)))
        def send_note():
            note_copy(j, blk).start()

    @pl.when(stays)
    def keep_note():
        note_local.start()

    for at in range(2, len(parts)):
        ready(at)
    z_step(FIRST, 1)
    z_step(SECOND, 1)
    y_own(SECOND)
    z_step(FIRST, 2)
    begin(BOTH)
    z_step(SECOND, 2)
    y_step(FIRST, 1)
    y_own(FIRST)
    y_own(BOTH)
    z_step(SECOND, 3)
    x_step(FIRST, 1, True)
    y_step(SECOND, 1)
    x_own(SECOND)
    z_step(BOTH, 1)
    cross_begin()
    x_step(FIRST, 2, True)
    z_step(FIRST, 3)
    y_step(FIRST, 2)
    cross_step(1)
    x_step(SECOND, 1, True)
    x_own(FIRST)
    y_step(SECOND, 2)
    y_step(SECOND, 3)
    x_step(FIRST, 1, False)
    z_step(BOTH, 2)
    x_step(SECOND, 1, False)
    y_step(BOTH, 1)
    x_step(FIRST, 2, False)
    z_step(BOTH, 3)
    x_step(SECOND, 2, True)
    y_step(FIRST, 3)
    x_step(FIRST, 3, True)
    cross_step(2)
    y_step(BOTH, 2)
    x_step(SECOND, 3, False)
    x_step(SECOND, 2, False)
    x_step(SECOND, 3, True)
    cross_step(3)
    y_step(BOTH, 3)
    x_step(FIRST, 3, False)

    while_last()
    other_starts = (other + x * 8, other + x * 8 + 2, other + QUART, other + QUART + 3)
    other_far = (other + (1 - x) * 8, other + (1 - x) * 8 + 2)

    def settle(group, carry):
        @pl.when(group != blk)
        def other_group():
            for kind in range(4):
                copy(group, other_starts[kind], SIZES[kind], r.core_sems, (kind, group), to_c).wait_recv()
                core_copy(kind, group).wait_send()
            for kind in (FIRST, SECOND):
                copy(group, other_far[kind], SIZES[kind], r.far_sems, (kind, group), to_c).wait_recv()
                far_copy(kind, group).wait_send()
                x_copy(kind, group).wait_send()

        return carry

    lax.fori_loop(0, 8, settle, 0)

    def sent_along(origin, carry):
        for kind in (FIRST, SECOND, BOTH):
            y_copy(kind, origin).wait_send()

            @pl.when(jnp.logical_and(origin <= z, z < 3))
            def up():
                z_copy(kind, 0, origin).wait_send()

            @pl.when(jnp.logical_and(origin >= z, z > 0))
            def down():
                z_copy(kind, 1, origin).wait_send()

        for side in (0, 1):
            @pl.when(jnp.logical_and(origin <= z, z < 3))
            def cross_up():
                z_cross(0, origin, side).wait_send()

            @pl.when(jnp.logical_and(origin >= z, z > 0))
            def cross_down():
                z_cross(1, origin, side).wait_send()

        return carry

    lax.fori_loop(0, 4, sent_along, 0)
    y_copy(CROSS, z).wait_send()
    for j in range(8):

        @pl.when(jnp.logical_not(is_me(j)))
        def sent_note():
            note_copy(j, blk).wait_send()

        @pl.when(jnp.logical_not(here_from(j)))
        def got_note():
            note_copy(j, j).wait_recv()

    @pl.when(stays)
    def kept_note():
        note_local.wait()


def local_any(
    inputs,
    cot_first,
    cot_second,
    valid_flags,
    lead_steps,
    masters,
    assignment,
    left_start,
    right_start,
    vectors,
    vec_moment,
):
    copies = lax.all_gather(masters.astype(jnp.bfloat16), "blk", axis=0, tiled=True)
    blocks = jnp.take(copies, assignment, axis=0)
    qkv_weight, out_weight, up_weight, down_weight = unpack(blocks)
    scaling = HD ** (-0.5)
    flags_low = valid_flags.astype(jnp.bfloat16)
    key_bias = (valid_flags.astype(jnp.float32) - 1.0) * masked
    lead_base = 8 + FF // D
    lead_table = vectors[lead_base:]
    samples = inputs.shape[0]
    patches = inputs.shape[1]

    def forward(hidden_in, lead_ids):
        chosen = (lead_ids[:, None] == jnp.arange(LEADS, dtype=jnp.int32)[None, :]).astype(
            jnp.float32
        )
        lead_rows = jnp.dot(chosen, lead_table, precision=HIGH)
        hidden = hidden_in + lead_rows[:, None, :]
        normed_low = norm_layer(hidden, vectors[0], vectors[1]).astype(jnp.bfloat16)
        packed = jnp.einsum(
            "spd,de->spe", normed_low, qkv_weight, preferred_element_type=jnp.float32
        )
        queries = (packed[..., :D] + vectors[2]).astype(jnp.bfloat16)
        keys_low = packed[..., D : 2 * D].astype(jnp.bfloat16)
        values_low = (packed[..., 2 * D :] + vectors[3]).astype(jnp.bfloat16)
        start_state = (
            jnp.full((samples, HEADS, patches), -1e30, jnp.float32),
            jnp.zeros((samples, HEADS, patches), jnp.float32),
            jnp.zeros((samples, HEADS, patches, HD), jnp.float32),
        )
        update = forward_update(heads_of(queries), scaling)
        gathered = None
        piece = (
            lax.all_gather(keys_low, "blk", axis=1, tiled=True),
            lax.all_gather(values_low, "blk", axis=1, tiled=True),
            lax.all_gather(flags_low, "blk", axis=1, tiled=True),
        )
        running_max, running_sum, weighted = in_blocks(
            update, start_state, piece, piece[0].shape[1]
        )
        attended = jnp.transpose(weighted / running_sum[..., None], (0, 2, 1, 3)).reshape(
            samples, patches, D
        )
        log_total = running_max + jnp.log(running_sum)
        attended_low = attended.astype(jnp.bfloat16)
        middle = (
            hidden
            + jnp.einsum(
                "spd,de->spe", attended_low, out_weight, preferred_element_type=jnp.float32
            )
            + vectors[4]
        )
        normed_two = norm_layer(middle, vectors[5], vectors[6]).astype(jnp.bfloat16)
        upward = jnp.einsum(
            "spd,df->spf", normed_two, up_weight, preferred_element_type=jnp.float32
        ) + vectors[8:lead_base].reshape(FF)
        activated = gelu_exact(upward).astype(jnp.bfloat16)
        result = (
            middle
            + jnp.einsum("spf,fd->spd", activated, down_weight, preferred_element_type=jnp.float32)
            + vectors[7]
        )
        saved = (
            hidden,
            normed_low,
            queries,
            keys_low,
            values_low,
            attended,
            attended_low,
            log_total,
            middle,
            normed_two,
            upward,
            activated,
            chosen,
            gathered,
        )
        return (result, saved)

    def backward(grad_out, saved):
        (
            hidden,
            normed_low,
            queries,
            keys_low,
            values_low,
            attended,
            attended_low,
            log_total,
            middle,
            normed_two,
            upward,
            activated,
            chosen,
            gathered,
        ) = saved
        grad_two = grad_out.astype(jnp.bfloat16)
        down_grad = jnp.einsum(
            "spf,spd->fd", activated, grad_two, preferred_element_type=jnp.float32
        )
        down_bias = jnp.sum(grad_two.astype(jnp.float32), axis=(0, 1))
        grad_act = jnp.einsum(
            "spd,fd->spf", grad_two, down_weight, preferred_element_type=jnp.float32
        )
        gelu_value, gelu_pull = jax.vjp(gelu_exact, upward)
        grad_up = gelu_pull(grad_act)[0].astype(jnp.bfloat16)
        up_grad = jnp.einsum("spd,spf->df", normed_two, grad_up, preferred_element_type=jnp.float32)
        up_bias = jnp.sum(grad_up.astype(jnp.float32), axis=(0, 1))
        grad_normed_two = jnp.einsum(
            "spf,df->spd", grad_up, up_weight, preferred_element_type=jnp.float32
        )
        norm_value, norm_pull = jax.vjp(norm_layer, middle, vectors[5], vectors[6])
        grad_middle_norm, gain_two, shift_two = norm_pull(grad_normed_two)
        grad_middle = grad_out + grad_middle_norm
        grad_one = grad_middle.astype(jnp.bfloat16)
        out_grad = jnp.einsum(
            "spd,spe->de", attended_low, grad_one, preferred_element_type=jnp.float32
        )
        out_bias = jnp.sum(grad_one.astype(jnp.float32), axis=(0, 1))
        grad_attended = jnp.einsum(
            "spe,de->spd", grad_one, out_weight, preferred_element_type=jnp.float32
        ).astype(jnp.bfloat16)
        inner = jnp.sum(
            (grad_attended.astype(jnp.float32) * attended).reshape(samples, patches, HEADS, HD),
            axis=-1,
        )
        inner_heads = jnp.transpose(inner, (0, 2, 1))
        zero_query = jnp.zeros((samples, patches, HEADS, HD), jnp.float32)
        update_query = query_grad_update(
            heads_of(queries), heads_of(grad_attended), log_total, inner_heads, scaling
        )
        piece = (
            lax.all_gather(keys_low, "blk", axis=1, tiled=True),
            lax.all_gather(values_low, "blk", axis=1, tiled=True),
            lax.all_gather(flags_low, "blk", axis=1, tiled=True),
        )
        grad_query = in_blocks(update_query, zero_query, piece, piece[0].shape[1])
        total_rows, inner_rows = (
            lax.all_gather(jnp.transpose(log_total, (0, 2, 1)), "blk", axis=1, tiled=True),
            lax.all_gather(inner, "blk", axis=1, tiled=True),
        )
        key_heads = heads_of(keys_low)
        value_heads = heads_of(values_low)
        zero_pair = (zero_query, zero_query)
        piece = (
            lax.all_gather(queries, "blk", axis=1, tiled=True),
            lax.all_gather(grad_attended, "blk", axis=1, tiled=True),
        )
        update_keys = key_grad_update(
            key_heads, value_heads, key_bias, total_rows, inner_rows, scaling, jnp.int32(0)
        )
        grad_keys, grad_values = in_blocks(update_keys, zero_pair, piece, piece[0].shape[1])
        grad_packed = jnp.concatenate(
            [
                grad_query.reshape(samples, patches, D),
                grad_keys.reshape(samples, patches, D),
                grad_values.reshape(samples, patches, D),
            ],
            axis=-1,
        ).astype(jnp.bfloat16)
        qkv_grad = jnp.einsum(
            "spd,spe->de", normed_low, grad_packed, preferred_element_type=jnp.float32
        )
        query_bias = jnp.sum(grad_packed[..., :D].astype(jnp.float32), axis=(0, 1))
        value_bias = jnp.sum(grad_packed[..., 2 * D :].astype(jnp.float32), axis=(0, 1))
        grad_normed = jnp.einsum(
            "spe,de->spd", grad_packed, qkv_weight, preferred_element_type=jnp.float32
        )
        first_value, first_pull = jax.vjp(norm_layer, hidden, vectors[0], vectors[1])
        grad_hidden_norm, gain_one, shift_one = first_pull(grad_normed)
        grad_hidden = grad_middle + grad_hidden_norm
        lead_grad = jnp.dot(chosen.T, jnp.sum(grad_hidden, axis=1), precision=HIGH)
        vec_rows = jnp.concatenate(
            [
                gain_one[None],
                shift_one[None],
                query_bias[None],
                value_bias[None],
                out_bias[None],
                gain_two[None],
                shift_two[None],
                down_bias[None],
                up_bias.reshape(FF // D, D),
                lead_grad,
            ],
            axis=0,
        )
        return (grad_hidden, (qkv_grad, out_grad, up_grad, down_grad), vec_rows)

    earlier, saved_one = forward(inputs.astype(jnp.float32), lead_steps[0])
    later, saved_two = forward(earlier, lead_steps[1])
    grad_between, mats_two, vec_two = backward(cot_second.astype(jnp.float32), saved_two)
    input_grad, mats_one, vec_one = backward(
        cot_first.astype(jnp.float32) + grad_between, saved_one
    )
    grad_blocks = jnp.concatenate(
        [
            carve(mats_one[0] + mats_two[0]),
            carve(mats_one[1] + mats_two[1]),
            carve(mats_one[2] + mats_two[2]),
            carve(mats_one[3] + mats_two[3]),
        ],
        axis=0,
    )
    position = jnp.arange(NB, dtype=jnp.int32)
    inverse = jnp.sum(
        jnp.where(assignment[None, :] == position[:, None], position[None, :], 0), axis=1
    )
    slotted = jnp.take(grad_blocks, inverse, axis=0)
    shared = lax.psum_scatter(slotted, "blk", scatter_dimension=0, tiled=True)
    matrix_grads = lax.psum(shared.astype(jnp.bfloat16), "samp").astype(jnp.float32)
    vec_grads = lax.psum(vec_one + vec_two, ("samp", "blk"))
    left_stats, right_stats, new_masters = jax.vmap(precondition)(
        matrix_grads, left_start, right_start, masters
    )
    scaled_vec = vec_grads * lax.rsqrt(
        jnp.mean(vec_grads * vec_grads, axis=1, keepdims=True) + 1e-06
    )
    vec_moments = 0.5 * vec_moment + 0.5 * scaled_vec * scaled_vec
    new_vectors = vectors - vector_rate * scaled_vec * lax.rsqrt(vec_moments)
    return (
        earlier.astype(jnp.bfloat16),
        later.astype(jnp.bfloat16),
        input_grad,
        matrix_grads,
        left_stats,
        right_stats,
        new_masters,
        new_masters.astype(jnp.bfloat16),
        vec_grads,
        vec_moments,
        new_vectors,
    )


TOKENS = 128
PAIR = 2 * HD
SEQ_ALL = 8 * TOKENS
QKV_AT, OUT_AT, UP_AT, DOWN_AT = 0, 48, 64, 128
WIDE = D // BS
DEEP = FF // BS
LEAD_AT = 8 + FF // D


def dot(left, right):
    return jnp.dot(left, right, preferred_element_type=FULL)


def dot_t(left, right):
    return lax.dot_general(left, right, (((1,), (1,)), ((), ())), preferred_element_type=FULL)


def normal(value):
    centred = value - jnp.mean(value, axis=-1, keepdims=True)
    rate = lax.rsqrt(jnp.mean(centred * centred, axis=-1, keepdims=True) + 1e-06)
    return (centred * rate, rate)


def normal_back(grad, unit, rate, gain):
    scaled = grad * gain
    return rate * (
        scaled
        - jnp.mean(scaled, axis=-1, keepdims=True)
        - unit * jnp.mean(scaled * unit, axis=-1, keepdims=True)
    )


def total(value):
    return jnp.sum(value, axis=0, keepdims=True)


def gelu_parts(value):
    phi = 0.5 + 0.5 * lax.erf(value * (0.5**0.5))
    return phi, value * phi


def gelu_slope(value, phi):
    return phi + value * jnp.exp(-0.5 * value * value) * ((2.0 * math.pi) ** -0.5)


class Weights:
    def __init__(self, slots, held):
        self.slots, self.held = slots, held

    def block(self, base, cols, row, col):
        return self.held[self.slots[base + row * cols + col]]

    def down_col(self, base, rows, cols, col):
        return jnp.concatenate([self.block(base, cols, row, col) for row in range(rows)], axis=0)

    def along_row(self, base, cols, row, first=0, last=None):
        return jnp.concatenate(
            [self.block(base, cols, row, col) for col in range(first, cols if last is None else last)], axis=1
        )


def lead_row(vecs, lead):
    row = jnp.zeros((1, D), FULL)
    for at in range(LEADS):
        row = row + jnp.where(lead == at, vecs[LEAD_AT + at : LEAD_AT + at + 1], 0.0)
    return row


def project(r, layer, hidden, vecs, weights):
    unit, unused = normal(hidden)
    normed = (unit * vecs[0:1] + vecs[1:2]).astype(LOW)
    for k in range(WIDE):
        r.left_held[layer, k] = normed[:, k * BS : (k + 1) * BS].T
    give_pool(r, True, layer, 0)
    for kind in (1, 0, 2):
        for step in range(WIDE):
            within = lax.rem(step + lax.div(r.plane.me, 2), WIDE)
            part = dot(normed, weights.down_col(QKV_AT, WIDE, 3 * WIDE, kind * WIDE + within))
            if kind != 1:
                row = 2 if kind == 0 else 3
                part = part + vecs[row : row + 1, pl.ds(pl.multiple_of(within * BS, BS), BS)]
            part = part.astype(LOW)
            for half in range(2):
                r.packed[kind, 2 * within + half] = part[:, half * PAIR : (half + 1) * PAIR]
                r.plane.send_or_keep(
                    r.packed.at[kind], r.held[layer].at[kind], r.in_sems[layer].at[kind], 2 * within + half
                )


def pool_at(left, kind):
    counts, bases = (LEFTS, LEFT_AT) if left else (RIGHTS, RIGHT_AT)
    return pl.ds(bases[kind], counts[kind])


def pool_copies(r, left, layer, kind):
    x, c, z, y = place()
    ids = pool_at(left, kind)
    at = (0 if left else 8) + 4 * layer + kind
    source = (r.left_held if left else r.right_held).at[layer, ids]

    def target(part):
        tokens = pl.ds((2 * part + layer) * TOKENS, TOKENS)
        return r.left_pool.at[ids, :, tokens] if left else r.right_pool.at[ids, tokens]

    here = pltpu.make_async_copy(source, target(0), r.pool_sems.at[0, at])
    there = pltpu.make_async_remote_copy(
        src_ref=source, dst_ref=target(1), send_sem=r.pool_sems.at[1, at], recv_sem=r.pool_sems.at[2, at],
        device_id=(2 * x + 1 - c, 2 * z + y), device_id_type=MESH,
    )
    return here, there


def give_pool(r, left, layer, kind):
    for copy in pool_copies(r, left, layer, kind):
        copy.start()


def feed(r, layer, hidden, vecs, weights, slope_held):
    attended = jnp.concatenate([r.o_land[j] for j in range(8)], axis=1)
    for k in range(WIDE):
        r.left_held[layer, WIDE + k] = attended[:, k * BS : (k + 1) * BS].T
    give_pool(r, True, layer, 1)
    branch = [dot(attended, weights.down_col(OUT_AT, WIDE, WIDE, n)) for n in range(WIDE)]
    middle = hidden + jnp.concatenate(branch, axis=1) + vecs[4:5]
    unit, unused = normal(middle)
    normed = (unit * vecs[5:6] + vecs[6:7]).astype(LOW)
    for k in range(WIDE):
        r.left_held[layer, 2 * WIDE + k] = normed[:, k * BS : (k + 1) * BS].T
    give_pool(r, True, layer, 2)
    per = D // BS
    for f in range(DEEP):
        bias = vecs[8 + f // per : 9 + f // per, (f % per) * BS : (f % per + 1) * BS]
        upward = dot(normed, weights.down_col(UP_AT, WIDE, DEEP, f)) + bias
        phi, activated = gelu_parts(upward)
        slope_held[f] = gelu_slope(upward, phi)
        activated = activated.astype(LOW)
        r.act_held[:, f * BS : (f + 1) * BS] = activated
        r.left_held[layer, 3 * WIDE + f] = activated.T
    give_pool(r, True, layer, 3)
    branch = [dot(r.act_held[...], weights.down_col(DOWN_AT, DEEP, WIDE, n)) for n in range(WIDE)]
    return middle, middle + jnp.concatenate(branch, axis=1) + vecs[7:8]


def feed_back(r, layer, grad_out, middle, slope_in, vecs, weights):
    rows = r.rows
    grad_two = grad_out.astype(LOW)
    for k in range(WIDE):
        r.right_held[layer, RIGHT_AT[3] + k] = grad_two[:, k * BS : (k + 1) * BS]
    give_pool(r, False, layer, 3)
    rows[7:8] += total(grad_two.astype(FULL))
    per = D // BS
    for f in range(DEEP):
        grad_act = dot_t(grad_two, weights.along_row(DOWN_AT, WIDE, f))
        grad_up = (grad_act * slope_in[f]).astype(LOW)
        r.right_held[layer, RIGHT_AT[2] + f] = grad_up
        rows[8 + f // per : 9 + f // per, (f % per) * BS : (f % per + 1) * BS] += total(grad_up.astype(FULL))
    give_pool(r, False, layer, 2)
    grad_up = jnp.concatenate([r.right_held[layer, RIGHT_AT[2] + f] for f in range(DEEP)], axis=1)
    grad_normed = jnp.concatenate(
        [dot_t(grad_up, weights.along_row(UP_AT, DEEP, k)) for k in range(WIDE)], axis=1
    )
    unit, rate = normal(middle)
    rows[5:6] += total(grad_normed * unit)
    rows[6:7] += total(grad_normed)
    grad_middle = grad_out + normal_back(grad_normed, unit, rate, vecs[5:6])
    grad_one = grad_middle.astype(LOW)
    for k in range(WIDE):
        r.right_held[layer, RIGHT_AT[1] + k] = grad_one[:, k * BS : (k + 1) * BS]
    give_pool(r, False, layer, 1)
    rows[4:5] += total(grad_one.astype(FULL))
    for k in range(WIDE):
        part = dot_t(grad_one, weights.along_row(OUT_AT, WIDE, k)).astype(LOW)
        for half in range(2):
            r.do_message[2 * k + half] = part[:, half * PAIR : (half + 1) * PAIR]
            r.plane.send_or_keep(r.do_message, r.do_land, r.do_sems[layer], 2 * k + half)
    return grad_middle


def project_back(r, layer, grad_middle, hidden, vecs, weights, lead):
    rows = r.rows

    def blocks_of_kind(kind):
        source, cols = (r.dq_land, slice(0, PAIR)) if kind == 0 else (r.dkv_land, slice((kind - 1) * PAIR, kind * PAIR))
        for within in range(WIDE):
            part = jnp.concatenate([source[2 * within, :, cols], source[2 * within + 1, :, cols]], axis=1)
            r.right_held[layer, kind * WIDE + within] = part
            if kind != 1:
                row = 2 if kind == 0 else 3
                rows[row : row + 1, within * BS : (within + 1) * BS] += total(part.astype(FULL))

    def back(first, last):
        part = jnp.concatenate([r.right_held[layer, n] for n in range(first, last)], axis=1)
        return jnp.concatenate(
            [dot_t(part, weights.along_row(QKV_AT, 3 * WIDE, k, first, last)) for k in range(WIDE)], axis=1
        )

    r.plane.received(r.dkv_land, r.dkv_sems[layer])
    blocks_of_kind(1)
    blocks_of_kind(2)
    grad_normed = back(WIDE, 3 * WIDE)
    r.plane.received(r.dq_land, r.dq_sems[layer])
    blocks_of_kind(0)
    give_pool(r, False, layer, 0)
    grad_normed = grad_normed + back(0, WIDE)
    unit, rate = normal(hidden)
    rows[0:1] += total(grad_normed * unit)
    rows[1:2] += total(grad_normed)
    grad_hidden = grad_middle + normal_back(grad_normed, unit, rate, vecs[0:1])
    sums = total(grad_hidden)
    for at in range(LEADS):
        rows[LEAD_AT + at : LEAD_AT + at + 1] += jnp.where(lead == at, sums, 0.0)
    return grad_hidden


def attend(r, layer):
    held, turned, stats, sems = r.held[layer], r.turned[layer], r.stats[layer], r.in_sems[layer]
    plane = r.plane
    plane.received(held.at[1], sems.at[1])
    keys = held[1].reshape(SEQ_ALL, PAIR).astype(FULL)
    for head in range(2):
        r.key_side[head] = key_columns(keys, r.neg[...], head).astype(LOW)

    def chunk(step, carry):
        at = lax.rem(step + lax.div(plane.me, 2), 4)
        first = pl.multiple_of(at * BS, BS)
        for half in range(2):
            plane.received_from(held.at[0], sems.at[0], 2 * at + half)
        queries = held[0, pl.ds(2 * at, 2)].reshape(BS, PAIR).astype(FULL)
        scales = []
        for head in range(2):
            scores = dot_t(r.key_side[head], query_columns(queries, head).astype(LOW))
            most = jnp.max(scores, axis=0, keepdims=True)
            expos = jnp.exp(scores - most)
            sums = jnp.sum(expos, axis=0, keepdims=True)
            r.expos[head] = expos.astype(LOW)
            stats[head : head + 1, pl.ds(first, BS)] = most + jnp.log(sums)
            scales.append(1.0 / sums)

        @pl.when(step == 0)
        def values_in():
            plane.received(held.at[2], sems.at[2])
            r.values_t[...] = held[2].reshape(SEQ_ALL, PAIR).T

        for head in range(2):
            side = slice(head * HD, (head + 1) * HD)
            turned[at, side] = dot(r.values_t[side], r.expos[head]) * scales[head]
        for half in range(2):
            to = 2 * at + half
            r.o_message[to] = turned[at, :, half * TOKENS : (half + 1) * TOKENS].astype(LOW).T
            plane.send_or_keep(r.o_message, r.o_land, r.o_sems[layer], to)
        return carry

    lax.fori_loop(0, SEQ_ALL // BS, chunk, 0)
    for kind in range(3):
        plane.sent(r.packed.at[kind], sems.at[kind])
    plane.received(r.o_land, r.o_sems[layer])
    plane.sent(r.o_message, r.o_sems[layer])


def attend_back(r, layer):
    held, turned, stats = r.held[layer], r.turned[layer], r.stats[layer]
    plane = r.plane
    queries = held[0].reshape(SEQ_ALL, PAIR).astype(FULL)
    keys = held[1].reshape(SEQ_ALL, PAIR).astype(FULL)
    keys_t = held[1].reshape(SEQ_ALL, PAIR).T
    r.grad_q[...] = jnp.zeros_like(r.grad_q)
    for head in range(2):
        side = query_columns(queries, head)
        r.query_side[head] = side.astype(LOW)
        r.query_plain[head] = jnp.where(own_columns(queries, head)[0], side, 0.0).astype(LOW)
        r.key_side[head] = key_columns(keys, r.neg[...], head).astype(LOW)
    plane.received(r.do_land, r.do_sems[layer])
    grads = r.do_land[...].reshape(SEQ_ALL, PAIR).astype(FULL)
    lane = lax.broadcasted_iota(jnp.int32, grads.shape, 1)
    r.do_side[0] = jnp.where(lane < HD, grads, 0.0).astype(LOW)
    r.do_side[1] = jnp.where(lane >= HD, grads, 0.0).astype(LOW)
    grads_t = r.do_land[...].reshape(SEQ_ALL, PAIR).T.astype(FULL)
    inner = []
    for head in range(2):
        side = slice(head * HD, (head + 1) * HD)
        inner.append(
            jnp.concatenate(
                [
                    jnp.sum(turned[at, side] * grads_t[side, at * BS : (at + 1) * BS], axis=0, keepdims=True)
                    for at in range(SEQ_ALL // BS)
                ],
                axis=1,
            )
        )
    left = lax.broadcasted_iota(jnp.int32, (BS, PAIR), 1) < HD
    keys_held = [keys_t[head * HD : (head + 1) * HD] for head in range(2)]
    for at in range(SEQ_ALL // BS):
        first = at * BS
        grad_k = []
        grad_v = None
        values = held[2, 2 * at : 2 * at + 2].reshape(BS, PAIR)
        for head in range(2):
            scores = dot_t(r.key_side[head, first : first + BS], r.query_side[head])
            probs = jnp.exp(scores - stats[head : head + 1])
            dprobs = dot_t(values, r.do_side[head])
            dscores = (probs * (dprobs - inner[head])).astype(LOW)
            term = dot(probs.astype(LOW), r.do_side[head])
            grad_v = term if grad_v is None else grad_v + term
            grad_k.append(dot(dscores, r.query_plain[head]))
            r.grad_q[head * HD : (head + 1) * HD] += dot(keys_held[head][:, first : first + BS], dscores)
        grad_k = jnp.where(left, grad_k[0], grad_k[1]).astype(LOW)
        grad_v = grad_v.astype(LOW)
        for half in range(2):
            to = 2 * at + half
            rows = slice(half * TOKENS, (half + 1) * TOKENS)
            r.dkv_message[to, :, :PAIR] = grad_k[rows]
            r.dkv_message[to, :, PAIR:] = grad_v[rows]
            plane.send_or_keep(r.dkv_message, r.dkv_land, r.dkv_sems[layer], to)
    for j in range(8):
        r.dq_message[j] = (r.grad_q[:, j * TOKENS : (j + 1) * TOKENS] * HD**-0.5).astype(LOW).T
        plane.send_or_keep(r.dq_message, r.dq_land, r.dq_sems[layer], j)


class Refs:
    pass


def names(**given):
    return tuple(given)


SCRATCH = dict(
    weights=pltpu.VMEM((NB, BS, BS), LOW),
    wide=pltpu.VMEM((2, QUART, BS, BS), FULL),
    notes=pltpu.VMEM((8, TOKENS), FULL),
    notes_land=pltpu.VMEM((8, 8, TOKENS), FULL),
    rows_land=pltpu.VMEM((1, TOKENS, D), LOW),
    first_land=pltpu.VMEM((1, TOKENS, D), LOW),
    second_land=pltpu.VMEM((1, TOKENS, D), LOW),
    pred_one=pltpu.VMEM((1, TOKENS, D), LOW),
    pred_two=pltpu.VMEM((1, TOKENS, D), LOW),
    hidden_one=pltpu.VMEM((TOKENS, D), FULL),
    hidden_two=pltpu.VMEM((TOKENS, D), FULL),
    middle_one=pltpu.VMEM((TOKENS, D), FULL),
    slope_one=pltpu.VMEM((DEEP, TOKENS, BS), FULL),
    slope_two=pltpu.VMEM((DEEP, TOKENS, BS), FULL),
    act_held=pltpu.VMEM((TOKENS, FF), LOW),
    left_held=pltpu.VMEM((2, 3 * WIDE + DEEP, BS, TOKENS), LOW),
    right_held=pltpu.VMEM((2, 5 * WIDE + DEEP, TOKENS, BS), LOW),
    packed=pltpu.VMEM((3, 8, TOKENS, PAIR), LOW),
    held=pltpu.VMEM((2, 3, 8, TOKENS, PAIR), LOW),
    values_t=pltpu.VMEM((PAIR, SEQ_ALL), LOW),
    expos=pltpu.VMEM((2, SEQ_ALL, BS), LOW),
    turned=pltpu.VMEM((2, SEQ_ALL // BS, PAIR, BS), FULL),
    stats=pltpu.VMEM((2, 8, SEQ_ALL), FULL),
    o_message=pltpu.VMEM((8, TOKENS, PAIR), LOW),
    o_land=pltpu.VMEM((8, TOKENS, PAIR), LOW),
    do_message=pltpu.VMEM((8, TOKENS, PAIR), LOW),
    do_land=pltpu.VMEM((8, TOKENS, PAIR), LOW),
    dq_message=pltpu.VMEM((8, TOKENS, PAIR), LOW),
    dq_land=pltpu.VMEM((8, TOKENS, PAIR), LOW),
    dkv_message=pltpu.VMEM((8, TOKENS, 2 * PAIR), LOW),
    dkv_land=pltpu.VMEM((8, TOKENS, 2 * PAIR), LOW),
    neg=pltpu.VMEM((SEQ_ALL, PAIR), FULL),
    query_side=pltpu.VMEM((2, SEQ_ALL, PAIR), LOW),
    query_plain=pltpu.VMEM((2, SEQ_ALL, PAIR), LOW),
    key_side=pltpu.VMEM((2, SEQ_ALL, PAIR), LOW),
    do_side=pltpu.VMEM((2, SEQ_ALL, PAIR), LOW),
    grad_q=pltpu.VMEM((PAIR, SEQ_ALL), FULL),
    load_sems=pltpu.SemaphoreType.DMA((7,)),
    z_sems=pltpu.SemaphoreType.DMA((2, 5, 2, 4)),
    y_sems=pltpu.SemaphoreType.DMA((2, 4, 4)),
    x_sems=pltpu.SemaphoreType.DMA((2, 2, 8)),
    core_sems=pltpu.SemaphoreType.DMA((2, 4, 8)),
    far_sems=pltpu.SemaphoreType.DMA((2, 2, 8)),
    note_send=pltpu.SemaphoreType.DMA((8,)),
    note_recv=pltpu.SemaphoreType.DMA((8,)),
    swap_local=pltpu.SemaphoreType.DMA((5,)),
    swap_send=pltpu.SemaphoreType.DMA((5,)),
    swap_recv=pltpu.SemaphoreType.DMA((5,)),
    plane_sems=pltpu.SemaphoreType.DMA((2, 7, 2, 8)),
    pool_sems=pltpu.SemaphoreType.DMA((3, 16)),
)
INPUTS = names(slots=0, lead_steps=0, flags=0, masters=0, rows_in=0, first_in=0, second_in=0, vectors=0)
OUTPUTS = names(left_pool=0, right_pool=0, pred_one_out=0, pred_two_out=0, input_grad=0, rows=0)


def model_kernel(*refs):
    r = Refs()
    for name, ref in zip(INPUTS + OUTPUTS + tuple(SCRATCH), refs):
        setattr(r, name, ref)
    for name in ("held", "turned", "stats"):
        setattr(r, name, [getattr(r, name).at[layer] for layer in range(2)])
    r.in_sems = [r.plane_sems.at[layer, pl.ds(0, 3)] for layer in range(2)]
    for at, name in enumerate(("o_sems", "do_sems", "dq_sems", "dkv_sems")):
        setattr(r, name, [r.plane_sems.at[layer, 3 + at] for layer in range(2)])
    swaps = [Swap(r.swap_local, r.swap_send, r.swap_recv, at) for at in range(5)]
    r.swap_rows = swaps[0]
    r.plane = Plane()
    vecs = r.vectors
    weights = Weights(r.slots, r.weights)

    def while_last():
        swaps[0].finish()
        r.rows[...] = jnp.zeros_like(r.rows)
        for layer in range(2):
            r.stats[layer][...] = jnp.zeros((8, SEQ_ALL), FULL)

    lane = lax.broadcasted_iota(jnp.int32, (1, TOKENS), 1)
    r.notes[...] = jnp.zeros_like(r.notes)
    r.notes[0:1] = r.flags[...].astype(FULL) - 1.0
    for at in range(2):
        r.notes[1:2] += jnp.where(lane == at, r.lead_steps[at, 0].astype(FULL), 0.0)
    gather_blocks(r, r.notes, while_last)
    mask_columns(r.notes_land, r.neg)
    leads = [r.notes_land[0, 1:2, at : at + 1] for at in range(2)]
    r.hidden_one[...] = r.rows_land[0].astype(FULL) + lead_row(vecs, leads[0])
    project(r, 0, r.hidden_one[...], vecs, weights)
    attend(r, 0)
    swaps[1].start(r.second_in, r.second_land)
    middle, result = feed(r, 0, r.hidden_one[...], vecs, weights, r.slope_one)
    r.middle_one[...] = middle
    r.pred_one[0] = result.astype(LOW)
    r.hidden_two[...] = result + lead_row(vecs, leads[1])
    project(r, 1, r.hidden_two[...], vecs, weights)
    attend(r, 1)
    swaps[3].start(r.pred_one, r.pred_one_out)
    middle, result = feed(r, 1, r.hidden_two[...], vecs, weights, r.slope_two)
    r.pred_two[0] = result.astype(LOW)
    swaps[2].start(r.first_in, r.first_land)
    swaps[1].finish()
    grad_middle = feed_back(r, 1, r.second_land[0].astype(FULL), middle, r.slope_two, vecs, weights)
    attend_back(r, 1)
    grad = project_back(r, 1, grad_middle, r.hidden_two[...], vecs, weights, leads[1])
    for source, sems in ((r.do_message, r.do_sems), (r.dkv_message, r.dkv_sems), (r.dq_message, r.dq_sems)):
        r.plane.sent(source, sems[1])
    swaps[2].finish()
    swaps[4].start(r.pred_two, r.pred_two_out)
    grad = grad + r.first_land[0].astype(FULL)
    grad_middle = feed_back(r, 0, grad, r.middle_one[...], r.slope_one, vecs, weights)
    attend_back(r, 0)
    grad = project_back(r, 0, grad_middle, r.hidden_one[...], vecs, weights, leads[0])
    r.input_grad[0] = grad.astype(LOW)
    for source, sems in ((r.do_message, r.do_sems), (r.dkv_message, r.dkv_sems), (r.dq_message, r.dq_sems)):
        r.plane.sent(source, sems[0])
    for left in (True, False):
        for layer in range(2):
            for kind in range(4):
                for copy in pool_copies(r, left, layer, kind):
                    copy.wait()
    swaps[3].finish()
    swaps[4].finish()


def model(slots, lead_steps, flags, masters, rows, first, second, vectors):
    return pl.pallas_call(
        model_kernel,
        out_shape=(
            shape((N_LEFT, BS, 4 * TOKENS)),
            shape((N_RIGHT, 4 * TOKENS, BS)),
            SHAPES["pred"],
            SHAPES["pred"],
            SHAPES["pred"],
            SHAPES["rows"],
        ),
        in_specs=[SMEM_IN] * 2 + [VMEM_AT] + [ANY_AT] * 4 + [VMEM_AT],
        out_specs=(ANY_AT,) * 4 + (VMEM_AT,) * 2,
        scratch_shapes=list(SCRATCH.values()),
        compiler_params=pltpu.CompilerParams(
            collective_id=0, has_side_effects=True, vmem_limit_bytes=63 * 1024 * 1024
        ),
        cost_estimate=pl.CostEstimate(flops=24 << 30, bytes_accessed=60 << 20, transcendentals=1 << 23),
        name="model",
    )(slots, lead_steps, flags, masters, rows, first, second, vectors)


SMEM_IN = pl.BlockSpec(memory_space=pltpu.SMEM)
VMEM_AT = pl.BlockSpec(memory_space=pltpu.VMEM)
ANY_AT = pl.BlockSpec(memory_space=pl.ANY)


def shape(dims, kind=LOW):
    return jax.ShapeDtypeStruct(dims, kind)


SHAPES = {"pred": shape((1, TOKENS, D)), "rows": shape((20, D), FULL)}


def bias_pieces():
    left = masked
    pieces = []
    for unused in range(3):
        piece = float(ml_dtypes.bfloat16(left))
        pieces.append(piece)
        left -= piece
    assert left == 0.0
    return pieces


MASK_PIECES = bias_pieces()


def own_columns(like, head):
    lane = lax.broadcasted_iota(jnp.int32, like.shape, 1)
    return (lane < HD) if head == 0 else (lane >= HD), lane - (HD if head == 0 else 0)


def key_columns(keys, neg, head):
    own, spot = own_columns(keys, head)
    side = jnp.zeros_like(keys)
    for at, piece in enumerate(MASK_PIECES):
        side = jnp.where(spot == at, neg * piece, side)
    return jnp.where(own, keys, side)


def query_columns(queries, head):
    own, spot = own_columns(queries, head)
    return jnp.where(own, queries * HD**-0.5, jnp.where((spot >= 0) & (spot < 3), 1.0, 0.0))


class Plane:
    def __init__(self):
        x, c, z, y = place()
        self.z = z
        self.me = 4 * c + 2 * x + y

    def device(self, j):
        return (turned_pair(lax.div(j, 2)), 2 * self.z + lax.rem(j, 2))

    def other(self, step):
        return lax.rem(self.me + step, 8)

    def others(self):
        return [self.device(self.other(step)) for step in range(1, 8)]

    def copy(self, src, dst, sems, send_at, recv_at, to):
        return pltpu.make_async_remote_copy(
            src_ref=src, dst_ref=dst, send_sem=sems.at[0, send_at], recv_sem=sems.at[1, recv_at],
            device_id=self.device(to), device_id_type=MESH,
        )

    def send(self, source, target, sems, to):
        self.copy(source.at[to], target.at[self.me], sems, to, self.me, to).start()

    def send_or_keep(self, source, target, sems, to):
        @pl.when(to != self.me)
        def away():
            self.send(source, target, sems, to)

        @pl.when(to == self.me)
        def keep():
            target[to] = source[to]

    def received(self, target, sems):
        for step in range(1, 8):
            j = self.other(step)
            self.copy(target.at[j], target.at[j], sems, j, j, j).wait_recv()

    def received_from(self, target, sems, j):
        @pl.when(j != self.me)
        def arrived():
            self.copy(target.at[j], target.at[j], sems, j, j, j).wait_recv()

    def sent(self, source, sems):
        for step in range(1, 8):
            j = self.other(step)
            self.copy(source.at[j], source.at[j], sems, j, j, j).wait_send()


def mask_columns(notes, neg):
    for j in range(8):
        neg[j * TOKENS : (j + 1) * TOKENS] = jnp.broadcast_to(notes[j, 0:1], (TOKENS, TOKENS)).T


LEFTS = (WIDE, WIDE, WIDE, DEEP)
RIGHTS = (3 * WIDE, WIDE, DEEP, WIDE)
LEFT_AT = (0, WIDE, 2 * WIDE, 3 * WIDE)
RIGHT_AT = (0, 3 * WIDE, 4 * WIDE, 4 * WIDE + DEEP)
N_LEFT = 3 * WIDE + DEEP
N_RIGHT = 5 * WIDE + DEEP


def pools_of(block):
    left = jnp.zeros_like(block)
    right = jnp.zeros_like(block)
    for at, base in enumerate((QKV_AT, OUT_AT, UP_AT, DOWN_AT)):
        inside = block >= base
        cols = RIGHTS[at]
        left = jnp.where(inside, LEFT_AT[at] + (block - base) // cols, left)
        right = jnp.where(inside, RIGHT_AT[at] + (block - base) % cols, right)
    return left, right


def halves(value):
    high = value.astype(LOW)
    return high, (value - high.astype(FULL)).astype(LOW)


def fine(left, right):
    return dot(
        jnp.concatenate([left[0], left[1], left[0]], axis=1),
        jnp.concatenate([right[0], right[0], right[1]], axis=0),
    )


def statistic(gram, shrink, diag, eye):
    return jnp.where(eye, 0.5 * diag, 0.0) + shrink * gram


def roots(stats, eye):
    scales = [jnp.sqrt(jnp.sum(jnp.sum(stat * stat, axis=1, keepdims=True), axis=0, keepdims=True)) for stat in stats]
    moving = [stat / scale for stat, scale in zip(stats, scales)]
    approx = [None] * len(stats)
    ahead = range(len(stats))
    for iteration in range(ITERS):
        factors = [(jnp.where(eye, 5.0, 0.0) - moving[i]) * 0.25 for i in ahead]
        parts = [halves(factor) for factor in factors]
        if iteration == 0:
            approx = [factors[i] * lax.rsqrt(jnp.sqrt(scales[i])) for i in ahead]
        else:
            approx = [fine(halves(approx[i]), parts[i]) for i in ahead]
        if iteration < ITERS - 1:
            squares = [halves(fine(parts[i], parts[i])) for i in ahead]
            fourths = [halves(fine(squares[i], squares[i])) for i in ahead]
            moving = [fine(fourths[i], halves(moving[i])) for i in ahead]
    return approx


PAIRED = 2
SUM_SCRATCH = dict(
    left_t=pltpu.VMEM((N_LEFT, BS, 4 * TOKENS), LOW),
    right_pool=pltpu.VMEM((N_RIGHT, 4 * TOKENS, BS), LOW),
    x_stage=pltpu.VMEM((2, 2, 4, PAIRED, BS, BS), LOW),
    x_land=pltpu.VMEM((2, 2, 4, PAIRED, BS, BS), LOW),
    yb_stage=pltpu.VMEM((4, QUART, BS, BS), LOW),
    yb_land=pltpu.VMEM((4, QUART, BS, BS), LOW),
    ym_stage=pltpu.VMEM((2, 4, PAIRED, BS, BS), LOW),
    ym_land=pltpu.VMEM((2, 4, PAIRED, BS, BS), LOW),
    zb_stage=pltpu.VMEM((4, QUART, BS, BS), LOW),
    zb_land=pltpu.VMEM((3, QUART, BS, BS), LOW),
    zm_stage=pltpu.VMEM((2, 4, PAIRED, BS, BS), LOW),
    zm_land=pltpu.VMEM((2, 3, PAIRED, BS, BS), LOW),
    both_stage=pltpu.VMEM((2, PAIRED, BS, BS), LOW),
    both_land=pltpu.VMEM((PAIRED, BS, BS), LOW),
    own=pltpu.VMEM((6, BS, BS), LOW),
    staged=pltpu.VMEM((6, BS, BS), LOW),
    pair_rows=pltpu.VMEM((20, D), FULL),
    chip_rows=pltpu.VMEM((20, D), FULL),
    plane_rows=pltpu.VMEM((20, D), FULL),
    row_land=pltpu.VMEM((3, 20, D), FULL),
    row_z=pltpu.VMEM((4, 20, D), FULL),
    pool_sems=pltpu.SemaphoreType.DMA((2,)),
    send_sems=pltpu.SemaphoreType.DMA((11, 4)),
    recv_sems=pltpu.SemaphoreType.DMA((11, 4)),
    row_send=pltpu.SemaphoreType.DMA((6,)),
    row_recv=pltpu.SemaphoreType.DMA((6,)),
    share_send=pltpu.SemaphoreType.DMA((6, 6)),
    share_recv=pltpu.SemaphoreType.DMA((6, 6)),
    local_sems=pltpu.SemaphoreType.DMA((9,)),
    swap_local=pltpu.SemaphoreType.DMA((1,)),
    swap_send=pltpu.SemaphoreType.DMA((1,)),
    swap_recv=pltpu.SemaphoreType.DMA((1,)),
)
SUM_INPUTS = names(left_ids=0, right_ids=0, rows_in=0, left_diag=0, right_diag=0, grad_in=0, left_in=0, right_in=0)
SUM_OUTPUTS = names(rows_out=0, grads_out=0, moves_out=0, grad_out=0)


def update_kernel(*refs):
    r = Refs()
    for name, ref in zip(SUM_INPUTS + SUM_OUTPUTS + tuple(SUM_SCRATCH), refs):
        setattr(r, name, ref)
    here = [
        pltpu.make_async_copy(r.right_in, r.right_pool, r.pool_sems.at[0]),
        pltpu.make_async_copy(r.left_in, r.left_t, r.pool_sems.at[1]),
    ]
    for copy in here:
        copy.start()
    x, c, z, y = place()
    samp = 2 * x + c
    blk = 2 * z + y
    to_c = (2 * x + 1 - c, blk)
    to_x = (2 * (1 - x) + c, blk)
    to_y = (samp, 2 * z + 1 - y)
    to_z = [(samp, 2 * lax.rem(z + step, 4) + y) for step in (1, 2, 3)]
    meet_all()
    swap = Swap(r.swap_local, r.swap_send, r.swap_recv)
    swap.start(r.grad_in, r.grad_out)
    row_copies = [push(r.rows_in, r.row_land.at[0], r.row_send.at[0], r.row_recv.at[0], to_c)]
    eye = lax.broadcasted_iota(jnp.int32, (BS, BS), 0) == lax.broadcasted_iota(jnp.int32, (BS, BS), 1)

    def group(half, k):
        return 2 * lax.rem(z + 1 + k, 4) + (1 - y if half == 0 else y)

    def part(half, k, offset, count=PAIRED):
        slot = group(half, k) * GROUP + c * HALF + offset
        return [dot(r.left_t[r.left_ids[slot + i]], r.right_pool[r.right_ids[slot + i]]) for i in range(count)]

    def mine(batch):
        return x * 8 + PAIRED * batch

    def other(batch):
        return (1 - x) * 8 + PAIRED * batch

    both = QUART

    def link(kind, k, stage, land, to):
        return pltpu.make_async_remote_copy(
            src_ref=stage, dst_ref=land, send_sem=r.send_sems.at[kind, k], recv_sem=r.recv_sems.at[kind, k],
            device_id=to, device_id_type=MESH,
        )

    def along_x(batch, half, k):
        return link(2 * batch + half, k, r.x_stage.at[batch, half, k], r.x_land.at[batch, half, k], to_x)

    def along_y_both(k):
        return link(4, k, r.yb_stage.at[k], r.yb_land.at[k], to_y)

    def along_y(batch, k):
        return link(5 + batch, k, r.ym_stage.at[batch, k], r.ym_land.at[batch, k], to_y)

    def along_z_both(k):
        return link(7, k, r.zb_stage.at[k], r.zb_land.at[k], (samp, group(1, k)))

    def along_z(batch, k):
        return link(8 + batch, k, r.zm_stage.at[batch, k], r.zm_land.at[batch, k], (samp, group(1, k)))

    def last():
        return link(10, 0, r.both_stage.at[1 - x], r.both_land, to_x)

    def send_x(batch, half, k):
        for i, value in enumerate(part(half, k, other(batch))):
            r.x_stage[batch, half, k, i] = value.astype(LOW)
        along_x(batch, half, k).start()

    def add_x_send_y(batch, k):
        values = part(0, k, mine(batch))
        along_x(batch, 0, k).wait_recv()
        for i, value in enumerate(values):
            r.ym_stage[batch, k, i] = (value + r.x_land[batch, 0, k, i].astype(FULL)).astype(LOW)
        along_y(batch, k).start()

    def add_both_send_z(batch, k):
        values = part(1, k, mine(batch))
        along_x(batch, 1, k).wait_recv()
        values = [value + r.x_land[batch, 1, k, i].astype(FULL) for i, value in enumerate(values)]
        along_y(batch, k).wait_recv()
        for i, value in enumerate(values):
            r.zm_stage[batch, k, i] = (value + r.ym_land[batch, k, i].astype(FULL)).astype(LOW)

        @pl.when(k < 3)
        def send_on():
            along_z(batch, k).start()

    def each(step):
        def body(k, carry):
            step(k)
            return carry

        lax.fori_loop(0, 4, body, 0)

    def slot_of(i, far=False):
        side = (1 - x) if far else x
        return c * HALF + (side * 8 + i if i < QUART else QUART + 2 * side + i - QUART)

    def share(kind, k, src, dst, to):
        return pltpu.make_async_remote_copy(
            src_ref=src, dst_ref=dst, send_sem=r.share_send.at[kind, k], recv_sem=r.share_recv.at[kind, k],
            device_id=to, device_id_type=MESH,
        )

    def grad_to(kind, pair, to):
        place_out = r.grads_out.at[pl.ds(slot_of(PAIRED * pair), PAIRED)]
        return share(kind, pair, r.own.at[pl.ds(PAIRED * pair, PAIRED)], place_out, to)

    def grad_on(pair):
        place_out = r.grads_out.at[pl.ds(slot_of(PAIRED * pair, True), PAIRED)]
        return share(2, pair, place_out, place_out, to_c)

    def grad_kept(pair):
        place_out = r.grads_out.at[pl.ds(slot_of(PAIRED * pair), PAIRED)]
        return pltpu.make_async_copy(r.own.at[pl.ds(PAIRED * pair, PAIRED)], place_out, r.local_sems.at[6 + pair])

    def move_to(kind, i, to):
        return share(kind, i, r.staged.at[i], r.moves_out.at[slot_of(i)], to)

    def move_on(i):
        place_out = r.moves_out.at[slot_of(i, True)]
        return share(5, i, place_out, place_out, to_c)

    def move_kept(i):
        return pltpu.make_async_copy(r.staged.at[i], r.moves_out.at[slot_of(i)], r.local_sems.at[i])

    def share_grads(pair, across=True):
        if across:
            grad_to(0, pair, to_x).start()
        grad_to(1, pair, to_c).start()
        grad_kept(pair).start()

    def directions(pair, across=True):
        held = []
        stats = []
        for i in range(PAIRED * pair, PAIRED * pair + PAIRED):
            low = r.own[i]
            grad = low.astype(FULL)
            mean = jnp.sum(jnp.sum(grad * grad, axis=1, keepdims=True), axis=0, keepdims=True) / (BS * BS)
            shrink = 0.5 / (mean + 1e-06)
            low_t = grad.T.astype(LOW)
            slot = slot_of(i)
            stats.append(statistic(dot(low, low_t), shrink, r.left_diag[pl.ds(slot, 1)], eye))
            stats.append(statistic(dot(low_t, low), shrink, r.right_diag[pl.ds(slot, 1)], eye))
            held.append((i, low, lax.rsqrt(mean + 1e-06)))
        sides = roots(stats, eye)
        for n, (i, low, rate) in enumerate(held):
            high, rest = halves(sides[2 * n])
            turned = dot(jnp.concatenate([high, rest], axis=1), jnp.concatenate([low, low], axis=0)) * rate
            r.staged[i] = fine(halves(turned), halves(sides[2 * n + 1])).astype(LOW)
            if across:
                move_to(3, i, to_x).start()
            move_to(4, i, to_c).start()
            move_kept(i).start()

    def finish_batch(batch):
        for k in range(3):
            along_z(batch, k).wait_recv()
        for i in range(PAIRED):
            value = r.zm_stage[batch, 3, i].astype(FULL)
            for k in range(3):
                value = value + r.zm_land[batch, k, i].astype(FULL)
            r.own[PAIRED * batch + i] = value.astype(LOW)
        share_grads(batch)

    def pass_on(pair):
        grad_to(0, pair, to_x).wait_recv()
        grad_on(pair).start()
        for i in range(PAIRED * pair, PAIRED * pair + PAIRED):
            move_to(3, i, to_x).wait_recv()
            move_on(i).start()

    for copy in here:
        copy.wait()

    @each
    def begin(k):
        for i, value in enumerate(part(0, k, both, QUART)):
            r.yb_stage[k, i] = value.astype(LOW)
        along_y_both(k).start()
        send_x(0, 0, k)

    @each
    def more(k):
        send_x(0, 1, k)

    row_copies[0].wait_recv()
    r.pair_rows[...] = r.rows_in[...] + r.row_land[0]
    row_copies.append(push(r.pair_rows, r.row_land.at[1], r.row_send.at[1], r.row_recv.at[1], to_x))

    @each
    def middle(k):
        add_x_send_y(0, k)
        values = part(1, k, both, QUART)
        along_y_both(k).wait_recv()
        for i, value in enumerate(values):
            r.zb_stage[k, i] = (value + r.yb_land[k, i].astype(FULL)).astype(LOW)

        @pl.when(k < 3)
        def send_on():
            along_z_both(k).start()

        send_x(1, 0, k)

    row_copies[1].wait_recv()
    r.chip_rows[...] = r.pair_rows[...] + r.row_land[1]
    row_copies.append(push(r.chip_rows, r.row_land.at[2], r.row_send.at[2], r.row_recv.at[2], to_y))

    @each
    def late(k):
        add_both_send_z(0, k)

    for k in range(3):
        along_z_both(k).wait_recv()
    for i in range(QUART):
        value = r.zb_stage[3, i].astype(FULL)
        for k in range(3):
            value = value + r.zb_land[k, i].astype(FULL)
        r.both_stage[i // 2, i % 2] = value.astype(LOW)
    last().start()

    @each
    def more_again(k):
        send_x(1, 1, k)

    @each
    def middle_again(k):
        add_x_send_y(1, k)

    row_copies[2].wait_recv()
    r.plane_rows[...] = r.chip_rows[...] + r.row_land[2]
    for step in range(3):
        row_copies.append(
            push(r.plane_rows, r.row_z.at[z], r.row_send.at[3 + step], r.row_recv.at[3 + step], to_z[step])
        )
    r.row_z[z] = r.plane_rows[...]
    last().wait_recv()
    for i in range(PAIRED):
        r.own[QUART + i] = (r.both_stage[x, i].astype(FULL) + r.both_land[i].astype(FULL)).astype(LOW)
    share_grads(2, False)
    directions(2, False)

    @each
    def late_again(k):
        add_both_send_z(1, k)

    grad_to(0, 2, to_x).start()
    for i in (QUART, QUART + 1):
        move_to(3, i, to_x).start()
    finish_batch(0)
    directions(0)
    for step in range(3):
        row_copies[3 + step].wait_recv()
    r.rows_out[...] = (r.row_z[0] + r.row_z[1]) + (r.row_z[2] + r.row_z[3])
    finish_batch(1)
    pass_on(2)
    directions(1)
    pass_on(0)
    pass_on(1)
    for pair in range(3):
        grad_to(1, pair, to_c).wait_recv()
        grad_on(pair).wait_recv()
        grad_to(0, pair, to_x).wait_send()
        grad_to(1, pair, to_c).wait_send()
        grad_on(pair).wait_send()
        grad_kept(pair).wait()
    for i in range(6):
        move_to(4, i, to_c).wait_recv()
        move_on(i).wait_recv()
        move_to(3, i, to_x).wait_send()
        move_to(4, i, to_c).wait_send()
        move_on(i).wait_send()
        move_kept(i).wait()
    for copy in row_copies:
        copy.wait_send()
    last().wait_send()

    @each
    def drain(k):
        along_y_both(k).wait_send()
        for batch in range(2):
            along_x(batch, 0, k).wait_send()
            along_x(batch, 1, k).wait_send()
            along_y(batch, k).wait_send()

        @pl.when(k < 3)
        def sent_on():
            along_z_both(k).wait_send()
            for batch in range(2):
                along_z(batch, k).wait_send()

    swap.finish()


def update(left_ids, right_ids, rows, left_start, right_start, grad, left_pool, right_pool):
    return pl.pallas_call(
        update_kernel,
        out_shape=(SHAPES["rows"], shape((GROUP, BS, BS)), shape((GROUP, BS, BS)), SHAPES["pred"]),
        in_specs=[SMEM_IN] * 2 + [VMEM_AT] * 3 + [ANY_AT] * 3,
        out_specs=(VMEM_AT,) + (ANY_AT,) * 3,
        scratch_shapes=list(SUM_SCRATCH.values()),
        compiler_params=pltpu.CompilerParams(
            collective_id=1, has_side_effects=True, vmem_limit_bytes=VMEM_ASK
        ),
        cost_estimate=pl.CostEstimate(flops=36 << 30, bytes_accessed=40 << 20, transcendentals=0),
        name="update",
    )(left_ids, right_ids, rows, left_start, right_start, grad, left_pool, right_pool)


STEP = 8


def finish_kernel(
    grad, move, weight, left_diag, right_diag, rows, vecs, moment, input_grad, pred_one, pred_two,
    grad_out, left_out, right_out, new_out, low_out,
    rows_out, moment_out, vecs_out, input_out, pred_one_out, pred_two_out,
):
    eye = lax.broadcasted_iota(jnp.int32, (BS, BS), 0) == lax.broadcasted_iota(jnp.int32, (BS, BS), 1)
    at = pl.program_id(0)

    def mean(value):
        return jnp.sum(jnp.sum(value, axis=1, keepdims=True), axis=0, keepdims=True) / (BS * BS)

    for i in range(STEP):
        low = grad[i]
        full = low.astype(FULL)
        grad_out[i] = full
        shrink = 0.5 / (mean(full * full) + 1e-06)
        low_t = full.T.astype(LOW)
        left_out[i] = statistic(dot(low, low_t), shrink, left_diag[pl.ds(at * STEP + i, 1)], eye)
        right_out[i] = statistic(dot(low_t, low), shrink, right_diag[pl.ds(at * STEP + i, 1)], eye)
        step = move[i].astype(FULL)
        start = weight[i]
        ratio = jnp.sqrt(mean(start * start)) * lax.rsqrt(mean(step * step) + 1e-06)
        new = start - step_rate * ratio * step
        new_out[i] = new
        low_out[i] = new.astype(LOW)

    @pl.when(at == 0)
    def small():
        value = rows[...]
        scaled = value * lax.rsqrt(jnp.mean(value * value, axis=1, keepdims=True) + 1e-06)
        moments = 0.5 * moment[...] + 0.5 * scaled * scaled
        rows_out[...] = value
        moment_out[...] = moments
        vecs_out[...] = vecs[...] - vector_rate * scaled * lax.rsqrt(moments)
        input_out[...] = input_grad[...].astype(FULL)
        pred_one_out[...] = pred_one[...]
        pred_two_out[...] = pred_two[...]


def finish_slots(grads, moves, masters, left_start, right_start, rows, vecs, moment, input_grad, pred_one, pred_two):
    block = pl.BlockSpec((STEP, BS, BS), lambda i: (i, 0, 0))
    diag = pl.BlockSpec((GROUP, BS), lambda i: (0, 0))
    row = pl.BlockSpec((20, D), lambda i: (0, 0))
    wide = pl.BlockSpec((1, TOKENS, D), lambda i: (0, 0, 0))
    return pl.pallas_call(
        finish_kernel,
        grid=(GROUP // STEP,),
        compiler_params=pltpu.CompilerParams(vmem_limit_bytes=VMEM_ASK),
        out_shape=tuple(shape((GROUP, BS, BS), kind) for kind in (FULL, FULL, FULL, FULL, LOW))
        + (SHAPES["rows"],) * 3
        + (shape((1, TOKENS, D), FULL),)
        + (SHAPES["pred"],) * 2,
        in_specs=[block, block, block, diag, diag, row, row, row, wide, wide, wide],
        out_specs=(block,) * 5 + (row,) * 3 + (wide,) * 3,
        cost_estimate=pl.CostEstimate(flops=2 << 30, bytes_accessed=41 << 20, transcendentals=0),
        name="finish_slots",
    )(grads, moves, masters, left_start, right_start, rows, vecs, moment, input_grad, pred_one, pred_two)


def local_tuned(
    inputs,
    cot_first,
    cot_second,
    valid_flags,
    lead_steps,
    masters,
    assignment,
    left_start,
    right_start,
    vectors,
    vec_moment,
):
    left_pool, right_pool, pred_one, pred_two, input_grad, rows = model(
        assignment, lead_steps, valid_flags, masters, inputs, cot_first, cot_second, vectors
    )
    position = jnp.arange(NB, dtype=jnp.int32)
    inverse = jnp.sum(
        jnp.where(assignment[None, :] == position[:, None], position[None, :], 0), axis=1
    )
    left_ids, right_ids = pools_of(inverse)
    vec_grads, grads, moves, input_grad = update(
        left_ids, right_ids, rows, left_start, right_start, input_grad, left_pool, right_pool
    )
    (
        matrix_grads, left_stats, right_stats, new_masters, new_copies,
        vec_grads, vec_moments, new_vectors, input_grad, pred_one, pred_two,
    ) = finish_slots(
        grads, moves, masters, left_start, right_start, vec_grads, vectors, vec_moment, input_grad, pred_one, pred_two
    )
    return (
        pred_one,
        pred_two,
        input_grad,
        matrix_grads,
        left_stats,
        right_stats,
        new_masters,
        new_copies,
        vec_grads,
        vec_moments,
        new_vectors,
    )


def solution(mesh):
    placed = (
        P("samp", "blk", None),
        P("samp", "blk", None),
        P("samp", "blk", None),
        P("samp", "blk"),
        P(None, "samp"),
        P("blk", None, None),
        P(),
        P("blk", None),
        P("blk", None),
        P(),
        P(),
    )
    fits = mesh.shape["samp"] == 4 and mesh.shape["blk"] == 8
    return jax.shard_map(
        local_tuned if fits else local_any,
        mesh=mesh,
        in_specs=placed,
        out_specs=(
            P("samp", "blk", None),
            P("samp", "blk", None),
            P("samp", "blk", None),
            P("blk", None, None),
            P("blk", None, None),
            P("blk", None, None),
            P("blk", None, None),
            P("blk", None, None),
            P(),
            P(),
            P(),
        ),
        check_vma=False,
    )
```
